32 devices in a mesh: ctx: 16 (over z, x, core), tp: 2 (over y).
Axes of the slice: x: 2, y: 2, z: 4, core: 2. Of those that a mesh axis runs over, the one named last changes fastest.
Arguments:
- features: bfloat16 [3, 2048, 8192], P(None, 'ctx', 'tp'), may hold values from -6 to 6
- conv_weight: float32 [3, 3, 8192], replicated, may hold values from -3 to 3
- decay_rates: float32 [16, 8192], P(None, ('tp', 'ctx')), may hold values from 1e-05 to 0.03
- residues: float32 [16, 8192], P(None, ('tp', 'ctx')), may hold values from -1.5 to 1.5
- skip_gain: float32 [8192], P(('tp', 'ctx')), may hold values from -1 to 1
- out_weight: bfloat16 [8192, 8192], P('tp', 'ctx'), may hold values from -0.0625 to 0.0625
Outputs:
- mixed: bfloat16 [2048, 8192], P('ctx', 'tp')
The draws below stay inside these ranges and needn't reach their ends.
All inputs are finite; a program needn't handle non-finite values.
Results may differ from the reference program's by a relative error of at most 0.014.
Values may be sent and summed in bfloat16 or wider, within the bound.
No kernel may reach another device: no remote copies, remote signals or barrier semaphores. Data moves between devices by JAX's collectives and lax.ppermute only.
A program may use at most 192 MiB of HBM per device.

```python
import math
import jax
import jax.numpy as jnp
from jax import lax

D = 8192
MODES = 16
SHORT = 3
SEQ = 2048
N_TP = 2


def shard_levels(stream_key, extent, shards, smallest, top_value):
    gain, own = 1.0, jax.random.fold_in(stream_key, 6)
    for dim, shards_of in shards:
        steps = jnp.exp(jax.random.uniform(jax.random.fold_in(own, dim), (shards_of,), jnp.float32, smallest / len(shards), top_value / len(shards)))
        gain = gain * jnp.repeat(steps, extent[dim] // shards_of).reshape([-1 if axis == dim else 1 for axis in range(len(extent))])
    return gain


def scatter_about(own_key, extent, scale, reach, split=(), kind=jnp.bfloat16):
    result = jax.random.normal(own_key, extent, jnp.float32) * scale
    if len(split) > 0:
        result = shard_levels(own_key, extent, split, -0.22, 0.18) * result
    return jnp.clip(result, min=-reach, max=reach).astype(kind)


def setup_inputs(seed: int = 0) -> dict:
    key_list = jax.random.split(jax.random.key(seed), 7)
    features = scatter_about(key_list[0], (3, SEQ, D), 1.0, 6.0, ((1, 16), (2, 2)))
    conv_weight = scatter_about(key_list[1], (3, SHORT, D), 0.6, 3.0, (), jnp.float32)
    decay_rates = jnp.clip(jnp.exp(math.log(0.03) - 8.006368 * jax.random.uniform(key_list[2], (MODES, D), jnp.float32) ** shard_levels(key_list[2], (MODES, D), ((1, 32),), -0.2, 0.2)), 9.999999747378752e-06, 0.03)
    residues = scatter_about(key_list[3], (MODES, D), 0.25, 1.5, ((1, 32),), jnp.float32)
    skip_gain = jnp.clip(jax.random.uniform(key_list[4], (D,), jnp.float32, -1.0, 1.0) * shard_levels(key_list[4], (D,), ((0, 32),), -0.4, 0.0), -1.0, 1.0)
    out_weight = scatter_about(key_list[5], (D, D), D ** -0.5, 0.0625, ((0, 2), (1, 16)))
    return {"features": features, "conv_weight": conv_weight, "decay_rates": decay_rates, "residues": residues, "skip_gain": skip_gain, "out_weight": out_weight}


def short_conv(signal_in, weights):
    values = signal_in.astype(jnp.float32)
    padded = jnp.pad(values, ((2, 0), (0, 0)))
    return weights[0] * values + weights[1] * padded[1:-1] + weights[2] * padded[:-2]

def filter_block(rates_block, residues_block, length):
    steps_axis = jnp.arange(length, dtype=jnp.float32)

    def add_mode(mode_index, total):
        rate_now = rates_block[mode_index][:, None]
        weight_now = residues_block[mode_index][:, None]
        return total + weight_now * jnp.sqrt(2.0 * rate_now) * jnp.exp(-rate_now * steps_axis)
    start = jnp.zeros((rates_block.shape[1], length), jnp.float32)
    return lax.fori_loop(0, rates_block.shape[0], add_mode, start)

def reference(features, conv_weight, decay_rates, residues, skip_gain, out_weight):
    query = short_conv(features[0], conv_weight[0])
    keyed = short_conv(features[1], conv_weight[1])
    valued = short_conv(features[2], conv_weight[2])
    gate_in = (keyed * valued).astype(jnp.bfloat16)
    width = gate_in.shape[1]
    length = gate_in.shape[0]
    block = math.gcd(width, 128)
    count = width // block
    channels = gate_in.astype(jnp.float32).T.reshape(count, block, length)
    rates_blocks = decay_rates.reshape(decay_rates.shape[0], count, block).transpose(1, 0, 2)
    residue_blocks = residues.reshape(residues.shape[0], count, block).transpose(1, 0, 2)

    def one_block(items):
        signal, rates_block, residues_block = items
        kernel = filter_block(rates_block, residues_block, length)
        spectrum = jnp.fft.rfft(signal, n=2 * length, axis=1) * jnp.fft.rfft(kernel, n=2 * length, axis=1)
        return jnp.fft.irfft(spectrum, n=2 * length, axis=1)[:, :length]
    convolved = lax.map(one_block, (channels, rates_blocks, residue_blocks)).reshape(width, length)
    long_out = (convolved + skip_gain[:, None] * gate_in.astype(jnp.float32).T).astype(jnp.bfloat16)
    gated = (query * long_out.T.astype(jnp.float32)).astype(jnp.bfloat16)
    share = width // N_TP
    total = jnp.zeros((length, width), jnp.float32)
    for block_index in range(N_TP):
        part = jnp.dot(gated[:, block_index * share:(block_index + 1) * share], out_weight[block_index * share:(block_index + 1) * share, :], preferred_element_type=jnp.float32).astype(jnp.bfloat16)
        part = lax.optimization_barrier(part)
        total = total + part.astype(jnp.float32)
    return total.astype(jnp.bfloat16)
```

```python
import functools

import jax
import jax.numpy as jnp
from jax import lax
from jax.experimental import pallas as pl
from jax.experimental.pallas import tpu as pltpu
from jax.sharding import PartitionSpec as P

LANES = 128
SUBLANES = 8
GROUP = LANES * SUBLANES
HALO = 2
CHUNKS = 4


def spread(scratch, halo, block, pitch):
    tokens = block.shape[0]
    for tile in range(SUBLANES):
        lanes = pl.ds(tile * LANES, LANES)
        scratch[pl.ds(tile * pitch + SUBLANES - HALO, HALO), :] = halo[:, lanes].astype(jnp.float32)
        scratch[pl.ds(tile * pitch + SUBLANES, tokens), :] = block[:, lanes].astype(jnp.float32)


def token(scratch, index, pitch):
    return scratch[pl.ds(index, SUBLANES, stride=pitch), :]


def state_kernel(modes, k_ref, v_ref, k_halo, v_halo, taps, params, u_ref, z_ref, k_rows, v_rows):
    tokens = k_ref.shape[1]
    pitch = tokens + SUBLANES
    spread(k_rows, k_halo.at[0], k_ref.at[0], pitch)
    spread(v_rows, v_halo.at[0], v_ref.at[0], pitch)
    k_taps = [taps[1, j] for j in range(3)]
    v_taps = [taps[2, j] for j in range(3)]
    decay = [jnp.exp(-params[m]) for m in range(modes)]

    def step(index, carry):
        k1, k2, v1, v2, states = carry
        for inner in range(SUBLANES):
            now = index * SUBLANES + inner
            k0 = token(k_rows, now + SUBLANES, pitch)
            v0 = token(v_rows, now + SUBLANES, pitch)
            keyed = k_taps[0] * k0 + k_taps[1] * k1 + k_taps[2] * k2
            valued = v_taps[0] * v0 + v_taps[1] * v1 + v_taps[2] * v2
            u = (keyed * valued).astype(jnp.bfloat16).astype(jnp.float32)
            u_ref[0, now] = u
            states = tuple(states[m] * decay[m] + u for m in range(modes))
            k1, k2, v1, v2 = k0, k1, v0, v1
        return k1, k2, v1, v2, states

    start = (
        token(k_rows, SUBLANES - 1, pitch),
        token(k_rows, SUBLANES - 2, pitch),
        token(v_rows, SUBLANES - 1, pitch),
        token(v_rows, SUBLANES - 2, pitch),
        tuple(jnp.zeros((SUBLANES, LANES), jnp.float32) for _ in range(modes)),
    )
    states = lax.fori_loop(0, tokens // SUBLANES, step, start)[-1]
    z_ref[0] = jnp.concatenate(states, axis=0).astype(z_ref.dtype)


def gated_kernel(modes, me_ref, q_ref, q_halo, u_ref, taps, params, z_ref, out_ref, q_rows, out_rows):
    tokens = q_ref.shape[1]
    pitch = tokens + SUBLANES
    spread(q_rows, q_halo.at[0], q_ref.at[0], pitch)
    q_taps = [taps[0, j] for j in range(3)]
    block_decay = jnp.concatenate([jnp.exp(-float(tokens) * params[m]) for m in range(modes)], axis=0)

    def carry_block(block, total):
        return total * block_decay + z_ref[block, 0].astype(jnp.float32)

    incoming = lax.fori_loop(
        0, me_ref[0], carry_block, jnp.zeros((modes * SUBLANES, LANES), jnp.float32)
    )
    decay = [jnp.exp(-params[m]) for m in range(modes)]
    weight = [params[modes + m] * jnp.sqrt(2.0 * params[m]) for m in range(modes)]
    skip = params[2 * modes]

    def step(index, carry):
        q1, q2, states = carry
        for inner in range(SUBLANES):
            now = index * SUBLANES + inner
            u = u_ref[0, now]
            q0 = token(q_rows, now + SUBLANES, pitch)
            query = q_taps[0] * q0 + q_taps[1] * q1 + q_taps[2] * q2
            states = tuple(states[m] * decay[m] + u for m in range(modes))
            terms = [weight[m] * states[m] for m in range(modes)] + [skip * u]
            while len(terms) > 1:
                terms = [a + b for a, b in zip(terms[::2], terms[1::2])] + terms[len(terms) & ~1 :]
            long_out = terms[0].astype(jnp.bfloat16).astype(jnp.float32)
            out_rows[pl.ds(now, SUBLANES, stride=pitch), :] = query * long_out
            q1, q2 = q0, q1
        return q1, q2, states

    start = (
        token(q_rows, SUBLANES - 1, pitch),
        token(q_rows, SUBLANES - 2, pitch),
        tuple(incoming[m * SUBLANES : (m + 1) * SUBLANES] for m in range(modes)),
    )
    lax.fori_loop(0, tokens // SUBLANES, step, start)
    for tile in range(SUBLANES):
        out_ref[:, pl.ds(tile * LANES, LANES)] = out_rows[pl.ds(tile * pitch, tokens), :].astype(
            out_ref.dtype
        )


def tp_exchange(parts):
    count = lax.axis_size("tp")
    if count != 2:
        return lax.all_to_all(parts, "tp", split_axis=0, concat_axis=0, tiled=True)
    me = lax.axis_index("tp")
    mine = lax.dynamic_index_in_dim(parts, me, 0, keepdims=False)
    other = lax.dynamic_index_in_dim(parts, 1 - me, 0, keepdims=False)
    got = lax.ppermute(other, "tp", [(0, 1), (1, 0)])
    return jnp.where(me == 0, jnp.stack([mine, got]), jnp.stack([got, mine]))


def per_device(features, conv_weight, decay_rates, residues, skip_gain, out_weight):
    tokens, width = features.shape[1:]
    modes = decay_rates.shape[0]
    ctx, tp = lax.axis_size("ctx"), lax.axis_size("tp")
    groups = width // GROUP
    me = lax.axis_index("ctx")
    tp_me = lax.axis_index("tp")

    halo = lax.ppermute(
        features[:, tokens - HALO :, :], "ctx", [(i, i + 1) for i in range(ctx - 1)]
    )
    params = jnp.concatenate([decay_rates, residues, skip_gain[None]], axis=0)
    params = lax.all_gather(params, "ctx", axis=0)
    params = params.transpose(1, 0, 2).reshape(2 * modes + 1, width // LANES, LANES)
    taps = lax.dynamic_slice_in_dim(conv_weight, tp_me * width, width, 2)
    taps = taps.reshape(3, 3, width // LANES, LANES)

    def stream(which):
        return pl.BlockSpec((1, tokens, GROUP), lambda g: (which, 0, g))

    def stream_halo(which):
        return pl.BlockSpec((1, HALO, GROUP), lambda g: (which, 0, g))

    taps_spec = pl.BlockSpec((3, 3, SUBLANES, LANES), lambda g: (0, 0, g, 0))
    params_spec = pl.BlockSpec((2 * modes + 1, SUBLANES, LANES), lambda g: (0, g, 0))
    u_spec = pl.BlockSpec((1, tokens, SUBLANES, LANES), lambda g: (g, 0, 0, 0))
    rows = pltpu.VMEM((SUBLANES * (tokens + SUBLANES), LANES), jnp.float32)
    limit = pltpu.CompilerParams(vmem_limit_bytes=32 * 1024 * 1024)

    u, z = pl.pallas_call(
        functools.partial(state_kernel, modes),
        grid=(groups,),
        in_specs=[stream(1), stream(2), stream_halo(1), stream_halo(2), taps_spec, params_spec],
        out_specs=[u_spec, pl.BlockSpec((1, modes * SUBLANES, LANES), lambda g: (g, 0, 0))],
        out_shape=[
            jax.ShapeDtypeStruct((groups, tokens, SUBLANES, LANES), jnp.float32),
            jax.ShapeDtypeStruct((groups, modes * SUBLANES, LANES), jnp.bfloat16),
        ],
        scratch_shapes=[rows, rows],
        compiler_params=limit,
        name="block_states",
    )(features, features, halo, halo, taps, params)

    blocks = lax.all_gather(z, "ctx", axis=0)

    gated = pl.pallas_call(
        functools.partial(gated_kernel, modes),
        grid=(groups,),
        in_specs=[
            pl.BlockSpec(memory_space=pltpu.SMEM),
            stream(0),
            stream_halo(0),
            u_spec,
            taps_spec,
            params_spec,
            pl.BlockSpec((ctx, 1, modes * SUBLANES, LANES), lambda g: (0, g, 0, 0)),
        ],
        out_specs=pl.BlockSpec((tokens, GROUP), lambda g: (0, g)),
        out_shape=jax.ShapeDtypeStruct((tokens, width), jnp.bfloat16),
        scratch_shapes=[rows, rows],
        compiler_params=limit,
        name="gated_block",
    )(jnp.reshape(me, (1,)), features, halo, u, taps, params, blocks)

    columns = out_weight.shape[1]
    part = tokens // CHUNKS
    outs = []
    for chunk in range(CHUNKS):
        mine = gated[chunk * part : (chunk + 1) * part]
        whole = lax.all_gather(mine, "ctx", axis=0, tiled=True)
        partial = jnp.dot(whole, out_weight, preferred_element_type=jnp.float32)
        partial = partial.astype(jnp.bfloat16).reshape(ctx * part, tp, columns // tp)
        shares = tp_exchange(partial.transpose(1, 0, 2))
        summed = jnp.sum(shares.astype(jnp.float32), axis=0).astype(jnp.bfloat16)
        summed = summed.reshape(ctx, part, columns // tp)
        local = lax.all_to_all(summed, "ctx", split_axis=0, concat_axis=0, tiled=True)
        placed = tp_exchange(local.reshape(tp, ctx // tp, part, columns // tp))
        outs.append(placed.transpose(2, 1, 0, 3).reshape(part, width))
    return jnp.concatenate(outs, axis=0)


def solution(mesh):
    in_specs = (
        P(None, "ctx", "tp"),
        P(),
        P(None, ("tp", "ctx")),
        P(None, ("tp", "ctx")),
        P(("tp", "ctx")),
        P("tp", "ctx"),
    )
    out_specs = P("ctx", "tp")
    return jax.shard_map(
        per_device, mesh=mesh, in_specs=in_specs, out_specs=out_specs, check_vma=False
    )
```

```python
import functools

import jax
import jax.numpy as jnp
from jax import lax
from jax.experimental import pallas as pl
from jax.experimental.pallas import tpu as pltpu
from jax.sharding import PartitionSpec as P

LANES = 128
SUBLANES = 8
GROUP = LANES * SUBLANES
HALO = 2
TAPS = 3
SIDE = 2


def spread(scratch, halo, block, pitch):
    tokens = block.shape[0]
    for tile in range(SUBLANES):
        lanes = pl.ds(tile * LANES, LANES)
        scratch[pl.ds(tile * pitch + SUBLANES - HALO, HALO), :] = halo[:, lanes].astype(jnp.float32)
        scratch[pl.ds(tile * pitch + SUBLANES, tokens), :] = block[:, lanes].astype(jnp.float32)


def token(scratch, index, pitch):
    return scratch[pl.ds(index, SUBLANES, stride=pitch), :]


def filter_kernel(features, halo, taps, u_ref, query_ref, *rows):
    tokens = features.shape[1]
    pitch = tokens + SUBLANES
    for which in range(3):
        spread(rows[which], halo.at[which], features.at[which], pitch)
    weights = [[taps[which, j] for j in range(TAPS)] for which in range(3)]

    def step(index, carry):
        carry = list(carry)
        for inner in range(SUBLANES):
            now = index * SUBLANES + inner
            filtered = []
            for which in range(3):
                last, before = carry[which]
                fresh = token(rows[which], now + SUBLANES, pitch)
                filtered.append(
                    weights[which][0] * fresh + weights[which][1] * last + weights[which][2] * before
                )
                carry[which] = (fresh, last)
            query_ref[0, now] = filtered[0]
            u_ref[0, now] = (filtered[1] * filtered[2]).astype(jnp.bfloat16).astype(jnp.float32)
        return tuple(carry)

    start = tuple(
        (token(rows[which], SUBLANES - 1, pitch), token(rows[which], SUBLANES - 2, pitch))
        for which in range(3)
    )
    lax.fori_loop(0, tokens // SUBLANES, step, start)


def gather_channels(rows, modes):
    owners = rows.shape[0]
    each = SUBLANES // owners
    return [
        jnp.concatenate([rows[o, pl.ds(m * each, each), :] for o in range(owners)], axis=0)
        for m in range(modes)
    ]


def state_kernel(modes, u_ref, rates, z_ref, packed):
    tokens = u_ref.shape[1]
    decay = [jnp.exp(-rate) for rate in gather_channels(rates, modes)]

    def step(index, states):
        for inner in range(SUBLANES):
            u = u_ref[0, index * SUBLANES + inner]
            states = tuple(states[m] * decay[m] + u for m in range(modes))
        return states

    zero = tuple(jnp.zeros((SUBLANES, LANES), jnp.float32) for _ in range(modes))
    states = lax.fori_loop(0, tokens // SUBLANES, step, zero)
    owners = packed.shape[0]
    each = SUBLANES // owners
    for m in range(modes):
        for o in range(owners):
            packed[o, pl.ds(m * each, each), :] = states[m][o * each : (o + 1) * each]
    z_ref[...] = packed[...].astype(z_ref.dtype)


def prefix_kernel(tokens, z_ref, rates, out_ref):
    count = z_ref.shape[0]
    decay = jnp.exp(-float(tokens) * rates[...])
    total = jnp.zeros(decay.shape, jnp.float32)
    for block in range(count):
        out_ref[block] = total.astype(out_ref.dtype)
        total = total * decay + z_ref[block].astype(jnp.float32)


def local_kernel(modes, u_ref, rates, others, y_ref):
    tokens = u_ref.shape[1]
    rate = gather_channels(rates, modes)
    rest = gather_channels(others, modes + 1)
    decay = [jnp.exp(-r) for r in rate]
    weight = [rest[m] * jnp.sqrt(2.0 * rate[m]) for m in range(modes)]
    skip = rest[modes]

    def step(index, states):
        for inner in range(SUBLANES):
            now = index * SUBLANES + inner
            u = u_ref[0, now]
            states = tuple(states[m] * decay[m] + u for m in range(modes))
            y_ref[0, now] = tree_sum([weight[m] * states[m] for m in range(modes)] + [skip * u])
        return states

    zero = tuple(jnp.zeros((SUBLANES, LANES), jnp.float32) for _ in range(modes))
    lax.fori_loop(0, tokens // SUBLANES, step, zero)


def tree_sum(terms):
    while len(terms) > 1:
        terms = [a + b for a, b in zip(terms[::2], terms[1::2])] + terms[len(terms) & ~1 :]
    return terms[0]


def gated_kernel(modes, query_ref, y_ref, rates, others, z_ref, out_ref, wide, out_rows):
    tokens = query_ref.shape[1]
    pitch = tokens + SUBLANES
    rate = gather_channels(rates, modes)
    rest = gather_channels(others, modes)
    wide[...] = z_ref[...].astype(jnp.float32)
    state = gather_channels(wide, modes)
    decay = [jnp.exp(-r) for r in rate]
    weighted = tuple(rest[m] * jnp.sqrt(2.0 * rate[m]) * state[m] for m in range(modes))

    def step(index, weighted):
        for inner in range(SUBLANES):
            now = index * SUBLANES + inner
            weighted = tuple(weighted[m] * decay[m] for m in range(modes))
            long_out = tree_sum([y_ref[0, now], *weighted])
            long_out = long_out.astype(jnp.bfloat16).astype(jnp.float32)
            out_rows[pl.ds(now, SUBLANES, stride=pitch), :] = query_ref[0, now] * long_out
        return weighted

    lax.fori_loop(0, tokens // SUBLANES, step, weighted)
    for tile in range(SUBLANES):
        out_ref[:, pl.ds(tile * LANES, LANES)] = out_rows[pl.ds(tile * pitch, tokens), :].astype(
            out_ref.dtype
        )


def ring_order(count):
    return [0] + list(range(1, count, 2)) + [i for i in range(count - 1, 0, -1) if i % 2 == 0]


def per_device(features, conv_weight, decay_rates, residues, skip_gain, out_weight):
    tokens, width = features.shape[1:]
    modes, owned = decay_rates.shape
    ctx, tp = lax.axis_size("ctx"), lax.axis_size("tp")
    slab = SIDE * SIDE
    slabs = ctx // slab
    groups = width // GROUP
    each = max(owned // LANES, 1)
    owners = SUBLANES // each
    lanes = min(owned, LANES)
    me, tp_me = lax.axis_index("ctx"), lax.axis_index("tp")
    order = ring_order(slabs)
    place = [order.index(z) for z in range(slabs)]

    def within_slab(array, mask):
        return lax.ppermute(array, "ctx", [(i, i ^ mask) for i in range(ctx)])

    def ring(array, by):
        pairs = []
        for i in range(ctx):
            z, rest = divmod(i, slab)
            pairs.append((i, order[(place[z] + by) % slabs] * slab + rest))
        return lax.ppermute(array, "ctx", pairs)

    halo = lax.ppermute(
        features[:, tokens - HALO :, :], "ctx", [(i, i + 1) for i in range(ctx - 1)]
    )

    def exchange(rows):
        return lax.all_to_all(rows, "ctx", split_axis=0, concat_axis=0, tiled=True)

    def widen(rows):
        if lanes == LANES:
            return rows
        return rows.transpose(1, 0, 2).reshape(-1, width // LANES, LANES).transpose(1, 0, 2)

    def narrow(rows):
        if lanes == LANES:
            return rows
        return rows.transpose(1, 0, 2).reshape(-1, ctx, lanes).transpose(1, 0, 2)

    def to_all(rows):
        rows = rows.reshape(-1, lanes)
        return widen(exchange(jnp.broadcast_to(rows[None], (ctx, *rows.shape))))

    rates = to_all(decay_rates)
    others = to_all(jnp.concatenate([residues, skip_gain[None]], axis=0))

    weights = [out_weight, within_slab(out_weight, 1), within_slab(out_weight, 2)]
    weights.append(within_slab(weights[2], 1))

    taps = lax.dynamic_slice_in_dim(conv_weight, tp_me * width, width, 2)
    taps = taps.reshape(3, TAPS, width // LANES, LANES)

    def owner_spec(count):
        return pl.BlockSpec((owners, count * each, LANES), lambda g: (g, 0, 0))

    series = pl.BlockSpec((1, tokens, SUBLANES, LANES), lambda g: (g, 0, 0, 0))
    series_shape = jax.ShapeDtypeStruct((groups, tokens, SUBLANES, LANES), jnp.float32)
    rows = pltpu.VMEM((SUBLANES * (tokens + SUBLANES), LANES), jnp.float32)
    limit = pltpu.CompilerParams(vmem_limit_bytes=32 * 1024 * 1024)

    u, query = pl.pallas_call(
        filter_kernel,
        grid=(groups,),
        in_specs=[
            pl.BlockSpec((3, tokens, GROUP), lambda g: (0, 0, g)),
            pl.BlockSpec((3, HALO, GROUP), lambda g: (0, 0, g)),
            pl.BlockSpec((3, TAPS, SUBLANES, LANES), lambda g: (0, 0, g, 0)),
        ],
        out_specs=[series, series],
        out_shape=[series_shape, series_shape],
        scratch_shapes=[rows, rows, rows],
        compiler_params=limit,
        name="short_filters",
    )(features, halo, taps)

    packed_shape = (groups * owners, modes * each, LANES)
    z = pl.pallas_call(
        functools.partial(state_kernel, modes),
        grid=(groups,),
        in_specs=[series, owner_spec(modes)],
        out_specs=owner_spec(modes),
        out_shape=jax.ShapeDtypeStruct(packed_shape, jnp.bfloat16),
        scratch_shapes=[pltpu.VMEM((owners, modes * each, LANES), jnp.float32)],
        compiler_params=limit,
        name="block_states",
    )(u, rates)
    z = exchange(narrow(z))

    local = pl.pallas_call(
        functools.partial(local_kernel, modes),
        grid=(groups,),
        in_specs=[series, owner_spec(modes), owner_spec(modes + 1)],
        out_specs=series,
        out_shape=series_shape,
        compiler_params=limit,
        name="local_convolution",
    )(u, rates, others)

    incoming = pl.pallas_call(
        functools.partial(prefix_kernel, tokens),
        out_shape=jax.ShapeDtypeStruct(z.shape, jnp.bfloat16),
        compiler_params=limit,
        name="state_prefix",
    )(z, decay_rates.reshape(modes * each, lanes))
    incoming = widen(exchange(incoming))

    gated = pl.pallas_call(
        functools.partial(gated_kernel, modes),
        grid=(groups,),
        in_specs=[series, series, owner_spec(modes), owner_spec(modes + 1), owner_spec(modes)],
        out_specs=pl.BlockSpec((tokens, GROUP), lambda g: (0, g)),
        out_shape=jax.ShapeDtypeStruct((tokens, width), jnp.bfloat16),
        scratch_shapes=[pltpu.VMEM((owners, modes * each, LANES), jnp.float32), rows],
        compiler_params=limit,
        name="gated_block",
    )(query, local, rates, others, incoming)

    columns = out_weight.shape[1]
    share = columns // tp
    half_of = [z * tp // slabs for z in range(slabs)]

    def project(block):
        parts = [jnp.dot(block, w, preferred_element_type=jnp.float32) for w in weights]
        parts = jnp.stack([p.astype(jnp.bfloat16) for p in parts])
        return parts.reshape(slab, tokens, tp, share).transpose(2, 0, 1, 3)

    def sum_over_tp(parts):
        if tp != 2:
            parts = lax.all_to_all(parts, "tp", split_axis=0, concat_axis=0, tiled=True)
            return jnp.sum(parts.astype(jnp.float32), axis=0).astype(jnp.bfloat16)
        mine = lax.dynamic_index_in_dim(parts, tp_me, 0, keepdims=False)
        other = lax.dynamic_index_in_dim(parts, 1 - tp_me, 0, keepdims=False)
        got = lax.ppermute(other, "tp", [(0, 1), (1, 0)])
        return (mine.astype(jnp.float32) + got.astype(jnp.float32)).astype(jnp.bfloat16)

    def deliver(summed, by, source_tp):
        pairs = []
        for i in range(ctx):
            z, rest = divmod(i, slab)
            target = order[(place[z] - by) % slabs] * slab + rest
            pair = (i * tp + source_tp, target * tp + half_of[z])
            if pair[0] != pair[1]:
                pairs.append(pair)
        moved = lax.ppermute(summed, ("ctx", "tp"), pairs)
        if by:
            return moved
        return jnp.where(tp_me == source_tp, summed, moved)

    held = gated
    arrived = []
    for step in range(slabs):
        following = ring(held, 1) if step < slabs - 1 else None
        summed = sum_over_tp(project(held))
        arrived.append([deliver(summed, step, t) for t in range(tp)])
        held = following

    slab_me = me // slab
    place_me = jnp.asarray(place)[slab_me]
    stacked = jnp.stack([jnp.stack(a) for a in arrived])
    kept = slabs // tp
    pieces = []
    for j in range(kept):
        place_from = jnp.asarray(place)[tp_me * kept + j]
        pieces.append(
            lax.dynamic_index_in_dim(stacked, (place_from - place_me) % slabs, 0, keepdims=False)
        )
    mixed = jnp.stack(pieces)
    rank = me % slab
    mixed = jnp.stack(
        [lax.dynamic_index_in_dim(mixed, rank ^ piece, 2, keepdims=False) for piece in range(slab)], axis=2
    )
    return mixed.transpose(3, 0, 2, 1, 4).reshape(tokens, width)


def solution(mesh):
    in_specs = (
        P(None, "ctx", "tp"),
        P(),
        P(None, ("tp", "ctx")),
        P(None, ("tp", "ctx")),
        P(("tp", "ctx")),
        P("tp", "ctx"),
    )
    out_specs = P("ctx", "tp")
    return jax.shard_map(
        per_device, mesh=mesh, in_specs=in_specs, out_specs=out_specs, check_vma=False
    )
```

```python
import functools

import jax
import jax.numpy as jnp
from jax import lax
from jax.experimental import pallas as pl
from jax.experimental.pallas import tpu as pltpu
from jax.sharding import PartitionSpec as P

LANES = 128
SUBLANES = 8
GROUP = LANES * SUBLANES
HALO = 2
TAPS = 3
SIDE = 2
SLAB = SIDE * SIDE
F32 = jnp.float32
BF16 = jnp.bfloat16


def spread(scratch, halo, block, pitch):
    tokens = block.shape[0]
    for tile in range(SUBLANES):
        lanes = pl.ds(tile * LANES, LANES)
        scratch[pl.ds(tile * pitch + SUBLANES - HALO, HALO), :] = halo[:, lanes].astype(F32)
        scratch[pl.ds(tile * pitch + SUBLANES, tokens), :] = block[:, lanes].astype(F32)


def token(scratch, index, pitch):
    return scratch[pl.ds(index, SUBLANES, stride=pitch), :]


def tree_sum(terms):
    while len(terms) > 1:
        terms = [a + b for a, b in zip(terms[::2], terms[1::2])] + terms[len(terms) & ~1 :]
    return terms[0]


def filter_kernel(features, halo, taps, u_ref, query_ref, *rows):
    tokens = features.shape[1]
    pitch = tokens + SUBLANES
    for which in range(3):
        spread(rows[which], halo.at[which], features.at[which], pitch)
    weights = [[taps[which, j] for j in range(TAPS)] for which in range(3)]

    def step(index, carry):
        carry = list(carry)
        for inner in range(SUBLANES):
            now = index * SUBLANES + inner
            filtered = []
            for which in range(3):
                last, before = carry[which]
                fresh = token(rows[which], now + SUBLANES, pitch)
                filtered.append(
                    weights[which][0] * fresh + weights[which][1] * last + weights[which][2] * before
                )
                carry[which] = (fresh, last)
            query_ref[0, now] = filtered[0]
            u_ref[0, now] = (filtered[1] * filtered[2]).astype(BF16).astype(F32)
        return tuple(carry)

    start = tuple(
        (token(rows[which], SUBLANES - 1, pitch), token(rows[which], SUBLANES - 2, pitch))
        for which in range(3)
    )
    lax.fori_loop(0, tokens // SUBLANES, step, start)


def registers(refs, rank, wide, count):
    each = SUBLANES // SLAB
    for d in range(SLAB):
        wide[d ^ rank, : count * each] = refs[d][0, : count * each].astype(F32)
    return [
        jnp.concatenate([wide[o, pl.ds(m * each, each), :] for o in range(SLAB)], axis=0)
        for m in range(count)
    ]


def state_kernel(modes, here, u_ref, *refs):
    rates, outs, wide = refs[:SLAB], refs[SLAB : 2 * SLAB], refs[-1]
    rank = here[1]
    tokens = u_ref.shape[1]
    decay = [jnp.exp(-rate) for rate in registers(rates, rank, wide, modes)]

    def step(index, states):
        for inner in range(SUBLANES):
            u = u_ref[0, index * SUBLANES + inner]
            states = tuple(states[m] * decay[m] + u for m in range(modes))
        return states

    zero = tuple(jnp.zeros((SUBLANES, LANES), F32) for _ in range(modes))
    states = lax.fori_loop(0, tokens // SUBLANES, step, zero)
    each = SUBLANES // SLAB
    for m in range(modes):
        for o in range(SLAB):
            wide[o, pl.ds(m * each, each), :] = states[m][o * each : (o + 1) * each]
    for d in range(SLAB):
        outs[d][0] = wide[d ^ rank, : modes * each].astype(BF16)


def slab_kernel(tokens, here, rates, *refs):
    states, out = refs[:SLAB], refs[SLAB]
    slabs = rates.shape[0]
    for g in range(slabs):
        rate = rates[lax.rem(g - here[0] + slabs, slabs)]
        total = None
        for d in range(SLAB):
            later = (SLAB - 1 - (here[1] ^ d)).astype(F32) * float(tokens)
            term = jnp.exp(-later * rate) * states[d][g].astype(F32)
            total = term if total is None else total + term
        out[g] = total.astype(BF16)


def incoming_kernel(tokens, here, rates, *refs):
    slabs = rates.shape[0]
    states, earlier, outs = refs[:SLAB], refs[SLAB : SLAB + slabs - 1], refs[SLAB + slabs - 1 :]
    for g in range(slabs):
        rate = rates[lax.rem(g - here[0] + slabs, slabs)]
        entering = earlier[0][g].astype(F32)
        for k in range(1, slabs - 1):
            entering += jnp.exp(-float(k * SLAB * tokens) * rate) * earlier[k][g].astype(F32)
        for d in range(SLAB):
            block = here[1] ^ d
            total = jnp.exp(-(block.astype(F32) * float(tokens)) * rate) * entering
            for e in range(SLAB):
                if e != d:
                    between = block - 1 - (here[1] ^ e)
                    factor = jnp.exp(-(jnp.maximum(between, 0).astype(F32) * float(tokens)) * rate)
                    factor = jnp.where(between >= 0, factor, jnp.zeros_like(factor))
                    total += factor * states[e][g].astype(F32)
            outs[d][g] = total.astype(BF16)


def local_kernel(modes, here, u_ref, *refs):
    rates, others, y_ref, wide = refs[:SLAB], refs[SLAB : 2 * SLAB], refs[-2], refs[-1]
    tokens = u_ref.shape[1]
    rate = registers(rates, here[1], wide, modes)
    rest = registers(others, here[1], wide, modes + 1)
    decay = [jnp.exp(-r) for r in rate]
    weight = [rest[m] * jnp.sqrt(2.0 * rate[m]) for m in range(modes)]
    skip = rest[modes]

    def step(index, states):
        for inner in range(SUBLANES):
            now = index * SUBLANES + inner
            u = u_ref[0, now]
            states = tuple(states[m] * decay[m] + u for m in range(modes))
            y_ref[0, now] = tree_sum([weight[m] * states[m] for m in range(modes)] + [skip * u])
        return states

    zero = tuple(jnp.zeros((SUBLANES, LANES), F32) for _ in range(modes))
    lax.fori_loop(0, tokens // SUBLANES, step, zero)


def gated_kernel(modes, here, query_ref, y_ref, *refs):
    rates, others, incoming = refs[:SLAB], refs[SLAB : 2 * SLAB], refs[2 * SLAB : 3 * SLAB]
    out_ref, wide, out_rows = refs[3 * SLAB :]
    tokens = query_ref.shape[1]
    pitch = tokens + SUBLANES
    rate = registers(rates, here[1], wide, modes)
    rest = registers(others, here[1], wide, modes)
    state = registers(incoming, here[1], wide, modes)
    decay = [jnp.exp(-r) for r in rate]
    weighted = tuple(rest[m] * jnp.sqrt(2.0 * rate[m]) * state[m] for m in range(modes))

    def step(index, weighted):
        for inner in range(SUBLANES):
            now = index * SUBLANES + inner
            weighted = tuple(weighted[m] * decay[m] for m in range(modes))
            long_out = tree_sum([y_ref[0, now], *weighted])
            long_out = long_out.astype(BF16).astype(F32)
            out_rows[pl.ds(now, SUBLANES, stride=pitch), :] = query_ref[0, now] * long_out
        return weighted

    lax.fori_loop(0, tokens // SUBLANES, step, weighted)
    for tile in range(SUBLANES):
        out_ref[:, pl.ds(tile * LANES, LANES)] = out_rows[pl.ds(tile * pitch, tokens), :].astype(BF16)


def project_kernel(count, pieces, here, *refs):
    blocks, sources = refs[:count], refs[count:-3]
    out_ref, slots, sems = refs[-3:]
    share = slots.shape[2]
    columns = pl.ds(pl.multiple_of(here[0] * share, share), share)
    copies = []
    for i in range(pieces):
        if len(sources) == pieces:
            source = sources[i].at[:, columns]
        else:
            source = sources[0].at[here[1 + i], :, columns]
        copies.append(pltpu.make_async_copy(source, slots.at[i], sems.at[i]))
        copies[-1].start()
    for i in range(pieces):
        copies[i].wait()
        for j in range(count):
            product = jnp.dot(blocks[j][...], slots[i], preferred_element_type=F32)
            out_ref[j, i] = product.astype(BF16)


def place_kernel(kept, steps, here, *refs):
    per_pair = 2 * steps
    sources, out_ref, sems = refs[: SIDE * per_pair], refs[-2], refs[-1]
    share = sources[0].shape[2]
    tp_me, rank = here[0], here[1]
    waits = []
    for slot in range(kept):
        step = here[2 + slot]
        for pair in range(SIDE):
            mine = sources[pair * per_pair : (pair + 1) * per_pair]
            for near in range(SIDE):
                piece = rank ^ (SIDE * pair + near)
                for t in range(SIDE):
                    start = ((slot * SLAB + piece) * SIDE + t) * share
                    target = out_ref.at[:, pl.ds(pl.multiple_of(start, share), share)]
                    sem = sems.at[len(waits)]
                    own = jnp.logical_and(step == 0, tp_me == t)
                    moved = jnp.logical_and(step == 0, tp_me != t)
                    choices = [(own, mine[0]), (moved, mine[1])]
                    choices += [(step == k, mine[2 * k + t]) for k in range(1, steps)]
                    for chosen, source in choices:
                        copy = pltpu.make_async_copy(source.at[near], target, sem)
                        pl.when(chosen)(copy.start)
                    waits.append(copy)
    for copy in waits:
        copy.wait()


def ring_order(count):
    return [0] + list(range(1, count, 2)) + [i for i in range(count - 1, 0, -1) if i % 2 == 0]


def any_size(features, conv_weight, decay_rates, residues, skip_gain, out_weight):
    tokens, width = features.shape[1:]
    ctx, tp = lax.axis_size("ctx"), lax.axis_size("tp")
    me, tp_me = lax.axis_index("ctx"), lax.axis_index("tp")
    halo = lax.ppermute(features[:, tokens - HALO :], "ctx", [(i, i + 1) for i in range(ctx - 1)])
    extended = jnp.concatenate([halo, features], axis=1).astype(F32)
    taps = lax.dynamic_slice_in_dim(conv_weight, tp_me * width, width, 2)
    filtered = sum(taps[:, j, None] * extended[:, HALO - j : HALO - j + tokens] for j in range(TAPS))
    u = (filtered[1] * filtered[2]).astype(BF16).astype(F32)
    rates, weights, skip = (
        lax.all_gather(a, "ctx", axis=a.ndim - 1, tiled=True) for a in (decay_rates, residues, skip_gain)
    )
    weights = weights * jnp.sqrt(2.0 * rates)
    decay = jnp.exp(-rates)
    zero = jnp.zeros(rates.shape, F32)
    left = lax.fori_loop(0, tokens, lambda t, s: s * decay + u[t], zero)
    lefts = lax.all_gather(left, "ctx")
    block_decay = jnp.exp(-float(tokens) * rates)
    entering = lax.fori_loop(0, me, lambda b, s: s * block_decay + lefts[b], zero)

    def advance(states, now):
        states = states * decay + now
        return states, jnp.sum(weights * states, axis=0) + skip * now

    long_out = lax.scan(advance, entering, u)[1].astype(BF16).astype(F32)
    gated = (filtered[0] * long_out).astype(BF16)
    whole = lax.all_gather(gated, "ctx", axis=0, tiled=True)
    partial = jnp.dot(whole, out_weight, preferred_element_type=F32).astype(BF16)
    share = partial.shape[1] // tp
    partial = partial.reshape(ctx * tokens, tp, share).transpose(1, 0, 2)
    partial = lax.all_to_all(partial, "tp", split_axis=0, concat_axis=0, tiled=True)
    summed = jnp.sum(partial.astype(F32), axis=0).astype(BF16).reshape(ctx, tokens, share)
    summed = lax.all_to_all(summed, "ctx", split_axis=0, concat_axis=0, tiled=True)
    placed = lax.all_to_all(
        summed.reshape(tp, ctx // tp, tokens, share), "tp", split_axis=0, concat_axis=0, tiled=True
    )
    return placed.transpose(2, 1, 0, 3).reshape(tokens, width)


def per_device(features, conv_weight, decay_rates, residues, skip_gain, out_weight):
    tokens, width = features.shape[1:]
    modes, owned = decay_rates.shape
    ctx, tp = lax.axis_size("ctx"), lax.axis_size("tp")
    depth, columns = out_weight.shape
    share = columns // tp
    if owned * SLAB != GROUP or tp != SIDE or share % LANES or ctx // SLAB < 3:
        return any_size(features, conv_weight, decay_rates, residues, skip_gain, out_weight)
    slabs = ctx // SLAB
    groups = width // GROUP
    each = owned // LANES
    me, tp_me = lax.axis_index("ctx"), lax.axis_index("tp")
    z_me, rank = me // SLAB, me % SLAB
    order = ring_order(slabs)
    place = [order.index(z) for z in range(slabs)]
    here = jnp.stack([z_me, rank]).astype(jnp.int32)

    def within_slab(array, mask):
        return lax.ppermute(array, "ctx", [(i, i ^ mask) for i in range(ctx)])

    def slab_all(array):
        return [array] + [within_slab(array, mask) for mask in range(1, SLAB)]

    def from_slab(array, by):
        return lax.ppermute(array, "ctx", [(i, (i - by * SLAB) % ctx) for i in range(ctx)])

    def ring(array):
        pairs = []
        for i in range(ctx):
            z, rest = divmod(i, SLAB)
            pairs.append((i, order[(place[z] + 1) % slabs] * SLAB + rest))
        return lax.ppermute(array, "ctx", pairs)

    halo = lax.ppermute(
        features[:, tokens - HALO :, :], "ctx", [(i, i + 1) for i in range(ctx - 1)]
    )
    rows = jnp.concatenate(
        [a.reshape(-1, LANES) for a in (decay_rates, residues, skip_gain)], axis=0
    )
    rows = jnp.stack([rows] + [from_slab(rows, by) for by in range(1, slabs)])
    my_rates = rows[:, : modes * each]
    rates = slab_all(my_rates)
    others = slab_all(rows[:, modes * each :])

    beside = within_slab(out_weight, 1)
    slab_weights = lax.all_gather(
        out_weight,
        "ctx",
        axis_index_groups=[list(range(z * SLAB, (z + 1) * SLAB)) for z in range(slabs)],
    )

    taps = lax.dynamic_slice_in_dim(conv_weight, tp_me * width, width, 2)
    taps = taps.reshape(3, TAPS, width // LANES, LANES)

    limit = pltpu.CompilerParams(vmem_limit_bytes=16 * 1024 * 1024)
    series_shape = jax.ShapeDtypeStruct((groups, tokens, SUBLANES, LANES), F32)
    state_shape = jax.ShapeDtypeStruct((groups, modes * each, LANES), BF16)
    scratch_rows = pltpu.VMEM((SUBLANES * (tokens + SUBLANES), LANES), F32)
    wide = pltpu.VMEM((SLAB, (modes + 4) * each, LANES), F32)
    series = pl.BlockSpec((1, tokens, SUBLANES, LANES), lambda g, here: (g, 0, 0, 0))
    state_spec = pl.BlockSpec((1, modes * each, LANES), lambda g, here: (g, 0, 0))

    def relative(count):
        return pl.BlockSpec(
            (1, count * each, LANES), lambda g, here: (lax.rem(g - here[0] + slabs, slabs), 0, 0)
        )

    def grouped(kernel, name, in_specs, out_specs, out_shape, scratch, ops):
        return pl.pallas_call(
            kernel,
            grid_spec=pltpu.PrefetchScalarGridSpec(
                num_scalar_prefetch=1,
                grid=(groups,),
                in_specs=in_specs,
                out_specs=out_specs,
                scratch_shapes=scratch,
            ),
            out_shape=out_shape,
            compiler_params=limit,
            cost_estimate=pl.CostEstimate(
                flops=ops * tokens * width, bytes_accessed=4 * tokens * width, transcendentals=0
            ),
            name=name,
        )

    u, query = pl.pallas_call(
        filter_kernel,
        grid=(groups,),
        in_specs=[
            pl.BlockSpec((3, tokens, GROUP), lambda g: (0, 0, g)),
            pl.BlockSpec((3, HALO, GROUP), lambda g: (0, 0, g)),
            pl.BlockSpec((3, TAPS, SUBLANES, LANES), lambda g: (0, 0, g, 0)),
        ],
        out_specs=[pl.BlockSpec((1, tokens, SUBLANES, LANES), lambda g: (g, 0, 0, 0))] * 2,
        out_shape=[series_shape, series_shape],
        scratch_shapes=[scratch_rows, scratch_rows, scratch_rows],
        compiler_params=limit,
        name="short_filters",
    )(features, halo, taps)

    left = grouped(
        functools.partial(state_kernel, modes),
        "block_states",
        [series] + [relative(modes)] * SLAB,
        [state_spec] * SLAB,
        [state_shape] * SLAB,
        [wide],
        2 * modes,
    )(here, u, *rates)
    left = [left[0]] + [within_slab(left[d], d) for d in range(1, SLAB)]

    smem = pl.BlockSpec(memory_space=pltpu.SMEM)
    vmem = pl.BlockSpec(memory_space=pltpu.VMEM)
    slab_left = pl.pallas_call(
        functools.partial(slab_kernel, tokens),
        in_specs=[smem] + [vmem] * (1 + SLAB),
        out_specs=vmem,
        out_shape=state_shape,
        compiler_params=limit,
        name="slab_states",
    )(here, my_rates, *left)
    earlier = [
        lax.ppermute(slab_left, "ctx", [(i, i + by * SLAB) for i in range(ctx - by * SLAB)])
        for by in range(1, slabs)
    ]

    local = grouped(
        functools.partial(local_kernel, modes),
        "local_convolution",
        [series] + [relative(modes)] * SLAB + [relative(modes + 1)] * SLAB,
        series,
        series_shape,
        [wide],
        4 * modes,
    )(here, u, *rates, *others)

    incoming = pl.pallas_call(
        functools.partial(incoming_kernel, tokens),
        in_specs=[smem] + [vmem] * (SLAB + slabs),
        out_specs=[vmem] * SLAB,
        out_shape=[state_shape] * SLAB,
        compiler_params=limit,
        name="incoming_states",
    )(here, my_rates, *left, *earlier)
    incoming = [incoming[0]] + [within_slab(incoming[d], d) for d in range(1, SLAB)]

    gated = grouped(
        functools.partial(gated_kernel, modes),
        "gated_block",
        [series] * 2 + [relative(modes)] * SLAB + [relative(modes + 1)] * SLAB + [state_spec] * SLAB,
        pl.BlockSpec((tokens, GROUP), lambda g, here: (0, g)),
        jax.ShapeDtypeStruct((tokens, width), BF16),
        [wide, scratch_rows],
        2 * modes,
    )(here, query, local, *rates, *others, *incoming)

    def project(blocks, which, share_index):
        scalars = jnp.stack([share_index, rank ^ 2, rank ^ 3]).astype(jnp.int32)
        sources = [out_weight, beside] if which == 0 else [slab_weights]
        rows = len(blocks) * tokens
        return pl.pallas_call(
            functools.partial(project_kernel, len(blocks), SIDE),
            in_specs=[smem]
            + [vmem] * len(blocks)
            + [pl.BlockSpec(memory_space=pl.ANY)] * len(sources),
            out_specs=vmem,
            out_shape=jax.ShapeDtypeStruct((len(blocks), SIDE, tokens, share), BF16),
            scratch_shapes=[
                pltpu.VMEM((SIDE, depth, share), BF16),
                pltpu.SemaphoreType.DMA((SIDE,)),
            ],
            compiler_params=limit,
            cost_estimate=pl.CostEstimate(
                flops=2 * rows * depth * SIDE * share,
                bytes_accessed=2 * depth * (rows + SIDE * share),
                transcendentals=0,
            ),
            name="project_block",
        )(scalars, *blocks, *sources)

    def summed_over_tp(blocks, which):
        away = project(blocks, which, 1 - tp_me)
        got = lax.ppermute(away, "tp", [(0, 1), (1, 0)])
        mine = project(blocks, which, tp_me)
        return (mine.astype(F32) + got.astype(F32)).astype(BF16)

    half_of = [z * tp // slabs for z in range(slabs)]

    def deliver(summed, by):
        pairs = [[], []]
        for i in range(ctx):
            z, rest = divmod(i, SLAB)
            target = order[(place[z] - by) % slabs] * SLAB + rest
            for t in range(tp):
                pairs[t].append((i * tp + t, target * tp + half_of[z]))
        if by == 0:
            moves = [p for p in pairs[0] + pairs[1] if p[0] != p[1]]
            return [summed, lax.ppermute(summed, ("ctx", "tp"), moves)]
        return [lax.ppermute(summed, ("ctx", "tp"), moves) for moves in pairs]

    blocks = [gated]
    arrived = [[], []]
    for step in range(slabs):
        if step < slabs - 1:
            blocks.append(ring(blocks[-1]))
        arrived[0] += deliver(summed_over_tp([blocks[step]], 0)[0], step)
    for first in range(0, slabs, 2):
        pair = summed_over_tp(blocks[first : first + 2], 1)
        for offset in range(pair.shape[0]):
            arrived[1] += deliver(pair[offset], first + offset)

    place_me = jnp.asarray(place)[z_me]
    kept = slabs // tp
    steps = [(jnp.asarray(place)[tp_me * kept + j] - place_me) % slabs for j in range(kept)]
    return pl.pallas_call(
        functools.partial(place_kernel, kept, slabs),
        in_specs=[smem] + [pl.BlockSpec(memory_space=pl.ANY)] * (SIDE * 2 * slabs),
        out_specs=pl.BlockSpec(memory_space=pl.ANY),
        out_shape=jax.ShapeDtypeStruct((tokens, width), BF16),
        scratch_shapes=[pltpu.SemaphoreType.DMA((kept * SLAB * SIDE,))],
        compiler_params=limit,
        name="place_columns",
    )(jnp.stack([tp_me, rank, *steps]).astype(jnp.int32), *arrived[0], *arrived[1])


def solution(mesh):
    in_specs = (
        P(None, "ctx", "tp"),
        P(),
        P(None, ("tp", "ctx")),
        P(None, ("tp", "ctx")),
        P(("tp", "ctx")),
        P("tp", "ctx"),
    )
    out_specs = P("ctx", "tp")
    return jax.shard_map(
        per_device, mesh=mesh, in_specs=in_specs, out_specs=out_specs, check_vma=False
    )
```

```python
import functools

import jax
import jax.numpy as jnp
from jax import lax
from jax.experimental import pallas as pl
from jax.experimental.pallas import tpu as pltpu
from jax.sharding import PartitionSpec as P

LANES = 128
SUBLANES = 8
GROUP = LANES * SUBLANES
HALO = 2
TAPS = 3
SIDE = 2
SLAB = SIDE * SIDE
F32 = jnp.float32
BF16 = jnp.bfloat16


def spread(scratch, halo, block, pitch):
    tokens = block.shape[0]
    for tile in range(SUBLANES):
        lanes = pl.ds(tile * LANES, LANES)
        scratch[pl.ds(tile * pitch + SUBLANES - HALO, HALO), :] = halo[:, lanes].astype(F32)
        scratch[pl.ds(tile * pitch + SUBLANES, tokens), :] = block[:, lanes].astype(F32)


def token(scratch, index, pitch):
    return scratch[pl.ds(index, SUBLANES, stride=pitch), :]


def tree_sum(terms):
    while len(terms) > 1:
        terms = [a + b for a, b in zip(terms[::2], terms[1::2])] + terms[len(terms) & ~1 :]
    return terms[0]


def filter_kernel(here, features, halo, taps, u_ref, query_ref, tap_rows, *rows):
    tokens = features.shape[1]
    pitch = tokens + SUBLANES
    for tile in range(SUBLANES):
        for which in range(3):
            for j in range(TAPS):
                row = which * TAPS + j
                tap_rows[row, tile : tile + 1] = taps[which, j : j + 1, tile * LANES : (tile + 1) * LANES]
    for which in range(3):
        spread(rows[which], halo.at[which], features.at[which], pitch)
    weights = [[tap_rows[which * TAPS + j] for j in range(TAPS)] for which in range(3)]

    def step(index, carry):
        carry = list(carry)
        for inner in range(SUBLANES):
            now = index * SUBLANES + inner
            filtered = []
            for which in range(3):
                last, before = carry[which]
                fresh = token(rows[which], now + SUBLANES, pitch)
                filtered.append(
                    weights[which][0] * fresh + weights[which][1] * last + weights[which][2] * before
                )
                carry[which] = (fresh, last)
            query_ref[0, now] = filtered[0]
            u_ref[0, now] = (filtered[1] * filtered[2]).astype(BF16).astype(F32)
        return tuple(carry)

    start = tuple(
        (token(rows[which], SUBLANES - 1, pitch), token(rows[which], SUBLANES - 2, pitch))
        for which in range(3)
    )
    lax.fori_loop(0, tokens // SUBLANES, step, start)


def registers(refs, rank, wide, first, count):
    pitch = wide.shape[0] // SUBLANES
    each = SUBLANES // SLAB
    for d in range(SLAB):
        for j in range(each):
            start = pl.multiple_of(((d ^ rank) * each + j) * pitch, SUBLANES)
            rows = refs[d][0, first : first + count, j * LANES : (j + 1) * LANES]
            wide[pl.ds(start, count), :] = rows.astype(F32)
    return [wide[pl.ds(m, SUBLANES, stride=pitch), :] for m in range(count)]


def state_kernel(modes, here, u_ref, *refs):
    rates, outs, wide = refs[:SLAB], refs[SLAB : 2 * SLAB], refs[-1]
    rank = here[1]
    tokens = u_ref.shape[1]
    decay = [jnp.exp(-rate) for rate in registers(rates, rank, wide, 0, modes)]

    def step(index, states):
        for inner in range(SUBLANES):
            u = u_ref[0, index * SUBLANES + inner]
            states = tuple(states[m] * decay[m] + u for m in range(modes))
        return states

    zero = tuple(jnp.zeros((SUBLANES, LANES), F32) for _ in range(modes))
    states = lax.fori_loop(0, tokens // SUBLANES, step, zero)
    each = SUBLANES // SLAB
    pitch = wide.shape[0] // SUBLANES
    for m in range(modes):
        wide[pl.ds(m, SUBLANES, stride=pitch), :] = states[m]
    for d in range(SLAB):
        for j in range(each):
            start = pl.multiple_of(((d ^ rank) * each + j) * pitch, SUBLANES)
            outs[d][0, :, j * LANES : (j + 1) * LANES] = wide[pl.ds(start, modes), :].astype(BF16)


def slab_kernel(tokens, here, rates, *refs):
    states, out = refs[:SLAB], refs[SLAB]
    slabs = rates.shape[0]
    for g in range(slabs):
        rate = rates[lax.rem(g - here[0] + slabs, slabs), : states[0].shape[1]]
        total = None
        for d in range(SLAB):
            later = (SLAB - 1 - (here[1] ^ d)).astype(F32) * float(tokens)
            term = jnp.exp(-later * rate) * states[d][g].astype(F32)
            total = term if total is None else total + term
        out[g] = total.astype(BF16)


def incoming_kernel(tokens, here, rates, *refs):
    slabs = rates.shape[0]
    states, earlier, outs = refs[:SLAB], refs[SLAB : SLAB + slabs - 1], refs[SLAB + slabs - 1 :]
    for g in range(slabs):
        rate = rates[lax.rem(g - here[0] + slabs, slabs), : states[0].shape[1]]
        entering = earlier[0][g].astype(F32)
        for k in range(1, slabs - 1):
            entering += jnp.exp(-float(k * SLAB * tokens) * rate) * earlier[k][g].astype(F32)
        for d in range(SLAB):
            block = here[1] ^ d
            total = jnp.exp(-(block.astype(F32) * float(tokens)) * rate) * entering
            for e in range(SLAB):
                if e != d:
                    between = block - 1 - (here[1] ^ e)
                    factor = jnp.exp(-(jnp.maximum(between, 0).astype(F32) * float(tokens)) * rate)
                    factor = jnp.where(between >= 0, factor, jnp.zeros_like(factor))
                    total += factor * states[e][g].astype(F32)
            outs[d][g] = total.astype(BF16)


def local_kernel(modes, here, u_ref, *refs):
    rates, y_ref, wide = refs[:SLAB], refs[-2], refs[-1]
    tokens = u_ref.shape[1]
    rate = registers(rates, here[1], wide, 0, modes)
    rest = registers(rates, here[1], wide, modes, modes + 1)
    decay = [jnp.exp(-r) for r in rate]
    weight = [rest[m] * jnp.sqrt(2.0 * rate[m]) for m in range(modes)]
    skip = rest[modes]

    def step(index, states):
        for inner in range(SUBLANES):
            now = index * SUBLANES + inner
            u = u_ref[0, now]
            states = tuple(states[m] * decay[m] + u for m in range(modes))
            y_ref[0, now] = tree_sum([weight[m] * states[m] for m in range(modes)] + [skip * u])
        return states

    zero = tuple(jnp.zeros((SUBLANES, LANES), F32) for _ in range(modes))
    lax.fori_loop(0, tokens // SUBLANES, step, zero)


def gated_kernel(modes, here, query_ref, y_ref, *refs):
    rates, incoming = refs[:SLAB], refs[SLAB : 2 * SLAB]
    out_ref, wide, out_rows = refs[2 * SLAB :]
    tokens = query_ref.shape[1]
    pitch = tokens + SUBLANES
    rate = registers(rates, here[1], wide, 0, modes)
    rest = registers(rates, here[1], wide, modes, modes)
    state = registers(incoming, here[1], wide, 0, modes)
    decay = [jnp.exp(-r) for r in rate]
    weighted = tuple(rest[m] * jnp.sqrt(2.0 * rate[m]) * state[m] for m in range(modes))

    def step(index, weighted):
        for inner in range(SUBLANES):
            now = index * SUBLANES + inner
            weighted = tuple(weighted[m] * decay[m] for m in range(modes))
            long_out = tree_sum([y_ref[0, now], *weighted])
            long_out = long_out.astype(BF16).astype(F32)
            out_rows[pl.ds(now, SUBLANES, stride=pitch), :] = query_ref[0, now] * long_out
        return weighted

    lax.fori_loop(0, tokens // SUBLANES, step, weighted)
    for tile in range(SUBLANES):
        out_ref[:, pl.ds(tile * LANES, LANES)] = out_rows[pl.ds(tile * pitch, tokens), :].astype(BF16)


def project_kernel(count, here, *refs):
    out_ref, slots, sems = refs[-3:]
    pieces, depth, share = slots.shape
    blocks, sources = refs[: SIDE * count], refs[SIDE * count : -3]
    half = depth // SIDE
    columns = pl.ds(pl.multiple_of(here[0] * share, share), share)
    copies = []
    for i in range(pieces):
        if len(sources) == pieces:
            source = sources[i].at[:, columns]
        else:
            source = sources[0].at[here[1 + i], :, columns]
        copies.append(pltpu.make_async_copy(source, slots.at[i], sems.at[i]))
        copies[-1].start()
    for i in range(pieces):
        copies[i].wait()
        for j in range(count):
            total = None
            for h in range(SIDE):
                term = jnp.dot(
                    blocks[SIDE * j + h][...],
                    slots[i, h * half : (h + 1) * half],
                    preferred_element_type=F32,
                )
                total = term if total is None else total + term
            out_ref[j, i] = total.astype(BF16)


def place_kernel(kept, steps, here, *refs):
    per_pair = 2 * steps
    sources, out_ref, sems = refs[: SIDE * per_pair], refs[-2], refs[-1]
    share = sources[0].shape[2]
    tp_me, rank = here[0], here[1]
    waits = []
    for slot in range(kept):
        step = here[2 + slot]
        for pair in range(SIDE):
            mine = sources[pair * per_pair : (pair + 1) * per_pair]
            for near in range(SIDE):
                piece = rank ^ (SIDE * pair + near)
                for t in range(SIDE):
                    start = ((slot * SLAB + piece) * SIDE + t) * share
                    target = out_ref.at[:, pl.ds(pl.multiple_of(start, share), share)]
                    sem = sems.at[len(waits)]
                    own = jnp.logical_and(step == 0, tp_me == t)
                    moved = jnp.logical_and(step == 0, tp_me != t)
                    choices = [(own, mine[0]), (moved, mine[1])]
                    choices += [(step == k, mine[2 * k + t]) for k in range(1, steps)]
                    for chosen, source in choices:
                        copy = pltpu.make_async_copy(source.at[near], target, sem)
                        pl.when(chosen)(copy.start)
                    waits.append(copy)
    for copy in waits:
        copy.wait()


def ring_order(count):
    return [0] + list(range(1, count, 2)) + [i for i in range(count - 1, 0, -1) if i % 2 == 0]


def any_size(features, conv_weight, decay_rates, residues, skip_gain, out_weight):
    tokens, width = features.shape[1:]
    ctx, tp = lax.axis_size("ctx"), lax.axis_size("tp")
    me, tp_me = lax.axis_index("ctx"), lax.axis_index("tp")
    halo = lax.ppermute(features[:, tokens - HALO :], "ctx", [(i, i + 1) for i in range(ctx - 1)])
    extended = jnp.concatenate([halo, features], axis=1).astype(F32)
    taps = lax.dynamic_slice_in_dim(conv_weight, tp_me * width, width, 2)
    filtered = sum(taps[:, j, None] * extended[:, HALO - j : HALO - j + tokens] for j in range(TAPS))
    u = (filtered[1] * filtered[2]).astype(BF16).astype(F32)
    rates, weights, skip = (
        lax.all_gather(a, "ctx", axis=a.ndim - 1, tiled=True) for a in (decay_rates, residues, skip_gain)
    )
    weights = weights * jnp.sqrt(2.0 * rates)
    decay = jnp.exp(-rates)
    zero = jnp.zeros(rates.shape, F32)
    left = lax.fori_loop(0, tokens, lambda t, s: s * decay + u[t], zero)
    lefts = lax.all_gather(left, "ctx")
    block_decay = jnp.exp(-float(tokens) * rates)
    entering = lax.fori_loop(0, me, lambda b, s: s * block_decay + lefts[b], zero)

    def advance(states, now):
        states = states * decay + now
        return states, jnp.sum(weights * states, axis=0) + skip * now

    long_out = lax.scan(advance, entering, u)[1].astype(BF16).astype(F32)
    gated = (filtered[0] * long_out).astype(BF16)
    whole = lax.all_gather(gated, "ctx", axis=0, tiled=True)
    partial = jnp.dot(whole, out_weight, preferred_element_type=F32).astype(BF16)
    share = partial.shape[1] // tp
    partial = partial.reshape(ctx * tokens, tp, share).transpose(1, 0, 2)
    partial = lax.all_to_all(partial, "tp", split_axis=0, concat_axis=0, tiled=True)
    summed = jnp.sum(partial.astype(F32), axis=0).astype(BF16).reshape(ctx, tokens, share)
    summed = lax.all_to_all(summed, "ctx", split_axis=0, concat_axis=0, tiled=True)
    placed = lax.all_to_all(
        summed.reshape(tp, ctx // tp, tokens, share), "tp", split_axis=0, concat_axis=0, tiled=True
    )
    return placed.transpose(2, 1, 0, 3).reshape(tokens, width)


def per_device(features, conv_weight, decay_rates, residues, skip_gain, out_weight):
    tokens, width = features.shape[1:]
    modes, owned = decay_rates.shape
    ctx, tp = lax.axis_size("ctx"), lax.axis_size("tp")
    depth, columns = out_weight.shape
    share = columns // tp
    if owned * SLAB != GROUP or tp != SIDE or share % LANES or ctx // SLAB < 3:
        return any_size(features, conv_weight, decay_rates, residues, skip_gain, out_weight)
    slabs = ctx // SLAB
    groups = width // GROUP
    me, tp_me = lax.axis_index("ctx"), lax.axis_index("tp")
    z_me, rank = me // SLAB, me % SLAB
    order = ring_order(slabs)
    place = [order.index(z) for z in range(slabs)]
    here = jnp.stack([z_me, rank, tp_me]).astype(jnp.int32)

    def within_slab(array, mask):
        return lax.ppermute(array, "ctx", [(i, i ^ mask) for i in range(ctx)])

    def slab_all(array):
        return [array] + [within_slab(array, mask) for mask in range(1, SLAB)]

    def from_slab(array, by):
        return lax.ppermute(array, "ctx", [(i, (i - by * SLAB) % ctx) for i in range(ctx)])

    def ring(array):
        pairs = []
        for i in range(ctx):
            z, rest = divmod(i, SLAB)
            pairs.append((i, order[(place[z] + 1) % slabs] * SLAB + rest))
        return lax.ppermute(array, "ctx", pairs)

    halo = lax.ppermute(
        features[:, tokens - HALO :, :], "ctx", [(i, i + 1) for i in range(ctx - 1)]
    )
    rows = jnp.concatenate([decay_rates, residues, skip_gain[None]], axis=0)
    rows = jnp.stack([rows] + [from_slab(rows, by) for by in range(1, slabs)])
    rates = slab_all(rows)

    beside = within_slab(out_weight, 1)
    slab_weights = lax.all_gather(
        out_weight,
        "ctx",
        axis_index_groups=[list(range(z * SLAB, (z + 1) * SLAB)) for z in range(slabs)],
    )

    limit = pltpu.CompilerParams(vmem_limit_bytes=16 * 1024 * 1024)
    series_shape = jax.ShapeDtypeStruct((groups, tokens, SUBLANES, LANES), F32)
    state_shape = jax.ShapeDtypeStruct((groups, modes, owned), BF16)
    scratch_rows = pltpu.VMEM((SUBLANES * (tokens + SUBLANES), LANES), F32)
    wide = pltpu.VMEM((SUBLANES * (modes + SUBLANES), LANES), F32)
    series = pl.BlockSpec((1, tokens, SUBLANES, LANES), lambda g, here: (g, 0, 0, 0))
    state_spec = pl.BlockSpec((1, modes, owned), lambda g, here: (g, 0, 0))
    rate_spec = pl.BlockSpec(
        (1, 2 * modes + 1, owned), lambda g, here: (lax.rem(g - here[0] + slabs, slabs), 0, 0)
    )

    def grouped(kernel, name, in_specs, out_specs, out_shape, scratch, ops, groups=groups):
        return pl.pallas_call(
            kernel,
            grid_spec=pltpu.PrefetchScalarGridSpec(
                num_scalar_prefetch=1,
                grid=(groups,),
                in_specs=in_specs,
                out_specs=out_specs,
                scratch_shapes=scratch,
            ),
            out_shape=out_shape,
            compiler_params=limit,
            cost_estimate=pl.CostEstimate(
                flops=ops * tokens * GROUP * groups,
                bytes_accessed=4 * tokens * GROUP * groups,
                transcendentals=0,
            ),
            name=name,
        )

    u, query = grouped(
        filter_kernel,
        "short_filters",
        [
            pl.BlockSpec((3, tokens, GROUP), lambda g, here: (0, 0, g)),
            pl.BlockSpec((3, HALO, GROUP), lambda g, here: (0, 0, g)),
            pl.BlockSpec((3, TAPS, GROUP), lambda g, here: (0, 0, here[2] * groups + g)),
        ],
        [series, series],
        [series_shape, series_shape],
        [pltpu.VMEM((3 * TAPS, SUBLANES, LANES), F32), scratch_rows, scratch_rows, scratch_rows],
        20,
    )(here, features, halo, conv_weight)

    left = grouped(
        functools.partial(state_kernel, modes),
        "block_states",
        [series] + [rate_spec] * SLAB,
        [state_spec] * SLAB,
        [state_shape] * SLAB,
        [wide],
        2 * modes,
    )(here, u, *rates)
    left = [left[0]] + [within_slab(left[d], d) for d in range(1, SLAB)]

    smem = pl.BlockSpec(memory_space=pltpu.SMEM)
    vmem = pl.BlockSpec(memory_space=pltpu.VMEM)
    slab_left = pl.pallas_call(
        functools.partial(slab_kernel, tokens),
        in_specs=[smem] + [vmem] * (1 + SLAB),
        out_specs=vmem,
        out_shape=state_shape,
        compiler_params=limit,
        name="slab_states",
    )(here, rows, *left)
    earlier = [
        lax.ppermute(slab_left, "ctx", [(i, i + by * SLAB) for i in range(ctx - by * SLAB)])
        for by in range(1, slabs)
    ]

    local = grouped(
        functools.partial(local_kernel, modes),
        "local_convolution",
        [series] + [rate_spec] * SLAB,
        series,
        series_shape,
        [wide],
        4 * modes,
    )(here, u, *rates)

    incoming = pl.pallas_call(
        functools.partial(incoming_kernel, tokens),
        in_specs=[smem] + [vmem] * (SLAB + slabs),
        out_specs=[vmem] * SLAB,
        out_shape=[state_shape] * SLAB,
        compiler_params=limit,
        name="incoming_states",
    )(here, rows, *left, *earlier)
    incoming = [incoming[0]] + [within_slab(incoming[d], d) for d in range(1, SLAB)]

    def gated_half(half):
        count = groups // SIDE
        first = half * count

        def shifted(spec):
            return pl.BlockSpec(spec.block_shape, lambda g, here: spec.index_map(g + first, here))

        return grouped(
            functools.partial(gated_kernel, modes),
            "gated_block",
            [shifted(s) for s in [series] * 2 + [rate_spec] * SLAB + [state_spec] * SLAB],
            pl.BlockSpec((tokens, GROUP), lambda g, here: (0, g)),
            jax.ShapeDtypeStruct((tokens, width // SIDE), BF16),
            [wide, scratch_rows],
            2 * modes,
            count,
        )(here, query, local, *rates, *incoming)

    def project(blocks, sources, share_index):
        scalars = jnp.stack([share_index, rank ^ 2, rank ^ 3]).astype(jnp.int32)
        rows = len(blocks) * tokens
        return pl.pallas_call(
            functools.partial(project_kernel, len(blocks)),
            in_specs=[smem]
            + [vmem] * (SIDE * len(blocks))
            + [pl.BlockSpec(memory_space=pltpu.HBM)] * len(sources),
            out_specs=vmem,
            out_shape=jax.ShapeDtypeStruct((len(blocks), SIDE, tokens, share), BF16),
            scratch_shapes=[
                pltpu.VMEM((SIDE, depth, share), BF16),
                pltpu.SemaphoreType.DMA((SIDE,)),
            ],
            compiler_params=pltpu.CompilerParams(vmem_limit_bytes=48 * 1024 * 1024),
            cost_estimate=pl.CostEstimate(
                flops=2 * rows * depth * SIDE * share,
                bytes_accessed=2 * depth * (rows + SIDE * share),
                transcendentals=0,
            ),
            name="project_block",
        )(scalars, *[h for b in blocks for h in b], *sources)

    def summed_over_tp(blocks, sources):
        away = project(blocks, sources, 1 - tp_me)
        got = lax.ppermute(away, "tp", [(0, 1), (1, 0)])
        mine = project(blocks, sources, tp_me)
        return (mine.astype(F32) + got.astype(F32)).astype(BF16)

    half_of = [z * tp // slabs for z in range(slabs)]

    def deliver(summed, by):
        pairs = [[], []]
        for i in range(ctx):
            z, rest = divmod(i, SLAB)
            target = order[(place[z] - by) % slabs] * SLAB + rest
            for t in range(tp):
                pairs[t].append((i * tp + t, target * tp + half_of[z]))
        if by == 0:
            moves = [p for p in pairs[0] + pairs[1] if p[0] != p[1]]
            return [summed, lax.ppermute(summed, ("ctx", "tp"), moves)]
        return [lax.ppermute(summed, ("ctx", "tp"), moves) for moves in pairs]

    blocks = [[gated_half(h) for h in range(SIDE)]]
    arrived = [[], []]
    for step in range(slabs):
        if step:
            blocks[step], summed, arrived[0] = lax.optimization_barrier(
                (blocks[step], summed, arrived[0])
            )
            arrived[0] += deliver(summed, step - 1)
        if step < slabs - 1:
            blocks.append([ring(h) for h in blocks[step]])
        summed = summed_over_tp([blocks[step]], [out_weight, beside])[0]
    arrived[0] += deliver(summed, slabs - 1)
    slab_weights, _ = lax.optimization_barrier((slab_weights, blocks[-1]))
    for first in range(0, slabs, 2):
        pair = summed_over_tp(blocks[first : first + 2], [slab_weights])
        for offset in range(pair.shape[0]):
            arrived[1] += deliver(pair[offset], first + offset)

    def place_of(z):
        return sum(jnp.where(z == k, place[k], 0) for k in range(slabs))

    kept = slabs // tp
    steps = [
        lax.rem(place_of(tp_me * kept + j) - place_of(z_me) + slabs, slabs) for j in range(kept)
    ]
    return pl.pallas_call(
        functools.partial(place_kernel, kept, slabs),
        in_specs=[smem] + [pl.BlockSpec(memory_space=pl.ANY)] * (SIDE * 2 * slabs),
        out_specs=pl.BlockSpec(memory_space=pl.ANY),
        out_shape=jax.ShapeDtypeStruct((tokens, width), BF16),
        scratch_shapes=[pltpu.SemaphoreType.DMA((kept * SLAB * SIDE,))],
        compiler_params=limit,
        name="place_columns",
    )(jnp.stack([tp_me, rank, *steps]).astype(jnp.int32), *arrived[0], *arrived[1])


def solution(mesh):
    in_specs = (
        P(None, "ctx", "tp"),
        P(),
        P(None, ("tp", "ctx")),
        P(None, ("tp", "ctx")),
        P(("tp", "ctx")),
        P("tp", "ctx"),
    )
    out_specs = P("ctx", "tp")
    return jax.shard_map(
        per_device, mesh=mesh, in_specs=in_specs, out_specs=out_specs, check_vma=False
    )
```

```python
import functools

import jax
import jax.numpy as jnp
from jax import lax
from jax.experimental import pallas as pl
from jax.experimental.pallas import tpu as pltpu
from jax.sharding import PartitionSpec as P

LANES = 128
SUBLANES = 8
GROUP = LANES * SUBLANES
HALO = 2
TAPS = 3
SIDE = 2
SLAB = SIDE * SIDE
F32 = jnp.float32
BF16 = jnp.bfloat16


def spread(scratch, halo, block, pitch):
    tokens = block.shape[0]
    for tile in range(SUBLANES):
        lanes = pl.ds(tile * LANES, LANES)
        scratch[pl.ds(tile * pitch + SUBLANES - HALO, HALO), :] = halo[:, lanes].astype(F32)
        scratch[pl.ds(tile * pitch + SUBLANES, tokens), :] = block[:, lanes].astype(F32)


def token(scratch, index, pitch):
    return scratch[pl.ds(index, SUBLANES, stride=pitch), :]


def tree_sum(terms):
    while len(terms) > 1:
        terms = [a + b for a, b in zip(terms[::2], terms[1::2])] + terms[len(terms) & ~1 :]
    return terms[0]


def filter_kernel(here, features, halo, taps, u_ref, query_ref, tap_rows, *rows):
    tokens = features.shape[1]
    pitch = tokens + SUBLANES
    for tile in range(SUBLANES):
        for which in range(3):
            for j in range(TAPS):
                row = which * TAPS + j
                tap_rows[row, tile : tile + 1] = taps[which, j : j + 1, tile * LANES : (tile + 1) * LANES]
    for which in range(3):
        spread(rows[which], halo.at[which], features.at[which], pitch)
    weights = [[tap_rows[which * TAPS + j] for j in range(TAPS)] for which in range(3)]

    def step(index, carry):
        carry = list(carry)
        for inner in range(SUBLANES):
            now = index * SUBLANES + inner
            filtered = []
            for which in range(3):
                last, before = carry[which]
                fresh = token(rows[which], now + SUBLANES, pitch)
                filtered.append(
                    weights[which][0] * fresh + weights[which][1] * last + weights[which][2] * before
                )
                carry[which] = (fresh, last)
            query_ref[0, now] = filtered[0]
            u_ref[0, now] = (filtered[1] * filtered[2]).astype(BF16).astype(F32)
        return tuple(carry)

    start = tuple(
        (token(rows[which], SUBLANES - 1, pitch), token(rows[which], SUBLANES - 2, pitch))
        for which in range(3)
    )
    lax.fori_loop(0, tokens // SUBLANES, step, start)


def registers(refs, rank, wide, first, count):
    pitch = wide.shape[0] // SUBLANES
    each = SUBLANES // SLAB
    for d in range(SLAB):
        for j in range(each):
            start = pl.multiple_of(((d ^ rank) * each + j) * pitch, SUBLANES)
            rows = refs[d][0, first : first + count, j * LANES : (j + 1) * LANES]
            wide[pl.ds(start, count), :] = rows.astype(F32)
    return [wide[pl.ds(m, SUBLANES, stride=pitch), :] for m in range(count)]


def state_kernel(modes, here, u_ref, *refs):
    rates, outs, wide = refs[:SLAB], refs[SLAB : 2 * SLAB], refs[-1]
    rank = here[1]
    tokens = u_ref.shape[1]
    decay = [jnp.exp(-rate) for rate in registers(rates, rank, wide, 0, modes)]

    def step(index, states):
        for inner in range(SUBLANES):
            u = u_ref[0, index * SUBLANES + inner]
            states = tuple(states[m] * decay[m] + u for m in range(modes))
        return states

    zero = tuple(jnp.zeros((SUBLANES, LANES), F32) for _ in range(modes))
    states = lax.fori_loop(0, tokens // SUBLANES, step, zero)
    each = SUBLANES // SLAB
    pitch = wide.shape[0] // SUBLANES
    for m in range(modes):
        wide[pl.ds(m, SUBLANES, stride=pitch), :] = states[m]
    for d in range(SLAB):
        for j in range(each):
            start = pl.multiple_of(((d ^ rank) * each + j) * pitch, SUBLANES)
            outs[d][0, :, j * LANES : (j + 1) * LANES] = wide[pl.ds(start, modes), :].astype(BF16)


def slab_kernel(tokens, here, rates, *refs):
    states, out = refs[:SLAB], refs[SLAB]
    slabs = rates.shape[0]
    for g in range(slabs):
        rate = rates[lax.rem(g - here[0] + slabs, slabs), : states[0].shape[1]]
        total = None
        for d in range(SLAB):
            later = (SLAB - 1 - (here[1] ^ d)).astype(F32) * float(tokens)
            term = jnp.exp(-later * rate) * states[d][g].astype(F32)
            total = term if total is None else total + term
        out[g] = total.astype(BF16)


def incoming_kernel(tokens, here, rates, *refs):
    slabs = rates.shape[0]
    states, earlier, outs = refs[:SLAB], refs[SLAB : SLAB + slabs - 1], refs[SLAB + slabs - 1 :]
    for g in range(slabs):
        rate = rates[lax.rem(g - here[0] + slabs, slabs), : states[0].shape[1]]
        entering = earlier[0][g].astype(F32)
        for k in range(1, slabs - 1):
            entering += jnp.exp(-float(k * SLAB * tokens) * rate) * earlier[k][g].astype(F32)
        for d in range(SLAB):
            block = here[1] ^ d
            total = jnp.exp(-(block.astype(F32) * float(tokens)) * rate) * entering
            for e in range(SLAB):
                if e != d:
                    between = block - 1 - (here[1] ^ e)
                    factor = jnp.exp(-(jnp.maximum(between, 0).astype(F32) * float(tokens)) * rate)
                    factor = jnp.where(between >= 0, factor, jnp.zeros_like(factor))
                    total += factor * states[e][g].astype(F32)
            outs[d][g] = total.astype(BF16)


def local_kernel(modes, here, u_ref, *refs):
    rates, y_ref, wide = refs[:SLAB], refs[-2], refs[-1]
    tokens = u_ref.shape[1]
    rate = registers(rates, here[1], wide, 0, modes)
    rest = registers(rates, here[1], wide, modes, modes + 1)
    decay = [jnp.exp(-r) for r in rate]
    weight = [rest[m] * jnp.sqrt(2.0 * rate[m]) for m in range(modes)]
    skip = rest[modes]

    def step(index, states):
        for inner in range(SUBLANES):
            now = index * SUBLANES + inner
            u = u_ref[0, now]
            states = tuple(states[m] * decay[m] + u for m in range(modes))
            y_ref[0, now] = tree_sum([weight[m] * states[m] for m in range(modes)] + [skip * u])
        return states

    zero = tuple(jnp.zeros((SUBLANES, LANES), F32) for _ in range(modes))
    lax.fori_loop(0, tokens // SUBLANES, step, zero)


def gated_kernel(modes, here, query_ref, y_ref, *refs):
    rates, incoming = refs[:SLAB], refs[SLAB : 2 * SLAB]
    out_ref, wide, out_rows = refs[2 * SLAB :]
    tokens = query_ref.shape[1]
    pitch = tokens + SUBLANES
    rate = registers(rates, here[1], wide, 0, modes)
    rest = registers(rates, here[1], wide, modes, modes)
    state = registers(incoming, here[1], wide, 0, modes)
    decay = [jnp.exp(-r) for r in rate]
    weighted = tuple(rest[m] * jnp.sqrt(2.0 * rate[m]) * state[m] for m in range(modes))

    def step(index, weighted):
        for inner in range(SUBLANES):
            now = index * SUBLANES + inner
            weighted = tuple(weighted[m] * decay[m] for m in range(modes))
            long_out = tree_sum([y_ref[0, now], *weighted])
            long_out = long_out.astype(BF16).astype(F32)
            out_rows[pl.ds(now, SUBLANES, stride=pitch), :] = query_ref[0, now] * long_out
        return weighted

    lax.fori_loop(0, tokens // SUBLANES, step, weighted)
    for tile in range(SUBLANES):
        out_ref[:, pl.ds(tile * LANES, LANES)] = out_rows[pl.ds(tile * pitch, tokens), :].astype(BF16)


def project_kernel(count, picks, here, *refs):
    out_ref, slots, sems = refs[-3:]
    depth, share = slots.shape[1:]
    blocks, sources = refs[: SIDE * count], refs[SIDE * count : -3]
    half = depth // SIDE
    columns = pl.ds(pl.multiple_of(here[0] * share, share), share)
    copies = []
    for i, (which, rank) in enumerate(picks):
        if rank is None:
            source = sources[which].at[:, columns]
        else:
            source = sources[which].at[here[rank], :, columns]
        copies.append(pltpu.make_async_copy(source, slots.at[i], sems.at[i]))
        copies[-1].start()
    for i in range(len(picks)):
        copies[i].wait()
        for j in range(count):
            total = None
            for h in range(SIDE):
                term = jnp.dot(
                    blocks[SIDE * j + h][...],
                    slots[i, h * half : (h + 1) * half],
                    preferred_element_type=F32,
                )
                total = term if total is None else total + term
            out_ref[j, i] = total.astype(BF16)


def place_kernel(kept, steps, here, *refs):
    per_pair = 2 * steps
    sources, out_ref = refs[: SIDE * per_pair], refs[-1]
    share = sources[0].shape[2]
    tp_me, rank = here[0], here[1]
    for slot in range(kept):
        step = here[2 + slot]
        for pair in range(SIDE):
            mine = sources[pair * per_pair : (pair + 1) * per_pair]
            for near in range(SIDE):
                piece = rank ^ (SIDE * pair + near)
                for t in range(SIDE):
                    start = ((slot * SLAB + piece) * SIDE + t) * share
                    target = pl.ds(pl.multiple_of(start, share), share)
                    own = jnp.logical_and(step == 0, tp_me == t)
                    moved = jnp.logical_and(step == 0, tp_me != t)
                    choices = [(own, mine[0]), (moved, mine[1])]
                    choices += [(step == k, mine[2 * k + t]) for k in range(1, steps)]
                    for chosen, source in choices:
                        index = near if source.shape[0] == SIDE else SIDE * pair + near

                        @pl.when(chosen)
                        def _(source=source, index=index, target=target):
                            out_ref[:, target] = source[index]


def ring_order(count):
    return [0] + list(range(1, count, 2)) + [i for i in range(count - 1, 0, -1) if i % 2 == 0]


def any_size(features, conv_weight, decay_rates, residues, skip_gain, out_weight):
    tokens, width = features.shape[1:]
    ctx, tp = lax.axis_size("ctx"), lax.axis_size("tp")
    me, tp_me = lax.axis_index("ctx"), lax.axis_index("tp")
    halo = lax.ppermute(features[:, tokens - HALO :], "ctx", [(i, i + 1) for i in range(ctx - 1)])
    extended = jnp.concatenate([halo, features], axis=1).astype(F32)
    taps = lax.dynamic_slice_in_dim(conv_weight, tp_me * width, width, 2)
    filtered = sum(taps[:, j, None] * extended[:, HALO - j : HALO - j + tokens] for j in range(TAPS))
    u = (filtered[1] * filtered[2]).astype(BF16).astype(F32)
    rates, weights, skip = (
        lax.all_gather(a, "ctx", axis=a.ndim - 1, tiled=True) for a in (decay_rates, residues, skip_gain)
    )
    weights = weights * jnp.sqrt(2.0 * rates)
    decay = jnp.exp(-rates)
    zero = jnp.zeros(rates.shape, F32)
    left = lax.fori_loop(0, tokens, lambda t, s: s * decay + u[t], zero)
    lefts = lax.all_gather(left, "ctx")
    block_decay = jnp.exp(-float(tokens) * rates)
    entering = lax.fori_loop(0, me, lambda b, s: s * block_decay + lefts[b], zero)

    def advance(states, now):
        states = states * decay + now
        return states, jnp.sum(weights * states, axis=0) + skip * now

    long_out = lax.scan(advance, entering, u)[1].astype(BF16).astype(F32)
    gated = (filtered[0] * long_out).astype(BF16)
    whole = lax.all_gather(gated, "ctx", axis=0, tiled=True)
    partial = jnp.dot(whole, out_weight, preferred_element_type=F32).astype(BF16)
    share = partial.shape[1] // tp
    partial = partial.reshape(ctx * tokens, tp, share).transpose(1, 0, 2)
    partial = lax.all_to_all(partial, "tp", split_axis=0, concat_axis=0, tiled=True)
    summed = jnp.sum(partial.astype(F32), axis=0).astype(BF16).reshape(ctx, tokens, share)
    summed = lax.all_to_all(summed, "ctx", split_axis=0, concat_axis=0, tiled=True)
    placed = lax.all_to_all(
        summed.reshape(tp, ctx // tp, tokens, share), "tp", split_axis=0, concat_axis=0, tiled=True
    )
    return placed.transpose(2, 1, 0, 3).reshape(tokens, width)


def per_device(features, conv_weight, decay_rates, residues, skip_gain, out_weight):
    tokens, width = features.shape[1:]
    modes, owned = decay_rates.shape
    ctx, tp = lax.axis_size("ctx"), lax.axis_size("tp")
    depth, columns = out_weight.shape
    share = columns // tp
    if owned * SLAB != GROUP or tp != SIDE or share % LANES or ctx // SLAB < 3:
        return any_size(features, conv_weight, decay_rates, residues, skip_gain, out_weight)
    slabs = ctx // SLAB
    groups = width // GROUP
    me, tp_me = lax.axis_index("ctx"), lax.axis_index("tp")
    z_me, rank = me // SLAB, me % SLAB
    order = ring_order(slabs)
    place = [order.index(z) for z in range(slabs)]
    here = jnp.stack([z_me, rank, tp_me]).astype(jnp.int32)

    def within_slab(array, mask):
        return lax.ppermute(array, "ctx", [(i, i ^ mask) for i in range(ctx)])

    def slab_all(array):
        return [array] + [within_slab(array, mask) for mask in range(1, SLAB)]

    def from_slab(array, by):
        return lax.ppermute(array, "ctx", [(i, (i - by * SLAB) % ctx) for i in range(ctx)])

    def ring(array):
        pairs = []
        for i in range(ctx):
            z, rest = divmod(i, SLAB)
            pairs.append((i, order[(place[z] + 1) % slabs] * SLAB + rest))
        return lax.ppermute(array, "ctx", pairs)

    halo = lax.ppermute(
        features[:, tokens - HALO :, :], "ctx", [(i, i + 1) for i in range(ctx - 1)]
    )
    rows = jnp.concatenate([decay_rates, residues, skip_gain[None]], axis=0)
    rows = jnp.stack([rows] + [from_slab(rows, by) for by in range(1, slabs)])
    rows, halo = lax.optimization_barrier((rows, halo))
    rates = slab_all(rows)

    beside = within_slab(out_weight, 1)
    slab_weights = lax.all_gather(
        out_weight,
        "ctx",
        axis_index_groups=[list(range(z * SLAB, (z + 1) * SLAB)) for z in range(slabs)],
    )

    limit = pltpu.CompilerParams(vmem_limit_bytes=52 * 1024 * 1024)
    light = pl.CostEstimate(flops=1, bytes_accessed=1, transcendentals=0)
    series_shape = jax.ShapeDtypeStruct((groups, tokens, SUBLANES, LANES), F32)
    state_shape = jax.ShapeDtypeStruct((groups, modes, owned), BF16)
    scratch_rows = pltpu.VMEM((SUBLANES * (tokens + SUBLANES), LANES), F32)
    wide = pltpu.VMEM((SUBLANES * (modes + SUBLANES), LANES), F32)
    series = pl.BlockSpec((1, tokens, SUBLANES, LANES), lambda g, here: (g, 0, 0, 0))
    state_spec = pl.BlockSpec((1, modes, owned), lambda g, here: (g, 0, 0))
    rate_spec = pl.BlockSpec(
        (1, 2 * modes + 1, owned), lambda g, here: (lax.rem(g - here[0] + slabs, slabs), 0, 0)
    )

    def grouped(kernel, name, in_specs, out_specs, out_shape, scratch, groups=groups):
        return pl.pallas_call(
            kernel,
            grid_spec=pltpu.PrefetchScalarGridSpec(
                num_scalar_prefetch=1,
                grid=(groups,),
                in_specs=in_specs,
                out_specs=out_specs,
                scratch_shapes=scratch,
            ),
            out_shape=out_shape,
            compiler_params=limit,
            cost_estimate=light,
            name=name,
        )

    u, query = grouped(
        filter_kernel,
        "short_filters",
        [
            pl.BlockSpec((3, tokens, GROUP), lambda g, here: (0, 0, g)),
            pl.BlockSpec((3, HALO, GROUP), lambda g, here: (0, 0, g)),
            pl.BlockSpec((3, TAPS, GROUP), lambda g, here: (0, 0, here[2] * groups + g)),
        ],
        [series, series],
        [series_shape, series_shape],
        [pltpu.VMEM((3 * TAPS, SUBLANES, LANES), F32), scratch_rows, scratch_rows, scratch_rows],
    )(here, features, halo, conv_weight)

    left = grouped(
        functools.partial(state_kernel, modes),
        "block_states",
        [series] + [rate_spec] * SLAB,
        [state_spec] * SLAB,
        [state_shape] * SLAB,
        [wide],
    )(here, u, *rates)
    left = [left[0]] + [within_slab(left[d], d) for d in range(1, SLAB)]

    smem = pl.BlockSpec(memory_space=pltpu.SMEM)
    vmem = pl.BlockSpec(memory_space=pltpu.VMEM)
    slab_left = pl.pallas_call(
        functools.partial(slab_kernel, tokens),
        in_specs=[smem] + [vmem] * (1 + SLAB),
        out_specs=vmem,
        out_shape=state_shape,
        compiler_params=limit,
        cost_estimate=light,
        name="slab_states",
    )(here, rows, *left)
    earlier = [
        lax.ppermute(slab_left, "ctx", [(i, i + by * SLAB) for i in range(ctx - by * SLAB)])
        for by in range(1, slabs)
    ]

    local = grouped(
        functools.partial(local_kernel, modes),
        "local_convolution",
        [series] + [rate_spec] * SLAB,
        series,
        series_shape,
        [wide],
    )(here, u, *rates)

    incoming = pl.pallas_call(
        functools.partial(incoming_kernel, tokens),
        in_specs=[smem] + [vmem] * (SLAB + slabs),
        out_specs=[vmem] * SLAB,
        out_shape=[state_shape] * SLAB,
        compiler_params=limit,
        cost_estimate=light,
        name="incoming_states",
    )(here, rows, *left, *earlier)
    incoming = [incoming[0]] + [within_slab(incoming[d], d) for d in range(1, SLAB)]

    def gated_half(half):
        count = groups // SIDE
        first = half * count

        def shifted(spec):
            return pl.BlockSpec(spec.block_shape, lambda g, here: spec.index_map(g + first, here))

        return grouped(
            functools.partial(gated_kernel, modes),
            "gated_block",
            [shifted(s) for s in [series] * 2 + [rate_spec] * SLAB + [state_spec] * SLAB],
            pl.BlockSpec((tokens, GROUP), lambda g, here: (0, g)),
            jax.ShapeDtypeStruct((tokens, width // SIDE), BF16),
            [wide, scratch_rows],
            count,
        )(here, query, local, *rates, *incoming)

    def project(blocks, sources, picks, share_index):
        scalars = jnp.stack([share_index, rank ^ 2, rank ^ 3]).astype(jnp.int32)
        return pl.pallas_call(
            functools.partial(project_kernel, len(blocks), picks),
            in_specs=[smem]
            + [vmem] * (SIDE * len(blocks))
            + [pl.BlockSpec(memory_space=pltpu.HBM)] * len(sources),
            out_specs=vmem,
            out_shape=jax.ShapeDtypeStruct((len(blocks), len(picks), tokens, share), BF16),
            scratch_shapes=[
                pltpu.VMEM((len(picks), depth, share), BF16),
                pltpu.SemaphoreType.DMA((len(picks),)),
            ],
            compiler_params=limit,
            cost_estimate=light,
            name="project_block",
        )(scalars, *[h for b in blocks for h in b], *sources)

    def summed_over_tp(blocks, sources, picks, away=None):
        if away is None:
            away = project(blocks, sources, picks, 1 - tp_me)
        got = lax.ppermute(away, "tp", [(0, 1), (1, 0)])
        mine = project(blocks, sources, picks, tp_me)
        return (mine.astype(F32) + got.astype(F32)).astype(BF16)

    half_of = [z * tp // slabs for z in range(slabs)]

    def deliver(summed, by):
        pairs = [[], []]
        for i in range(ctx):
            z, rest = divmod(i, SLAB)
            target = order[(place[z] - by) % slabs] * SLAB + rest
            for t in range(tp):
                pairs[t].append((i * tp + t, target * tp + half_of[z]))
        if by == 0:
            moves = [p for p in pairs[0] + pairs[1] if p[0] != p[1]]
            return [summed, lax.ppermute(summed, ("ctx", "tp"), moves)]
        return [lax.ppermute(summed, ("ctx", "tp"), moves) for moves in pairs]

    near, far, both = (
        ((0, None), (1, None)),
        ((0, 1), (0, 2)),
        ((0, None), (1, None), (2, 1), (2, 2)),
    )
    blocks = [[gated_half(h) for h in range(SIDE)]]
    arrived = [[], []]
    summed = None
    for step in range(slabs - 1):
        first, second = blocks[step]
        if step:
            second, summed, arrived[0] = lax.optimization_barrier((second, summed, arrived[0]))
            arrived[0] += deliver(summed, step - 1)
        blocks.append([ring(first), ring(second)])
        summed = summed_over_tp([blocks[step]], [out_weight, beside], near)[0]
    slab_weights, summed, arrived[0] = lax.optimization_barrier((slab_weights, summed, arrived[0]))
    arrived[0] += deliver(summed, slabs - 2)
    away = project(blocks[: slabs - 1], [slab_weights], far, 1 - tp_me)
    _, blocks[-1] = lax.optimization_barrier((away, blocks[-1]))
    batch = summed_over_tp(blocks[: slabs - 1], [slab_weights], far, away)
    for step in range(slabs - 1):
        arrived[1] += deliver(batch[step], step)
    last = summed_over_tp(blocks[slabs - 1 :], [out_weight, beside, slab_weights], both)
    last = deliver(last[0], slabs - 1)
    arrived = [a + last for a in arrived]

    def place_of(z):
        return sum(jnp.where(z == k, place[k], 0) for k in range(slabs))

    kept = slabs // tp
    steps = [
        lax.rem(place_of(tp_me * kept + j) - place_of(z_me) + slabs, slabs) for j in range(kept)
    ]
    return pl.pallas_call(
        functools.partial(place_kernel, kept, slabs),
        in_specs=[smem] + [vmem] * (SIDE * 2 * slabs),
        out_specs=vmem,
        out_shape=jax.ShapeDtypeStruct((tokens, width), BF16),
        compiler_params=limit,
        cost_estimate=light,
        name="place_columns",
    )(jnp.stack([tp_me, rank, *steps]).astype(jnp.int32), *arrived[0], *arrived[1])


def solution(mesh):
    in_specs = (
        P(None, "ctx", "tp"),
        P(),
        P(None, ("tp", "ctx")),
        P(None, ("tp", "ctx")),
        P(("tp", "ctx")),
        P("tp", "ctx"),
    )
    out_specs = P("ctx", "tp")
    return jax.shard_map(
        per_device, mesh=mesh, in_specs=in_specs, out_specs=out_specs, check_vma=False
    )
```

```python
import functools

import jax
import jax.numpy as jnp
from jax import lax
from jax.experimental import pallas as pl
from jax.experimental.pallas import tpu as pltpu
from jax.sharding import PartitionSpec as P

LANES = 128
SUBLANES = 8
GROUP = LANES * SUBLANES
HALO = 2
TAPS = 3
SIDE = 2
SLAB = SIDE * SIDE
F32 = jnp.float32
BF16 = jnp.bfloat16


def spread(scratch, halo, block, pitch):
    tokens = block.shape[0]
    for tile in range(SUBLANES):
        lanes = pl.ds(tile * LANES, LANES)
        scratch[pl.ds(tile * pitch + SUBLANES - HALO, HALO), :] = halo[:, lanes].astype(F32)
        scratch[pl.ds(tile * pitch + SUBLANES, tokens), :] = block[:, lanes].astype(F32)


def token(scratch, index, pitch):
    return scratch[pl.ds(index, SUBLANES, stride=pitch), :]


def tree_sum(terms):
    while len(terms) > 1:
        terms = [a + b for a, b in zip(terms[::2], terms[1::2])] + terms[len(terms) & ~1 :]
    return terms[0]


def filter_kernel(here, features, halo, taps, u_ref, query_ref, tap_rows, *rows):
    tokens = features.shape[1]
    pitch = tokens + SUBLANES
    for tile in range(SUBLANES):
        for which in range(3):
            for j in range(TAPS):
                row = which * TAPS + j
                tap_rows[row, tile : tile + 1] = taps[which, j : j + 1, tile * LANES : (tile + 1) * LANES]
    for which in range(3):
        spread(rows[which], halo.at[which], features.at[which], pitch)
    weights = [[tap_rows[which * TAPS + j] for j in range(TAPS)] for which in range(3)]

    def step(index, carry):
        carry = list(carry)
        for inner in range(SUBLANES):
            now = index * SUBLANES + inner
            filtered = []
            for which in range(3):
                last, before = carry[which]
                fresh = token(rows[which], now + SUBLANES, pitch)
                filtered.append(
                    weights[which][0] * fresh + weights[which][1] * last + weights[which][2] * before
                )
                carry[which] = (fresh, last)
            query_ref[0, now] = filtered[0]
            u_ref[0, now] = (filtered[1] * filtered[2]).astype(BF16).astype(F32)
        return tuple(carry)

    start = tuple(
        (token(rows[which], SUBLANES - 1, pitch), token(rows[which], SUBLANES - 2, pitch))
        for which in range(3)
    )
    lax.fori_loop(0, tokens // SUBLANES, step, start)


def registers(refs, rank, wide, first, count):
    pitch = wide.shape[0] // SUBLANES
    each = SUBLANES // SLAB
    for d in range(SLAB):
        for j in range(each):
            start = pl.multiple_of(((d ^ rank) * each + j) * pitch, SUBLANES)
            rows = refs[d][0, first : first + count, j * LANES : (j + 1) * LANES]
            wide[pl.ds(start, count), :] = rows.astype(F32)
    return [wide[pl.ds(m, SUBLANES, stride=pitch), :] for m in range(count)]


def state_kernel(modes, here, u_ref, *refs):
    rates, outs, wide = refs[:SLAB], refs[SLAB : 2 * SLAB], refs[-1]
    rank = here[1]
    tokens = u_ref.shape[1]
    decay = [jnp.exp(-rate) for rate in registers(rates, rank, wide, 0, modes)]

    def step(index, states):
        for inner in range(SUBLANES):
            u = u_ref[0, index * SUBLANES + inner]
            states = tuple(states[m] * decay[m] + u for m in range(modes))
        return states

    zero = tuple(jnp.zeros((SUBLANES, LANES), F32) for _ in range(modes))
    states = lax.fori_loop(0, tokens // SUBLANES, step, zero)
    each = SUBLANES // SLAB
    pitch = wide.shape[0] // SUBLANES
    for m in range(modes):
        wide[pl.ds(m, SUBLANES, stride=pitch), :] = states[m]
    for d in range(SLAB):
        for j in range(each):
            start = pl.multiple_of(((d ^ rank) * each + j) * pitch, SUBLANES)
            outs[d][0, :, j * LANES : (j + 1) * LANES] = wide[pl.ds(start, modes), :].astype(BF16)


def slab_kernel(tokens, here, rates, *refs):
    states, out = refs[:SLAB], refs[SLAB]
    slabs = rates.shape[0]
    for g in range(slabs):
        rate = rates[lax.rem(g - here[0] + slabs, slabs), : states[0].shape[1]]
        total = None
        for d in range(SLAB):
            later = (SLAB - 1 - (here[1] ^ d)).astype(F32) * float(tokens)
            term = jnp.exp(-later * rate) * states[d][g].astype(F32)
            total = term if total is None else total + term
        out[g] = total.astype(BF16)


def incoming_kernel(tokens, here, rates, *refs):
    slabs = rates.shape[0]
    states, earlier, outs = refs[:SLAB], refs[SLAB : SLAB + slabs - 1], refs[SLAB + slabs - 1 :]
    for g in range(slabs):
        rate = rates[lax.rem(g - here[0] + slabs, slabs), : states[0].shape[1]]
        entering = earlier[0][g].astype(F32)
        for k in range(1, slabs - 1):
            entering += jnp.exp(-float(k * SLAB * tokens) * rate) * earlier[k][g].astype(F32)
        for d in range(SLAB):
            block = here[1] ^ d
            total = jnp.exp(-(block.astype(F32) * float(tokens)) * rate) * entering
            for e in range(SLAB):
                if e != d:
                    between = block - 1 - (here[1] ^ e)
                    factor = jnp.exp(-(jnp.maximum(between, 0).astype(F32) * float(tokens)) * rate)
                    factor = jnp.where(between >= 0, factor, jnp.zeros_like(factor))
                    total += factor * states[e][g].astype(F32)
            outs[d][g] = total.astype(BF16)


def local_kernel(modes, here, u_ref, *refs):
    rates, y_ref, wide = refs[:SLAB], refs[-2], refs[-1]
    tokens = u_ref.shape[1]
    rate = registers(rates, here[1], wide, 0, modes)
    rest = registers(rates, here[1], wide, modes, modes + 1)
    decay = [jnp.exp(-r) for r in rate]
    weight = [rest[m] * jnp.sqrt(2.0 * rate[m]) for m in range(modes)]
    skip = rest[modes]

    def step(index, states):
        for inner in range(SUBLANES):
            now = index * SUBLANES + inner
            u = u_ref[0, now]
            states = tuple(states[m] * decay[m] + u for m in range(modes))
            y_ref[0, now] = tree_sum([weight[m] * states[m] for m in range(modes)] + [skip * u])
        return states

    zero = tuple(jnp.zeros((SUBLANES, LANES), F32) for _ in range(modes))
    lax.fori_loop(0, tokens // SUBLANES, step, zero)


def gated_kernel(modes, here, query_ref, y_ref, *refs):
    rates, incoming = refs[:SLAB], refs[SLAB : 2 * SLAB]
    out_ref, wide, out_rows = refs[2 * SLAB :]
    tokens = query_ref.shape[1]
    pitch = tokens + SUBLANES
    rate = registers(rates, here[1], wide, 0, modes)
    rest = registers(rates, here[1], wide, modes, modes)
    state = registers(incoming, here[1], wide, 0, modes)
    decay = [jnp.exp(-r) for r in rate]
    weighted = tuple(rest[m] * jnp.sqrt(2.0 * rate[m]) * state[m] for m in range(modes))

    def step(index, weighted):
        for inner in range(SUBLANES):
            now = index * SUBLANES + inner
            weighted = tuple(weighted[m] * decay[m] for m in range(modes))
            long_out = tree_sum([y_ref[0, now], *weighted])
            long_out = long_out.astype(BF16).astype(F32)
            out_rows[pl.ds(now, SUBLANES, stride=pitch), :] = query_ref[0, now] * long_out
        return weighted

    lax.fori_loop(0, tokens // SUBLANES, step, weighted)
    for tile in range(SUBLANES):
        out_ref[:, pl.ds(tile * LANES, LANES)] = out_rows[pl.ds(tile * pitch, tokens), :].astype(BF16)


def project_kernel(count, picks, here, *refs):
    out_ref, slots, sems = refs[-3:]
    depth, share = slots.shape[1:]
    blocks, sources = refs[: SIDE * count], refs[SIDE * count : -3]
    half = depth // SIDE
    columns = pl.ds(pl.multiple_of(here[0] * share, share), share)
    copies = []
    for i, (which, rank) in enumerate(picks):
        if rank is None:
            source = sources[which].at[:, columns]
        else:
            source = sources[which].at[here[rank], :, columns]
        copies.append(pltpu.make_async_copy(source, slots.at[i], sems.at[i]))
        copies[-1].start()
    for i in range(len(picks)):
        copies[i].wait()
        for j in range(count):
            total = None
            for h in range(SIDE):
                term = jnp.dot(
                    blocks[SIDE * j + h][...],
                    slots[i, h * half : (h + 1) * half],
                    preferred_element_type=F32,
                )
                total = term if total is None else total + term
            out_ref[j, i] = total.astype(BF16)


def place_kernel(kept, steps, here, *refs):
    per_pair = 2 * steps
    sources, out_ref = refs[: SIDE * per_pair], refs[-1]
    share = sources[0].shape[2]
    tp_me, rank = here[0], here[1]
    for slot in range(kept):
        step = here[2 + slot]
        for pair in range(SIDE):
            mine = sources[pair * per_pair : (pair + 1) * per_pair]
            for near in range(SIDE):
                piece = rank ^ (SIDE * pair + near)
                for t in range(SIDE):
                    start = ((slot * SLAB + piece) * SIDE + t) * share
                    target = pl.ds(pl.multiple_of(start, share), share)
                    own = jnp.logical_and(step == 0, tp_me == t)
                    moved = jnp.logical_and(step == 0, tp_me != t)
                    choices = [(own, mine[0]), (moved, mine[1])]
                    choices += [(step == k, mine[2 * k + t]) for k in range(1, steps)]
                    for chosen, source in choices:
                        index = near if source.shape[0] == SIDE else SIDE * pair + near

                        @pl.when(chosen)
                        def _(source=source, index=index, target=target):
                            out_ref[:, target] = source[index]


def ring_order(count):
    return [0] + list(range(1, count, 2)) + [i for i in range(count - 1, 0, -1) if i % 2 == 0]


def any_size(features, conv_weight, decay_rates, residues, skip_gain, out_weight):
    tokens, width = features.shape[1:]
    ctx, tp = lax.axis_size("ctx"), lax.axis_size("tp")
    me, tp_me = lax.axis_index("ctx"), lax.axis_index("tp")
    halo = lax.ppermute(features[:, tokens - HALO :], "ctx", [(i, i + 1) for i in range(ctx - 1)])
    extended = jnp.concatenate([halo, features], axis=1).astype(F32)
    taps = lax.dynamic_slice_in_dim(conv_weight, tp_me * width, width, 2)
    filtered = sum(taps[:, j, None] * extended[:, HALO - j : HALO - j + tokens] for j in range(TAPS))
    u = (filtered[1] * filtered[2]).astype(BF16).astype(F32)
    rates, weights, skip = (
        lax.all_gather(a, "ctx", axis=a.ndim - 1, tiled=True) for a in (decay_rates, residues, skip_gain)
    )
    weights = weights * jnp.sqrt(2.0 * rates)
    decay = jnp.exp(-rates)
    zero = jnp.zeros(rates.shape, F32)
    left = lax.fori_loop(0, tokens, lambda t, s: s * decay + u[t], zero)
    lefts = lax.all_gather(left, "ctx")
    block_decay = jnp.exp(-float(tokens) * rates)
    entering = lax.fori_loop(0, me, lambda b, s: s * block_decay + lefts[b], zero)

    def advance(states, now):
        states = states * decay + now
        return states, jnp.sum(weights * states, axis=0) + skip * now

    long_out = lax.scan(advance, entering, u)[1].astype(BF16).astype(F32)
    gated = (filtered[0] * long_out).astype(BF16)
    whole = lax.all_gather(gated, "ctx", axis=0, tiled=True)
    partial = jnp.dot(whole, out_weight, preferred_element_type=F32).astype(BF16)
    share = partial.shape[1] // tp
    partial = partial.reshape(ctx * tokens, tp, share).transpose(1, 0, 2)
    partial = lax.all_to_all(partial, "tp", split_axis=0, concat_axis=0, tiled=True)
    summed = jnp.sum(partial.astype(F32), axis=0).astype(BF16).reshape(ctx, tokens, share)
    summed = lax.all_to_all(summed, "ctx", split_axis=0, concat_axis=0, tiled=True)
    placed = lax.all_to_all(
        summed.reshape(tp, ctx // tp, tokens, share), "tp", split_axis=0, concat_axis=0, tiled=True
    )
    return placed.transpose(2, 1, 0, 3).reshape(tokens, width)


def per_device(features, conv_weight, decay_rates, residues, skip_gain, out_weight):
    tokens, width = features.shape[1:]
    modes, owned = decay_rates.shape
    ctx, tp = lax.axis_size("ctx"), lax.axis_size("tp")
    depth, columns = out_weight.shape
    share = columns // tp
    if owned * SLAB != GROUP or tp != SIDE or share % LANES or ctx // SLAB < 3:
        return any_size(features, conv_weight, decay_rates, residues, skip_gain, out_weight)
    slabs = ctx // SLAB
    groups = width // GROUP
    me, tp_me = lax.axis_index("ctx"), lax.axis_index("tp")
    z_me, rank = me // SLAB, me % SLAB
    order = ring_order(slabs)
    place = [order.index(z) for z in range(slabs)]
    here = jnp.stack([z_me, rank, tp_me]).astype(jnp.int32)

    def within_slab(array, mask):
        return lax.ppermute(array, "ctx", [(i, i ^ mask) for i in range(ctx)])

    def from_slab(array, by):
        return lax.ppermute(array, "ctx", [(i, (i - by * SLAB) % ctx) for i in range(ctx)])

    def ring(array):
        pairs = []
        for i in range(ctx):
            z, rest = divmod(i, SLAB)
            pairs.append((i, order[(place[z] + 1) % slabs] * SLAB + rest))
        return lax.ppermute(array, "ctx", pairs)

    halo = lax.ppermute(
        features[:, tokens - HALO :, :], "ctx", [(i, i + 1) for i in range(ctx - 1)]
    )
    rows = jnp.concatenate([decay_rates, residues, skip_gain[None]], axis=0)
    rows = jnp.stack([rows] + [from_slab(rows, by) for by in range(1, slabs)])
    rows, halo = lax.optimization_barrier((rows, halo))
    rates = [rows, within_slab(rows, 1), within_slab(rows, 2)]
    rates.append(within_slab(rates[2], 1))

    beside = within_slab(out_weight, 1)
    slab_weights = lax.all_gather(
        out_weight,
        "ctx",
        axis_index_groups=[list(range(z * SLAB, (z + 1) * SLAB)) for z in range(slabs)],
    )

    limit = pltpu.CompilerParams(vmem_limit_bytes=16 * 1024 * 1024)
    large = pltpu.CompilerParams(vmem_limit_bytes=48 * 1024 * 1024)
    light = pl.CostEstimate(flops=1, bytes_accessed=1, transcendentals=0)
    series_shape = jax.ShapeDtypeStruct((groups, tokens, SUBLANES, LANES), F32)
    state_shape = jax.ShapeDtypeStruct((groups, modes, owned), BF16)
    scratch_rows = pltpu.VMEM((SUBLANES * (tokens + SUBLANES), LANES), F32)
    wide = pltpu.VMEM((SUBLANES * (modes + SUBLANES), LANES), F32)
    series = pl.BlockSpec((1, tokens, SUBLANES, LANES), lambda g, here: (g, 0, 0, 0))
    state_spec = pl.BlockSpec((1, modes, owned), lambda g, here: (g, 0, 0))
    rate_spec = pl.BlockSpec(
        (1, 2 * modes + 1, owned), lambda g, here: (lax.rem(g - here[0] + slabs, slabs), 0, 0)
    )

    def grouped(kernel, name, in_specs, out_specs, out_shape, scratch, groups=groups):
        return pl.pallas_call(
            kernel,
            grid_spec=pltpu.PrefetchScalarGridSpec(
                num_scalar_prefetch=1,
                grid=(groups,),
                in_specs=in_specs,
                out_specs=out_specs,
                scratch_shapes=scratch,
            ),
            out_shape=out_shape,
            compiler_params=limit,
            cost_estimate=light,
            name=name,
        )

    u, query = grouped(
        filter_kernel,
        "short_filters",
        [
            pl.BlockSpec((3, tokens, GROUP), lambda g, here: (0, 0, g)),
            pl.BlockSpec((3, HALO, GROUP), lambda g, here: (0, 0, g)),
            pl.BlockSpec((3, TAPS, GROUP), lambda g, here: (0, 0, here[2] * groups + g)),
        ],
        [series, series],
        [series_shape, series_shape],
        [pltpu.VMEM((3 * TAPS, SUBLANES, LANES), F32), scratch_rows, scratch_rows, scratch_rows],
    )(here, features, halo, conv_weight)

    left = grouped(
        functools.partial(state_kernel, modes),
        "block_states",
        [series] + [rate_spec] * SLAB,
        [state_spec] * SLAB,
        [state_shape] * SLAB,
        [wide],
    )(here, u, *rates)
    left = [left[0]] + [within_slab(left[d], d) for d in range(1, SLAB)]

    smem = pl.BlockSpec(memory_space=pltpu.SMEM)
    vmem = pl.BlockSpec(memory_space=pltpu.VMEM)
    slab_left = pl.pallas_call(
        functools.partial(slab_kernel, tokens),
        in_specs=[smem] + [vmem] * (1 + SLAB),
        out_specs=vmem,
        out_shape=state_shape,
        compiler_params=limit,
        cost_estimate=light,
        name="slab_states",
    )(here, rates[0], *left)
    earlier = [
        lax.ppermute(slab_left, "ctx", [(i, i + by * SLAB) for i in range(ctx - by * SLAB)])
        for by in range(1, slabs)
    ]

    local = grouped(
        functools.partial(local_kernel, modes),
        "local_convolution",
        [series] + [rate_spec] * SLAB,
        series,
        series_shape,
        [wide],
    )(here, u, *rates)
    earlier, local = lax.optimization_barrier((earlier, local))

    incoming = pl.pallas_call(
        functools.partial(incoming_kernel, tokens),
        in_specs=[smem] + [vmem] * (SLAB + slabs),
        out_specs=[vmem] * SLAB,
        out_shape=[state_shape] * SLAB,
        compiler_params=limit,
        cost_estimate=light,
        name="incoming_states",
    )(here, rates[0], *left, *earlier)
    incoming = [incoming[0]] + [within_slab(incoming[d], d) for d in range(1, SLAB)]

    def gated_half(half):
        count = groups // SIDE
        first = half * count

        def shifted(spec):
            return pl.BlockSpec(spec.block_shape, lambda g, here: spec.index_map(g + first, here))

        return grouped(
            functools.partial(gated_kernel, modes),
            "gated_block",
            [shifted(s) for s in [series] * 2 + [rate_spec] * SLAB + [state_spec] * SLAB],
            pl.BlockSpec((tokens, GROUP), lambda g, here: (0, g)),
            jax.ShapeDtypeStruct((tokens, width // SIDE), BF16),
            [wide, scratch_rows],
            count,
        )(here, query, local, *rates, *incoming)

    def project(blocks, sources, picks, share_index):
        scalars = jnp.stack([share_index, rank ^ 2, rank ^ 3]).astype(jnp.int32)
        return pl.pallas_call(
            functools.partial(project_kernel, len(blocks), picks),
            in_specs=[smem]
            + [vmem] * (SIDE * len(blocks))
            + [pl.BlockSpec(memory_space=pltpu.HBM)] * len(sources),
            out_specs=vmem,
            out_shape=jax.ShapeDtypeStruct((len(blocks), len(picks), tokens, share), BF16),
            scratch_shapes=[
                pltpu.VMEM((len(picks), depth, share), BF16),
                pltpu.SemaphoreType.DMA((len(picks),)),
            ],
            compiler_params=large,
            cost_estimate=light,
            name="project_block",
        )(scalars, *[h for b in blocks for h in b], *sources)

    def project_both(blocks, sources, picks):
        away = project(blocks, sources, picks, 1 - tp_me)
        got = lax.ppermute(away, "tp", [(0, 1), (1, 0)])
        return project(blocks, sources, picks, tp_me), got

    def total(mine, got):
        return (mine.astype(F32) + got.astype(F32)).astype(BF16)

    half_of = [z * tp // slabs for z in range(slabs)]

    def deliver(summed, by):
        pairs = [[], []]
        for i in range(ctx):
            z, rest = divmod(i, SLAB)
            target = order[(place[z] - by) % slabs] * SLAB + rest
            for t in range(tp):
                pairs[t].append((i * tp + t, target * tp + half_of[z]))
        if by == 0:
            moves = [p for p in pairs[0] + pairs[1] if p[0] != p[1]]
            return [summed, lax.ppermute(summed, ("ctx", "tp"), moves)]
        return [lax.ppermute(summed, ("ctx", "tp"), moves) for moves in pairs]

    near, far, both = (
        ((0, None), (1, None)),
        ((0, 1), (0, 2)),
        ((0, None), (1, None), (2, 1), (2, 2)),
    )
    near, far, both = (
        ((0, None), (1, None)),
        ((0, 1), (0, 2)),
        ((0, None), (1, None), (2, 1), (2, 2)),
    )
    blocks = [[gated_half(h) for h in range(SIDE)]]
    arrived = [[], []]
    for step in range(slabs - 1):
        first, second = blocks[step]
        if step:
            first, _ = lax.optimization_barrier((first, mine))
        blocks.append([ring(first), ring(second)])
        block = blocks[step]
        if step > 1:
            block, arrived[0] = lax.optimization_barrier((block, arrived[0]))
        if step:
            arrived[0] += deliver(total(mine, got)[0], step - 1)
        mine, got = project_both([block], [out_weight, beside], near)
    slab_weights, mine, arrived[0] = lax.optimization_barrier((slab_weights, mine, arrived[0]))
    arrived[0] += deliver(total(mine, got)[0], slabs - 2)
    mine, got = project_both(blocks[: slabs - 1], [slab_weights], far)
    batch = total(mine, got)
    for step in range(slabs - 1):
        arrived[1] += deliver(batch[step], step)
    _, block = lax.optimization_barrier((mine, blocks[-1]))
    mine, got = project_both([block], [out_weight, beside, slab_weights], both)
    last = deliver(total(mine, got)[0], slabs - 1)
    arrived = [a + last for a in arrived]

    def place_of(z):
        return sum(jnp.where(z == k, place[k], 0) for k in range(slabs))

    kept = slabs // tp
    steps = [
        lax.rem(place_of(tp_me * kept + j) - place_of(z_me) + slabs, slabs) for j in range(kept)
    ]
    return pl.pallas_call(
        functools.partial(place_kernel, kept, slabs),
        in_specs=[smem] + [vmem] * (SIDE * 2 * slabs),
        out_specs=vmem,
        out_shape=jax.ShapeDtypeStruct((tokens, width), BF16),
        compiler_params=limit,
        cost_estimate=light,
        name="place_columns",
    )(jnp.stack([tp_me, rank, *steps]).astype(jnp.int32), *arrived[0], *arrived[1])


def solution(mesh):
    in_specs = (
        P(None, "ctx", "tp"),
        P(),
        P(None, ("tp", "ctx")),
        P(None, ("tp", "ctx")),
        P(("tp", "ctx")),
        P("tp", "ctx"),
    )
    out_specs = P("ctx", "tp")
    return jax.shard_map(
        per_device, mesh=mesh, in_specs=in_specs, out_specs=out_specs, check_vma=False
    )
```

```python
import functools

import jax
import jax.numpy as jnp
from jax import lax
from jax.experimental import pallas as pl
from jax.experimental.pallas import tpu as pltpu
from jax.sharding import PartitionSpec as P

LANES = 128
SUBLANES = 8
GROUP = LANES * SUBLANES
HALO = 2
TAPS = 3
SIDE = 2
SLAB = SIDE * SIDE
F32 = jnp.float32
BF16 = jnp.bfloat16


def spread(scratch, halo, block, pitch):
    tokens = block.shape[0]
    for tile in range(SUBLANES):
        lanes = pl.ds(tile * LANES, LANES)
        scratch[pl.ds(tile * pitch + SUBLANES - HALO, HALO), :] = halo[:, lanes].astype(F32)
        scratch[pl.ds(tile * pitch + SUBLANES, tokens), :] = block[:, lanes].astype(F32)


def token(scratch, index, pitch):
    return scratch[pl.ds(index, SUBLANES, stride=pitch), :]


def tree_sum(terms):
    while len(terms) > 1:
        terms = [a + b for a, b in zip(terms[::2], terms[1::2])] + terms[len(terms) & ~1 :]
    return terms[0]


def filter_kernel(here, features, halo, taps, u_ref, query_ref, tap_rows, *rows):
    tokens = features.shape[1]
    pitch = tokens + SUBLANES
    for tile in range(SUBLANES):
        for which in range(3):
            for j in range(TAPS):
                row = which * TAPS + j
                tap_rows[row, tile : tile + 1] = taps[which, j : j + 1, tile * LANES : (tile + 1) * LANES]
    for which in range(3):
        spread(rows[which], halo.at[which], features.at[which], pitch)
    weights = [[tap_rows[which * TAPS + j] for j in range(TAPS)] for which in range(3)]

    def step(index, carry):
        carry = list(carry)
        for inner in range(SUBLANES):
            now = index * SUBLANES + inner
            filtered = []
            for which in range(3):
                last, before = carry[which]
                fresh = token(rows[which], now + SUBLANES, pitch)
                filtered.append(
                    weights[which][0] * fresh + weights[which][1] * last + weights[which][2] * before
                )
                carry[which] = (fresh, last)
            query_ref[0, now] = filtered[0]
            u_ref[0, now] = (filtered[1] * filtered[2]).astype(BF16).astype(F32)
        return tuple(carry)

    start = tuple(
        (token(rows[which], SUBLANES - 1, pitch), token(rows[which], SUBLANES - 2, pitch))
        for which in range(3)
    )
    lax.fori_loop(0, tokens // SUBLANES, step, start)


def registers(refs, rank, wide, first, count):
    pitch = wide.shape[0] // SUBLANES
    each = SUBLANES // SLAB
    for d in range(SLAB):
        for j in range(each):
            start = pl.multiple_of(((d ^ rank) * each + j) * pitch, SUBLANES)
            rows = refs[d][0, first : first + count, j * LANES : (j + 1) * LANES]
            wide[pl.ds(start, count), :] = rows.astype(F32)
    return [wide[pl.ds(m, SUBLANES, stride=pitch), :] for m in range(count)]


def state_kernel(modes, here, u_ref, *refs):
    rates, outs, wide = refs[:SLAB], refs[SLAB : 2 * SLAB], refs[-1]
    rank = here[1]
    tokens = u_ref.shape[1]
    decay = [jnp.exp(-rate) for rate in registers(rates, rank, wide, 0, modes)]

    def step(index, states):
        for inner in range(SUBLANES):
            u = u_ref[0, index * SUBLANES + inner]
            states = tuple(states[m] * decay[m] + u for m in range(modes))
        return states

    zero = tuple(jnp.zeros((SUBLANES, LANES), F32) for _ in range(modes))
    states = lax.fori_loop(0, tokens // SUBLANES, step, zero)
    each = SUBLANES // SLAB
    pitch = wide.shape[0] // SUBLANES
    for m in range(modes):
        wide[pl.ds(m, SUBLANES, stride=pitch), :] = states[m]
    for d in range(SLAB):
        for j in range(each):
            start = pl.multiple_of(((d ^ rank) * each + j) * pitch, SUBLANES)
            outs[d][0, :, j * LANES : (j + 1) * LANES] = wide[pl.ds(start, modes), :].astype(BF16)


def slab_kernel(tokens, here, rates, *refs):
    states, out = refs[:SLAB], refs[SLAB]
    slabs = rates.shape[0]
    for g in range(slabs):
        rate = rates[lax.rem(g - here[0] + slabs, slabs), : states[0].shape[1]]
        total = None
        for d in range(SLAB):
            later = (SLAB - 1 - (here[1] ^ d)).astype(F32) * float(tokens)
            term = jnp.exp(-later * rate) * states[d][g].astype(F32)
            total = term if total is None else total + term
        out[g] = total.astype(BF16)


def incoming_kernel(tokens, here, rates, *refs):
    slabs = rates.shape[0]
    states, earlier, outs = refs[:SLAB], refs[SLAB : SLAB + slabs - 1], refs[SLAB + slabs - 1 :]
    for g in range(slabs):
        rate = rates[lax.rem(g - here[0] + slabs, slabs), : states[0].shape[1]]
        entering = earlier[0][g].astype(F32)
        for k in range(1, slabs - 1):
            entering += jnp.exp(-float(k * SLAB * tokens) * rate) * earlier[k][g].astype(F32)
        for d in range(SLAB):
            block = here[1] ^ d
            total = jnp.exp(-(block.astype(F32) * float(tokens)) * rate) * entering
            for e in range(SLAB):
                if e != d:
                    between = block - 1 - (here[1] ^ e)
                    factor = jnp.exp(-(jnp.maximum(between, 0).astype(F32) * float(tokens)) * rate)
                    factor = jnp.where(between >= 0, factor, jnp.zeros_like(factor))
                    total += factor * states[e][g].astype(F32)
            outs[d][g] = total.astype(BF16)


def local_kernel(modes, here, u_ref, *refs):
    rates, y_ref, wide = refs[:SLAB], refs[-2], refs[-1]
    tokens = u_ref.shape[1]
    rate = registers(rates, here[1], wide, 0, modes)
    rest = registers(rates, here[1], wide, modes, modes + 1)
    decay = [jnp.exp(-r) for r in rate]
    weight = [rest[m] * jnp.sqrt(2.0 * rate[m]) for m in range(modes)]
    skip = rest[modes]

    def step(index, states):
        for inner in range(SUBLANES):
            now = index * SUBLANES + inner
            u = u_ref[0, now]
            states = tuple(states[m] * decay[m] + u for m in range(modes))
            y_ref[0, now] = tree_sum([weight[m] * states[m] for m in range(modes)] + [skip * u])
        return states

    zero = tuple(jnp.zeros((SUBLANES, LANES), F32) for _ in range(modes))
    lax.fori_loop(0, tokens // SUBLANES, step, zero)


def gated_kernel(modes, here, query_ref, y_ref, *refs):
    rates, incoming = refs[:SLAB], refs[SLAB : 2 * SLAB]
    out_ref, wide, out_rows = refs[2 * SLAB :]
    tokens = query_ref.shape[1]
    pitch = tokens + SUBLANES
    rate = registers(rates, here[1], wide, 0, modes)
    rest = registers(rates, here[1], wide, modes, modes)
    state = registers(incoming, here[1], wide, 0, modes)
    decay = [jnp.exp(-r) for r in rate]
    weighted = tuple(rest[m] * jnp.sqrt(2.0 * rate[m]) * state[m] for m in range(modes))

    def step(index, weighted):
        for inner in range(SUBLANES):
            now = index * SUBLANES + inner
            weighted = tuple(weighted[m] * decay[m] for m in range(modes))
            long_out = tree_sum([y_ref[0, now], *weighted])
            long_out = long_out.astype(BF16).astype(F32)
            out_rows[pl.ds(now, SUBLANES, stride=pitch), :] = query_ref[0, now] * long_out
        return weighted

    lax.fori_loop(0, tokens // SUBLANES, step, weighted)
    for tile in range(SUBLANES):
        out_ref[:, pl.ds(tile * LANES, LANES)] = out_rows[pl.ds(tile * pitch, tokens), :].astype(BF16)


def project_kernel(count, picks, here, *refs):
    out_ref, slots, sems = refs[-3:]
    depth, share = slots.shape[1:]
    blocks, sources = refs[: SIDE * count], refs[SIDE * count : -3]
    half = depth // SIDE
    columns = pl.ds(pl.multiple_of(here[0] * share, share), share)
    copies = []
    for i, (which, rank) in enumerate(picks):
        if rank is None:
            source = sources[which].at[:, columns]
        else:
            source = sources[which].at[here[rank], :, columns]
        copies.append(pltpu.make_async_copy(source, slots.at[i], sems.at[i]))
        copies[-1].start()
    for i in range(len(picks)):
        copies[i].wait()
        for j in range(count):
            total = None
            for h in range(SIDE):
                term = jnp.dot(
                    blocks[SIDE * j + h][...],
                    slots[i, h * half : (h + 1) * half],
                    preferred_element_type=F32,
                )
                total = term if total is None else total + term
            out_ref[j, i] = total.astype(BF16)


def place_kernel(kept, steps, here, *refs):
    per_pair = 2 * steps
    sources, out_ref = refs[: SIDE * per_pair], refs[-1]
    share = sources[0].shape[2]
    tp_me, rank = here[0], here[1]
    for slot in range(kept):
        step = here[2 + slot]
        for pair in range(SIDE):
            mine = sources[pair * per_pair : (pair + 1) * per_pair]
            for near in range(SIDE):
                piece = rank ^ (SIDE * pair + near)
                for t in range(SIDE):
                    start = ((slot * SLAB + piece) * SIDE + t) * share
                    target = pl.ds(pl.multiple_of(start, share), share)
                    own = jnp.logical_and(step == 0, tp_me == t)
                    moved = jnp.logical_and(step == 0, tp_me != t)
                    choices = [(own, mine[0]), (moved, mine[1])]
                    choices += [(step == k, mine[2 * k + t]) for k in range(1, steps)]
                    for chosen, source in choices:
                        index = near if source.shape[0] == SIDE else SIDE * pair + near

                        @pl.when(chosen)
                        def _(source=source, index=index, target=target):
                            out_ref[:, target] = source[index]


def ring_order(count):
    return [0] + list(range(1, count, 2)) + [i for i in range(count - 1, 0, -1) if i % 2 == 0]


def any_size(features, conv_weight, decay_rates, residues, skip_gain, out_weight):
    tokens, width = features.shape[1:]
    ctx, tp = lax.axis_size("ctx"), lax.axis_size("tp")
    me, tp_me = lax.axis_index("ctx"), lax.axis_index("tp")
    halo = lax.ppermute(features[:, tokens - HALO :], "ctx", [(i, i + 1) for i in range(ctx - 1)])
    extended = jnp.concatenate([halo, features], axis=1).astype(F32)
    taps = lax.dynamic_slice_in_dim(conv_weight, tp_me * width, width, 2)
    filtered = sum(taps[:, j, None] * extended[:, HALO - j : HALO - j + tokens] for j in range(TAPS))
    u = (filtered[1] * filtered[2]).astype(BF16).astype(F32)
    rates, weights, skip = (
        lax.all_gather(a, "ctx", axis=a.ndim - 1, tiled=True) for a in (decay_rates, residues, skip_gain)
    )
    weights = weights * jnp.sqrt(2.0 * rates)
    decay = jnp.exp(-rates)
    zero = jnp.zeros(rates.shape, F32)
    left = lax.fori_loop(0, tokens, lambda t, s: s * decay + u[t], zero)
    lefts = lax.all_gather(left, "ctx")
    block_decay = jnp.exp(-float(tokens) * rates)
    entering = lax.fori_loop(0, me, lambda b, s: s * block_decay + lefts[b], zero)

    def advance(states, now):
        states = states * decay + now
        return states, jnp.sum(weights * states, axis=0) + skip * now

    long_out = lax.scan(advance, entering, u)[1].astype(BF16).astype(F32)
    gated = (filtered[0] * long_out).astype(BF16)
    whole = lax.all_gather(gated, "ctx", axis=0, tiled=True)
    partial = jnp.dot(whole, out_weight, preferred_element_type=F32).astype(BF16)
    share = partial.shape[1] // tp
    partial = partial.reshape(ctx * tokens, tp, share).transpose(1, 0, 2)
    partial = lax.all_to_all(partial, "tp", split_axis=0, concat_axis=0, tiled=True)
    summed = jnp.sum(partial.astype(F32), axis=0).astype(BF16).reshape(ctx, tokens, share)
    summed = lax.all_to_all(summed, "ctx", split_axis=0, concat_axis=0, tiled=True)
    placed = lax.all_to_all(
        summed.reshape(tp, ctx // tp, tokens, share), "tp", split_axis=0, concat_axis=0, tiled=True
    )
    return placed.transpose(2, 1, 0, 3).reshape(tokens, width)


def per_device(features, conv_weight, decay_rates, residues, skip_gain, out_weight):
    tokens, width = features.shape[1:]
    modes, owned = decay_rates.shape
    ctx, tp = lax.axis_size("ctx"), lax.axis_size("tp")
    depth, columns = out_weight.shape
    share = columns // tp
    if owned * SLAB != GROUP or tp != SIDE or share % LANES or ctx // SLAB < 3:
        return any_size(features, conv_weight, decay_rates, residues, skip_gain, out_weight)
    slabs = ctx // SLAB
    groups = width // GROUP
    me, tp_me = lax.axis_index("ctx"), lax.axis_index("tp")
    z_me, rank = me // SLAB, me % SLAB
    order = ring_order(slabs)
    place = [order.index(z) for z in range(slabs)]
    here = jnp.stack([z_me, rank, tp_me]).astype(jnp.int32)

    def within_slab(array, mask):
        return lax.ppermute(array, "ctx", [(i, i ^ mask) for i in range(ctx)])

    def from_slab(array, by):
        return lax.ppermute(array, "ctx", [(i, (i - by * SLAB) % ctx) for i in range(ctx)])

    def ring(array):
        pairs = []
        for i in range(ctx):
            z, rest = divmod(i, SLAB)
            pairs.append((i, order[(place[z] + 1) % slabs] * SLAB + rest))
        return lax.ppermute(array, "ctx", pairs)

    halo = lax.ppermute(
        features[:, tokens - HALO :, :], "ctx", [(i, i + 1) for i in range(ctx - 1)]
    )
    rows = jnp.concatenate([decay_rates, residues, skip_gain[None]], axis=0)
    rows = jnp.stack([rows] + [from_slab(rows, by) for by in range(1, slabs)])
    rows, halo = lax.optimization_barrier((rows, halo))
    rates = [rows, within_slab(rows, 1), within_slab(rows, 2)]

    beside = within_slab(out_weight, 1)
    slab_weights = lax.all_gather(
        out_weight,
        "ctx",
        axis_index_groups=[list(range(z * SLAB, (z + 1) * SLAB)) for z in range(slabs)],
    )

    limit = pltpu.CompilerParams(vmem_limit_bytes=16 * 1024 * 1024)
    large = pltpu.CompilerParams(vmem_limit_bytes=48 * 1024 * 1024)
    light = pl.CostEstimate(flops=1, bytes_accessed=1, transcendentals=0)
    series_shape = jax.ShapeDtypeStruct((groups, tokens, SUBLANES, LANES), F32)
    state_shape = jax.ShapeDtypeStruct((groups, modes, owned), BF16)
    scratch_rows = pltpu.VMEM((SUBLANES * (tokens + SUBLANES), LANES), F32)
    wide = pltpu.VMEM((SUBLANES * (modes + SUBLANES), LANES), F32)
    series = pl.BlockSpec((1, tokens, SUBLANES, LANES), lambda g, here: (g, 0, 0, 0))
    state_spec = pl.BlockSpec((1, modes, owned), lambda g, here: (g, 0, 0))
    rate_spec = pl.BlockSpec(
        (1, 2 * modes + 1, owned), lambda g, here: (lax.rem(g - here[0] + slabs, slabs), 0, 0)
    )

    def grouped(kernel, name, in_specs, out_specs, out_shape, scratch, groups=groups):
        return pl.pallas_call(
            kernel,
            grid_spec=pltpu.PrefetchScalarGridSpec(
                num_scalar_prefetch=1,
                grid=(groups,),
                in_specs=in_specs,
                out_specs=out_specs,
                scratch_shapes=scratch,
            ),
            out_shape=out_shape,
            compiler_params=limit,
            cost_estimate=light,
            name=name,
        )

    u, query = grouped(
        filter_kernel,
        "short_filters",
        [
            pl.BlockSpec((3, tokens, GROUP), lambda g, here: (0, 0, g)),
            pl.BlockSpec((3, HALO, GROUP), lambda g, here: (0, 0, g)),
            pl.BlockSpec((3, TAPS, GROUP), lambda g, here: (0, 0, here[2] * groups + g)),
        ],
        [series, series],
        [series_shape, series_shape],
        [pltpu.VMEM((3 * TAPS, SUBLANES, LANES), F32), scratch_rows, scratch_rows, scratch_rows],
    )(here, features, halo, conv_weight)

    passed, u = lax.optimization_barrier((rates[2], u))
    rates.append(within_slab(passed, 1))

    left = grouped(
        functools.partial(state_kernel, modes),
        "block_states",
        [series] + [rate_spec] * SLAB,
        [state_spec] * SLAB,
        [state_shape] * SLAB,
        [wide],
    )(here, u, *rates)
    left = [left[0]] + [within_slab(left[d], d) for d in range(1, SLAB)]

    smem = pl.BlockSpec(memory_space=pltpu.SMEM)
    vmem = pl.BlockSpec(memory_space=pltpu.VMEM)
    slab_left = pl.pallas_call(
        functools.partial(slab_kernel, tokens),
        in_specs=[smem] + [vmem] * (1 + SLAB),
        out_specs=vmem,
        out_shape=state_shape,
        compiler_params=limit,
        cost_estimate=light,
        name="slab_states",
    )(here, rates[0], *left)
    earlier = [
        lax.ppermute(slab_left, "ctx", [(i, i + by * SLAB) for i in range(ctx - by * SLAB)])
        for by in range(1, slabs)
    ]

    local = grouped(
        functools.partial(local_kernel, modes),
        "local_convolution",
        [series] + [rate_spec] * SLAB,
        series,
        series_shape,
        [wide],
    )(here, u, *rates)
    earlier, local = lax.optimization_barrier((earlier, local))

    incoming = pl.pallas_call(
        functools.partial(incoming_kernel, tokens),
        in_specs=[smem] + [vmem] * (SLAB + slabs),
        out_specs=[vmem] * SLAB,
        out_shape=[state_shape] * SLAB,
        compiler_params=limit,
        cost_estimate=light,
        name="incoming_states",
    )(here, rates[0], *left, *earlier)
    incoming = [incoming[0]] + [within_slab(incoming[d], d) for d in range(1, SLAB)]

    def gated_half(half):
        count = groups // SIDE
        first = half * count

        def shifted(spec):
            return pl.BlockSpec(spec.block_shape, lambda g, here: spec.index_map(g + first, here))

        return grouped(
            functools.partial(gated_kernel, modes),
            "gated_block",
            [shifted(s) for s in [series] * 2 + [rate_spec] * SLAB + [state_spec] * SLAB],
            pl.BlockSpec((tokens, GROUP), lambda g, here: (0, g)),
            jax.ShapeDtypeStruct((tokens, width // SIDE), BF16),
            [wide, scratch_rows],
            count,
        )(here, query, local, *rates, *incoming)

    def project(blocks, sources, picks, share_index):
        scalars = jnp.stack([share_index, rank ^ 2, rank ^ 3]).astype(jnp.int32)
        return pl.pallas_call(
            functools.partial(project_kernel, len(blocks), picks),
            in_specs=[smem]
            + [vmem] * (SIDE * len(blocks))
            + [pl.BlockSpec(memory_space=pltpu.HBM)] * len(sources),
            out_specs=vmem,
            out_shape=jax.ShapeDtypeStruct((len(blocks), len(picks), tokens, share), BF16),
            scratch_shapes=[
                pltpu.VMEM((len(picks), depth, share), BF16),
                pltpu.SemaphoreType.DMA((len(picks),)),
            ],
            compiler_params=large,
            cost_estimate=light,
            name="project_block",
        )(scalars, *[h for b in blocks for h in b], *sources)

    def project_away(blocks, sources, picks):
        away = project(blocks, sources, picks, 1 - tp_me)
        return away, lax.ppermute(away, "tp", [(0, 1), (1, 0)])

    def project_mine(blocks, sources, picks, after):
        blocks, _ = lax.optimization_barrier((blocks, after))
        return project(blocks, sources, picks, tp_me)

    def total(mine, got):
        return (mine.astype(F32) + got.astype(F32)).astype(BF16)

    half_of = [z * tp // slabs for z in range(slabs)]

    def deliver(summed, by):
        pairs = [[], []]
        for i in range(ctx):
            z, rest = divmod(i, SLAB)
            target = order[(place[z] - by) % slabs] * SLAB + rest
            for t in range(tp):
                pairs[t].append((i * tp + t, target * tp + half_of[z]))
        if by == 0:
            moves = [p for p in pairs[0] + pairs[1] if p[0] != p[1]]
            return [summed, lax.ppermute(summed, ("ctx", "tp"), moves)]
        return [lax.ppermute(summed, ("ctx", "tp"), moves) for moves in pairs]

    near, far, both = (
        ((0, None), (1, None)),
        ((0, 1), (0, 2)),
        ((0, None), (1, None), (2, 1), (2, 2)),
    )
    near, far, both = (
        ((0, None), (1, None)),
        ((0, 1), (0, 2)),
        ((0, None), (1, None), (2, 1), (2, 2)),
    )
    blocks = [[gated_half(h) for h in range(SIDE)]]
    arrived = [[], []]
    for step in range(slabs - 1):
        first, second = blocks[step]
        if step:
            first, _ = lax.optimization_barrier((first, mine))
        blocks.append([ring(first), ring(second)])
        block = blocks[step]
        if step > 1:
            block, arrived[0] = lax.optimization_barrier((block, arrived[0]))
        if step:
            arrived[0] += deliver(total(mine, got)[0], step - 1)
        away, got = project_away([block], [out_weight, beside], near)
        mine = project_mine([block], [out_weight, beside], near, away)
    summed = total(mine, got)[0]
    slab_weights, summed, arrived[0] = lax.optimization_barrier((slab_weights, summed, arrived[0]))
    arrived[0] += deliver(summed, slabs - 2)
    away, got = project_away(blocks[: slabs - 1], [slab_weights], far)
    block, _ = lax.optimization_barrier((blocks[-1], (away, summed)))
    sources = [out_weight, beside, slab_weights]
    last_away, last_got = project_away([block], sources, both)
    mine = project_mine(blocks[: slabs - 1], [slab_weights], far, last_away)
    last_mine = project_mine([block], sources, both, last_away)
    last = deliver(total(last_mine, last_got)[0], slabs - 1)
    batch = total(mine, got)
    for step in range(slabs - 1):
        arrived[1] += deliver(batch[step], step)
    arrived = [a + last for a in arrived]

    def place_of(z):
        return sum(jnp.where(z == k, place[k], 0) for k in range(slabs))

    kept = slabs // tp
    steps = [
        lax.rem(place_of(tp_me * kept + j) - place_of(z_me) + slabs, slabs) for j in range(kept)
    ]
    return pl.pallas_call(
        functools.partial(place_kernel, kept, slabs),
        in_specs=[smem] + [vmem] * (SIDE * 2 * slabs),
        out_specs=vmem,
        out_shape=jax.ShapeDtypeStruct((tokens, width), BF16),
        compiler_params=limit,
        cost_estimate=light,
        name="place_columns",
    )(jnp.stack([tp_me, rank, *steps]).astype(jnp.int32), *arrived[0], *arrived[1])


def solution(mesh):
    in_specs = (
        P(None, "ctx", "tp"),
        P(),
        P(None, ("tp", "ctx")),
        P(None, ("tp", "ctx")),
        P(("tp", "ctx")),
        P("tp", "ctx"),
    )
    out_specs = P("ctx", "tp")
    return jax.shard_map(
        per_device, mesh=mesh, in_specs=in_specs, out_specs=out_specs, check_vma=False
    )
```

```python
import functools

import jax
import jax.numpy as jnp
from jax import lax
from jax.experimental import pallas as pl
from jax.experimental.pallas import tpu as pltpu
from jax.sharding import PartitionSpec as P

LANES = 128
SUBLANES = 8
GROUP = LANES * SUBLANES
HALO = 2
TAPS = 3
SIDE = 2
SLAB = SIDE * SIDE
F32 = jnp.float32
BF16 = jnp.bfloat16


def spread(scratch, halo, block, pitch):
    tokens = block.shape[0]
    for tile in range(SUBLANES):
        lanes = pl.ds(tile * LANES, LANES)
        scratch[pl.ds(tile * pitch + SUBLANES - HALO, HALO), :] = halo[:, lanes].astype(F32)
        scratch[pl.ds(tile * pitch + SUBLANES, tokens), :] = block[:, lanes].astype(F32)


def token(scratch, index, pitch):
    return scratch[pl.ds(index, SUBLANES, stride=pitch), :]


def tree_sum(terms):
    while len(terms) > 1:
        terms = [a + b for a, b in zip(terms[::2], terms[1::2])] + terms[len(terms) & ~1 :]
    return terms[0]


def filter_kernel(here, features, halo, taps, u_ref, query_ref, tap_rows, *rows):
    tokens = features.shape[1]
    pitch = tokens + SUBLANES
    for tile in range(SUBLANES):
        for which in range(3):
            for j in range(TAPS):
                row = which * TAPS + j
                tap_rows[row, tile : tile + 1] = taps[which, j : j + 1, tile * LANES : (tile + 1) * LANES]
    for which in range(3):
        spread(rows[which], halo.at[which], features.at[which], pitch)
    weights = [[tap_rows[which * TAPS + j] for j in range(TAPS)] for which in range(3)]

    def step(index, carry):
        carry = list(carry)
        for inner in range(SUBLANES):
            now = index * SUBLANES + inner
            filtered = []
            for which in range(3):
                last, before = carry[which]
                fresh = token(rows[which], now + SUBLANES, pitch)
                filtered.append(
                    weights[which][0] * fresh + weights[which][1] * last + weights[which][2] * before
                )
                carry[which] = (fresh, last)
            query_ref[0, now] = filtered[0]
            u_ref[0, now] = (filtered[1] * filtered[2]).astype(BF16).astype(F32)
        return tuple(carry)

    start = tuple(
        (token(rows[which], SUBLANES - 1, pitch), token(rows[which], SUBLANES - 2, pitch))
        for which in range(3)
    )
    lax.fori_loop(0, tokens // SUBLANES, step, start)


def registers(refs, rank, wide, first, count):
    pitch = wide.shape[0] // SUBLANES
    each = SUBLANES // SLAB
    for d in range(SLAB):
        for j in range(each):
            start = pl.multiple_of(((d ^ rank) * each + j) * pitch, SUBLANES)
            rows = refs[d][0, first : first + count, j * LANES : (j + 1) * LANES]
            wide[pl.ds(start, count), :] = rows.astype(F32)
    return [wide[pl.ds(m, SUBLANES, stride=pitch), :] for m in range(count)]


def state_kernel(modes, here, u_ref, *refs):
    rates, outs, wide = refs[:SLAB], refs[SLAB : 2 * SLAB], refs[-1]
    rank = here[1]
    tokens = u_ref.shape[1]
    decay = [jnp.exp(-rate) for rate in registers(rates, rank, wide, 0, modes)]

    def step(index, states):
        for inner in range(SUBLANES):
            u = u_ref[0, index * SUBLANES + inner]
            states = tuple(states[m] * decay[m] + u for m in range(modes))
        return states

    zero = tuple(jnp.zeros((SUBLANES, LANES), F32) for _ in range(modes))
    states = lax.fori_loop(0, tokens // SUBLANES, step, zero)
    each = SUBLANES // SLAB
    pitch = wide.shape[0] // SUBLANES
    for m in range(modes):
        wide[pl.ds(m, SUBLANES, stride=pitch), :] = states[m]
    for d in range(SLAB):
        for j in range(each):
            start = pl.multiple_of(((d ^ rank) * each + j) * pitch, SUBLANES)
            outs[d][0, :, j * LANES : (j + 1) * LANES] = wide[pl.ds(start, modes), :].astype(BF16)


def slab_kernel(tokens, here, rates, *refs):
    states, out = refs[:SLAB], refs[SLAB]
    slabs = rates.shape[0]
    for g in range(slabs):
        rate = rates[lax.rem(g - here[0] + slabs, slabs), : states[0].shape[1]]
        total = None
        for d in range(SLAB):
            later = (SLAB - 1 - (here[1] ^ d)).astype(F32) * float(tokens)
            term = jnp.exp(-later * rate) * states[d][g].astype(F32)
            total = term if total is None else total + term
        out[g] = total.astype(BF16)


def incoming_kernel(tokens, here, rates, *refs):
    slabs = rates.shape[0]
    states, earlier, outs = refs[:SLAB], refs[SLAB : SLAB + slabs - 1], refs[SLAB + slabs - 1 :]
    for g in range(slabs):
        rate = rates[lax.rem(g - here[0] + slabs, slabs), : states[0].shape[1]]
        entering = earlier[0][g].astype(F32)
        for k in range(1, slabs - 1):
            entering += jnp.exp(-float(k * SLAB * tokens) * rate) * earlier[k][g].astype(F32)
        for d in range(SLAB):
            block = here[1] ^ d
            total = jnp.exp(-(block.astype(F32) * float(tokens)) * rate) * entering
            for e in range(SLAB):
                if e != d:
                    between = block - 1 - (here[1] ^ e)
                    factor = jnp.exp(-(jnp.maximum(between, 0).astype(F32) * float(tokens)) * rate)
                    factor = jnp.where(between >= 0, factor, jnp.zeros_like(factor))
                    total += factor * states[e][g].astype(F32)
            outs[d][g] = total.astype(BF16)


def local_kernel(modes, here, u_ref, *refs):
    rates, y_ref, wide = refs[:SLAB], refs[-2], refs[-1]
    tokens = u_ref.shape[1]
    rate = registers(rates, here[1], wide, 0, modes)
    rest = registers(rates, here[1], wide, modes, modes + 1)
    decay = [jnp.exp(-r) for r in rate]
    weight = [rest[m] * jnp.sqrt(2.0 * rate[m]) for m in range(modes)]
    skip = rest[modes]

    def step(index, states):
        for inner in range(SUBLANES):
            now = index * SUBLANES + inner
            u = u_ref[0, now]
            states = tuple(states[m] * decay[m] + u for m in range(modes))
            y_ref[0, now] = tree_sum([weight[m] * states[m] for m in range(modes)] + [skip * u])
        return states

    zero = tuple(jnp.zeros((SUBLANES, LANES), F32) for _ in range(modes))
    lax.fori_loop(0, tokens // SUBLANES, step, zero)


def gated_kernel(modes, here, query_ref, y_ref, *refs):
    rates, incoming = refs[:SLAB], refs[SLAB : 2 * SLAB]
    out_ref, wide, out_rows = refs[2 * SLAB :]
    tokens = query_ref.shape[1]
    pitch = tokens + SUBLANES
    rate = registers(rates, here[1], wide, 0, modes)
    rest = registers(rates, here[1], wide, modes, modes)
    state = registers(incoming, here[1], wide, 0, modes)
    decay = [jnp.exp(-r) for r in rate]
    weighted = tuple(rest[m] * jnp.sqrt(2.0 * rate[m]) * state[m] for m in range(modes))

    def step(index, weighted):
        for inner in range(SUBLANES):
            now = index * SUBLANES + inner
            weighted = tuple(weighted[m] * decay[m] for m in range(modes))
            long_out = tree_sum([y_ref[0, now], *weighted])
            long_out = long_out.astype(BF16).astype(F32)
            out_rows[pl.ds(now, SUBLANES, stride=pitch), :] = query_ref[0, now] * long_out
        return weighted

    lax.fori_loop(0, tokens // SUBLANES, step, weighted)
    for tile in range(SUBLANES):
        out_ref[:, pl.ds(tile * LANES, LANES)] = out_rows[pl.ds(tile * pitch, tokens), :].astype(BF16)


def project_kernel(count, picks, here, *refs):
    out_ref, slots, sems = refs[-3:]
    depth, share = slots.shape[1:]
    blocks, sources = refs[: SIDE * count], refs[SIDE * count : -3]
    half = depth // SIDE
    columns = pl.ds(pl.multiple_of(here[0] * share, share), share)
    copies = []
    for i, (which, rank) in enumerate(picks):
        if rank is None:
            source = sources[which].at[:, columns]
        else:
            source = sources[which].at[here[rank], :, columns]
        copies.append(pltpu.make_async_copy(source, slots.at[i], sems.at[i]))
        copies[-1].start()
    for i in range(len(picks)):
        copies[i].wait()
        for j in range(count):
            total = None
            for h in range(SIDE):
                term = jnp.dot(
                    blocks[SIDE * j + h][...],
                    slots[i, h * half : (h + 1) * half],
                    preferred_element_type=F32,
                )
                total = term if total is None else total + term
            out_ref[j, i] = total.astype(BF16)


def place_kernel(kept, steps, here, *refs):
    per_pair = 2 * steps
    sources, out_ref = refs[: SIDE * per_pair], refs[-1]
    share = sources[0].shape[2]
    tp_me, rank = here[0], here[1]
    for slot in range(kept):
        step = here[2 + slot]
        for pair in range(SIDE):
            mine = sources[pair * per_pair : (pair + 1) * per_pair]
            for near in range(SIDE):
                piece = rank ^ (SIDE * pair + near)
                for t in range(SIDE):
                    start = ((slot * SLAB + piece) * SIDE + t) * share
                    target = pl.ds(pl.multiple_of(start, share), share)
                    own = jnp.logical_and(step == 0, tp_me == t)
                    moved = jnp.logical_and(step == 0, tp_me != t)
                    choices = [(own, mine[0]), (moved, mine[1])]
                    choices += [(step == k, mine[2 * k + t]) for k in range(1, steps)]
                    for chosen, source in choices:
                        index = near if source.shape[0] == SIDE else SIDE * pair + near

                        @pl.when(chosen)
                        def _(source=source, index=index, target=target):
                            out_ref[:, target] = source[index]


def ring_order(count):
    return [0] + list(range(1, count, 2)) + [i for i in range(count - 1, 0, -1) if i % 2 == 0]


def any_size(features, conv_weight, decay_rates, residues, skip_gain, out_weight):
    tokens, width = features.shape[1:]
    ctx, tp = lax.axis_size("ctx"), lax.axis_size("tp")
    me, tp_me = lax.axis_index("ctx"), lax.axis_index("tp")
    halo = lax.ppermute(features[:, tokens - HALO :], "ctx", [(i, i + 1) for i in range(ctx - 1)])
    extended = jnp.concatenate([halo, features], axis=1).astype(F32)
    taps = lax.dynamic_slice_in_dim(conv_weight, tp_me * width, width, 2)
    filtered = sum(taps[:, j, None] * extended[:, HALO - j : HALO - j + tokens] for j in range(TAPS))
    u = (filtered[1] * filtered[2]).astype(BF16).astype(F32)
    rates, weights, skip = (
        lax.all_gather(a, "ctx", axis=a.ndim - 1, tiled=True) for a in (decay_rates, residues, skip_gain)
    )
    weights = weights * jnp.sqrt(2.0 * rates)
    decay = jnp.exp(-rates)
    zero = jnp.zeros(rates.shape, F32)
    left = lax.fori_loop(0, tokens, lambda t, s: s * decay + u[t], zero)
    lefts = lax.all_gather(left, "ctx")
    block_decay = jnp.exp(-float(tokens) * rates)
    entering = lax.fori_loop(0, me, lambda b, s: s * block_decay + lefts[b], zero)

    def advance(states, now):
        states = states * decay + now
        return states, jnp.sum(weights * states, axis=0) + skip * now

    long_out = lax.scan(advance, entering, u)[1].astype(BF16).astype(F32)
    gated = (filtered[0] * long_out).astype(BF16)
    whole = lax.all_gather(gated, "ctx", axis=0, tiled=True)
    partial = jnp.dot(whole, out_weight, preferred_element_type=F32).astype(BF16)
    share = partial.shape[1] // tp
    partial = partial.reshape(ctx * tokens, tp, share).transpose(1, 0, 2)
    partial = lax.all_to_all(partial, "tp", split_axis=0, concat_axis=0, tiled=True)
    summed = jnp.sum(partial.astype(F32), axis=0).astype(BF16).reshape(ctx, tokens, share)
    summed = lax.all_to_all(summed, "ctx", split_axis=0, concat_axis=0, tiled=True)
    placed = lax.all_to_all(
        summed.reshape(tp, ctx // tp, tokens, share), "tp", split_axis=0, concat_axis=0, tiled=True
    )
    return placed.transpose(2, 1, 0, 3).reshape(tokens, width)


def per_device(features, conv_weight, decay_rates, residues, skip_gain, out_weight):
    tokens, width = features.shape[1:]
    modes, owned = decay_rates.shape
    ctx, tp = lax.axis_size("ctx"), lax.axis_size("tp")
    depth, columns = out_weight.shape
    share = columns // tp
    if owned * SLAB != GROUP or tp != SIDE or share % LANES or ctx // SLAB < 3:
        return any_size(features, conv_weight, decay_rates, residues, skip_gain, out_weight)
    slabs = ctx // SLAB
    groups = width // GROUP
    me, tp_me = lax.axis_index("ctx"), lax.axis_index("tp")
    z_me, rank = me // SLAB, me % SLAB
    order = ring_order(slabs)
    place = [order.index(z) for z in range(slabs)]
    here = jnp.stack([z_me, rank, tp_me]).astype(jnp.int32)

    def within_slab(array, mask):
        return lax.ppermute(array, "ctx", [(i, i ^ mask) for i in range(ctx)])

    def from_slab(array, by):
        return lax.ppermute(array, "ctx", [(i, (i - by * SLAB) % ctx) for i in range(ctx)])

    def ring(array):
        pairs = []
        for i in range(ctx):
            z, rest = divmod(i, SLAB)
            pairs.append((i, order[(place[z] + 1) % slabs] * SLAB + rest))
        return lax.ppermute(array, "ctx", pairs)

    halo = lax.ppermute(
        features[:, tokens - HALO :, :], "ctx", [(i, i + 1) for i in range(ctx - 1)]
    )
    rows = jnp.concatenate([decay_rates, residues, skip_gain[None]], axis=0)
    rows = jnp.stack([rows] + [from_slab(rows, by) for by in range(1, slabs)])
    rows, halo = lax.optimization_barrier((rows, halo))
    rates = [rows, within_slab(rows, 1), within_slab(rows, 2)]

    beside = within_slab(out_weight, 1)
    slab_weights = lax.all_gather(
        out_weight,
        "ctx",
        axis_index_groups=[list(range(z * SLAB, (z + 1) * SLAB)) for z in range(slabs)],
    )

    limit = pltpu.CompilerParams(vmem_limit_bytes=16 * 1024 * 1024)
    large = pltpu.CompilerParams(vmem_limit_bytes=48 * 1024 * 1024)
    light = pl.CostEstimate(flops=1, bytes_accessed=1, transcendentals=0)
    series_shape = jax.ShapeDtypeStruct((groups, tokens, SUBLANES, LANES), F32)
    state_shape = jax.ShapeDtypeStruct((groups, modes, owned), BF16)
    scratch_rows = pltpu.VMEM((SUBLANES * (tokens + SUBLANES), LANES), F32)
    wide = pltpu.VMEM((SUBLANES * (modes + SUBLANES), LANES), F32)
    series = pl.BlockSpec((1, tokens, SUBLANES, LANES), lambda g, here: (g, 0, 0, 0))
    state_spec = pl.BlockSpec((1, modes, owned), lambda g, here: (g, 0, 0))
    rate_spec = pl.BlockSpec(
        (1, 2 * modes + 1, owned), lambda g, here: (lax.rem(g - here[0] + slabs, slabs), 0, 0)
    )

    def grouped(kernel, name, in_specs, out_specs, out_shape, scratch, groups=groups):
        return pl.pallas_call(
            kernel,
            grid_spec=pltpu.PrefetchScalarGridSpec(
                num_scalar_prefetch=1,
                grid=(groups,),
                in_specs=in_specs,
                out_specs=out_specs,
                scratch_shapes=scratch,
            ),
            out_shape=out_shape,
            compiler_params=limit,
            cost_estimate=light,
            name=name,
        )

    u, query = grouped(
        filter_kernel,
        "short_filters",
        [
            pl.BlockSpec((3, tokens, GROUP), lambda g, here: (0, 0, g)),
            pl.BlockSpec((3, HALO, GROUP), lambda g, here: (0, 0, g)),
            pl.BlockSpec((3, TAPS, GROUP), lambda g, here: (0, 0, here[2] * groups + g)),
        ],
        [series, series],
        [series_shape, series_shape],
        [pltpu.VMEM((3 * TAPS, SUBLANES, LANES), F32), scratch_rows, scratch_rows, scratch_rows],
    )(here, features, halo, conv_weight)

    passed, u = lax.optimization_barrier((rates[2], u))
    rates.append(within_slab(passed, 1))

    left = grouped(
        functools.partial(state_kernel, modes),
        "block_states",
        [series] + [rate_spec] * SLAB,
        [state_spec] * SLAB,
        [state_shape] * SLAB,
        [wide],
    )(here, u, *rates)
    left = [left[0]] + [within_slab(left[d], d) for d in range(1, SLAB)]

    smem = pl.BlockSpec(memory_space=pltpu.SMEM)
    vmem = pl.BlockSpec(memory_space=pltpu.VMEM)
    slab_left = pl.pallas_call(
        functools.partial(slab_kernel, tokens),
        in_specs=[smem] + [vmem] * (1 + SLAB),
        out_specs=vmem,
        out_shape=state_shape,
        compiler_params=limit,
        cost_estimate=light,
        name="slab_states",
    )(here, rates[0], *left)
    earlier = [
        lax.ppermute(slab_left, "ctx", [(i, i + by * SLAB) for i in range(ctx - by * SLAB)])
        for by in range(1, slabs)
    ]

    local = grouped(
        functools.partial(local_kernel, modes),
        "local_convolution",
        [series] + [rate_spec] * SLAB,
        series,
        series_shape,
        [wide],
    )(here, u, *rates)
    earlier, local = lax.optimization_barrier((earlier, local))

    incoming = pl.pallas_call(
        functools.partial(incoming_kernel, tokens),
        in_specs=[smem] + [vmem] * (SLAB + slabs),
        out_specs=[vmem] * SLAB,
        out_shape=[state_shape] * SLAB,
        compiler_params=limit,
        cost_estimate=light,
        name="incoming_states",
    )(here, rates[0], *left, *earlier)
    incoming = [incoming[0]] + [within_slab(incoming[d], d) for d in range(1, SLAB)]

    def gated_half(half):
        count = groups // SIDE
        first = half * count

        def shifted(spec):
            return pl.BlockSpec(spec.block_shape, lambda g, here: spec.index_map(g + first, here))

        return grouped(
            functools.partial(gated_kernel, modes),
            "gated_block",
            [shifted(s) for s in [series] * 2 + [rate_spec] * SLAB + [state_spec] * SLAB],
            pl.BlockSpec((tokens, GROUP), lambda g, here: (0, g)),
            jax.ShapeDtypeStruct((tokens, width // SIDE), BF16),
            [wide, scratch_rows],
            count,
        )(here, query, local, *rates, *incoming)

    def project(blocks, sources, picks, share_index):
        scalars = jnp.stack([share_index, rank ^ 2, rank ^ 3]).astype(jnp.int32)
        return pl.pallas_call(
            functools.partial(project_kernel, len(blocks), picks),
            in_specs=[smem]
            + [vmem] * (SIDE * len(blocks))
            + [pl.BlockSpec(memory_space=pltpu.HBM)] * len(sources),
            out_specs=vmem,
            out_shape=jax.ShapeDtypeStruct((len(blocks), len(picks), tokens, share), BF16),
            scratch_shapes=[
                pltpu.VMEM((len(picks), depth, share), BF16),
                pltpu.SemaphoreType.DMA((len(picks),)),
            ],
            compiler_params=large,
            cost_estimate=light,
            name="project_block",
        )(scalars, *[h for b in blocks for h in b], *sources)

    def project_away(blocks, sources, picks):
        away = project(blocks, sources, picks, 1 - tp_me)
        return away, lax.ppermute(away, "tp", [(0, 1), (1, 0)])

    def project_mine(blocks, sources, picks, after):
        blocks, _ = lax.optimization_barrier((blocks, after))
        return project(blocks, sources, picks, tp_me)

    def total(mine, got):
        return (mine.astype(F32) + got.astype(F32)).astype(BF16)

    half_of = [z * tp // slabs for z in range(slabs)]

    def deliver(summed, by):
        pairs = [[], []]
        for i in range(ctx):
            z, rest = divmod(i, SLAB)
            target = order[(place[z] - by) % slabs] * SLAB + rest
            for t in range(tp):
                pairs[t].append((i * tp + t, target * tp + half_of[z]))
        if by == 0:
            moves = [p for p in pairs[0] + pairs[1] if p[0] != p[1]]
            return [summed, lax.ppermute(summed, ("ctx", "tp"), moves)]
        return [lax.ppermute(summed, ("ctx", "tp"), moves) for moves in pairs]

    near, far, both = (
        ((0, None), (1, None)),
        ((0, 1), (0, 2)),
        ((0, None), (1, None), (2, 1), (2, 2)),
    )
    near, far, both = (
        ((0, None), (1, None)),
        ((0, 1), (0, 2)),
        ((0, None), (1, None), (2, 1), (2, 2)),
    )
    blocks = [[gated_half(h) for h in range(SIDE)]]
    arrived = [[], []]
    for step in range(slabs - 1):
        if step:
            blocks[step], summed, arrived[0] = lax.optimization_barrier(
                (blocks[step], summed, arrived[0])
            )
            arrived[0] += deliver(summed, step - 1)
        blocks.append([ring(h) for h in blocks[step]])
        away, got = project_away([blocks[step]], [out_weight, beside], near)
        mine = project_mine([blocks[step]], [out_weight, beside], near, away)
        summed = total(mine, got)[0]
    slab_weights, _ = lax.optimization_barrier((slab_weights, mine))
    away, got = project_away(blocks[: slabs - 1], [slab_weights], far)
    block, summed, arrived[0], _ = lax.optimization_barrier(
        (blocks[-1], summed, arrived[0], away)
    )
    arrived[0] += deliver(summed, slabs - 2)
    sources = [out_weight, beside, slab_weights]
    last_away, last_got = project_away([block], sources, both)
    mine = project_mine(blocks[: slabs - 1], [slab_weights], far, last_away)
    last_mine = project_mine([block], sources, both, last_away)
    last = deliver(total(last_mine, last_got)[0], slabs - 1)
    batch = total(mine, got)
    for step in range(slabs - 1):
        arrived[1] += deliver(batch[step], step)
    arrived = [a + last for a in arrived]

    def place_of(z):
        return sum(jnp.where(z == k, place[k], 0) for k in range(slabs))

    kept = slabs // tp
    steps = [
        lax.rem(place_of(tp_me * kept + j) - place_of(z_me) + slabs, slabs) for j in range(kept)
    ]
    return pl.pallas_call(
        functools.partial(place_kernel, kept, slabs),
        in_specs=[smem] + [vmem] * (SIDE * 2 * slabs),
        out_specs=vmem,
        out_shape=jax.ShapeDtypeStruct((tokens, width), BF16),
        compiler_params=limit,
        cost_estimate=light,
        name="place_columns",
    )(jnp.stack([tp_me, rank, *steps]).astype(jnp.int32), *arrived[0], *arrived[1])


def solution(mesh):
    in_specs = (
        P(None, "ctx", "tp"),
        P(),
        P(None, ("tp", "ctx")),
        P(None, ("tp", "ctx")),
        P(("tp", "ctx")),
        P("tp", "ctx"),
    )
    out_specs = P("ctx", "tp")
    return jax.shard_map(
        per_device, mesh=mesh, in_specs=in_specs, out_specs=out_specs, check_vma=False
    )
```

```python
import functools

import jax
import jax.numpy as jnp
from jax import lax
from jax.experimental import pallas as pl
from jax.experimental.pallas import tpu as pltpu
from jax.sharding import PartitionSpec as P

LANES = 128
SUBLANES = 8
GROUP = LANES * SUBLANES
HALO = 2
TAPS = 3
SIDE = 2
SLAB = SIDE * SIDE
F32 = jnp.float32
BF16 = jnp.bfloat16


def spread(scratch, halo, block, pitch):
    tokens = block.shape[0]
    for tile in range(SUBLANES):
        lanes = pl.ds(tile * LANES, LANES)
        scratch[pl.ds(tile * pitch + SUBLANES - HALO, HALO), :] = halo[:, lanes].astype(F32)
        scratch[pl.ds(tile * pitch + SUBLANES, tokens), :] = block[:, lanes].astype(F32)


def token(scratch, index, pitch):
    return scratch[pl.ds(index, SUBLANES, stride=pitch), :]


def tree_sum(terms):
    while len(terms) > 1:
        terms = [a + b for a, b in zip(terms[::2], terms[1::2])] + terms[len(terms) & ~1 :]
    return terms[0]


def filter_kernel(here, features, halo, taps, u_ref, query_ref, tap_rows, *rows):
    tokens = features.shape[1]
    pitch = tokens + SUBLANES
    for tile in range(SUBLANES):
        for which in range(3):
            for j in range(TAPS):
                row = which * TAPS + j
                tap_rows[row, tile : tile + 1] = taps[which, j : j + 1, tile * LANES : (tile + 1) * LANES]
    for which in range(3):
        spread(rows[which], halo.at[which], features.at[which], pitch)
    weights = [[tap_rows[which * TAPS + j] for j in range(TAPS)] for which in range(3)]

    def step(index, carry):
        carry = list(carry)
        for inner in range(SUBLANES):
            now = index * SUBLANES + inner
            filtered = []
            for which in range(3):
                last, before = carry[which]
                fresh = token(rows[which], now + SUBLANES, pitch)
                filtered.append(
                    weights[which][0] * fresh + weights[which][1] * last + weights[which][2] * before
                )
                carry[which] = (fresh, last)
            query_ref[0, now] = filtered[0]
            u_ref[0, now] = (filtered[1] * filtered[2]).astype(BF16).astype(F32)
        return tuple(carry)

    start = tuple(
        (token(rows[which], SUBLANES - 1, pitch), token(rows[which], SUBLANES - 2, pitch))
        for which in range(3)
    )
    lax.fori_loop(0, tokens // SUBLANES, step, start)


def registers(refs, rank, wide, first, count):
    pitch = wide.shape[0] // SUBLANES
    each = SUBLANES // SLAB
    for d in range(SLAB):
        for j in range(each):
            start = pl.multiple_of(((d ^ rank) * each + j) * pitch, SUBLANES)
            rows = refs[d][0, first : first + count, j * LANES : (j + 1) * LANES]
            wide[pl.ds(start, count), :] = rows.astype(F32)
    return [wide[pl.ds(m, SUBLANES, stride=pitch), :] for m in range(count)]


def state_kernel(modes, here, u_ref, *refs):
    rates, outs, wide = refs[:SLAB], refs[SLAB : 2 * SLAB], refs[-1]
    rank = here[1]
    tokens = u_ref.shape[1]
    decay = [jnp.exp(-rate) for rate in registers(rates, rank, wide, 0, modes)]

    def step(index, states):
        for inner in range(SUBLANES):
            u = u_ref[0, index * SUBLANES + inner]
            states = tuple(states[m] * decay[m] + u for m in range(modes))
        return states

    zero = tuple(jnp.zeros((SUBLANES, LANES), F32) for _ in range(modes))
    states = lax.fori_loop(0, tokens // SUBLANES, step, zero)
    each = SUBLANES // SLAB
    pitch = wide.shape[0] // SUBLANES
    for m in range(modes):
        wide[pl.ds(m, SUBLANES, stride=pitch), :] = states[m]
    for d in range(SLAB):
        for j in range(each):
            start = pl.multiple_of(((d ^ rank) * each + j) * pitch, SUBLANES)
            outs[d][0, :, j * LANES : (j + 1) * LANES] = wide[pl.ds(start, modes), :].astype(BF16)


def slab_kernel(tokens, here, rates, *refs):
    states, out = refs[:SLAB], refs[SLAB]
    slabs = rates.shape[0]
    for g in range(slabs):
        rate = rates[lax.rem(g - here[0] + slabs, slabs), : states[0].shape[1]]
        total = None
        for d in range(SLAB):
            later = (SLAB - 1 - (here[1] ^ d)).astype(F32) * float(tokens)
            term = jnp.exp(-later * rate) * states[d][g].astype(F32)
            total = term if total is None else total + term
        out[g] = total.astype(BF16)


def incoming_kernel(tokens, here, rates, *refs):
    slabs = rates.shape[0]
    states, earlier, outs = refs[:SLAB], refs[SLAB : SLAB + slabs - 1], refs[SLAB + slabs - 1 :]
    for g in range(slabs):
        rate = rates[lax.rem(g - here[0] + slabs, slabs), : states[0].shape[1]]
        entering = earlier[0][g].astype(F32)
        for k in range(1, slabs - 1):
            entering += jnp.exp(-float(k * SLAB * tokens) * rate) * earlier[k][g].astype(F32)
        for d in range(SLAB):
            block = here[1] ^ d
            total = jnp.exp(-(block.astype(F32) * float(tokens)) * rate) * entering
            for e in range(SLAB):
                if e != d:
                    between = block - 1 - (here[1] ^ e)
                    factor = jnp.exp(-(jnp.maximum(between, 0).astype(F32) * float(tokens)) * rate)
                    factor = jnp.where(between >= 0, factor, jnp.zeros_like(factor))
                    total += factor * states[e][g].astype(F32)
            outs[d][g] = total.astype(BF16)


def local_kernel(modes, here, u_ref, *refs):
    rates, y_ref, wide = refs[:SLAB], refs[-2], refs[-1]
    tokens = u_ref.shape[1]
    rate = registers(rates, here[1], wide, 0, modes)
    rest = registers(rates, here[1], wide, modes, modes + 1)
    decay = [jnp.exp(-r) for r in rate]
    weight = [rest[m] * jnp.sqrt(2.0 * rate[m]) for m in range(modes)]
    skip = rest[modes]

    def step(index, states):
        for inner in range(SUBLANES):
            now = index * SUBLANES + inner
            u = u_ref[0, now]
            states = tuple(states[m] * decay[m] + u for m in range(modes))
            y_ref[0, now] = tree_sum([weight[m] * states[m] for m in range(modes)] + [skip * u])
        return states

    zero = tuple(jnp.zeros((SUBLANES, LANES), F32) for _ in range(modes))
    lax.fori_loop(0, tokens // SUBLANES, step, zero)


def gated_kernel(modes, here, query_ref, y_ref, *refs):
    rates, incoming = refs[:SLAB], refs[SLAB : 2 * SLAB]
    out_ref, wide, out_rows = refs[2 * SLAB :]
    tokens = query_ref.shape[1]
    pitch = tokens + SUBLANES
    rate = registers(rates, here[1], wide, 0, modes)
    rest = registers(rates, here[1], wide, modes, modes)
    state = registers(incoming, here[1], wide, 0, modes)
    decay = [jnp.exp(-r) for r in rate]
    weighted = tuple(rest[m] * jnp.sqrt(2.0 * rate[m]) * state[m] for m in range(modes))

    def step(index, weighted):
        for inner in range(SUBLANES):
            now = index * SUBLANES + inner
            weighted = tuple(weighted[m] * decay[m] for m in range(modes))
            long_out = tree_sum([y_ref[0, now], *weighted])
            long_out = long_out.astype(BF16).astype(F32)
            out_rows[pl.ds(now, SUBLANES, stride=pitch), :] = query_ref[0, now] * long_out
        return weighted

    lax.fori_loop(0, tokens // SUBLANES, step, weighted)
    for tile in range(SUBLANES):
        out_ref[:, pl.ds(tile * LANES, LANES)] = out_rows[pl.ds(tile * pitch, tokens), :].astype(BF16)


def project_kernel(count, picks, here, *refs):
    out_ref, slots, sems = refs[-3:]
    depth, share = slots.shape[1:]
    blocks, sources = refs[: SIDE * count], refs[SIDE * count : -3]
    half = depth // SIDE
    columns = pl.ds(pl.multiple_of(here[0] * share, share), share)
    copies = []
    for i, (which, rank) in enumerate(picks):
        if rank is None:
            source = sources[which].at[:, columns]
        else:
            source = sources[which].at[here[rank], :, columns]
        copies.append(pltpu.make_async_copy(source, slots.at[i], sems.at[i]))
        copies[-1].start()
    for i in range(len(picks)):
        copies[i].wait()
        for j in range(count):
            total = None
            for h in range(SIDE):
                term = jnp.dot(
                    blocks[SIDE * j + h][...],
                    slots[i, h * half : (h + 1) * half],
                    preferred_element_type=F32,
                )
                total = term if total is None else total + term
            out_ref[j, i] = total.astype(BF16)


def place_kernel(kept, steps, here, *refs):
    per_pair = 2 * steps
    sources, out_ref = refs[: SIDE * per_pair], refs[-1]
    share = sources[0].shape[2]
    tp_me, rank = here[0], here[1]
    for slot in range(kept):
        step = here[2 + slot]
        for pair in range(SIDE):
            mine = sources[pair * per_pair : (pair + 1) * per_pair]
            for near in range(SIDE):
                piece = rank ^ (SIDE * pair + near)
                for t in range(SIDE):
                    start = ((slot * SLAB + piece) * SIDE + t) * share
                    target = pl.ds(pl.multiple_of(start, share), share)
                    own = jnp.logical_and(step == 0, tp_me == t)
                    moved = jnp.logical_and(step == 0, tp_me != t)
                    choices = [(own, mine[0]), (moved, mine[1])]
                    choices += [(step == k, mine[2 * k + t]) for k in range(1, steps)]
                    for chosen, source in choices:
                        index = near if source.shape[0] == SIDE else SIDE * pair + near

                        @pl.when(chosen)
                        def _(source=source, index=index, target=target):
                            out_ref[:, target] = source[index]


def ring_order(count):
    return [0] + list(range(1, count, 2)) + [i for i in range(count - 1, 0, -1) if i % 2 == 0]


def any_size(features, conv_weight, decay_rates, residues, skip_gain, out_weight):
    tokens, width = features.shape[1:]
    ctx, tp = lax.axis_size("ctx"), lax.axis_size("tp")
    me, tp_me = lax.axis_index("ctx"), lax.axis_index("tp")
    halo = lax.ppermute(features[:, tokens - HALO :], "ctx", [(i, i + 1) for i in range(ctx - 1)])
    extended = jnp.concatenate([halo, features], axis=1).astype(F32)
    taps = lax.dynamic_slice_in_dim(conv_weight, tp_me * width, width, 2)
    filtered = sum(taps[:, j, None] * extended[:, HALO - j : HALO - j + tokens] for j in range(TAPS))
    u = (filtered[1] * filtered[2]).astype(BF16).astype(F32)
    rates, weights, skip = (
        lax.all_gather(a, "ctx", axis=a.ndim - 1, tiled=True) for a in (decay_rates, residues, skip_gain)
    )
    weights = weights * jnp.sqrt(2.0 * rates)
    decay = jnp.exp(-rates)
    zero = jnp.zeros(rates.shape, F32)
    left = lax.fori_loop(0, tokens, lambda t, s: s * decay + u[t], zero)
    lefts = lax.all_gather(left, "ctx")
    block_decay = jnp.exp(-float(tokens) * rates)
    entering = lax.fori_loop(0, me, lambda b, s: s * block_decay + lefts[b], zero)

    def advance(states, now):
        states = states * decay + now
        return states, jnp.sum(weights * states, axis=0) + skip * now

    long_out = lax.scan(advance, entering, u)[1].astype(BF16).astype(F32)
    gated = (filtered[0] * long_out).astype(BF16)
    whole = lax.all_gather(gated, "ctx", axis=0, tiled=True)
    partial = jnp.dot(whole, out_weight, preferred_element_type=F32).astype(BF16)
    share = partial.shape[1] // tp
    partial = partial.reshape(ctx * tokens, tp, share).transpose(1, 0, 2)
    partial = lax.all_to_all(partial, "tp", split_axis=0, concat_axis=0, tiled=True)
    summed = jnp.sum(partial.astype(F32), axis=0).astype(BF16).reshape(ctx, tokens, share)
    summed = lax.all_to_all(summed, "ctx", split_axis=0, concat_axis=0, tiled=True)
    placed = lax.all_to_all(
        summed.reshape(tp, ctx // tp, tokens, share), "tp", split_axis=0, concat_axis=0, tiled=True
    )
    return placed.transpose(2, 1, 0, 3).reshape(tokens, width)


def per_device(features, conv_weight, decay_rates, residues, skip_gain, out_weight):
    tokens, width = features.shape[1:]
    modes, owned = decay_rates.shape
    ctx, tp = lax.axis_size("ctx"), lax.axis_size("tp")
    depth, columns = out_weight.shape
    share = columns // tp
    if owned * SLAB != GROUP or tp != SIDE or share % LANES or ctx // SLAB < 3:
        return any_size(features, conv_weight, decay_rates, residues, skip_gain, out_weight)
    slabs = ctx // SLAB
    groups = width // GROUP
    me, tp_me = lax.axis_index("ctx"), lax.axis_index("tp")
    z_me, rank = me // SLAB, me % SLAB
    order = ring_order(slabs)
    place = [order.index(z) for z in range(slabs)]
    here = jnp.stack([z_me, rank, tp_me]).astype(jnp.int32)

    def within_slab(array, mask):
        return lax.ppermute(array, "ctx", [(i, i ^ mask) for i in range(ctx)])

    def from_slab(array, by):
        return lax.ppermute(array, "ctx", [(i, (i - by * SLAB) % ctx) for i in range(ctx)])

    def ring(array):
        pairs = []
        for i in range(ctx):
            z, rest = divmod(i, SLAB)
            pairs.append((i, order[(place[z] + 1) % slabs] * SLAB + rest))
        return lax.ppermute(array, "ctx", pairs)

    halo = lax.ppermute(
        features[:, tokens - HALO :, :], "ctx", [(i, i + 1) for i in range(ctx - 1)]
    )
    rows = jnp.concatenate([decay_rates, residues, skip_gain[None]], axis=0)
    rows = jnp.stack([rows] + [from_slab(rows, by) for by in range(1, slabs)])
    rows, halo = lax.optimization_barrier((rows, halo))
    rates = [rows, within_slab(rows, 1), within_slab(rows, 2)]

    beside = within_slab(out_weight, 1)
    slab_weights = lax.all_gather(
        out_weight,
        "ctx",
        axis_index_groups=[list(range(z * SLAB, (z + 1) * SLAB)) for z in range(slabs)],
    )

    limit = pltpu.CompilerParams(vmem_limit_bytes=16 * 1024 * 1024)
    large = pltpu.CompilerParams(vmem_limit_bytes=48 * 1024 * 1024)
    light = pl.CostEstimate(flops=1, bytes_accessed=1, transcendentals=0)
    series_shape = jax.ShapeDtypeStruct((groups, tokens, SUBLANES, LANES), F32)
    state_shape = jax.ShapeDtypeStruct((groups, modes, owned), BF16)
    scratch_rows = pltpu.VMEM((SUBLANES * (tokens + SUBLANES), LANES), F32)
    wide = pltpu.VMEM((SUBLANES * (modes + SUBLANES), LANES), F32)
    series = pl.BlockSpec((1, tokens, SUBLANES, LANES), lambda g, here: (g, 0, 0, 0))
    state_spec = pl.BlockSpec((1, modes, owned), lambda g, here: (g, 0, 0))
    rate_spec = pl.BlockSpec(
        (1, 2 * modes + 1, owned), lambda g, here: (lax.rem(g - here[0] + slabs, slabs), 0, 0)
    )

    def grouped(kernel, name, in_specs, out_specs, out_shape, scratch, groups=groups):
        return pl.pallas_call(
            kernel,
            grid_spec=pltpu.PrefetchScalarGridSpec(
                num_scalar_prefetch=1,
                grid=(groups,),
                in_specs=in_specs,
                out_specs=out_specs,
                scratch_shapes=scratch,
            ),
            out_shape=out_shape,
            compiler_params=limit,
            cost_estimate=light,
            name=name,
        )

    u, query = grouped(
        filter_kernel,
        "short_filters",
        [
            pl.BlockSpec((3, tokens, GROUP), lambda g, here: (0, 0, g)),
            pl.BlockSpec((3, HALO, GROUP), lambda g, here: (0, 0, g)),
            pl.BlockSpec((3, TAPS, GROUP), lambda g, here: (0, 0, here[2] * groups + g)),
        ],
        [series, series],
        [series_shape, series_shape],
        [pltpu.VMEM((3 * TAPS, SUBLANES, LANES), F32), scratch_rows, scratch_rows, scratch_rows],
    )(here, features, halo, conv_weight)

    passed, u = lax.optimization_barrier((rates[2], u))
    rates.append(within_slab(passed, 1))

    left = grouped(
        functools.partial(state_kernel, modes),
        "block_states",
        [series] + [rate_spec] * SLAB,
        [state_spec] * SLAB,
        [state_shape] * SLAB,
        [wide],
    )(here, u, *rates)
    left = [left[0]] + [within_slab(left[d], d) for d in range(1, SLAB)]

    smem = pl.BlockSpec(memory_space=pltpu.SMEM)
    vmem = pl.BlockSpec(memory_space=pltpu.VMEM)
    slab_left = pl.pallas_call(
        functools.partial(slab_kernel, tokens),
        in_specs=[smem] + [vmem] * (1 + SLAB),
        out_specs=vmem,
        out_shape=state_shape,
        compiler_params=limit,
        cost_estimate=light,
        name="slab_states",
    )(here, rates[0], *left)
    earlier = [
        lax.ppermute(slab_left, "ctx", [(i, i + by * SLAB) for i in range(ctx - by * SLAB)])
        for by in range(1, slabs)
    ]

    local = grouped(
        functools.partial(local_kernel, modes),
        "local_convolution",
        [series] + [rate_spec] * SLAB,
        series,
        series_shape,
        [wide],
    )(here, u, *rates)
    earlier, local = lax.optimization_barrier((earlier, local))

    incoming = pl.pallas_call(
        functools.partial(incoming_kernel, tokens),
        in_specs=[smem] + [vmem] * (SLAB + slabs),
        out_specs=[vmem] * SLAB,
        out_shape=[state_shape] * SLAB,
        compiler_params=limit,
        cost_estimate=light,
        name="incoming_states",
    )(here, rates[0], *left, *earlier)
    incoming = [incoming[0]] + [within_slab(incoming[d], d) for d in range(1, SLAB)]

    def gated_half(half):
        count = groups // SIDE
        first = half * count

        def shifted(spec):
            return pl.BlockSpec(spec.block_shape, lambda g, here: spec.index_map(g + first, here))

        return grouped(
            functools.partial(gated_kernel, modes),
            "gated_block",
            [shifted(s) for s in [series] * 2 + [rate_spec] * SLAB + [state_spec] * SLAB],
            pl.BlockSpec((tokens, GROUP), lambda g, here: (0, g)),
            jax.ShapeDtypeStruct((tokens, width // SIDE), BF16),
            [wide, scratch_rows],
            count,
        )(here, query, local, *rates, *incoming)

    def project(blocks, sources, picks, share_index):
        scalars = jnp.stack([share_index, rank ^ 2, rank ^ 3]).astype(jnp.int32)
        return pl.pallas_call(
            functools.partial(project_kernel, len(blocks), picks),
            in_specs=[smem]
            + [vmem] * (SIDE * len(blocks))
            + [pl.BlockSpec(memory_space=pltpu.HBM)] * len(sources),
            out_specs=vmem,
            out_shape=jax.ShapeDtypeStruct((len(blocks), len(picks), tokens, share), BF16),
            scratch_shapes=[
                pltpu.VMEM((len(picks), depth, share), BF16),
                pltpu.SemaphoreType.DMA((len(picks),)),
            ],
            compiler_params=large,
            cost_estimate=light,
            name="project_block",
        )(scalars, *[h for b in blocks for h in b], *sources)

    def project_away(blocks, sources, picks):
        away = project(blocks, sources, picks, 1 - tp_me)
        return away, lax.ppermute(away, "tp", [(0, 1), (1, 0)])

    def project_mine(blocks, sources, picks, after):
        blocks, _ = lax.optimization_barrier((blocks, after))
        return project(blocks, sources, picks, tp_me)

    def total(mine, got):
        return (mine.astype(F32) + got.astype(F32)).astype(BF16)

    half_of = [z * tp // slabs for z in range(slabs)]

    def deliver(summed, by):
        pairs = [[], []]
        for i in range(ctx):
            z, rest = divmod(i, SLAB)
            target = order[(place[z] - by) % slabs] * SLAB + rest
            for t in range(tp):
                pairs[t].append((i * tp + t, target * tp + half_of[z]))
        if by == 0:
            moves = [p for p in pairs[0] + pairs[1] if p[0] != p[1]]
            return [summed, lax.ppermute(summed, ("ctx", "tp"), moves)]
        return [lax.ppermute(summed, ("ctx", "tp"), moves) for moves in pairs]

    near, far, both = (
        ((0, None), (1, None)),
        ((0, 1), (0, 2)),
        ((0, None), (1, None), (2, 1), (2, 2)),
    )
    near, far, both = (
        ((0, None), (1, None)),
        ((0, 1), (0, 2)),
        ((0, None), (1, None), (2, 1), (2, 2)),
    )
    blocks = [[gated_half(h) for h in range(SIDE)]]
    arrived = [[], []]
    for step in range(slabs - 1):
        if step:
            blocks[step], summed, arrived[0] = lax.optimization_barrier(
                (blocks[step], summed, arrived[0])
            )
            arrived[0] += deliver(summed, step - 1)
        blocks.append([ring(h) for h in blocks[step]])
        away, got = project_away([blocks[step]], [out_weight, beside], near)
        mine = project_mine([blocks[step]], [out_weight, beside], near, away)
        summed = total(mine, got)[0]
    slab_weights, summed = lax.optimization_barrier((slab_weights, summed))
    away, got = project_away(blocks[: slabs - 1], [slab_weights], far)
    mine = project_mine(blocks[: slabs - 1], [slab_weights], far, away)
    block, _ = lax.optimization_barrier((blocks[-1], mine))
    sources = [out_weight, beside, slab_weights]
    last_away, last_got = project_away([block], sources, both)
    last_mine = project_mine([block], sources, both, last_away)
    batch = total(mine, got)
    for step in range(slabs - 2):
        arrived[1] += deliver(batch[step], step)
    late = deliver(jnp.concatenate([summed, batch[slabs - 2]]), slabs - 2)
    late += deliver(total(last_mine, last_got)[0], slabs - 1)
    arrived = [a + late for a in arrived]

    def place_of(z):
        return sum(jnp.where(z == k, place[k], 0) for k in range(slabs))

    kept = slabs // tp
    steps = [
        lax.rem(place_of(tp_me * kept + j) - place_of(z_me) + slabs, slabs) for j in range(kept)
    ]
    return pl.pallas_call(
        functools.partial(place_kernel, kept, slabs),
        in_specs=[smem] + [vmem] * (SIDE * 2 * slabs),
        out_specs=vmem,
        out_shape=jax.ShapeDtypeStruct((tokens, width), BF16),
        compiler_params=limit,
        cost_estimate=light,
        name="place_columns",
    )(jnp.stack([tp_me, rank, *steps]).astype(jnp.int32), *arrived[0], *arrived[1])


def solution(mesh):
    in_specs = (
        P(None, "ctx", "tp"),
        P(),
        P(None, ("tp", "ctx")),
        P(None, ("tp", "ctx")),
        P(("tp", "ctx")),
        P("tp", "ctx"),
    )
    out_specs = P("ctx", "tp")
    return jax.shard_map(
        per_device, mesh=mesh, in_specs=in_specs, out_specs=out_specs, check_vma=False
    )
```

```python
import functools

import jax
import jax.numpy as jnp
from jax import lax
from jax.experimental import pallas as pl
from jax.experimental.pallas import tpu as pltpu
from jax.sharding import PartitionSpec as P

LANES = 128
SUBLANES = 8
GROUP = LANES * SUBLANES
HALO = 2
TAPS = 3
SIDE = 2
SLAB = SIDE * SIDE
F32 = jnp.float32
BF16 = jnp.bfloat16


def spread(scratch, halo, block, pitch):
    tokens = block.shape[0]
    for tile in range(SUBLANES):
        lanes = pl.ds(tile * LANES, LANES)
        scratch[pl.ds(tile * pitch + SUBLANES - HALO, HALO), :] = halo[:, lanes].astype(F32)
        scratch[pl.ds(tile * pitch + SUBLANES, tokens), :] = block[:, lanes].astype(F32)


def token(scratch, index, pitch):
    return scratch[pl.ds(index, SUBLANES, stride=pitch), :]


def tree_sum(terms):
    while len(terms) > 1:
        terms = [a + b for a, b in zip(terms[::2], terms[1::2])] + terms[len(terms) & ~1 :]
    return terms[0]


def filter_kernel(here, features, halo, taps, u_ref, query_ref, tap_rows, *rows):
    tokens = features.shape[1]
    pitch = tokens + SUBLANES
    for tile in range(SUBLANES):
        for which in range(3):
            for j in range(TAPS):
                row = which * TAPS + j
                tap_rows[row, tile : tile + 1] = taps[which, j : j + 1, tile * LANES : (tile + 1) * LANES]
    for which in range(3):
        spread(rows[which], halo.at[which], features.at[which], pitch)
    weights = [[tap_rows[which * TAPS + j] for j in range(TAPS)] for which in range(3)]

    def step(index, carry):
        carry = list(carry)
        for inner in range(SUBLANES):
            now = index * SUBLANES + inner
            filtered = []
            for which in range(3):
                last, before = carry[which]
                fresh = token(rows[which], now + SUBLANES, pitch)
                filtered.append(
                    weights[which][0] * fresh + weights[which][1] * last + weights[which][2] * before
                )
                carry[which] = (fresh, last)
            query_ref[0, now] = filtered[0]
            u_ref[0, now] = (filtered[1] * filtered[2]).astype(BF16).astype(F32)
        return tuple(carry)

    start = tuple(
        (token(rows[which], SUBLANES - 1, pitch), token(rows[which], SUBLANES - 2, pitch))
        for which in range(3)
    )
    lax.fori_loop(0, tokens // SUBLANES, step, start)


def registers(refs, rank, wide, first, count):
    pitch = wide.shape[0] // SUBLANES
    each = SUBLANES // SLAB
    for d in range(SLAB):
        for j in range(each):
            start = pl.multiple_of(((d ^ rank) * each + j) * pitch, SUBLANES)
            rows = refs[d][0, first : first + count, j * LANES : (j + 1) * LANES]
            wide[pl.ds(start, count), :] = rows.astype(F32)
    return [wide[pl.ds(m, SUBLANES, stride=pitch), :] for m in range(count)]


def state_kernel(modes, here, u_ref, *refs):
    rates, outs, wide = refs[:SLAB], refs[SLAB : 2 * SLAB], refs[-1]
    rank = here[1]
    tokens = u_ref.shape[1]
    decay = [jnp.exp(-rate) for rate in registers(rates, rank, wide, 0, modes)]

    def step(index, states):
        for inner in range(SUBLANES):
            u = u_ref[0, index * SUBLANES + inner]
            states = tuple(states[m] * decay[m] + u for m in range(modes))
        return states

    zero = tuple(jnp.zeros((SUBLANES, LANES), F32) for _ in range(modes))
    states = lax.fori_loop(0, tokens // SUBLANES, step, zero)
    each = SUBLANES // SLAB
    pitch = wide.shape[0] // SUBLANES
    for m in range(modes):
        wide[pl.ds(m, SUBLANES, stride=pitch), :] = states[m]
    for d in range(SLAB):
        for j in range(each):
            start = pl.multiple_of(((d ^ rank) * each + j) * pitch, SUBLANES)
            outs[d][0, :, j * LANES : (j + 1) * LANES] = wide[pl.ds(start, modes), :].astype(BF16)


def slab_kernel(tokens, here, rates, *refs):
    states, out = refs[:SLAB], refs[SLAB]
    slabs = rates.shape[0]
    for g in range(slabs):
        rate = rates[lax.rem(g - here[0] + slabs, slabs), : states[0].shape[1]]
        total = None
        for d in range(SLAB):
            later = (SLAB - 1 - (here[1] ^ d)).astype(F32) * float(tokens)
            term = jnp.exp(-later * rate) * states[d][g].astype(F32)
            total = term if total is None else total + term
        out[g] = total.astype(BF16)


def incoming_kernel(tokens, here, rates, *refs):
    slabs = rates.shape[0]
    states, earlier, outs = refs[:SLAB], refs[SLAB : SLAB + slabs - 1], refs[SLAB + slabs - 1 :]
    for g in range(slabs):
        rate = rates[lax.rem(g - here[0] + slabs, slabs), : states[0].shape[1]]
        entering = earlier[0][g].astype(F32)
        for k in range(1, slabs - 1):
            entering += jnp.exp(-float(k * SLAB * tokens) * rate) * earlier[k][g].astype(F32)
        for d in range(SLAB):
            block = here[1] ^ d
            total = jnp.exp(-(block.astype(F32) * float(tokens)) * rate) * entering
            for e in range(SLAB):
                if e != d:
                    between = block - 1 - (here[1] ^ e)
                    factor = jnp.exp(-(jnp.maximum(between, 0).astype(F32) * float(tokens)) * rate)
                    factor = jnp.where(between >= 0, factor, jnp.zeros_like(factor))
                    total += factor * states[e][g].astype(F32)
            outs[d][g] = total.astype(BF16)


def local_kernel(modes, here, u_ref, *refs):
    rates, y_ref, wide = refs[:SLAB], refs[-2], refs[-1]
    tokens = u_ref.shape[1]
    rate = registers(rates, here[1], wide, 0, modes)
    rest = registers(rates, here[1], wide, modes, modes + 1)
    decay = [jnp.exp(-r) for r in rate]
    weight = [rest[m] * jnp.sqrt(2.0 * rate[m]) for m in range(modes)]
    skip = rest[modes]

    def step(index, states):
        for inner in range(SUBLANES):
            now = index * SUBLANES + inner
            u = u_ref[0, now]
            states = tuple(states[m] * decay[m] + u for m in range(modes))
            y_ref[0, now] = tree_sum([weight[m] * states[m] for m in range(modes)] + [skip * u])
        return states

    zero = tuple(jnp.zeros((SUBLANES, LANES), F32) for _ in range(modes))
    lax.fori_loop(0, tokens // SUBLANES, step, zero)


def gated_kernel(modes, here, query_ref, y_ref, *refs):
    rates, incoming = refs[:SLAB], refs[SLAB : 2 * SLAB]
    out_ref, wide, out_rows = refs[2 * SLAB :]
    tokens = query_ref.shape[1]
    pitch = tokens + SUBLANES
    rate = registers(rates, here[1], wide, 0, modes)
    rest = registers(rates, here[1], wide, modes, modes)
    state = registers(incoming, here[1], wide, 0, modes)
    decay = [jnp.exp(-r) for r in rate]
    weighted = tuple(rest[m] * jnp.sqrt(2.0 * rate[m]) * state[m] for m in range(modes))

    def step(index, weighted):
        for inner in range(SUBLANES):
            now = index * SUBLANES + inner
            weighted = tuple(weighted[m] * decay[m] for m in range(modes))
            long_out = tree_sum([y_ref[0, now], *weighted])
            long_out = long_out.astype(BF16).astype(F32)
            out_rows[pl.ds(now, SUBLANES, stride=pitch), :] = query_ref[0, now] * long_out
        return weighted

    lax.fori_loop(0, tokens // SUBLANES, step, weighted)
    for tile in range(SUBLANES):
        out_ref[:, pl.ds(tile * LANES, LANES)] = out_rows[pl.ds(tile * pitch, tokens), :].astype(BF16)


def project_kernel(count, picks, first, added, here, *refs):
    out_ref, slots, sems = refs[-3:]
    depth, share = slots.shape[1:]
    blocks, sources = refs[:-3], refs[:-3]
    runs = depth // blocks[0].shape[1]
    blocks, sources = blocks[: runs * count], sources[runs * count :]
    rows = pl.ds(first, depth)
    columns = pl.ds(pl.multiple_of(here[0] * share, share), share)
    copies = []
    for i, (which, rank) in enumerate(picks):
        source = sources[which] if rank is None else sources[which].at[here[rank]]
        copies.append(pltpu.make_async_copy(source.at[rows, columns], slots.at[i], sems.at[i]))
        copies[-1].start()
    for i in range(len(picks)):
        copies[i].wait()
        for j in range(count):
            total = sources[-1][here[0], j, i] if added else None
            for h in range(runs):
                size = depth // runs
                term = jnp.dot(
                    blocks[runs * j + h][...],
                    slots[i, h * size : (h + 1) * size],
                    preferred_element_type=F32,
                )
                total = term if total is None else total + term
            if out_ref.ndim == 4:
                out_ref[j, i] = total.astype(out_ref.dtype)
            else:
                part = out_ref.shape[-1]
                for t in range(out_ref.shape[0]):
                    out_ref[t, j, i] = total[:, t * part : (t + 1) * part].astype(out_ref.dtype)


def place_kernel(kept, steps, here, *refs):
    sources, out_ref = refs[:-1], refs[-1]
    share = sources[0].shape[2]
    tp_me, rank = here[0], here[1]
    for slot in range(kept):
        step = here[2 + slot]
        for t in range(SIDE):
            own = jnp.logical_and(step == 0, tp_me == t)
            moved = jnp.logical_and(step == 0, tp_me != t)
            choices = [(own, sources[0]), (moved, sources[1])]
            choices += [(step == k, sources[2 * k + t]) for k in range(1, steps)]
            for chosen, source in choices:

                @pl.when(chosen)
                def _(source=source, slot=slot, t=t):
                    for piece in range(SLAB):
                        start = ((slot * SLAB + (rank ^ piece)) * SIDE + t) * share
                        out_ref[:, pl.ds(pl.multiple_of(start, share), share)] = source[piece]


def ring_order(count):
    return [0] + list(range(1, count, 2)) + [i for i in range(count - 1, 0, -1) if i % 2 == 0]


def any_size(features, conv_weight, decay_rates, residues, skip_gain, out_weight):
    tokens, width = features.shape[1:]
    ctx, tp = lax.axis_size("ctx"), lax.axis_size("tp")
    me, tp_me = lax.axis_index("ctx"), lax.axis_index("tp")
    halo = lax.ppermute(features[:, tokens - HALO :], "ctx", [(i, i + 1) for i in range(ctx - 1)])
    extended = jnp.concatenate([halo, features], axis=1).astype(F32)
    taps = lax.dynamic_slice_in_dim(conv_weight, tp_me * width, width, 2)
    filtered = sum(taps[:, j, None] * extended[:, HALO - j : HALO - j + tokens] for j in range(TAPS))
    u = (filtered[1] * filtered[2]).astype(BF16).astype(F32)
    rates, weights, skip = (
        lax.all_gather(a, "ctx", axis=a.ndim - 1, tiled=True) for a in (decay_rates, residues, skip_gain)
    )
    weights = weights * jnp.sqrt(2.0 * rates)
    decay = jnp.exp(-rates)
    zero = jnp.zeros(rates.shape, F32)
    left = lax.fori_loop(0, tokens, lambda t, s: s * decay + u[t], zero)
    lefts = lax.all_gather(left, "ctx")
    block_decay = jnp.exp(-float(tokens) * rates)
    entering = lax.fori_loop(0, me, lambda b, s: s * block_decay + lefts[b], zero)

    def advance(states, now):
        states = states * decay + now
        return states, jnp.sum(weights * states, axis=0) + skip * now

    long_out = lax.scan(advance, entering, u)[1].astype(BF16).astype(F32)
    gated = (filtered[0] * long_out).astype(BF16)
    whole = lax.all_gather(gated, "ctx", axis=0, tiled=True)
    partial = jnp.dot(whole, out_weight, preferred_element_type=F32).astype(BF16)
    share = partial.shape[1] // tp
    partial = partial.reshape(ctx * tokens, tp, share).transpose(1, 0, 2)
    partial = lax.all_to_all(partial, "tp", split_axis=0, concat_axis=0, tiled=True)
    summed = jnp.sum(partial.astype(F32), axis=0).astype(BF16).reshape(ctx, tokens, share)
    summed = lax.all_to_all(summed, "ctx", split_axis=0, concat_axis=0, tiled=True)
    placed = lax.all_to_all(
        summed.reshape(tp, ctx // tp, tokens, share), "tp", split_axis=0, concat_axis=0, tiled=True
    )
    return placed.transpose(2, 1, 0, 3).reshape(tokens, width)


def per_device(features, conv_weight, decay_rates, residues, skip_gain, out_weight):
    tokens, width = features.shape[1:]
    modes, owned = decay_rates.shape
    ctx, tp = lax.axis_size("ctx"), lax.axis_size("tp")
    depth, columns = out_weight.shape
    share = columns // tp
    if owned * SLAB != GROUP or tp != SIDE or share % LANES or ctx // SLAB < 3:
        return any_size(features, conv_weight, decay_rates, residues, skip_gain, out_weight)
    slabs = ctx // SLAB
    groups = width // GROUP
    me, tp_me = lax.axis_index("ctx"), lax.axis_index("tp")
    z_me, rank = me // SLAB, me % SLAB
    order = ring_order(slabs)
    place = [order.index(z) for z in range(slabs)]
    here = jnp.stack([z_me, rank, tp_me]).astype(jnp.int32)

    def within_slab(array, mask):
        return lax.ppermute(array, "ctx", [(i, i ^ mask) for i in range(ctx)])

    def from_slab(array, by):
        return lax.ppermute(array, "ctx", [(i, (i - by * SLAB) % ctx) for i in range(ctx)])

    def ring(array):
        pairs = []
        for i in range(ctx):
            z, rest = divmod(i, SLAB)
            pairs.append((i, order[(place[z] + 1) % slabs] * SLAB + rest))
        return lax.ppermute(array, "ctx", pairs)

    halo = lax.ppermute(
        features[:, tokens - HALO :, :], "ctx", [(i, i + 1) for i in range(ctx - 1)]
    )
    rows = jnp.concatenate([decay_rates, residues, skip_gain[None]], axis=0)
    rows = jnp.stack([rows] + [from_slab(rows, by) for by in range(1, slabs)])
    rows, halo = lax.optimization_barrier((rows, halo))
    rates = [rows, within_slab(rows, 1), within_slab(rows, 2)]

    beside = within_slab(out_weight, 1)
    slab_weights = lax.all_gather(
        out_weight,
        "ctx",
        axis_index_groups=[list(range(z * SLAB, (z + 1) * SLAB)) for z in range(slabs)],
    )

    limit = pltpu.CompilerParams(vmem_limit_bytes=16 * 1024 * 1024)
    large = pltpu.CompilerParams(vmem_limit_bytes=48 * 1024 * 1024)
    light = pl.CostEstimate(flops=1, bytes_accessed=1, transcendentals=0)
    series_shape = jax.ShapeDtypeStruct((groups, tokens, SUBLANES, LANES), F32)
    state_shape = jax.ShapeDtypeStruct((groups, modes, owned), BF16)
    scratch_rows = pltpu.VMEM((SUBLANES * (tokens + SUBLANES), LANES), F32)
    wide = pltpu.VMEM((SUBLANES * (modes + SUBLANES), LANES), F32)
    series = pl.BlockSpec((1, tokens, SUBLANES, LANES), lambda g, here: (g, 0, 0, 0))
    state_spec = pl.BlockSpec((1, modes, owned), lambda g, here: (g, 0, 0))
    rate_spec = pl.BlockSpec(
        (1, 2 * modes + 1, owned), lambda g, here: (lax.rem(g - here[0] + slabs, slabs), 0, 0)
    )

    def grouped(kernel, name, in_specs, out_specs, out_shape, scratch, groups=groups):
        return pl.pallas_call(
            kernel,
            grid_spec=pltpu.PrefetchScalarGridSpec(
                num_scalar_prefetch=1,
                grid=(groups,),
                in_specs=in_specs,
                out_specs=out_specs,
                scratch_shapes=scratch,
            ),
            out_shape=out_shape,
            compiler_params=limit,
            cost_estimate=light,
            name=name,
        )

    u, query = grouped(
        filter_kernel,
        "short_filters",
        [
            pl.BlockSpec((3, tokens, GROUP), lambda g, here: (0, 0, g)),
            pl.BlockSpec((3, HALO, GROUP), lambda g, here: (0, 0, g)),
            pl.BlockSpec((3, TAPS, GROUP), lambda g, here: (0, 0, here[2] * groups + g)),
        ],
        [series, series],
        [series_shape, series_shape],
        [pltpu.VMEM((3 * TAPS, SUBLANES, LANES), F32), scratch_rows, scratch_rows, scratch_rows],
    )(here, features, halo, conv_weight)

    passed, u = lax.optimization_barrier((rates[2], u))
    rates.append(within_slab(passed, 1))

    left = grouped(
        functools.partial(state_kernel, modes),
        "block_states",
        [series] + [rate_spec] * SLAB,
        [state_spec] * SLAB,
        [state_shape] * SLAB,
        [wide],
    )(here, u, *rates)
    left = [left[0]] + [within_slab(left[d], d) for d in range(1, SLAB)]

    smem = pl.BlockSpec(memory_space=pltpu.SMEM)
    vmem = pl.BlockSpec(memory_space=pltpu.VMEM)
    slab_left = pl.pallas_call(
        functools.partial(slab_kernel, tokens),
        in_specs=[smem] + [vmem] * (1 + SLAB),
        out_specs=vmem,
        out_shape=state_shape,
        compiler_params=limit,
        cost_estimate=light,
        name="slab_states",
    )(here, rates[0], *left)
    earlier = [
        lax.ppermute(slab_left, "ctx", [(i, i + by * SLAB) for i in range(ctx - by * SLAB)])
        for by in range(1, slabs)
    ]

    local = grouped(
        functools.partial(local_kernel, modes),
        "local_convolution",
        [series] + [rate_spec] * SLAB,
        series,
        series_shape,
        [wide],
    )(here, u, *rates)
    earlier, local = lax.optimization_barrier((earlier, local))

    incoming = pl.pallas_call(
        functools.partial(incoming_kernel, tokens),
        in_specs=[smem] + [vmem] * (SLAB + slabs),
        out_specs=[vmem] * SLAB,
        out_shape=[state_shape] * SLAB,
        compiler_params=limit,
        cost_estimate=light,
        name="incoming_states",
    )(here, rates[0], *left, *earlier)
    incoming = [incoming[0]] + [within_slab(incoming[d], d) for d in range(1, SLAB)]

    def gated_half(half):
        count = groups // SIDE
        first = half * count

        def shifted(spec):
            return pl.BlockSpec(spec.block_shape, lambda g, here: spec.index_map(g + first, here))

        return grouped(
            functools.partial(gated_kernel, modes),
            "gated_block",
            [shifted(s) for s in [series] * 2 + [rate_spec] * SLAB + [state_spec] * SLAB],
            pl.BlockSpec((tokens, GROUP), lambda g, here: (0, g)),
            jax.ShapeDtypeStruct((tokens, width // SIDE), BF16),
            [wide, scratch_rows],
            count,
        )(here, query, local, *rates, *incoming)

    def project(blocks, sources, picks, share_index, partial=None, halves=(0, 1)):
        scalars = jnp.stack([share_index if share_index is not None else 0, rank ^ 2, rank ^ 3])
        run = depth // SIDE
        wide_share = columns if share_index is None else share
        shape = (len(blocks), len(picks), tokens, share)
        if share_index is None:
            out = jax.ShapeDtypeStruct((tp, *shape), F32)
        else:
            out = jax.ShapeDtypeStruct(shape, BF16)
        return pl.pallas_call(
            functools.partial(
                project_kernel, len(blocks), picks, halves[0] * run, partial is not None
            ),
            in_specs=[smem]
            + [vmem] * (len(halves) * len(blocks))
            + [pl.BlockSpec(memory_space=pltpu.HBM)] * len(sources)
            + ([vmem] if partial is not None else []),
            out_specs=vmem,
            out_shape=out,
            scratch_shapes=[
                pltpu.VMEM((len(picks), len(halves) * run, wide_share), BF16),
                pltpu.SemaphoreType.DMA((len(picks),)),
            ],
            compiler_params=large,
            cost_estimate=light,
            name="project_block",
        )(
            scalars.astype(jnp.int32),
            *[b[h] for b in blocks for h in halves],
            *sources,
            *([partial] if partial is not None else []),
        )

    def project_away(blocks, sources, picks):
        away = project(blocks, sources, picks, 1 - tp_me)
        return away, lax.ppermute(away, "tp", [(0, 1), (1, 0)])

    def project_mine(blocks, sources, picks, after):
        blocks, _ = lax.optimization_barrier((blocks, after))
        return project(blocks, sources, picks, tp_me)

    def total(mine, got):
        return (mine.astype(F32) + got.astype(F32)).astype(BF16)

    half_of = [z * tp // slabs for z in range(slabs)]

    def deliver(summed, by):
        pairs = [[], []]
        for i in range(ctx):
            z, rest = divmod(i, SLAB)
            target = order[(place[z] - by) % slabs] * SLAB + rest
            for t in range(tp):
                pairs[t].append((i * tp + t, target * tp + half_of[z]))
        if by == 0:
            moves = [p for p in pairs[0] + pairs[1] if p[0] != p[1]]
            return [summed, lax.ppermute(summed, ("ctx", "tp"), moves)]
        return [lax.ppermute(summed, ("ctx", "tp"), moves) for moves in pairs]

    near, far, both = (
        ((0, None), (1, None)),
        ((0, 1), (0, 2)),
        ((0, None), (1, None), (2, 1), (2, 2)),
    )
    near, far, both = (
        ((0, None), (1, None)),
        ((0, 1), (0, 2)),
        ((0, None), (1, None), (2, 1), (2, 2)),
    )
    blocks = [[gated_half(h) for h in range(SIDE)]]
    sums = []
    for step in range(slabs - 1):
        if step:
            blocks[step], summed = lax.optimization_barrier((blocks[step], summed))
            sums.append(summed)
        blocks.append([ring(h) for h in blocks[step]])
        away, got = project_away([blocks[step]], [out_weight, beside], near)
        mine = project_mine([blocks[step]], [out_weight, beside], near, away)
        summed = total(mine, got)[0]
    slab_weights, _ = lax.optimization_barrier((slab_weights, mine))
    earlier_mine, earlier_got = mine, got
    away, got = project_away(blocks[: slabs - 1], [slab_weights], far)
    mine = project_mine(blocks[: slabs - 1], [slab_weights], far, away)
    sources = [out_weight, beside, slab_weights]
    head, _ = lax.optimization_barrier((blocks[-1][0], mine))
    partial = project([[head]], sources, both, None, None, (0,))
    tail, partial, got, earlier_got = lax.optimization_barrier(
        (blocks[-1][1], partial, got, earlier_got)
    )
    sums.append(total(earlier_mine, earlier_got)[0])
    last_away = project([[None, tail]], sources, both, 1 - tp_me, partial, (1,))
    last_got = lax.ppermute(last_away, "tp", [(0, 1), (1, 0)])
    tail, _ = lax.optimization_barrier((tail, last_away))
    last_mine = project([[None, tail]], sources, both, tp_me, partial, (1,))
    batch = total(mine, got)
    arrived = []
    for step in range(slabs - 1):
        arrived += deliver(jnp.concatenate([sums[step], batch[step]]), step)
    arrived += deliver(total(last_mine, last_got)[0], slabs - 1)

    def place_of(z):
        return sum(jnp.where(z == k, place[k], 0) for k in range(slabs))

    kept = slabs // tp
    steps = [
        lax.rem(place_of(tp_me * kept + j) - place_of(z_me) + slabs, slabs) for j in range(kept)
    ]
    return pl.pallas_call(
        functools.partial(place_kernel, kept, slabs),
        in_specs=[smem] + [vmem] * (SIDE * slabs),
        out_specs=vmem,
        out_shape=jax.ShapeDtypeStruct((tokens, width), BF16),
        compiler_params=limit,
        cost_estimate=light,
        name="place_columns",
    )(jnp.stack([tp_me, rank, *steps]).astype(jnp.int32), *arrived)


def solution(mesh):
    in_specs = (
        P(None, "ctx", "tp"),
        P(),
        P(None, ("tp", "ctx")),
        P(None, ("tp", "ctx")),
        P(("tp", "ctx")),
        P("tp", "ctx"),
    )
    out_specs = P("ctx", "tp")
    return jax.shard_map(
        per_device, mesh=mesh, in_specs=in_specs, out_specs=out_specs, check_vma=False
    )
```

```python
import functools

import jax
import jax.numpy as jnp
from jax import lax
from jax.experimental import pallas as pl
from jax.experimental.pallas import tpu as pltpu
from jax.sharding import PartitionSpec as P

LANES = 128
SUBLANES = 8
GROUP = LANES * SUBLANES
HALO = 2
TAPS = 3
SIDE = 2
SLAB = SIDE * SIDE
F32 = jnp.float32
BF16 = jnp.bfloat16


def spread(scratch, halo, block, pitch):
    tokens = block.shape[0]
    for tile in range(SUBLANES):
        lanes = pl.ds(tile * LANES, LANES)
        scratch[pl.ds(tile * pitch + SUBLANES - HALO, HALO), :] = halo[:, lanes].astype(F32)
        scratch[pl.ds(tile * pitch + SUBLANES, tokens), :] = block[:, lanes].astype(F32)


def token(scratch, index, pitch):
    return scratch[pl.ds(index, SUBLANES, stride=pitch), :]


def tree_sum(terms):
    while len(terms) > 1:
        terms = [a + b for a, b in zip(terms[::2], terms[1::2])] + terms[len(terms) & ~1 :]
    return terms[0]


def filter_kernel(here, features, halo, taps, u_ref, query_ref, tap_rows, *rows):
    tokens = features.shape[1]
    pitch = tokens + SUBLANES
    for tile in range(SUBLANES):
        for which in range(3):
            for j in range(TAPS):
                row = which * TAPS + j
                tap_rows[row, tile : tile + 1] = taps[which, j : j + 1, tile * LANES : (tile + 1) * LANES]
    for which in range(3):
        spread(rows[which], halo.at[which], features.at[which], pitch)
    weights = [[tap_rows[which * TAPS + j] for j in range(TAPS)] for which in range(3)]

    def step(index, carry):
        carry = list(carry)
        for inner in range(SUBLANES):
            now = index * SUBLANES + inner
            filtered = []
            for which in range(3):
                last, before = carry[which]
                fresh = token(rows[which], now + SUBLANES, pitch)
                filtered.append(
                    weights[which][0] * fresh + weights[which][1] * last + weights[which][2] * before
                )
                carry[which] = (fresh, last)
            query_ref[0, now] = filtered[0]
            u_ref[0, now] = (filtered[1] * filtered[2]).astype(BF16).astype(F32)
        return tuple(carry)

    start = tuple(
        (token(rows[which], SUBLANES - 1, pitch), token(rows[which], SUBLANES - 2, pitch))
        for which in range(3)
    )
    lax.fori_loop(0, tokens // SUBLANES, step, start)


def registers(refs, rank, wide, first, count):
    pitch = wide.shape[0] // SUBLANES
    each = SUBLANES // SLAB
    for d in range(SLAB):
        for j in range(each):
            start = pl.multiple_of(((d ^ rank) * each + j) * pitch, SUBLANES)
            rows = refs[d][0, first : first + count, j * LANES : (j + 1) * LANES]
            wide[pl.ds(start, count), :] = rows.astype(F32)
    return [wide[pl.ds(m, SUBLANES, stride=pitch), :] for m in range(count)]


def state_kernel(modes, here, u_ref, *refs):
    rates, outs, wide = refs[:SLAB], refs[SLAB : 2 * SLAB], refs[-1]
    rank = here[1]
    tokens = u_ref.shape[1]
    decay = [jnp.exp(-rate) for rate in registers(rates, rank, wide, 0, modes)]

    def step(index, states):
        for inner in range(SUBLANES):
            u = u_ref[0, index * SUBLANES + inner]
            states = tuple(states[m] * decay[m] + u for m in range(modes))
        return states

    zero = tuple(jnp.zeros((SUBLANES, LANES), F32) for _ in range(modes))
    states = lax.fori_loop(0, tokens // SUBLANES, step, zero)
    each = SUBLANES // SLAB
    pitch = wide.shape[0] // SUBLANES
    for m in range(modes):
        wide[pl.ds(m, SUBLANES, stride=pitch), :] = states[m]
    for d in range(SLAB):
        for j in range(each):
            start = pl.multiple_of(((d ^ rank) * each + j) * pitch, SUBLANES)
            outs[d][0, :, j * LANES : (j + 1) * LANES] = wide[pl.ds(start, modes), :].astype(BF16)


def slab_kernel(tokens, here, rates, *refs):
    states, out = refs[:SLAB], refs[SLAB]
    slabs = rates.shape[0]
    for g in range(slabs):
        rate = rates[lax.rem(g - here[0] + slabs, slabs), : states[0].shape[1]]
        total = None
        for d in range(SLAB):
            later = (SLAB - 1 - (here[1] ^ d)).astype(F32) * float(tokens)
            term = jnp.exp(-later * rate) * states[d][g].astype(F32)
            total = term if total is None else total + term
        out[g] = total.astype(BF16)


def incoming_kernel(tokens, here, rates, *refs):
    slabs = rates.shape[0]
    states, earlier, outs = refs[:SLAB], refs[SLAB : SLAB + slabs - 1], refs[SLAB + slabs - 1 :]
    for g in range(slabs):
        rate = rates[lax.rem(g - here[0] + slabs, slabs), : states[0].shape[1]]
        entering = earlier[0][g].astype(F32)
        for k in range(1, slabs - 1):
            entering += jnp.exp(-float(k * SLAB * tokens) * rate) * earlier[k][g].astype(F32)
        for d in range(SLAB):
            block = here[1] ^ d
            total = jnp.exp(-(block.astype(F32) * float(tokens)) * rate) * entering
            for e in range(SLAB):
                if e != d:
                    between = block - 1 - (here[1] ^ e)
                    factor = jnp.exp(-(jnp.maximum(between, 0).astype(F32) * float(tokens)) * rate)
                    factor = jnp.where(between >= 0, factor, jnp.zeros_like(factor))
                    total += factor * states[e][g].astype(F32)
            outs[d][g] = total.astype(BF16)


def local_kernel(modes, here, u_ref, *refs):
    rates, y_ref, wide = refs[:SLAB], refs[-2], refs[-1]
    tokens = u_ref.shape[1]
    rate = registers(rates, here[1], wide, 0, modes)
    rest = registers(rates, here[1], wide, modes, modes + 1)
    decay = [jnp.exp(-r) for r in rate]
    weight = [rest[m] * jnp.sqrt(2.0 * rate[m]) for m in range(modes)]
    skip = rest[modes]

    def step(index, states):
        for inner in range(SUBLANES):
            now = index * SUBLANES + inner
            u = u_ref[0, now]
            states = tuple(states[m] * decay[m] + u for m in range(modes))
            y_ref[0, now] = tree_sum([weight[m] * states[m] for m in range(modes)] + [skip * u])
        return states

    zero = tuple(jnp.zeros((SUBLANES, LANES), F32) for _ in range(modes))
    lax.fori_loop(0, tokens // SUBLANES, step, zero)


def gated_kernel(modes, here, query_ref, y_ref, *refs):
    rates, incoming = refs[:SLAB], refs[SLAB : 2 * SLAB]
    out_ref, wide, out_rows = refs[2 * SLAB :]
    tokens = query_ref.shape[1]
    pitch = tokens + SUBLANES
    rate = registers(rates, here[1], wide, 0, modes)
    rest = registers(rates, here[1], wide, modes, modes)
    state = registers(incoming, here[1], wide, 0, modes)
    decay = [jnp.exp(-r) for r in rate]
    weighted = tuple(rest[m] * jnp.sqrt(2.0 * rate[m]) * state[m] for m in range(modes))

    def step(index, weighted):
        for inner in range(SUBLANES):
            now = index * SUBLANES + inner
            weighted = tuple(weighted[m] * decay[m] for m in range(modes))
            long_out = tree_sum([y_ref[0, now], *weighted])
            long_out = long_out.astype(BF16).astype(F32)
            out_rows[pl.ds(now, SUBLANES, stride=pitch), :] = query_ref[0, now] * long_out
        return weighted

    lax.fori_loop(0, tokens // SUBLANES, step, weighted)
    for tile in range(SUBLANES):
        out_ref[:, pl.ds(tile * LANES, LANES)] = out_rows[pl.ds(tile * pitch, tokens), :].astype(BF16)


def project_kernel(count, picks, first, added, here, *refs):
    out_ref, slots, sems = refs[-3:]
    depth, share = slots.shape[1:]
    blocks, sources = refs[:-3], refs[:-3]
    runs = depth // blocks[0].shape[1]
    blocks, sources = blocks[: runs * count], sources[runs * count :]
    rows = pl.ds(first, depth)
    columns = pl.ds(pl.multiple_of(here[0] * share, share), share)
    copies = []
    for i, (which, rank) in enumerate(picks):
        source = sources[which] if rank is None else sources[which].at[here[rank]]
        copies.append(pltpu.make_async_copy(source.at[rows, columns], slots.at[i], sems.at[i]))
        copies[-1].start()
    for i in range(len(picks)):
        copies[i].wait()
        for j in range(count):
            total = sources[-1][here[0], j, i] if added else None
            for h in range(runs):
                size = depth // runs
                term = jnp.dot(
                    blocks[runs * j + h][...],
                    slots[i, h * size : (h + 1) * size],
                    preferred_element_type=F32,
                )
                total = term if total is None else total + term
            if out_ref.ndim == 4:
                out_ref[j, i] = total.astype(out_ref.dtype)
            else:
                part = out_ref.shape[-1]
                for t in range(out_ref.shape[0]):
                    out_ref[t, j, i] = total[:, t * part : (t + 1) * part].astype(out_ref.dtype)


def place_kernel(kept, steps, here, *refs):
    sources, out_ref = refs[:-1], refs[-1]
    share = sources[0].shape[2]
    tp_me, rank = here[0], here[1]
    for slot in range(kept):
        step = here[2 + slot]
        for t in range(SIDE):
            own = jnp.logical_and(step == 0, tp_me == t)
            moved = jnp.logical_and(step == 0, tp_me != t)
            choices = [(own, sources[0]), (moved, sources[1])]
            choices += [(step == k, sources[2 * k + t]) for k in range(1, steps)]
            for chosen, source in choices:

                @pl.when(chosen)
                def _(source=source, slot=slot, t=t):
                    for piece in range(SLAB):
                        start = ((slot * SLAB + (rank ^ piece)) * SIDE + t) * share
                        out_ref[:, pl.ds(pl.multiple_of(start, share), share)] = source[piece]


def ring_order(count):
    return [0] + list(range(1, count, 2)) + [i for i in range(count - 1, 0, -1) if i % 2 == 0]


def any_size(features, conv_weight, decay_rates, residues, skip_gain, out_weight):
    tokens, width = features.shape[1:]
    ctx, tp = lax.axis_size("ctx"), lax.axis_size("tp")
    me, tp_me = lax.axis_index("ctx"), lax.axis_index("tp")
    halo = lax.ppermute(features[:, tokens - HALO :], "ctx", [(i, i + 1) for i in range(ctx - 1)])
    extended = jnp.concatenate([halo, features], axis=1).astype(F32)
    taps = lax.dynamic_slice_in_dim(conv_weight, tp_me * width, width, 2)
    filtered = sum(taps[:, j, None] * extended[:, HALO - j : HALO - j + tokens] for j in range(TAPS))
    u = (filtered[1] * filtered[2]).astype(BF16).astype(F32)
    rates, weights, skip = (
        lax.all_gather(a, "ctx", axis=a.ndim - 1, tiled=True) for a in (decay_rates, residues, skip_gain)
    )
    weights = weights * jnp.sqrt(2.0 * rates)
    decay = jnp.exp(-rates)
    zero = jnp.zeros(rates.shape, F32)
    left = lax.fori_loop(0, tokens, lambda t, s: s * decay + u[t], zero)
    lefts = lax.all_gather(left, "ctx")
    block_decay = jnp.exp(-float(tokens) * rates)
    entering = lax.fori_loop(0, me, lambda b, s: s * block_decay + lefts[b], zero)

    def advance(states, now):
        states = states * decay + now
        return states, jnp.sum(weights * states, axis=0) + skip * now

    long_out = lax.scan(advance, entering, u)[1].astype(BF16).astype(F32)
    gated = (filtered[0] * long_out).astype(BF16)
    whole = lax.all_gather(gated, "ctx", axis=0, tiled=True)
    partial = jnp.dot(whole, out_weight, preferred_element_type=F32).astype(BF16)
    share = partial.shape[1] // tp
    partial = partial.reshape(ctx * tokens, tp, share).transpose(1, 0, 2)
    partial = lax.all_to_all(partial, "tp", split_axis=0, concat_axis=0, tiled=True)
    summed = jnp.sum(partial.astype(F32), axis=0).astype(BF16).reshape(ctx, tokens, share)
    summed = lax.all_to_all(summed, "ctx", split_axis=0, concat_axis=0, tiled=True)
    placed = lax.all_to_all(
        summed.reshape(tp, ctx // tp, tokens, share), "tp", split_axis=0, concat_axis=0, tiled=True
    )
    return placed.transpose(2, 1, 0, 3).reshape(tokens, width)


def per_device(features, conv_weight, decay_rates, residues, skip_gain, out_weight):
    tokens, width = features.shape[1:]
    modes, owned = decay_rates.shape
    ctx, tp = lax.axis_size("ctx"), lax.axis_size("tp")
    depth, columns = out_weight.shape
    share = columns // tp
    if owned * SLAB != GROUP or tp != SIDE or share % LANES or ctx // SLAB < 3:
        return any_size(features, conv_weight, decay_rates, residues, skip_gain, out_weight)
    slabs = ctx // SLAB
    groups = width // GROUP
    me, tp_me = lax.axis_index("ctx"), lax.axis_index("tp")
    z_me, rank = me // SLAB, me % SLAB
    order = ring_order(slabs)
    place = [order.index(z) for z in range(slabs)]
    here = jnp.stack([z_me, rank, tp_me]).astype(jnp.int32)

    def within_slab(array, mask):
        return lax.ppermute(array, "ctx", [(i, i ^ mask) for i in range(ctx)])

    def from_slab(array, by):
        return lax.ppermute(array, "ctx", [(i, (i - by * SLAB) % ctx) for i in range(ctx)])

    def ring(array):
        pairs = []
        for i in range(ctx):
            z, rest = divmod(i, SLAB)
            pairs.append((i, order[(place[z] + 1) % slabs] * SLAB + rest))
        return lax.ppermute(array, "ctx", pairs)

    halo = lax.ppermute(
        features[:, tokens - HALO :, :], "ctx", [(i, i + 1) for i in range(ctx - 1)]
    )
    rows = jnp.concatenate([decay_rates, residues, skip_gain[None]], axis=0)
    rows = jnp.stack([rows] + [from_slab(rows, by) for by in range(1, slabs)])
    rows, halo = lax.optimization_barrier((rows, halo))
    rates = [rows, within_slab(rows, 1), within_slab(rows, 2)]

    beside = within_slab(out_weight, 1)
    slab_weights = lax.all_gather(
        out_weight,
        "ctx",
        axis_index_groups=[list(range(z * SLAB, (z + 1) * SLAB)) for z in range(slabs)],
    )

    limit = pltpu.CompilerParams(vmem_limit_bytes=16 * 1024 * 1024)
    large = pltpu.CompilerParams(vmem_limit_bytes=48 * 1024 * 1024)
    light = pl.CostEstimate(flops=1, bytes_accessed=1, transcendentals=0)
    series_shape = jax.ShapeDtypeStruct((groups, tokens, SUBLANES, LANES), F32)
    state_shape = jax.ShapeDtypeStruct((groups, modes, owned), BF16)
    scratch_rows = pltpu.VMEM((SUBLANES * (tokens + SUBLANES), LANES), F32)
    wide = pltpu.VMEM((SUBLANES * (modes + SUBLANES), LANES), F32)
    series = pl.BlockSpec((1, tokens, SUBLANES, LANES), lambda g, here: (g, 0, 0, 0))
    state_spec = pl.BlockSpec((1, modes, owned), lambda g, here: (g, 0, 0))
    rate_spec = pl.BlockSpec(
        (1, 2 * modes + 1, owned), lambda g, here: (lax.rem(g - here[0] + slabs, slabs), 0, 0)
    )

    def grouped(kernel, name, in_specs, out_specs, out_shape, scratch, groups=groups):
        return pl.pallas_call(
            kernel,
            grid_spec=pltpu.PrefetchScalarGridSpec(
                num_scalar_prefetch=1,
                grid=(groups,),
                in_specs=in_specs,
                out_specs=out_specs,
                scratch_shapes=scratch,
            ),
            out_shape=out_shape,
            compiler_params=limit,
            cost_estimate=light,
            name=name,
        )

    u, query = grouped(
        filter_kernel,
        "short_filters",
        [
            pl.BlockSpec((3, tokens, GROUP), lambda g, here: (0, 0, g)),
            pl.BlockSpec((3, HALO, GROUP), lambda g, here: (0, 0, g)),
            pl.BlockSpec((3, TAPS, GROUP), lambda g, here: (0, 0, here[2] * groups + g)),
        ],
        [series, series],
        [series_shape, series_shape],
        [pltpu.VMEM((3 * TAPS, SUBLANES, LANES), F32), scratch_rows, scratch_rows, scratch_rows],
    )(here, features, halo, conv_weight)

    passed, u = lax.optimization_barrier((rates[2], u))
    rates.append(within_slab(passed, 1))

    left = grouped(
        functools.partial(state_kernel, modes),
        "block_states",
        [series] + [rate_spec] * SLAB,
        [state_spec] * SLAB,
        [state_shape] * SLAB,
        [wide],
    )(here, u, *rates)
    left = [left[0]] + [within_slab(left[d], d) for d in range(1, SLAB)]

    smem = pl.BlockSpec(memory_space=pltpu.SMEM)
    vmem = pl.BlockSpec(memory_space=pltpu.VMEM)
    slab_left = pl.pallas_call(
        functools.partial(slab_kernel, tokens),
        in_specs=[smem] + [vmem] * (1 + SLAB),
        out_specs=vmem,
        out_shape=state_shape,
        compiler_params=limit,
        cost_estimate=light,
        name="slab_states",
    )(here, rates[0], *left)
    earlier = [
        lax.ppermute(slab_left, "ctx", [(i, i + by * SLAB) for i in range(ctx - by * SLAB)])
        for by in range(1, slabs)
    ]

    local = grouped(
        functools.partial(local_kernel, modes),
        "local_convolution",
        [series] + [rate_spec] * SLAB,
        series,
        series_shape,
        [wide],
    )(here, u, *rates)
    earlier, local = lax.optimization_barrier((earlier, local))

    incoming = pl.pallas_call(
        functools.partial(incoming_kernel, tokens),
        in_specs=[smem] + [vmem] * (SLAB + slabs),
        out_specs=[vmem] * SLAB,
        out_shape=[state_shape] * SLAB,
        compiler_params=limit,
        cost_estimate=light,
        name="incoming_states",
    )(here, rates[0], *left, *earlier)
    incoming = [incoming[0]] + [within_slab(incoming[d], d) for d in range(1, SLAB)]

    def gated_half(half):
        count = groups // SIDE
        first = half * count

        def shifted(spec):
            return pl.BlockSpec(spec.block_shape, lambda g, here: spec.index_map(g + first, here))

        return grouped(
            functools.partial(gated_kernel, modes),
            "gated_block",
            [shifted(s) for s in [series] * 2 + [rate_spec] * SLAB + [state_spec] * SLAB],
            pl.BlockSpec((tokens, GROUP), lambda g, here: (0, g)),
            jax.ShapeDtypeStruct((tokens, width // SIDE), BF16),
            [wide, scratch_rows],
            count,
        )(here, query, local, *rates, *incoming)

    def project(blocks, sources, picks, share_index, partial=None, halves=(0, 1)):
        scalars = jnp.stack([share_index if share_index is not None else 0, rank ^ 2, rank ^ 3])
        run = depth // SIDE
        wide_share = columns if share_index is None else share
        shape = (len(blocks), len(picks), tokens, share)
        if share_index is None:
            out = jax.ShapeDtypeStruct((tp, *shape), F32)
        else:
            out = jax.ShapeDtypeStruct(shape, BF16)
        return pl.pallas_call(
            functools.partial(
                project_kernel, len(blocks), picks, halves[0] * run, partial is not None
            ),
            in_specs=[smem]
            + [vmem] * (len(halves) * len(blocks))
            + [pl.BlockSpec(memory_space=pltpu.HBM)] * len(sources)
            + ([vmem] if partial is not None else []),
            out_specs=vmem,
            out_shape=out,
            scratch_shapes=[
                pltpu.VMEM((len(picks), len(halves) * run, wide_share), BF16),
                pltpu.SemaphoreType.DMA((len(picks),)),
            ],
            compiler_params=large,
            cost_estimate=light,
            name="project_block",
        )(
            scalars.astype(jnp.int32),
            *[b[h] for b in blocks for h in halves],
            *sources,
            *([partial] if partial is not None else []),
        )

    def project_away(blocks, sources, picks):
        away = project(blocks, sources, picks, 1 - tp_me)
        return away, lax.ppermute(away, "tp", [(0, 1), (1, 0)])

    def project_mine(blocks, sources, picks, after):
        blocks, _ = lax.optimization_barrier((blocks, after))
        return project(blocks, sources, picks, tp_me)

    def total(mine, got):
        return (mine.astype(F32) + got.astype(F32)).astype(BF16)

    half_of = [z * tp // slabs for z in range(slabs)]

    def deliver(summed, by):
        pairs = [[], []]
        for i in range(ctx):
            z, rest = divmod(i, SLAB)
            target = order[(place[z] - by) % slabs] * SLAB + rest
            for t in range(tp):
                pairs[t].append((i * tp + t, target * tp + half_of[z]))
        if by == 0:
            moves = [p for p in pairs[0] + pairs[1] if p[0] != p[1]]
            return [summed, lax.ppermute(summed, ("ctx", "tp"), moves)]
        return [lax.ppermute(summed, ("ctx", "tp"), moves) for moves in pairs]

    near, far, both = (
        ((0, None), (1, None)),
        ((0, 1), (0, 2)),
        ((0, None), (1, None), (2, 1), (2, 2)),
    )
    near, far, both = (
        ((0, None), (1, None)),
        ((0, 1), (0, 2)),
        ((0, None), (1, None), (2, 1), (2, 2)),
    )
    blocks = [[gated_half(h) for h in range(SIDE)]]
    kept_parts, got_parts = [], []
    mine = None
    for step in range(slabs - 1):
        first, second = block = blocks[step]
        if step:
            second, mine = lax.optimization_barrier((second, mine))
            block, _ = lax.optimization_barrier((block, mine))
        if step > 1:
            block, _ = lax.optimization_barrier((block, got_parts[: step - 1]))
        blocks.append([ring(first), ring(second)])
        away, got = project_away([block], [out_weight, beside], near)
        mine = project_mine([block], [out_weight, beside], near, away)
        kept_parts.append(mine)
        got_parts.append(got)
    slab_weights, _ = lax.optimization_barrier((slab_weights, (mine, got_parts[:-1])))
    away, got = project_away(blocks[: slabs - 1], [slab_weights], far)
    mine = project_mine(blocks[: slabs - 1], [slab_weights], far, away)
    sources = [out_weight, beside, slab_weights]
    head, _ = lax.optimization_barrier((blocks[-1][0], mine))
    partial = project([[head]], sources, both, None, None, (0,))
    tail, partial = lax.optimization_barrier((blocks[-1][1], partial))
    last_away = project([[None, tail]], sources, both, 1 - tp_me, partial, (1,))
    last_got = lax.ppermute(last_away, "tp", [(0, 1), (1, 0)])
    tail, got, got_parts, _ = lax.optimization_barrier((tail, got, got_parts, last_away))
    last_mine = project([[None, tail]], sources, both, tp_me, partial, (1,))
    batch = total(mine, got)
    arrived = []
    for step in range(slabs - 1):
        summed = total(kept_parts[step], got_parts[step])[0]
        arrived += deliver(jnp.concatenate([summed, batch[step]]), step)
    arrived += deliver(total(last_mine, last_got)[0], slabs - 1)

    def place_of(z):
        return sum(jnp.where(z == k, place[k], 0) for k in range(slabs))

    kept = slabs // tp
    steps = [
        lax.rem(place_of(tp_me * kept + j) - place_of(z_me) + slabs, slabs) for j in range(kept)
    ]
    return pl.pallas_call(
        functools.partial(place_kernel, kept, slabs),
        in_specs=[smem] + [vmem] * (SIDE * slabs),
        out_specs=vmem,
        out_shape=jax.ShapeDtypeStruct((tokens, width), BF16),
        compiler_params=limit,
        cost_estimate=light,
        name="place_columns",
    )(jnp.stack([tp_me, rank, *steps]).astype(jnp.int32), *arrived)


def solution(mesh):
    in_specs = (
        P(None, "ctx", "tp"),
        P(),
        P(None, ("tp", "ctx")),
        P(None, ("tp", "ctx")),
        P(("tp", "ctx")),
        P("tp", "ctx"),
    )
    out_specs = P("ctx", "tp")
    return jax.shard_map(
        per_device, mesh=mesh, in_specs=in_specs, out_specs=out_specs, check_vma=False
    )
```

```python
import functools

import jax
import jax.numpy as jnp
from jax import lax
from jax.experimental import pallas as pl
from jax.experimental.pallas import tpu as pltpu
from jax.sharding import PartitionSpec as P

LANES = 128
SUBLANES = 8
GROUP = LANES * SUBLANES
HALO = 2
TAPS = 3
SIDE = 2
SLAB = SIDE * SIDE
F32 = jnp.float32
BF16 = jnp.bfloat16


def spread(scratch, halo, block, pitch):
    tokens = block.shape[0]
    for tile in range(SUBLANES):
        lanes = pl.ds(tile * LANES, LANES)
        scratch[pl.ds(tile * pitch + SUBLANES - HALO, HALO), :] = halo[:, lanes].astype(F32)
        scratch[pl.ds(tile * pitch + SUBLANES, tokens), :] = block[:, lanes].astype(F32)


def token(scratch, index, pitch):
    return scratch[pl.ds(index, SUBLANES, stride=pitch), :]


def tree_sum(terms):
    while len(terms) > 1:
        terms = [a + b for a, b in zip(terms[::2], terms[1::2])] + terms[len(terms) & ~1 :]
    return terms[0]


def filter_kernel(here, features, halo, taps, u_ref, query_ref, tap_rows, *rows):
    tokens = features.shape[1]
    pitch = tokens + SUBLANES
    for tile in range(SUBLANES):
        for which in range(3):
            for j in range(TAPS):
                row = which * TAPS + j
                tap_rows[row, tile : tile + 1] = taps[which, j : j + 1, tile * LANES : (tile + 1) * LANES]
    for which in range(3):
        spread(rows[which], halo.at[which], features.at[which], pitch)
    weights = [[tap_rows[which * TAPS + j] for j in range(TAPS)] for which in range(3)]

    def step(index, carry):
        carry = list(carry)
        for inner in range(SUBLANES):
            now = index * SUBLANES + inner
            filtered = []
            for which in range(3):
                last, before = carry[which]
                fresh = token(rows[which], now + SUBLANES, pitch)
                filtered.append(
                    weights[which][0] * fresh + weights[which][1] * last + weights[which][2] * before
                )
                carry[which] = (fresh, last)
            query_ref[0, now] = filtered[0]
            u_ref[0, now] = (filtered[1] * filtered[2]).astype(BF16).astype(F32)
        return tuple(carry)

    start = tuple(
        (token(rows[which], SUBLANES - 1, pitch), token(rows[which], SUBLANES - 2, pitch))
        for which in range(3)
    )
    lax.fori_loop(0, tokens // SUBLANES, step, start)


def registers(refs, rank, wide, first, count):
    pitch = wide.shape[0] // SUBLANES
    each = SUBLANES // SLAB
    for d in range(SLAB):
        for j in range(each):
            start = pl.multiple_of(((d ^ rank) * each + j) * pitch, SUBLANES)
            rows = refs[d][0, first : first + count, j * LANES : (j + 1) * LANES]
            wide[pl.ds(start, count), :] = rows.astype(F32)
    return [wide[pl.ds(m, SUBLANES, stride=pitch), :] for m in range(count)]


def state_kernel(modes, here, u_ref, *refs):
    rates, outs, wide = refs[:SLAB], refs[SLAB : 2 * SLAB], refs[-1]
    rank = here[1]
    tokens = u_ref.shape[1]
    decay = [jnp.exp(-rate) for rate in registers(rates, rank, wide, 0, modes)]

    def step(index, states):
        for inner in range(SUBLANES):
            u = u_ref[0, index * SUBLANES + inner]
            states = tuple(states[m] * decay[m] + u for m in range(modes))
        return states

    zero = tuple(jnp.zeros((SUBLANES, LANES), F32) for _ in range(modes))
    states = lax.fori_loop(0, tokens // SUBLANES, step, zero)
    each = SUBLANES // SLAB
    pitch = wide.shape[0] // SUBLANES
    for m in range(modes):
        wide[pl.ds(m, SUBLANES, stride=pitch), :] = states[m]
    for d in range(SLAB):
        for j in range(each):
            start = pl.multiple_of(((d ^ rank) * each + j) * pitch, SUBLANES)
            outs[d][0, :, j * LANES : (j + 1) * LANES] = wide[pl.ds(start, modes), :].astype(BF16)


def slab_kernel(tokens, here, rates, *refs):
    states, out = refs[:SLAB], refs[SLAB]
    slabs = rates.shape[0]
    for g in range(slabs):
        rate = rates[lax.rem(g - here[0] + slabs, slabs), : states[0].shape[1]]
        total = None
        for d in range(SLAB):
            later = (SLAB - 1 - (here[1] ^ d)).astype(F32) * float(tokens)
            term = jnp.exp(-later * rate) * states[d][g].astype(F32)
            total = term if total is None else total + term
        out[g] = total.astype(BF16)


def incoming_kernel(tokens, here, rates, *refs):
    slabs = rates.shape[0]
    states, earlier, outs = refs[:SLAB], refs[SLAB : SLAB + slabs - 1], refs[SLAB + slabs - 1 :]
    for g in range(slabs):
        rate = rates[lax.rem(g - here[0] + slabs, slabs), : states[0].shape[1]]
        entering = earlier[0][g].astype(F32)
        for k in range(1, slabs - 1):
            entering += jnp.exp(-float(k * SLAB * tokens) * rate) * earlier[k][g].astype(F32)
        for d in range(SLAB):
            block = here[1] ^ d
            total = jnp.exp(-(block.astype(F32) * float(tokens)) * rate) * entering
            for e in range(SLAB):
                if e != d:
                    between = block - 1 - (here[1] ^ e)
                    factor = jnp.exp(-(jnp.maximum(between, 0).astype(F32) * float(tokens)) * rate)
                    factor = jnp.where(between >= 0, factor, jnp.zeros_like(factor))
                    total += factor * states[e][g].astype(F32)
            outs[d][g] = total.astype(BF16)


def local_kernel(modes, here, u_ref, *refs):
    rates, y_ref, wide = refs[:SLAB], refs[-2], refs[-1]
    tokens = u_ref.shape[1]
    rate = registers(rates, here[1], wide, 0, modes)
    rest = registers(rates, here[1], wide, modes, modes + 1)
    decay = [jnp.exp(-r) for r in rate]
    weight = [rest[m] * jnp.sqrt(2.0 * rate[m]) for m in range(modes)]
    skip = rest[modes]

    def step(index, states):
        for inner in range(SUBLANES):
            now = index * SUBLANES + inner
            u = u_ref[0, now]
            states = tuple(states[m] * decay[m] + u for m in range(modes))
            y_ref[0, now] = tree_sum([weight[m] * states[m] for m in range(modes)] + [skip * u])
        return states

    zero = tuple(jnp.zeros((SUBLANES, LANES), F32) for _ in range(modes))
    lax.fori_loop(0, tokens // SUBLANES, step, zero)


def gated_kernel(modes, here, query_ref, y_ref, *refs):
    rates, incoming = refs[:SLAB], refs[SLAB : 2 * SLAB]
    out_ref, wide, out_rows = refs[2 * SLAB :]
    tokens = query_ref.shape[1]
    pitch = tokens + SUBLANES
    rate = registers(rates, here[1], wide, 0, modes)
    rest = registers(rates, here[1], wide, modes, modes)
    state = registers(incoming, here[1], wide, 0, modes)
    decay = [jnp.exp(-r) for r in rate]
    weighted = tuple(rest[m] * jnp.sqrt(2.0 * rate[m]) * state[m] for m in range(modes))

    def step(index, weighted):
        for inner in range(SUBLANES):
            now = index * SUBLANES + inner
            weighted = tuple(weighted[m] * decay[m] for m in range(modes))
            long_out = tree_sum([y_ref[0, now], *weighted])
            long_out = long_out.astype(BF16).astype(F32)
            out_rows[pl.ds(now, SUBLANES, stride=pitch), :] = query_ref[0, now] * long_out
        return weighted

    lax.fori_loop(0, tokens // SUBLANES, step, weighted)
    for tile in range(SUBLANES):
        out_ref[:, pl.ds(tile * LANES, LANES)] = out_rows[pl.ds(tile * pitch, tokens), :].astype(BF16)


def project_kernel(count, picks, first, added, here, *refs):
    out_ref, slots, sems = refs[-3:]
    depth, share = slots.shape[1:]
    blocks, sources = refs[:-3], refs[:-3]
    runs = depth // blocks[0].shape[1]
    blocks, sources = blocks[: runs * count], sources[runs * count :]
    rows = pl.ds(first, depth)
    columns = pl.ds(pl.multiple_of(here[0] * share, share), share)
    copies = []
    for i, (which, rank) in enumerate(picks):
        source = sources[which] if rank is None else sources[which].at[here[rank]]
        copies.append(pltpu.make_async_copy(source.at[rows, columns], slots.at[i], sems.at[i]))
        copies[-1].start()
    for i in range(len(picks)):
        copies[i].wait()
        for j in range(count):
            total = sources[-1][here[0], j, i] if added else None
            for h in range(runs):
                size = depth // runs
                term = jnp.dot(
                    blocks[runs * j + h][...],
                    slots[i, h * size : (h + 1) * size],
                    preferred_element_type=F32,
                )
                total = term if total is None else total + term
            if out_ref.ndim == 4:
                out_ref[j, i] = total.astype(out_ref.dtype)
            else:
                part = out_ref.shape[-1]
                for t in range(out_ref.shape[0]):
                    out_ref[t, j, i] = total[:, t * part : (t + 1) * part].astype(out_ref.dtype)


def place_kernel(kept, steps, here, *refs):
    sources, out_ref = refs[:-1], refs[-1]
    share = sources[0].shape[2]
    tp_me, rank = here[0], here[1]
    for slot in range(kept):
        step = here[2 + slot]
        for t in range(SIDE):
            own = jnp.logical_and(step == 0, tp_me == t)
            moved = jnp.logical_and(step == 0, tp_me != t)
            choices = [(own, sources[0]), (moved, sources[1])]
            choices += [(step == k, sources[2 * k + t]) for k in range(1, steps)]
            for chosen, source in choices:

                @pl.when(chosen)
                def _(source=source, slot=slot, t=t):
                    for piece in range(SLAB):
                        start = ((slot * SLAB + (rank ^ piece)) * SIDE + t) * share
                        out_ref[:, pl.ds(pl.multiple_of(start, share), share)] = source[piece]


def ring_order(count):
    return [0] + list(range(1, count, 2)) + [i for i in range(count - 1, 0, -1) if i % 2 == 0]


def any_size(features, conv_weight, decay_rates, residues, skip_gain, out_weight):
    tokens, width = features.shape[1:]
    ctx, tp = lax.axis_size("ctx"), lax.axis_size("tp")
    me, tp_me = lax.axis_index("ctx"), lax.axis_index("tp")
    halo = lax.ppermute(features[:, tokens - HALO :], "ctx", [(i, i + 1) for i in range(ctx - 1)])
    extended = jnp.concatenate([halo, features], axis=1).astype(F32)
    taps = lax.dynamic_slice_in_dim(conv_weight, tp_me * width, width, 2)
    filtered = sum(taps[:, j, None] * extended[:, HALO - j : HALO - j + tokens] for j in range(TAPS))
    u = (filtered[1] * filtered[2]).astype(BF16).astype(F32)
    rates, weights, skip = (
        lax.all_gather(a, "ctx", axis=a.ndim - 1, tiled=True) for a in (decay_rates, residues, skip_gain)
    )
    weights = weights * jnp.sqrt(2.0 * rates)
    decay = jnp.exp(-rates)
    zero = jnp.zeros(rates.shape, F32)
    left = lax.fori_loop(0, tokens, lambda t, s: s * decay + u[t], zero)
    lefts = lax.all_gather(left, "ctx")
    block_decay = jnp.exp(-float(tokens) * rates)
    entering = lax.fori_loop(0, me, lambda b, s: s * block_decay + lefts[b], zero)

    def advance(states, now):
        states = states * decay + now
        return states, jnp.sum(weights * states, axis=0) + skip * now

    long_out = lax.scan(advance, entering, u)[1].astype(BF16).astype(F32)
    gated = (filtered[0] * long_out).astype(BF16)
    whole = lax.all_gather(gated, "ctx", axis=0, tiled=True)
    partial = jnp.dot(whole, out_weight, preferred_element_type=F32).astype(BF16)
    share = partial.shape[1] // tp
    partial = partial.reshape(ctx * tokens, tp, share).transpose(1, 0, 2)
    partial = lax.all_to_all(partial, "tp", split_axis=0, concat_axis=0, tiled=True)
    summed = jnp.sum(partial.astype(F32), axis=0).astype(BF16).reshape(ctx, tokens, share)
    summed = lax.all_to_all(summed, "ctx", split_axis=0, concat_axis=0, tiled=True)
    placed = lax.all_to_all(
        summed.reshape(tp, ctx // tp, tokens, share), "tp", split_axis=0, concat_axis=0, tiled=True
    )
    return placed.transpose(2, 1, 0, 3).reshape(tokens, width)


def per_device(features, conv_weight, decay_rates, residues, skip_gain, out_weight):
    tokens, width = features.shape[1:]
    modes, owned = decay_rates.shape
    ctx, tp = lax.axis_size("ctx"), lax.axis_size("tp")
    depth, columns = out_weight.shape
    share = columns // tp
    if owned * SLAB != GROUP or tp != SIDE or share % LANES or ctx // SLAB < 3:
        return any_size(features, conv_weight, decay_rates, residues, skip_gain, out_weight)
    slabs = ctx // SLAB
    groups = width // GROUP
    me, tp_me = lax.axis_index("ctx"), lax.axis_index("tp")
    z_me, rank = me // SLAB, me % SLAB
    order = ring_order(slabs)
    place = [order.index(z) for z in range(slabs)]
    here = jnp.stack([z_me, rank, tp_me]).astype(jnp.int32)

    def within_slab(array, mask):
        return lax.ppermute(array, "ctx", [(i, i ^ mask) for i in range(ctx)])

    def from_slab(array, by):
        return lax.ppermute(array, "ctx", [(i, (i - by * SLAB) % ctx) for i in range(ctx)])

    def ring(array):
        pairs = []
        for i in range(ctx):
            z, rest = divmod(i, SLAB)
            pairs.append((i, order[(place[z] + 1) % slabs] * SLAB + rest))
        return lax.ppermute(array, "ctx", pairs)

    halo = lax.ppermute(
        features[:, tokens - HALO :, :], "ctx", [(i, i + 1) for i in range(ctx - 1)]
    )
    rows = jnp.concatenate([decay_rates, residues, skip_gain[None]], axis=0)
    rows = jnp.stack([rows] + [from_slab(rows, by) for by in range(1, slabs)])
    rows, halo = lax.optimization_barrier((rows, halo))
    rates = [rows, within_slab(rows, 1), within_slab(rows, 2)]

    beside = within_slab(out_weight, 1)
    slab_weights = lax.all_gather(
        out_weight,
        "ctx",
        axis_index_groups=[list(range(z * SLAB, (z + 1) * SLAB)) for z in range(slabs)],
    )

    limit = pltpu.CompilerParams(vmem_limit_bytes=16 * 1024 * 1024)
    large = pltpu.CompilerParams(vmem_limit_bytes=48 * 1024 * 1024)
    light = pl.CostEstimate(flops=1, bytes_accessed=1, transcendentals=0)
    series_shape = jax.ShapeDtypeStruct((groups, tokens, SUBLANES, LANES), F32)
    state_shape = jax.ShapeDtypeStruct((groups, modes, owned), BF16)
    scratch_rows = pltpu.VMEM((SUBLANES * (tokens + SUBLANES), LANES), F32)
    wide = pltpu.VMEM((SUBLANES * (modes + SUBLANES), LANES), F32)
    series = pl.BlockSpec((1, tokens, SUBLANES, LANES), lambda g, here: (g, 0, 0, 0))
    state_spec = pl.BlockSpec((1, modes, owned), lambda g, here: (g, 0, 0))
    rate_spec = pl.BlockSpec(
        (1, 2 * modes + 1, owned), lambda g, here: (lax.rem(g - here[0] + slabs, slabs), 0, 0)
    )

    def grouped(kernel, name, in_specs, out_specs, out_shape, scratch, groups=groups):
        return pl.pallas_call(
            kernel,
            grid_spec=pltpu.PrefetchScalarGridSpec(
                num_scalar_prefetch=1,
                grid=(groups,),
                in_specs=in_specs,
                out_specs=out_specs,
                scratch_shapes=scratch,
            ),
            out_shape=out_shape,
            compiler_params=limit,
            cost_estimate=light,
            name=name,
        )

    u, query = grouped(
        filter_kernel,
        "short_filters",
        [
            pl.BlockSpec((3, tokens, GROUP), lambda g, here: (0, 0, g)),
            pl.BlockSpec((3, HALO, GROUP), lambda g, here: (0, 0, g)),
            pl.BlockSpec((3, TAPS, GROUP), lambda g, here: (0, 0, here[2] * groups + g)),
        ],
        [series, series],
        [series_shape, series_shape],
        [pltpu.VMEM((3 * TAPS, SUBLANES, LANES), F32), scratch_rows, scratch_rows, scratch_rows],
    )(here, features, halo, conv_weight)

    passed, u = lax.optimization_barrier((rates[2], u))
    rates.append(within_slab(passed, 1))

    left = grouped(
        functools.partial(state_kernel, modes),
        "block_states",
        [series] + [rate_spec] * SLAB,
        [state_spec] * SLAB,
        [state_shape] * SLAB,
        [wide],
    )(here, u, *rates)
    left = [left[0]] + [within_slab(left[d], d) for d in range(1, SLAB)]

    smem = pl.BlockSpec(memory_space=pltpu.SMEM)
    vmem = pl.BlockSpec(memory_space=pltpu.VMEM)
    slab_left = pl.pallas_call(
        functools.partial(slab_kernel, tokens),
        in_specs=[smem] + [vmem] * (1 + SLAB),
        out_specs=vmem,
        out_shape=state_shape,
        compiler_params=limit,
        cost_estimate=light,
        name="slab_states",
    )(here, rates[0], *left)
    earlier = [
        lax.ppermute(slab_left, "ctx", [(i, i + by * SLAB) for i in range(ctx - by * SLAB)])
        for by in range(1, slabs)
    ]

    local = grouped(
        functools.partial(local_kernel, modes),
        "local_convolution",
        [series] + [rate_spec] * SLAB,
        series,
        series_shape,
        [wide],
    )(here, u, *rates)
    earlier, local = lax.optimization_barrier((earlier, local))

    incoming = pl.pallas_call(
        functools.partial(incoming_kernel, tokens),
        in_specs=[smem] + [vmem] * (SLAB + slabs),
        out_specs=[vmem] * SLAB,
        out_shape=[state_shape] * SLAB,
        compiler_params=limit,
        cost_estimate=light,
        name="incoming_states",
    )(here, rates[0], *left, *earlier)
    incoming = [incoming[0]] + [within_slab(incoming[d], d) for d in range(1, SLAB)]

    def gated_half(half):
        count = groups // SIDE
        first = half * count

        def shifted(spec):
            return pl.BlockSpec(spec.block_shape, lambda g, here: spec.index_map(g + first, here))

        return grouped(
            functools.partial(gated_kernel, modes),
            "gated_block",
            [shifted(s) for s in [series] * 2 + [rate_spec] * SLAB + [state_spec] * SLAB],
            pl.BlockSpec((tokens, GROUP), lambda g, here: (0, g)),
            jax.ShapeDtypeStruct((tokens, width // SIDE), BF16),
            [wide, scratch_rows],
            count,
        )(here, query, local, *rates, *incoming)

    def project(blocks, sources, picks, share_index, partial=None, halves=(0, 1)):
        scalars = jnp.stack([share_index if share_index is not None else 0, rank ^ 2, rank ^ 3])
        run = depth // SIDE
        wide_share = columns if share_index is None else share
        shape = (len(blocks), len(picks), tokens, share)
        if share_index is None:
            out = jax.ShapeDtypeStruct((tp, *shape), F32)
        else:
            out = jax.ShapeDtypeStruct(shape, BF16)
        return pl.pallas_call(
            functools.partial(
                project_kernel, len(blocks), picks, halves[0] * run, partial is not None
            ),
            in_specs=[smem]
            + [vmem] * (len(halves) * len(blocks))
            + [pl.BlockSpec(memory_space=pltpu.HBM)] * len(sources)
            + ([vmem] if partial is not None else []),
            out_specs=vmem,
            out_shape=out,
            scratch_shapes=[
                pltpu.VMEM((len(picks), len(halves) * run, wide_share), BF16),
                pltpu.SemaphoreType.DMA((len(picks),)),
            ],
            compiler_params=large,
            cost_estimate=light,
            name="project_block",
        )(
            scalars.astype(jnp.int32),
            *[b[h] for b in blocks for h in halves],
            *sources,
            *([partial] if partial is not None else []),
        )

    def project_away(blocks, sources, picks):
        away = project(blocks, sources, picks, 1 - tp_me)
        return away, lax.ppermute(away, "tp", [(0, 1), (1, 0)])

    def project_mine(blocks, sources, picks, after):
        blocks, _ = lax.optimization_barrier((blocks, after))
        return project(blocks, sources, picks, tp_me)

    def total(mine, got):
        return (mine.astype(F32) + got.astype(F32)).astype(BF16)

    half_of = [z * tp // slabs for z in range(slabs)]

    def deliver(summed, by):
        pairs = [[], []]
        for i in range(ctx):
            z, rest = divmod(i, SLAB)
            target = order[(place[z] - by) % slabs] * SLAB + rest
            for t in range(tp):
                pairs[t].append((i * tp + t, target * tp + half_of[z]))
        if by == 0:
            moves = [p for p in pairs[0] + pairs[1] if p[0] != p[1]]
            return [summed, lax.ppermute(summed, ("ctx", "tp"), moves)]
        return [lax.ppermute(summed, ("ctx", "tp"), moves) for moves in pairs]

    near, far, both = (
        ((0, None), (1, None)),
        ((0, 1), (0, 2)),
        ((0, None), (1, None), (2, 1), (2, 2)),
    )
    near, far, both = (
        ((0, None), (1, None)),
        ((0, 1), (0, 2)),
        ((0, None), (1, None), (2, 1), (2, 2)),
    )
    blocks = [[gated_half(h) for h in range(SIDE)]]
    kept_parts, got_parts = [], []
    mine, got = None, None
    for step in range(slabs - 1):
        first, second = block = blocks[step]
        if step:
            second, mine = lax.optimization_barrier((second, mine))
            block, _ = lax.optimization_barrier((block, mine))
        blocks.append([ring(first), ring(second)])
        away, coming = project_away([block], [out_weight, beside], near)
        mine = project_mine([block], [out_weight, beside], near, (away, got))
        got = coming
        kept_parts.append(mine)
        got_parts.append(got)
    slab_weights, _ = lax.optimization_barrier((slab_weights, mine))
    away, batch_got = project_away(blocks[: slabs - 1], [slab_weights], far)
    sources = [out_weight, beside, slab_weights]
    head, _ = lax.optimization_barrier((blocks[-1][0], away))
    partial = project([[head]], sources, both, None, None, (0,))
    tail = blocks[-1][1]
    last_away = project([[None, tail]], sources, both, 1 - tp_me, partial, (1,))
    last_got = lax.ppermute(last_away, "tp", [(0, 1), (1, 0)])
    batch_mine = project_mine(blocks[: slabs - 1], [slab_weights], far, (last_away, got))
    batch_got, got_parts, _ = lax.optimization_barrier((batch_got, got_parts, last_away))
    batch = total(batch_mine, batch_got)
    arrived = []
    for step in range(slabs - 1):
        summed = total(kept_parts[step], got_parts[step])[0]
        arrived += deliver(jnp.concatenate([summed, batch[step]]), step)
    tail, _ = lax.optimization_barrier((tail, (batch_mine, arrived[2])))
    last_mine = project([[None, tail]], sources, both, tp_me, partial, (1,))
    arrived += deliver(total(last_mine, last_got)[0], slabs - 1)

    def place_of(z):
        return sum(jnp.where(z == k, place[k], 0) for k in range(slabs))

    kept = slabs // tp
    steps = [
        lax.rem(place_of(tp_me * kept + j) - place_of(z_me) + slabs, slabs) for j in range(kept)
    ]
    return pl.pallas_call(
        functools.partial(place_kernel, kept, slabs),
        in_specs=[smem] + [vmem] * (SIDE * slabs),
        out_specs=vmem,
        out_shape=jax.ShapeDtypeStruct((tokens, width), BF16),
        compiler_params=limit,
        cost_estimate=light,
        name="place_columns",
    )(jnp.stack([tp_me, rank, *steps]).astype(jnp.int32), *arrived)


def solution(mesh):
    in_specs = (
        P(None, "ctx", "tp"),
        P(),
        P(None, ("tp", "ctx")),
        P(None, ("tp", "ctx")),
        P(("tp", "ctx")),
        P("tp", "ctx"),
    )
    out_specs = P("ctx", "tp")
    return jax.shard_map(
        per_device, mesh=mesh, in_specs=in_specs, out_specs=out_specs, check_vma=False
    )
```

```python
import functools

import jax
import jax.numpy as jnp
from jax import lax
from jax.experimental import pallas as pl
from jax.experimental.pallas import tpu as pltpu
from jax.sharding import PartitionSpec as P

LANES = 128
SUBLANES = 8
GROUP = LANES * SUBLANES
HALO = 2
TAPS = 3
SIDE = 2
SLAB = SIDE * SIDE
F32 = jnp.float32
BF16 = jnp.bfloat16


def spread(scratch, halo, block, pitch):
    tokens = block.shape[0]
    for tile in range(SUBLANES):
        lanes = pl.ds(tile * LANES, LANES)
        scratch[pl.ds(tile * pitch + SUBLANES - HALO, HALO), :] = halo[:, lanes].astype(F32)
        scratch[pl.ds(tile * pitch + SUBLANES, tokens), :] = block[:, lanes].astype(F32)


def token(scratch, index, pitch):
    return scratch[pl.ds(index, SUBLANES, stride=pitch), :]


def tree_sum(terms):
    while len(terms) > 1:
        terms = [a + b for a, b in zip(terms[::2], terms[1::2])] + terms[len(terms) & ~1 :]
    return terms[0]


def filter_kernel(here, features, halo, taps, u_ref, query_ref, tap_rows, *rows):
    tokens = features.shape[1]
    pitch = tokens + SUBLANES
    for tile in range(SUBLANES):
        for which in range(3):
            for j in range(TAPS):
                row = which * TAPS + j
                tap_rows[row, tile : tile + 1] = taps[which, j : j + 1, tile * LANES : (tile + 1) * LANES]
    for which in range(3):
        spread(rows[which], halo.at[which], features.at[which], pitch)
    weights = [[tap_rows[which * TAPS + j] for j in range(TAPS)] for which in range(3)]

    def step(index, carry):
        carry = list(carry)
        for inner in range(SUBLANES):
            now = index * SUBLANES + inner
            filtered = []
            for which in range(3):
                last, before = carry[which]
                fresh = token(rows[which], now + SUBLANES, pitch)
                filtered.append(
                    weights[which][0] * fresh + weights[which][1] * last + weights[which][2] * before
                )
                carry[which] = (fresh, last)
            query_ref[0, now] = filtered[0]
            u_ref[0, now] = (filtered[1] * filtered[2]).astype(BF16).astype(F32)
        return tuple(carry)

    start = tuple(
        (token(rows[which], SUBLANES - 1, pitch), token(rows[which], SUBLANES - 2, pitch))
        for which in range(3)
    )
    lax.fori_loop(0, tokens // SUBLANES, step, start)


def registers(refs, rank, wide, first, count):
    pitch = wide.shape[0] // SUBLANES
    each = SUBLANES // SLAB
    for d in range(SLAB):
        for j in range(each):
            start = pl.multiple_of(((d ^ rank) * each + j) * pitch, SUBLANES)
            rows = refs[d][0, first : first + count, j * LANES : (j + 1) * LANES]
            wide[pl.ds(start, count), :] = rows.astype(F32)
    return [wide[pl.ds(m, SUBLANES, stride=pitch), :] for m in range(count)]


def state_kernel(modes, here, u_ref, *refs):
    rates, outs, wide = refs[:SLAB], refs[SLAB : 2 * SLAB], refs[-1]
    rank = here[1]
    tokens = u_ref.shape[1]
    decay = [jnp.exp(-rate) for rate in registers(rates, rank, wide, 0, modes)]

    def step(index, states):
        for inner in range(SUBLANES):
            u = u_ref[0, index * SUBLANES + inner]
            states = tuple(states[m] * decay[m] + u for m in range(modes))
        return states

    zero = tuple(jnp.zeros((SUBLANES, LANES), F32) for _ in range(modes))
    states = lax.fori_loop(0, tokens // SUBLANES, step, zero)
    each = SUBLANES // SLAB
    pitch = wide.shape[0] // SUBLANES
    for m in range(modes):
        wide[pl.ds(m, SUBLANES, stride=pitch), :] = states[m]
    for d in range(SLAB):
        for j in range(each):
            start = pl.multiple_of(((d ^ rank) * each + j) * pitch, SUBLANES)
            outs[d][0, :, j * LANES : (j + 1) * LANES] = wide[pl.ds(start, modes), :].astype(BF16)


def slab_kernel(tokens, here, rates, *refs):
    states, out = refs[:SLAB], refs[SLAB]
    slabs = rates.shape[0]
    for g in range(slabs):
        rate = rates[lax.rem(g - here[0] + slabs, slabs), : states[0].shape[1]]
        total = None
        for d in range(SLAB):
            later = (SLAB - 1 - (here[1] ^ d)).astype(F32) * float(tokens)
            term = jnp.exp(-later * rate) * states[d][g].astype(F32)
            total = term if total is None else total + term
        out[g] = total.astype(BF16)


def incoming_kernel(tokens, here, rates, *refs):
    slabs = rates.shape[0]
    states, earlier, outs = refs[:SLAB], refs[SLAB : SLAB + slabs - 1], refs[SLAB + slabs - 1 :]
    for g in range(slabs):
        rate = rates[lax.rem(g - here[0] + slabs, slabs), : states[0].shape[1]]
        entering = jnp.zeros(rate.shape, F32)
        for k in range(slabs - 1):
            term = jnp.exp(-float(k * SLAB * tokens) * rate) * earlier[k][g].astype(F32)
            entering += jnp.where(here[0] > k, term, jnp.zeros_like(term))
        for d in range(SLAB):
            block = here[1] ^ d
            total = jnp.exp(-(block.astype(F32) * float(tokens)) * rate) * entering
            for e in range(SLAB):
                if e != d:
                    between = block - 1 - (here[1] ^ e)
                    factor = jnp.exp(-(jnp.maximum(between, 0).astype(F32) * float(tokens)) * rate)
                    factor = jnp.where(between >= 0, factor, jnp.zeros_like(factor))
                    total += factor * states[e][g].astype(F32)
            outs[d][g] = total.astype(BF16)


def local_kernel(modes, here, u_ref, *refs):
    rates, y_ref, wide = refs[:SLAB], refs[-2], refs[-1]
    tokens = u_ref.shape[1]
    rate = registers(rates, here[1], wide, 0, modes)
    rest = registers(rates, here[1], wide, modes, modes + 1)
    decay = [jnp.exp(-r) for r in rate]
    weight = [rest[m] * jnp.sqrt(2.0 * rate[m]) for m in range(modes)]
    skip = rest[modes]

    def step(index, states):
        for inner in range(SUBLANES):
            now = index * SUBLANES + inner
            u = u_ref[0, now]
            states = tuple(states[m] * decay[m] + u for m in range(modes))
            y_ref[0, now] = tree_sum([weight[m] * states[m] for m in range(modes)] + [skip * u])
        return states

    zero = tuple(jnp.zeros((SUBLANES, LANES), F32) for _ in range(modes))
    lax.fori_loop(0, tokens // SUBLANES, step, zero)


def gated_kernel(modes, here, query_ref, y_ref, *refs):
    rates, incoming = refs[:SLAB], refs[SLAB : 2 * SLAB]
    out_ref, wide, out_rows = refs[2 * SLAB :]
    tokens = query_ref.shape[1]
    pitch = tokens + SUBLANES
    rate = registers(rates, here[1], wide, 0, modes)
    rest = registers(rates, here[1], wide, modes, modes)
    state = registers(incoming, here[1], wide, 0, modes)
    decay = [jnp.exp(-r) for r in rate]
    weighted = tuple(rest[m] * jnp.sqrt(2.0 * rate[m]) * state[m] for m in range(modes))

    def step(index, weighted):
        for inner in range(SUBLANES):
            now = index * SUBLANES + inner
            weighted = tuple(weighted[m] * decay[m] for m in range(modes))
            long_out = tree_sum([y_ref[0, now], *weighted])
            long_out = long_out.astype(BF16).astype(F32)
            out_rows[pl.ds(now, SUBLANES, stride=pitch), :] = query_ref[0, now] * long_out
        return weighted

    lax.fori_loop(0, tokens // SUBLANES, step, weighted)
    for tile in range(SUBLANES):
        out_ref[:, pl.ds(tile * LANES, LANES)] = out_rows[pl.ds(tile * pitch, tokens), :].astype(BF16)


def project_kernel(count, picks, first, added, here, *refs):
    out_ref, slots, sems = refs[-3:]
    depth, share = slots.shape[1:]
    blocks, sources = refs[:-3], refs[:-3]
    runs = depth // blocks[0].shape[1]
    blocks, sources = blocks[: runs * count], sources[runs * count :]
    rows = pl.ds(first, depth)
    columns = pl.ds(pl.multiple_of(here[0] * share, share), share)
    copies = []
    for i, (which, rank) in enumerate(picks):
        source = sources[which] if rank is None else sources[which].at[here[rank]]
        copies.append(pltpu.make_async_copy(source.at[rows, columns], slots.at[i], sems.at[i]))
        copies[-1].start()
    for i in range(len(picks)):
        copies[i].wait()
        for j in range(count):
            total = sources[-1][here[0], j, i] if added else None
            for h in range(runs):
                size = depth // runs
                term = jnp.dot(
                    blocks[runs * j + h][...],
                    slots[i, h * size : (h + 1) * size],
                    preferred_element_type=F32,
                )
                total = term if total is None else total + term
            if out_ref.ndim == 4:
                out_ref[j, i] = total.astype(out_ref.dtype)
            else:
                part = out_ref.shape[-1]
                for t in range(out_ref.shape[0]):
                    out_ref[t, j, i] = total[:, t * part : (t + 1) * part].astype(out_ref.dtype)


def place_kernel(kept, counts, here, *refs):
    out_ref = refs[-1]
    share = refs[0].shape[2]
    rank = here[0]
    starts = [sum(counts[:k]) for k in range(len(counts))]
    for slot in range(kept):
        for t in range(SIDE):
            for k, count in enumerate(counts):

                @pl.when(here[1 + slot * SIDE + t] == k)
                def _(slot=slot, t=t, k=k, count=count):
                    for piece in range(SLAB):
                        each = SLAB // count
                        source = refs[starts[k] + piece // each]
                        start = ((slot * SLAB + (rank ^ piece)) * SIDE + t) * share
                        out_ref[:, pl.ds(pl.multiple_of(start, share), share)] = source[piece % each]


def ring_order(count):
    return [0] + list(range(1, count, 2)) + [i for i in range(count - 1, 0, -1) if i % 2 == 0]


def any_size(features, conv_weight, decay_rates, residues, skip_gain, out_weight):
    tokens, width = features.shape[1:]
    ctx, tp = lax.axis_size("ctx"), lax.axis_size("tp")
    me, tp_me = lax.axis_index("ctx"), lax.axis_index("tp")
    halo = lax.ppermute(features[:, tokens - HALO :], "ctx", [(i, i + 1) for i in range(ctx - 1)])
    extended = jnp.concatenate([halo, features], axis=1).astype(F32)
    taps = lax.dynamic_slice_in_dim(conv_weight, tp_me * width, width, 2)
    filtered = sum(taps[:, j, None] * extended[:, HALO - j : HALO - j + tokens] for j in range(TAPS))
    u = (filtered[1] * filtered[2]).astype(BF16).astype(F32)
    rates, weights, skip = (
        lax.all_gather(a, "ctx", axis=a.ndim - 1, tiled=True) for a in (decay_rates, residues, skip_gain)
    )
    weights = weights * jnp.sqrt(2.0 * rates)
    decay = jnp.exp(-rates)
    zero = jnp.zeros(rates.shape, F32)
    left = lax.fori_loop(0, tokens, lambda t, s: s * decay + u[t], zero)
    lefts = lax.all_gather(left, "ctx")
    block_decay = jnp.exp(-float(tokens) * rates)
    entering = lax.fori_loop(0, me, lambda b, s: s * block_decay + lefts[b], zero)

    def advance(states, now):
        states = states * decay + now
        return states, jnp.sum(weights * states, axis=0) + skip * now

    long_out = lax.scan(advance, entering, u)[1].astype(BF16).astype(F32)
    gated = (filtered[0] * long_out).astype(BF16)
    whole = lax.all_gather(gated, "ctx", axis=0, tiled=True)
    partial = jnp.dot(whole, out_weight, preferred_element_type=F32).astype(BF16)
    share = partial.shape[1] // tp
    partial = partial.reshape(ctx * tokens, tp, share).transpose(1, 0, 2)
    partial = lax.all_to_all(partial, "tp", split_axis=0, concat_axis=0, tiled=True)
    summed = jnp.sum(partial.astype(F32), axis=0).astype(BF16).reshape(ctx, tokens, share)
    summed = lax.all_to_all(summed, "ctx", split_axis=0, concat_axis=0, tiled=True)
    placed = lax.all_to_all(
        summed.reshape(tp, ctx // tp, tokens, share), "tp", split_axis=0, concat_axis=0, tiled=True
    )
    return placed.transpose(2, 1, 0, 3).reshape(tokens, width)


def per_device(features, conv_weight, decay_rates, residues, skip_gain, out_weight):
    tokens, width = features.shape[1:]
    modes, owned = decay_rates.shape
    ctx, tp = lax.axis_size("ctx"), lax.axis_size("tp")
    depth, columns = out_weight.shape
    share = columns // tp
    if owned * SLAB != GROUP or tp != SIDE or share % LANES or ctx // SLAB < 4 or ctx // SLAB % 2:
        return any_size(features, conv_weight, decay_rates, residues, skip_gain, out_weight)
    slabs = ctx // SLAB
    groups = width // GROUP
    me, tp_me = lax.axis_index("ctx"), lax.axis_index("tp")
    z_me, rank = me // SLAB, me % SLAB
    order = ring_order(slabs)
    place = [order.index(z) for z in range(slabs)]
    here = jnp.stack([z_me, rank, tp_me]).astype(jnp.int32)

    def within_slab(array, mask):
        return lax.ppermute(array, "ctx", [(i, i ^ mask) for i in range(ctx)])

    def from_slab(array, by):
        return lax.ppermute(array, "ctx", [(i, (i - by * SLAB) % ctx) for i in range(ctx)])

    def ring(array):
        pairs = []
        for i in range(ctx):
            z, rest = divmod(i, SLAB)
            pairs.append((i, order[(place[z] + 1) % slabs] * SLAB + rest))
        return lax.ppermute(array, "ctx", pairs)

    halo = lax.ppermute(
        features[:, tokens - HALO :, :], "ctx", [(i, i + 1) for i in range(ctx - 1)]
    )
    rows = jnp.concatenate([decay_rates, residues, skip_gain[None]], axis=0)
    rows = jnp.stack([rows] + [from_slab(rows, by) for by in range(1, slabs)])
    rows, halo = lax.optimization_barrier((rows, halo))
    rates = [rows, within_slab(rows, 1), within_slab(rows, 2)]

    beside = within_slab(out_weight, 1)
    slab_weights = lax.all_gather(
        out_weight,
        "ctx",
        axis_index_groups=[list(range(z * SLAB, (z + 1) * SLAB)) for z in range(slabs)],
    )

    limit = pltpu.CompilerParams(vmem_limit_bytes=16 * 1024 * 1024)
    large = pltpu.CompilerParams(vmem_limit_bytes=48 * 1024 * 1024)
    light = pl.CostEstimate(flops=1, bytes_accessed=1, transcendentals=0)
    series_shape = jax.ShapeDtypeStruct((groups, tokens, SUBLANES, LANES), F32)
    state_shape = jax.ShapeDtypeStruct((groups, modes, owned), BF16)
    scratch_rows = pltpu.VMEM((SUBLANES * (tokens + SUBLANES), LANES), F32)
    wide = pltpu.VMEM((SUBLANES * (modes + SUBLANES), LANES), F32)
    series = pl.BlockSpec((1, tokens, SUBLANES, LANES), lambda g, here: (g, 0, 0, 0))
    state_spec = pl.BlockSpec((1, modes, owned), lambda g, here: (g, 0, 0))
    rate_spec = pl.BlockSpec(
        (1, 2 * modes + 1, owned), lambda g, here: (lax.rem(g - here[0] + slabs, slabs), 0, 0)
    )

    def grouped(kernel, name, in_specs, out_specs, out_shape, scratch, groups=groups):
        return pl.pallas_call(
            kernel,
            grid_spec=pltpu.PrefetchScalarGridSpec(
                num_scalar_prefetch=1,
                grid=(groups,),
                in_specs=in_specs,
                out_specs=out_specs,
                scratch_shapes=scratch,
            ),
            out_shape=out_shape,
            compiler_params=limit,
            cost_estimate=light,
            name=name,
        )

    u, query = grouped(
        filter_kernel,
        "short_filters",
        [
            pl.BlockSpec((3, tokens, GROUP), lambda g, here: (0, 0, g)),
            pl.BlockSpec((3, HALO, GROUP), lambda g, here: (0, 0, g)),
            pl.BlockSpec((3, TAPS, GROUP), lambda g, here: (0, 0, here[2] * groups + g)),
        ],
        [series, series],
        [series_shape, series_shape],
        [pltpu.VMEM((3 * TAPS, SUBLANES, LANES), F32), scratch_rows, scratch_rows, scratch_rows],
    )(here, features, halo, conv_weight)

    passed, u = lax.optimization_barrier((rates[2], u))
    rates.append(within_slab(passed, 1))

    left = grouped(
        functools.partial(state_kernel, modes),
        "block_states",
        [series] + [rate_spec] * SLAB,
        [state_spec] * SLAB,
        [state_shape] * SLAB,
        [wide],
    )(here, u, *rates)
    left = [left[0]] + [within_slab(left[d], d) for d in range(1, SLAB)]

    local = grouped(
        functools.partial(local_kernel, modes),
        "local_convolution",
        [series] + [rate_spec] * SLAB,
        series,
        series_shape,
        [wide],
    )(here, u, *rates)
    left, local = lax.optimization_barrier((left, local))

    smem = pl.BlockSpec(memory_space=pltpu.SMEM)
    vmem = pl.BlockSpec(memory_space=pltpu.VMEM)
    slab_left = pl.pallas_call(
        functools.partial(slab_kernel, tokens),
        in_specs=[smem] + [vmem] * (1 + SLAB),
        out_specs=vmem,
        out_shape=state_shape,
        compiler_params=limit,
        cost_estimate=light,
        name="slab_states",
    )(here, rates[0], *left)
    earlier = [from_slab(slab_left, -by) for by in range(1, slabs)]

    incoming = pl.pallas_call(
        functools.partial(incoming_kernel, tokens),
        in_specs=[smem] + [vmem] * (SLAB + slabs),
        out_specs=[vmem] * SLAB,
        out_shape=[state_shape] * SLAB,
        compiler_params=limit,
        cost_estimate=light,
        name="incoming_states",
    )(here, rates[0], *left, *earlier)
    incoming = [incoming[0]] + [within_slab(incoming[d], d) for d in range(1, SLAB)]

    def gated_half(half):
        count = groups // SIDE
        first = half * count

        def shifted(spec):
            return pl.BlockSpec(spec.block_shape, lambda g, here: spec.index_map(g + first, here))

        return grouped(
            functools.partial(gated_kernel, modes),
            "gated_block",
            [shifted(s) for s in [series] * 2 + [rate_spec] * SLAB + [state_spec] * SLAB],
            pl.BlockSpec((tokens, GROUP), lambda g, here: (0, g)),
            jax.ShapeDtypeStruct((tokens, width // SIDE), BF16),
            [wide, scratch_rows],
            count,
        )(here, query, local, *rates, *incoming)

    def project(blocks, sources, picks, share_index, partial=None, halves=(0, 1)):
        scalars = jnp.stack([share_index if share_index is not None else 0, rank ^ 2, rank ^ 3])
        run = depth // SIDE
        wide_share = columns if share_index is None else share
        shape = (len(blocks), len(picks), tokens, share)
        if share_index is None:
            out = jax.ShapeDtypeStruct((tp, *shape), F32)
        else:
            out = jax.ShapeDtypeStruct(shape, BF16)
        return pl.pallas_call(
            functools.partial(
                project_kernel, len(blocks), picks, halves[0] * run, partial is not None
            ),
            in_specs=[smem]
            + [vmem] * (len(halves) * len(blocks))
            + [pl.BlockSpec(memory_space=pltpu.HBM)] * len(sources)
            + ([vmem] if partial is not None else []),
            out_specs=vmem,
            out_shape=out,
            scratch_shapes=[
                pltpu.VMEM((len(picks), len(halves) * run, wide_share), BF16),
                pltpu.SemaphoreType.DMA((len(picks),)),
            ],
            compiler_params=large,
            cost_estimate=light,
            name="project_block",
        )(
            scalars.astype(jnp.int32),
            *[b[h] for b in blocks for h in halves],
            *sources,
            *([partial] if partial is not None else []),
        )

    def project_away(blocks, sources, picks):
        away = project(blocks, sources, picks, 1 - tp_me)
        return away, lax.ppermute(away, "tp", [(0, 1), (1, 0)])

    def project_mine(blocks, sources, picks, after):
        blocks, _ = lax.optimization_barrier((blocks, after))
        return project(blocks, sources, picks, tp_me)

    def total(mine, got):
        return (mine.astype(F32) + got.astype(F32)).astype(BF16)

    half_of = [z * tp // slabs for z in range(slabs)]

    def deliver(classes, by):
        pairs = []
        for i in range(ctx):
            z, rest = divmod(i, SLAB)
            for t in range(tp):
                target = order[(place[z] - by - t * slabs // tp) % slabs] * SLAB + rest
                pairs.append((i * tp + t, target * tp + half_of[z]))
        moved = jnp.where(tp_me == 0, classes[by], classes[(by + slabs // tp) % slabs])
        return lax.ppermute(moved, ("ctx", "tp"), pairs)

    near, far, both = (
        ((0, None), (1, None)),
        ((0, 1), (0, 2)),
        ((0, None), (1, None), (2, 1), (2, 2)),
    )
    near, far, both = (
        ((0, None), (1, None)),
        ((0, 1), (0, 2)),
        ((0, None), (1, None), (2, 1), (2, 2)),
    )
    blocks = [[gated_half(h) for h in range(SIDE)]]
    kept_parts, got_parts = [], []
    mine, got = None, None
    for step in range(slabs - 1):
        first, second = block = blocks[step]
        if step:
            second, mine = lax.optimization_barrier((second, mine))
            block, _ = lax.optimization_barrier((block, mine))
        blocks.append([ring(first), ring(second)])
        away, coming = project_away([block], [out_weight, beside], near)
        mine = project_mine([block], [out_weight, beside], near, (away, got))
        got = coming
        kept_parts.append(mine)
        got_parts.append(got)
    slab_weights, _ = lax.optimization_barrier((slab_weights, mine))
    away, batch_got = project_away(blocks[: slabs - 1], [slab_weights], far)
    batch_mine = project_mine(blocks[: slabs - 1], [slab_weights], far, away)
    sources = [out_weight, beside, slab_weights]
    head, _ = lax.optimization_barrier((blocks[-1][0], batch_mine))
    partial = project([[head]], sources, both, None, None, (0,))
    tail = blocks[-1][1]
    last_away = project([[None, tail]], sources, both, 1 - tp_me, partial, (1,))
    last_got = lax.ppermute(last_away, "tp", [(0, 1), (1, 0)])
    batch_got, got_parts, _ = lax.optimization_barrier((batch_got, got_parts, last_away))
    near_sums = [total(m, g)[0] for m, g in zip(kept_parts, got_parts)]
    sums = [jnp.concatenate(parts) for parts in zip(near_sums, total(batch_mine, batch_got))]
    late = ((slabs - 1) % (slabs // tp), slabs - 1)
    arrived = {by: [deliver(sums, by)] for by in range(slabs) if by not in late}
    tail, _ = lax.optimization_barrier((tail, (last_away, arrived[0])))
    last_mine = project([[None, tail]], sources, both, tp_me, partial, (1,))
    sums.append(total(last_mine, last_got)[0])
    for by in late:
        arrived[by] = [deliver(sums, by)]
    arrived = [arrived[by] for by in range(slabs)]

    def place_of(z):
        return sum(jnp.where(z == k, place[k], 0) for k in range(slabs))

    kept = slabs // tp
    which = [
        lax.rem(place_of(tp_me * kept + j) - place_of(z_me) + slabs + t * slabs // tp, slabs)
        for j in range(kept)
        for t in range(tp)
    ]
    counts = [len(parts) for parts in arrived]
    return pl.pallas_call(
        functools.partial(place_kernel, kept, counts),
        in_specs=[smem] + [vmem] * sum(counts),
        out_specs=vmem,
        out_shape=jax.ShapeDtypeStruct((tokens, width), BF16),
        compiler_params=limit,
        cost_estimate=light,
        name="place_columns",
    )(jnp.stack([rank, *which]).astype(jnp.int32), *[a for parts in arrived for a in parts])


def solution(mesh):
    in_specs = (
        P(None, "ctx", "tp"),
        P(),
        P(None, ("tp", "ctx")),
        P(None, ("tp", "ctx")),
        P(("tp", "ctx")),
        P("tp", "ctx"),
    )
    out_specs = P("ctx", "tp")
    return jax.shard_map(
        per_device, mesh=mesh, in_specs=in_specs, out_specs=out_specs, check_vma=False
    )
```

```python
import functools

import jax
import jax.numpy as jnp
from jax import lax
from jax.experimental import pallas as pl
from jax.experimental.pallas import tpu as pltpu
from jax.sharding import PartitionSpec as P

LANES = 128
SUBLANES = 8
GROUP = LANES * SUBLANES
HALO = 2
TAPS = 3
SIDE = 2
SLAB = SIDE * SIDE
F32 = jnp.float32
BF16 = jnp.bfloat16


def spread(scratch, halo, block, pitch):
    tokens = block.shape[0]
    for tile in range(SUBLANES):
        lanes = pl.ds(tile * LANES, LANES)
        scratch[pl.ds(tile * pitch + SUBLANES - HALO, HALO), :] = halo[:, lanes].astype(F32)
        scratch[pl.ds(tile * pitch + SUBLANES, tokens), :] = block[:, lanes].astype(F32)


def token(scratch, index, pitch):
    return scratch[pl.ds(index, SUBLANES, stride=pitch), :]


def tree_sum(terms):
    while len(terms) > 1:
        terms = [a + b for a, b in zip(terms[::2], terms[1::2])] + terms[len(terms) & ~1 :]
    return terms[0]


def filter_kernel(here, features, halo, taps, u_ref, query_ref, tap_rows, *rows):
    tokens = features.shape[1]
    pitch = tokens + SUBLANES
    for tile in range(SUBLANES):
        for which in range(3):
            for j in range(TAPS):
                row = which * TAPS + j
                tap_rows[row, tile : tile + 1] = taps[which, j : j + 1, tile * LANES : (tile + 1) * LANES]
    for which in range(3):
        spread(rows[which], halo.at[which], features.at[which], pitch)
    weights = [[tap_rows[which * TAPS + j] for j in range(TAPS)] for which in range(3)]

    def step(index, carry):
        carry = list(carry)
        for inner in range(SUBLANES):
            now = index * SUBLANES + inner
            filtered = []
            for which in range(3):
                last, before = carry[which]
                fresh = token(rows[which], now + SUBLANES, pitch)
                filtered.append(
                    weights[which][0] * fresh + weights[which][1] * last + weights[which][2] * before
                )
                carry[which] = (fresh, last)
            query_ref[0, now] = filtered[0]
            u_ref[0, now] = (filtered[1] * filtered[2]).astype(BF16).astype(F32)
        return tuple(carry)

    start = tuple(
        (token(rows[which], SUBLANES - 1, pitch), token(rows[which], SUBLANES - 2, pitch))
        for which in range(3)
    )
    lax.fori_loop(0, tokens // SUBLANES, step, start)


def registers(refs, rank, wide, first, count):
    pitch = wide.shape[0] // SUBLANES
    each = SUBLANES // SLAB
    for d in range(SLAB):
        for j in range(each):
            start = pl.multiple_of(((d ^ rank) * each + j) * pitch, SUBLANES)
            rows = refs[d][0, first : first + count, j * LANES : (j + 1) * LANES]
            wide[pl.ds(start, count), :] = rows.astype(F32)
    return [wide[pl.ds(m, SUBLANES, stride=pitch), :] for m in range(count)]


def state_kernel(modes, here, u_ref, *refs):
    rates, outs, wide = refs[:SLAB], refs[SLAB : 2 * SLAB], refs[-1]
    rank = here[1]
    tokens = u_ref.shape[1]
    decay = [jnp.exp(-rate) for rate in registers(rates, rank, wide, 0, modes)]

    def step(index, states):
        for inner in range(SUBLANES):
            u = u_ref[0, index * SUBLANES + inner]
            states = tuple(states[m] * decay[m] + u for m in range(modes))
        return states

    zero = tuple(jnp.zeros((SUBLANES, LANES), F32) for _ in range(modes))
    states = lax.fori_loop(0, tokens // SUBLANES, step, zero)
    each = SUBLANES // SLAB
    pitch = wide.shape[0] // SUBLANES
    for m in range(modes):
        wide[pl.ds(m, SUBLANES, stride=pitch), :] = states[m]
    for d in range(SLAB):
        for j in range(each):
            start = pl.multiple_of(((d ^ rank) * each + j) * pitch, SUBLANES)
            outs[d][0, :, j * LANES : (j + 1) * LANES] = wide[pl.ds(start, modes), :].astype(BF16)


def slab_kernel(tokens, here, rates, *refs):
    states, out = refs[:SLAB], refs[SLAB]
    slabs = rates.shape[0]
    for g in range(slabs):
        rate = rates[lax.rem(g - here[0] + slabs, slabs), : states[0].shape[1]]
        total = None
        for d in range(SLAB):
            later = (SLAB - 1 - (here[1] ^ d)).astype(F32) * float(tokens)
            term = jnp.exp(-later * rate) * states[d][g].astype(F32)
            total = term if total is None else total + term
        out[g] = total.astype(BF16)


def incoming_kernel(tokens, here, rates, *refs):
    slabs = rates.shape[0]
    states, earlier, outs = refs[:SLAB], refs[SLAB : SLAB + slabs - 1], refs[SLAB + slabs - 1 :]
    for g in range(slabs):
        rate = rates[lax.rem(g - here[0] + slabs, slabs), : states[0].shape[1]]
        entering = jnp.zeros(rate.shape, F32)
        for k in range(slabs - 1):
            term = jnp.exp(-float(k * SLAB * tokens) * rate) * earlier[k][g].astype(F32)
            entering += jnp.where(here[0] > k, term, jnp.zeros_like(term))
        for d in range(SLAB):
            block = here[1] ^ d
            total = jnp.exp(-(block.astype(F32) * float(tokens)) * rate) * entering
            for e in range(SLAB):
                if e != d:
                    between = block - 1 - (here[1] ^ e)
                    factor = jnp.exp(-(jnp.maximum(between, 0).astype(F32) * float(tokens)) * rate)
                    factor = jnp.where(between >= 0, factor, jnp.zeros_like(factor))
                    total += factor * states[e][g].astype(F32)
            outs[d][g] = total.astype(BF16)


def local_kernel(modes, here, u_ref, *refs):
    rates, y_ref, wide = refs[:SLAB], refs[-2], refs[-1]
    tokens = u_ref.shape[1]
    rate = registers(rates, here[1], wide, 0, modes)
    rest = registers(rates, here[1], wide, modes, modes + 1)
    decay = [jnp.exp(-r) for r in rate]
    weight = [rest[m] * jnp.sqrt(2.0 * rate[m]) for m in range(modes)]
    skip = rest[modes]

    def step(index, states):
        for inner in range(SUBLANES):
            now = index * SUBLANES + inner
            u = u_ref[0, now]
            states = tuple(states[m] * decay[m] + u for m in range(modes))
            y_ref[0, now] = tree_sum([weight[m] * states[m] for m in range(modes)] + [skip * u])
        return states

    zero = tuple(jnp.zeros((SUBLANES, LANES), F32) for _ in range(modes))
    lax.fori_loop(0, tokens // SUBLANES, step, zero)


def gated_kernel(modes, here, query_ref, y_ref, *refs):
    rates, incoming = refs[:SLAB], refs[SLAB : 2 * SLAB]
    out_ref, wide, out_rows = refs[2 * SLAB :]
    tokens = query_ref.shape[1]
    pitch = tokens + SUBLANES
    rate = registers(rates, here[1], wide, 0, modes)
    rest = registers(rates, here[1], wide, modes, modes)
    state = registers(incoming, here[1], wide, 0, modes)
    decay = [jnp.exp(-r) for r in rate]
    weighted = tuple(rest[m] * jnp.sqrt(2.0 * rate[m]) * state[m] for m in range(modes))

    def step(index, weighted):
        for inner in range(SUBLANES):
            now = index * SUBLANES + inner
            weighted = tuple(weighted[m] * decay[m] for m in range(modes))
            long_out = tree_sum([y_ref[0, now], *weighted])
            long_out = long_out.astype(BF16).astype(F32)
            out_rows[pl.ds(now, SUBLANES, stride=pitch), :] = query_ref[0, now] * long_out
        return weighted

    lax.fori_loop(0, tokens // SUBLANES, step, weighted)
    for tile in range(SUBLANES):
        out_ref[:, pl.ds(tile * LANES, LANES)] = out_rows[pl.ds(tile * pitch, tokens), :].astype(BF16)


def project_kernel(count, picks, first, added, here, *refs):
    out_ref, slots, sems = refs[-3:]
    depth, share = slots.shape[1:]
    blocks, sources = refs[:-3], refs[:-3]
    runs = depth // blocks[0].shape[1]
    blocks, sources = blocks[: runs * count], sources[runs * count :]
    rows = pl.ds(first, depth)
    columns = pl.ds(pl.multiple_of(here[0] * share, share), share)
    copies = []
    for i, (which, rank) in enumerate(picks):
        source = sources[which] if rank is None else sources[which].at[here[rank]]
        copies.append(pltpu.make_async_copy(source.at[rows, columns], slots.at[i], sems.at[i]))
        copies[-1].start()
    tokens, size = blocks[0].shape
    stacked = [
        jnp.concatenate([blocks[runs * j + h][...] for j in range(count)], axis=0) for h in range(runs)
    ]
    for i in range(len(picks)):
        copies[i].wait()
        products = None
        for h in range(runs):
            term = jnp.dot(
                stacked[h], slots[i, h * size : (h + 1) * size], preferred_element_type=F32
            )
            products = term if products is None else products + term
        for j in range(count):
            total = products[j * tokens : (j + 1) * tokens]
            if added:
                total = sources[-1][here[0], j, i] + total
            if out_ref.ndim == 4:
                out_ref[j, i] = total.astype(out_ref.dtype)
            else:
                part = out_ref.shape[-1]
                for t in range(out_ref.shape[0]):
                    out_ref[t, j, i] = total[:, t * part : (t + 1) * part].astype(out_ref.dtype)


def place_kernel(kept, counts, here, *refs):
    out_ref = refs[-1]
    share = refs[0].shape[2]
    rank = here[0]
    starts = [sum(counts[:k]) for k in range(len(counts))]
    for slot in range(kept):
        for t in range(SIDE):
            for k, count in enumerate(counts):

                @pl.when(here[1 + slot * SIDE + t] == k)
                def _(slot=slot, t=t, k=k, count=count):
                    for piece in range(SLAB):
                        each = SLAB // count
                        source = refs[starts[k] + piece // each]
                        start = ((slot * SLAB + (rank ^ piece)) * SIDE + t) * share
                        out_ref[:, pl.ds(pl.multiple_of(start, share), share)] = source[piece % each]


def ring_order(count):
    return [0] + list(range(1, count, 2)) + [i for i in range(count - 1, 0, -1) if i % 2 == 0]


def any_size(features, conv_weight, decay_rates, residues, skip_gain, out_weight):
    tokens, width = features.shape[1:]
    ctx, tp = lax.axis_size("ctx"), lax.axis_size("tp")
    me, tp_me = lax.axis_index("ctx"), lax.axis_index("tp")
    halo = lax.ppermute(features[:, tokens - HALO :], "ctx", [(i, i + 1) for i in range(ctx - 1)])
    extended = jnp.concatenate([halo, features], axis=1).astype(F32)
    taps = lax.dynamic_slice_in_dim(conv_weight, tp_me * width, width, 2)
    filtered = sum(taps[:, j, None] * extended[:, HALO - j : HALO - j + tokens] for j in range(TAPS))
    u = (filtered[1] * filtered[2]).astype(BF16).astype(F32)
    rates, weights, skip = (
        lax.all_gather(a, "ctx", axis=a.ndim - 1, tiled=True) for a in (decay_rates, residues, skip_gain)
    )
    weights = weights * jnp.sqrt(2.0 * rates)
    decay = jnp.exp(-rates)
    zero = jnp.zeros(rates.shape, F32)
    left = lax.fori_loop(0, tokens, lambda t, s: s * decay + u[t], zero)
    lefts = lax.all_gather(left, "ctx")
    block_decay = jnp.exp(-float(tokens) * rates)
    entering = lax.fori_loop(0, me, lambda b, s: s * block_decay + lefts[b], zero)

    def advance(states, now):
        states = states * decay + now
        return states, jnp.sum(weights * states, axis=0) + skip * now

    long_out = lax.scan(advance, entering, u)[1].astype(BF16).astype(F32)
    gated = (filtered[0] * long_out).astype(BF16)
    whole = lax.all_gather(gated, "ctx", axis=0, tiled=True)
    partial = jnp.dot(whole, out_weight, preferred_element_type=F32).astype(BF16)
    share = partial.shape[1] // tp
    partial = partial.reshape(ctx * tokens, tp, share).transpose(1, 0, 2)
    partial = lax.all_to_all(partial, "tp", split_axis=0, concat_axis=0, tiled=True)
    summed = jnp.sum(partial.astype(F32), axis=0).astype(BF16).reshape(ctx, tokens, share)
    summed = lax.all_to_all(summed, "ctx", split_axis=0, concat_axis=0, tiled=True)
    placed = lax.all_to_all(
        summed.reshape(tp, ctx // tp, tokens, share), "tp", split_axis=0, concat_axis=0, tiled=True
    )
    return placed.transpose(2, 1, 0, 3).reshape(tokens, width)


def per_device(features, conv_weight, decay_rates, residues, skip_gain, out_weight):
    tokens, width = features.shape[1:]
    modes, owned = decay_rates.shape
    ctx, tp = lax.axis_size("ctx"), lax.axis_size("tp")
    depth, columns = out_weight.shape
    share = columns // tp
    if owned * SLAB != GROUP or tp != SIDE or share % LANES or ctx // SLAB < 4 or ctx // SLAB % 2:
        return any_size(features, conv_weight, decay_rates, residues, skip_gain, out_weight)
    slabs = ctx // SLAB
    groups = width // GROUP
    me, tp_me = lax.axis_index("ctx"), lax.axis_index("tp")
    z_me, rank = me // SLAB, me % SLAB
    order = ring_order(slabs)
    place = [order.index(z) for z in range(slabs)]
    here = jnp.stack([z_me, rank, tp_me]).astype(jnp.int32)

    def within_slab(array, mask):
        return lax.ppermute(array, "ctx", [(i, i ^ mask) for i in range(ctx)])

    def from_slab(array, by):
        return lax.ppermute(array, "ctx", [(i, (i - by * SLAB) % ctx) for i in range(ctx)])

    def ring(array):
        pairs = []
        for i in range(ctx):
            z, rest = divmod(i, SLAB)
            pairs.append((i, order[(place[z] + 1) % slabs] * SLAB + rest))
        return lax.ppermute(array, "ctx", pairs)

    halo = lax.ppermute(
        features[:, tokens - HALO :, :], "ctx", [(i, i + 1) for i in range(ctx - 1)]
    )
    rows = jnp.concatenate([decay_rates, residues, skip_gain[None]], axis=0)
    rows = jnp.stack([rows] + [from_slab(rows, by) for by in range(1, slabs)])
    rows, halo = lax.optimization_barrier((rows, halo))
    rates = [rows, within_slab(rows, 1), within_slab(rows, 2)]

    beside = within_slab(out_weight, 1)
    slab_weights = lax.all_gather(
        out_weight,
        "ctx",
        axis_index_groups=[list(range(z * SLAB, (z + 1) * SLAB)) for z in range(slabs)],
    )

    limit = pltpu.CompilerParams(vmem_limit_bytes=16 * 1024 * 1024)
    large = pltpu.CompilerParams(vmem_limit_bytes=48 * 1024 * 1024)
    light = pl.CostEstimate(flops=1, bytes_accessed=1, transcendentals=0)
    series_shape = jax.ShapeDtypeStruct((groups, tokens, SUBLANES, LANES), F32)
    state_shape = jax.ShapeDtypeStruct((groups, modes, owned), BF16)
    scratch_rows = pltpu.VMEM((SUBLANES * (tokens + SUBLANES), LANES), F32)
    wide = pltpu.VMEM((SUBLANES * (modes + SUBLANES), LANES), F32)
    series = pl.BlockSpec((1, tokens, SUBLANES, LANES), lambda g, here: (g, 0, 0, 0))
    state_spec = pl.BlockSpec((1, modes, owned), lambda g, here: (g, 0, 0))
    rate_spec = pl.BlockSpec(
        (1, 2 * modes + 1, owned), lambda g, here: (lax.rem(g - here[0] + slabs, slabs), 0, 0)
    )

    def grouped(kernel, name, in_specs, out_specs, out_shape, scratch, groups=groups):
        return pl.pallas_call(
            kernel,
            grid_spec=pltpu.PrefetchScalarGridSpec(
                num_scalar_prefetch=1,
                grid=(groups,),
                in_specs=in_specs,
                out_specs=out_specs,
                scratch_shapes=scratch,
            ),
            out_shape=out_shape,
            compiler_params=limit,
            cost_estimate=light,
            name=name,
        )

    u, query = grouped(
        filter_kernel,
        "short_filters",
        [
            pl.BlockSpec((3, tokens, GROUP), lambda g, here: (0, 0, g)),
            pl.BlockSpec((3, HALO, GROUP), lambda g, here: (0, 0, g)),
            pl.BlockSpec((3, TAPS, GROUP), lambda g, here: (0, 0, here[2] * groups + g)),
        ],
        [series, series],
        [series_shape, series_shape],
        [pltpu.VMEM((3 * TAPS, SUBLANES, LANES), F32), scratch_rows, scratch_rows, scratch_rows],
    )(here, features, halo, conv_weight)

    passed, u = lax.optimization_barrier((rates[2], u))
    rates.append(within_slab(passed, 1))

    left = grouped(
        functools.partial(state_kernel, modes),
        "block_states",
        [series] + [rate_spec] * SLAB,
        [state_spec] * SLAB,
        [state_shape] * SLAB,
        [wide],
    )(here, u, *rates)
    left = [left[0]] + [within_slab(left[d], d) for d in range(1, SLAB)]

    local = grouped(
        functools.partial(local_kernel, modes),
        "local_convolution",
        [series] + [rate_spec] * SLAB,
        series,
        series_shape,
        [wide],
    )(here, u, *rates)
    left, local = lax.optimization_barrier((left, local))

    smem = pl.BlockSpec(memory_space=pltpu.SMEM)
    vmem = pl.BlockSpec(memory_space=pltpu.VMEM)
    slab_left = pl.pallas_call(
        functools.partial(slab_kernel, tokens),
        in_specs=[smem] + [vmem] * (1 + SLAB),
        out_specs=vmem,
        out_shape=state_shape,
        compiler_params=limit,
        cost_estimate=light,
        name="slab_states",
    )(here, rates[0], *left)
    earlier = [from_slab(slab_left, -by) for by in range(1, slabs)]

    incoming = pl.pallas_call(
        functools.partial(incoming_kernel, tokens),
        in_specs=[smem] + [vmem] * (SLAB + slabs),
        out_specs=[vmem] * SLAB,
        out_shape=[state_shape] * SLAB,
        compiler_params=limit,
        cost_estimate=light,
        name="incoming_states",
    )(here, rates[0], *left, *earlier)
    incoming = [incoming[0]] + [within_slab(incoming[d], d) for d in range(1, SLAB)]

    def gated_half(half):
        count = groups // SIDE
        first = half * count

        def shifted(spec):
            return pl.BlockSpec(spec.block_shape, lambda g, here: spec.index_map(g + first, here))

        return grouped(
            functools.partial(gated_kernel, modes),
            "gated_block",
            [shifted(s) for s in [series] * 2 + [rate_spec] * SLAB + [state_spec] * SLAB],
            pl.BlockSpec((tokens, GROUP), lambda g, here: (0, g)),
            jax.ShapeDtypeStruct((tokens, width // SIDE), BF16),
            [wide, scratch_rows],
            count,
        )(here, query, local, *rates, *incoming)

    def project(blocks, sources, picks, share_index, partial=None, halves=(0, 1)):
        scalars = jnp.stack([share_index if share_index is not None else 0, rank ^ 2, rank ^ 3])
        run = depth // SIDE
        wide_share = columns if share_index is None else share
        shape = (len(blocks), len(picks), tokens, share)
        if share_index is None:
            out = jax.ShapeDtypeStruct((tp, *shape), F32)
        else:
            out = jax.ShapeDtypeStruct(shape, BF16)
        return pl.pallas_call(
            functools.partial(
                project_kernel, len(blocks), picks, halves[0] * run, partial is not None
            ),
            in_specs=[smem]
            + [vmem] * (len(halves) * len(blocks))
            + [pl.BlockSpec(memory_space=pltpu.HBM)] * len(sources)
            + ([vmem] if partial is not None else []),
            out_specs=vmem,
            out_shape=out,
            scratch_shapes=[
                pltpu.VMEM((len(picks), len(halves) * run, wide_share), BF16),
                pltpu.SemaphoreType.DMA((len(picks),)),
            ],
            compiler_params=large,
            cost_estimate=light,
            name="project_block",
        )(
            scalars.astype(jnp.int32),
            *[b[h] for b in blocks for h in halves],
            *sources,
            *([partial] if partial is not None else []),
        )

    def project_away(blocks, sources, picks):
        away = project(blocks, sources, picks, 1 - tp_me)
        return away, lax.ppermute(away, "tp", [(0, 1), (1, 0)])

    def project_mine(blocks, sources, picks, after):
        blocks, _ = lax.optimization_barrier((blocks, after))
        return project(blocks, sources, picks, tp_me)

    def total(mine, got):
        return (mine.astype(F32) + got.astype(F32)).astype(BF16)

    half_of = [z * tp // slabs for z in range(slabs)]

    def deliver(classes, by):
        pairs = []
        for i in range(ctx):
            z, rest = divmod(i, SLAB)
            for t in range(tp):
                target = order[(place[z] - by - t * slabs // tp) % slabs] * SLAB + rest
                pairs.append((i * tp + t, target * tp + half_of[z]))
        moved = jnp.where(tp_me == 0, classes[by], classes[(by + slabs // tp) % slabs])
        return lax.ppermute(moved, ("ctx", "tp"), pairs)

    near, far, both = (
        ((0, None), (1, None)),
        ((0, 1), (0, 2)),
        ((0, None), (1, None), (2, 1), (2, 2)),
    )
    blocks = [[gated_half(h) for h in range(SIDE)]]
    kept_parts, got_parts = [], []
    mine, got = None, None
    for step in range(slabs - 1):
        first, second = block = blocks[step]
        if step:
            second, mine = lax.optimization_barrier((second, mine))
            block, _ = lax.optimization_barrier((block, mine))
        blocks.append([ring(first), ring(second)])
        away, coming = project_away([block], [out_weight, beside], near)
        mine = project_mine([block], [out_weight, beside], near, (away, got))
        got = coming
        kept_parts.append(mine)
        got_parts.append(got)
    slab_weights, _ = lax.optimization_barrier((slab_weights, mine))
    away, batch_got = project_away(blocks[: slabs - 1], [slab_weights], far)
    batch_mine = project_mine(blocks[: slabs - 1], [slab_weights], far, away)
    sources = [out_weight, beside, slab_weights]
    head, _ = lax.optimization_barrier((blocks[-1][0], batch_mine))
    partial = project([[head]], sources, both, None, None, (0,))
    tail = blocks[-1][1]
    last_away = project([[None, tail]], sources, both, 1 - tp_me, partial, (1,))
    last_got = lax.ppermute(last_away, "tp", [(0, 1), (1, 0)])
    batch_got, got_parts, _ = lax.optimization_barrier((batch_got, got_parts, last_away))
    near_sums = [total(m, g)[0] for m, g in zip(kept_parts, got_parts)]
    sums = [jnp.concatenate(parts) for parts in zip(near_sums, total(batch_mine, batch_got))]
    late = ((slabs - 1) % (slabs // tp), slabs - 1)
    arrived = {by: [deliver(sums, by)] for by in range(slabs) if by not in late}
    tail, _ = lax.optimization_barrier((tail, (last_away, arrived[0])))
    last_mine = project([[None, tail]], sources, both, tp_me, partial, (1,))
    sums.append(total(last_mine, last_got)[0])
    for by in late:
        arrived[by] = [deliver(sums, by)]
    arrived = [arrived[by] for by in range(slabs)]

    def place_of(z):
        return sum(jnp.where(z == k, place[k], 0) for k in range(slabs))

    kept = slabs // tp
    which = [
        lax.rem(place_of(tp_me * kept + j) - place_of(z_me) + slabs + t * slabs // tp, slabs)
        for j in range(kept)
        for t in range(tp)
    ]
    counts = [len(parts) for parts in arrived]
    return pl.pallas_call(
        functools.partial(place_kernel, kept, counts),
        in_specs=[smem] + [vmem] * sum(counts),
        out_specs=vmem,
        out_shape=jax.ShapeDtypeStruct((tokens, width), BF16),
        compiler_params=limit,
        cost_estimate=light,
        name="place_columns",
    )(jnp.stack([rank, *which]).astype(jnp.int32), *[a for parts in arrived for a in parts])


def solution(mesh):
    in_specs = (
        P(None, "ctx", "tp"),
        P(),
        P(None, ("tp", "ctx")),
        P(None, ("tp", "ctx")),
        P(("tp", "ctx")),
        P("tp", "ctx"),
    )
    out_specs = P("ctx", "tp")
    return jax.shard_map(
        per_device, mesh=mesh, in_specs=in_specs, out_specs=out_specs, check_vma=False
    )
```

```python
import functools

import jax
import jax.numpy as jnp
from jax import lax
from jax.experimental import pallas as pl
from jax.experimental.pallas import tpu as pltpu
from jax.sharding import PartitionSpec as P

LANES = 128
SUBLANES = 8
GROUP = LANES * SUBLANES
HALO = 2
TAPS = 3
SIDE = 2
SLAB = SIDE * SIDE
F32 = jnp.float32
BF16 = jnp.bfloat16


def spread(scratch, halo, block, pitch):
    tokens = block.shape[0]
    for tile in range(SUBLANES):
        lanes = pl.ds(tile * LANES, LANES)
        scratch[pl.ds(tile * pitch + SUBLANES - HALO, HALO), :] = halo[:, lanes].astype(F32)
        scratch[pl.ds(tile * pitch + SUBLANES, tokens), :] = block[:, lanes].astype(F32)


def token(scratch, index, pitch):
    return scratch[pl.ds(index, SUBLANES, stride=pitch), :]


def tree_sum(terms):
    while len(terms) > 1:
        terms = [a + b for a, b in zip(terms[::2], terms[1::2])] + terms[len(terms) & ~1 :]
    return terms[0]


def filter_kernel(here, features, halo, taps, u_ref, query_ref, tap_rows, *rows):
    tokens = features.shape[1]
    pitch = tokens + SUBLANES
    for tile in range(SUBLANES):
        for which in range(3):
            for j in range(TAPS):
                row = which * TAPS + j
                tap_rows[row, tile : tile + 1] = taps[which, j : j + 1, tile * LANES : (tile + 1) * LANES]
    for which in range(3):
        spread(rows[which], halo.at[which], features.at[which], pitch)
    weights = [[tap_rows[which * TAPS + j] for j in range(TAPS)] for which in range(3)]

    def step(index, carry):
        carry = list(carry)
        for inner in range(SUBLANES):
            now = index * SUBLANES + inner
            filtered = []
            for which in range(3):
                last, before = carry[which]
                fresh = token(rows[which], now + SUBLANES, pitch)
                filtered.append(
                    weights[which][0] * fresh + weights[which][1] * last + weights[which][2] * before
                )
                carry[which] = (fresh, last)
            query_ref[0, now] = filtered[0]
            u_ref[0, now] = (filtered[1] * filtered[2]).astype(BF16).astype(F32)
        return tuple(carry)

    start = tuple(
        (token(rows[which], SUBLANES - 1, pitch), token(rows[which], SUBLANES - 2, pitch))
        for which in range(3)
    )
    lax.fori_loop(0, tokens // SUBLANES, step, start)


def registers(refs, rank, wide, first, count):
    pitch = wide.shape[0] // SUBLANES
    each = SUBLANES // SLAB
    for d in range(SLAB):
        for j in range(each):
            start = pl.multiple_of(((d ^ rank) * each + j) * pitch, SUBLANES)
            rows = refs[d][0, first : first + count, j * LANES : (j + 1) * LANES]
            wide[pl.ds(start, count), :] = rows.astype(F32)
    return [wide[pl.ds(m, SUBLANES, stride=pitch), :] for m in range(count)]


def state_kernel(modes, here, u_ref, *refs):
    rates, outs, wide = refs[:SLAB], refs[SLAB : 2 * SLAB], refs[-1]
    rank = here[1]
    tokens = u_ref.shape[1]
    decay = [jnp.exp(-rate) for rate in registers(rates, rank, wide, 0, modes)]

    def step(index, states):
        for inner in range(SUBLANES):
            u = u_ref[0, index * SUBLANES + inner]
            states = tuple(states[m] * decay[m] + u for m in range(modes))
        return states

    zero = tuple(jnp.zeros((SUBLANES, LANES), F32) for _ in range(modes))
    states = lax.fori_loop(0, tokens // SUBLANES, step, zero)
    each = SUBLANES // SLAB
    pitch = wide.shape[0] // SUBLANES
    for m in range(modes):
        wide[pl.ds(m, SUBLANES, stride=pitch), :] = states[m]
    for d in range(SLAB):
        for j in range(each):
            start = pl.multiple_of(((d ^ rank) * each + j) * pitch, SUBLANES)
            outs[d][0, :, j * LANES : (j + 1) * LANES] = wide[pl.ds(start, modes), :].astype(BF16)


def slab_kernel(tokens, here, rates, *refs):
    states, out = refs[:SLAB], refs[SLAB]
    slabs = rates.shape[0]
    for g in range(slabs):
        rate = rates[lax.rem(g - here[0] + slabs, slabs), : states[0].shape[1]]
        total = None
        for d in range(SLAB):
            later = (SLAB - 1 - (here[1] ^ d)).astype(F32) * float(tokens)
            term = jnp.exp(-later * rate) * states[d][g].astype(F32)
            total = term if total is None else total + term
        out[g] = total.astype(BF16)


def incoming_kernel(tokens, here, rates, *refs):
    slabs = rates.shape[0]
    states, earlier, outs = refs[:SLAB], refs[SLAB : SLAB + slabs - 1], refs[SLAB + slabs - 1 :]
    for g in range(slabs):
        rate = rates[lax.rem(g - here[0] + slabs, slabs), : states[0].shape[1]]
        entering = jnp.zeros(rate.shape, F32)
        for k in range(slabs - 1):
            term = jnp.exp(-float(k * SLAB * tokens) * rate) * earlier[k][g].astype(F32)
            entering += jnp.where(here[0] > k, term, jnp.zeros_like(term))
        for d in range(SLAB):
            block = here[1] ^ d
            total = jnp.exp(-(block.astype(F32) * float(tokens)) * rate) * entering
            for e in range(SLAB):
                if e != d:
                    between = block - 1 - (here[1] ^ e)
                    factor = jnp.exp(-(jnp.maximum(between, 0).astype(F32) * float(tokens)) * rate)
                    factor = jnp.where(between >= 0, factor, jnp.zeros_like(factor))
                    total += factor * states[e][g].astype(F32)
            outs[d][g] = total.astype(BF16)


def local_kernel(modes, here, u_ref, *refs):
    rates, y_ref, wide = refs[:SLAB], refs[-2], refs[-1]
    tokens = u_ref.shape[1]
    rate = registers(rates, here[1], wide, 0, modes)
    rest = registers(rates, here[1], wide, modes, modes + 1)
    decay = [jnp.exp(-r) for r in rate]
    weight = [rest[m] * jnp.sqrt(2.0 * rate[m]) for m in range(modes)]
    skip = rest[modes]

    def step(index, states):
        for inner in range(SUBLANES):
            now = index * SUBLANES + inner
            u = u_ref[0, now]
            states = tuple(states[m] * decay[m] + u for m in range(modes))
            y_ref[0, now] = tree_sum([weight[m] * states[m] for m in range(modes)] + [skip * u])
        return states

    zero = tuple(jnp.zeros((SUBLANES, LANES), F32) for _ in range(modes))
    lax.fori_loop(0, tokens // SUBLANES, step, zero)


def gated_kernel(modes, here, query_ref, y_ref, *refs):
    rates, incoming = refs[:SLAB], refs[SLAB : 2 * SLAB]
    out_ref, wide, out_rows = refs[2 * SLAB :]
    tokens = query_ref.shape[1]
    pitch = tokens + SUBLANES
    rate = registers(rates, here[1], wide, 0, modes)
    rest = registers(rates, here[1], wide, modes, modes)
    state = registers(incoming, here[1], wide, 0, modes)
    decay = [jnp.exp(-r) for r in rate]
    weighted = tuple(rest[m] * jnp.sqrt(2.0 * rate[m]) * state[m] for m in range(modes))

    def step(index, weighted):
        for inner in range(SUBLANES):
            now = index * SUBLANES + inner
            weighted = tuple(weighted[m] * decay[m] for m in range(modes))
            long_out = tree_sum([y_ref[0, now], *weighted])
            long_out = long_out.astype(BF16).astype(F32)
            out_rows[pl.ds(now, SUBLANES, stride=pitch), :] = query_ref[0, now] * long_out
        return weighted

    lax.fori_loop(0, tokens // SUBLANES, step, weighted)
    for tile in range(SUBLANES):
        out_ref[:, pl.ds(tile * LANES, LANES)] = out_rows[pl.ds(tile * pitch, tokens), :].astype(BF16)


def project_kernel(count, picks, first, added, here, *refs):
    out_ref, slots, held, sems = refs[-4:]
    depth, share = slots.shape[1:]
    runs = held.shape[0] // count
    blocks, sources = refs[: runs * count], refs[runs * count : -4]
    rows = pl.ds(first, depth)
    columns = pl.ds(pl.multiple_of(here[0] * share, share), share)
    copies = []
    for i, (which, rank) in enumerate(picks):
        source = sources[which] if rank is None else sources[which].at[here[rank]]
        copies.append(pltpu.make_async_copy(source.at[rows, columns], slots.at[i], sems.at[i]))
    fetches = [
        pltpu.make_async_copy(block, held.at[k], sems.at[len(picks) + k]) for k, block in enumerate(blocks)
    ]
    copies[0].start()
    for copy in fetches + copies[1:]:
        copy.start()
    for copy in fetches:
        copy.wait()
    for i in range(len(picks)):
        copies[i].wait()
        for j in range(count):
            total = sources[-1][here[0], j, i] if added else None
            for h in range(runs):
                size = depth // runs
                term = jnp.dot(
                    held[runs * j + h],
                    slots[i, h * size : (h + 1) * size],
                    preferred_element_type=F32,
                )
                total = term if total is None else total + term
            if out_ref.ndim == 4:
                out_ref[j, i] = total.astype(out_ref.dtype)
            else:
                part = out_ref.shape[-1]
                for t in range(out_ref.shape[0]):
                    out_ref[t, j, i] = total[:, t * part : (t + 1) * part].astype(out_ref.dtype)


def place_kernel(kept, counts, here, *refs):
    out_ref = refs[-1]
    share = refs[0].shape[2]
    rank = here[0]
    starts = [sum(counts[:k]) for k in range(len(counts))]
    for slot in range(kept):
        for t in range(SIDE):
            for k, count in enumerate(counts):

                @pl.when(here[1 + slot * SIDE + t] == k)
                def _(slot=slot, t=t, k=k, count=count):
                    for piece in range(SLAB):
                        each = SLAB // count
                        source = refs[starts[k] + piece // each]
                        start = ((slot * SLAB + (rank ^ piece)) * SIDE + t) * share
                        out_ref[:, pl.ds(pl.multiple_of(start, share), share)] = source[piece % each]


def ring_order(count):
    return [0] + list(range(1, count, 2)) + [i for i in range(count - 1, 0, -1) if i % 2 == 0]


def any_size(features, conv_weight, decay_rates, residues, skip_gain, out_weight):
    tokens, width = features.shape[1:]
    ctx, tp = lax.axis_size("ctx"), lax.axis_size("tp")
    me, tp_me = lax.axis_index("ctx"), lax.axis_index("tp")
    halo = lax.ppermute(features[:, tokens - HALO :], "ctx", [(i, i + 1) for i in range(ctx - 1)])
    extended = jnp.concatenate([halo, features], axis=1).astype(F32)
    taps = lax.dynamic_slice_in_dim(conv_weight, tp_me * width, width, 2)
    filtered = sum(taps[:, j, None] * extended[:, HALO - j : HALO - j + tokens] for j in range(TAPS))
    u = (filtered[1] * filtered[2]).astype(BF16).astype(F32)
    rates, weights, skip = (
        lax.all_gather(a, "ctx", axis=a.ndim - 1, tiled=True) for a in (decay_rates, residues, skip_gain)
    )
    weights = weights * jnp.sqrt(2.0 * rates)
    decay = jnp.exp(-rates)
    zero = jnp.zeros(rates.shape, F32)
    left = lax.fori_loop(0, tokens, lambda t, s: s * decay + u[t], zero)
    lefts = lax.all_gather(left, "ctx")
    block_decay = jnp.exp(-float(tokens) * rates)
    entering = lax.fori_loop(0, me, lambda b, s: s * block_decay + lefts[b], zero)

    def advance(states, now):
        states = states * decay + now
        return states, jnp.sum(weights * states, axis=0) + skip * now

    long_out = lax.scan(advance, entering, u)[1].astype(BF16).astype(F32)
    gated = (filtered[0] * long_out).astype(BF16)
    whole = lax.all_gather(gated, "ctx", axis=0, tiled=True)
    partial = jnp.dot(whole, out_weight, preferred_element_type=F32).astype(BF16)
    share = partial.shape[1] // tp
    partial = partial.reshape(ctx * tokens, tp, share).transpose(1, 0, 2)
    partial = lax.all_to_all(partial, "tp", split_axis=0, concat_axis=0, tiled=True)
    summed = jnp.sum(partial.astype(F32), axis=0).astype(BF16).reshape(ctx, tokens, share)
    summed = lax.all_to_all(summed, "ctx", split_axis=0, concat_axis=0, tiled=True)
    placed = lax.all_to_all(
        summed.reshape(tp, ctx // tp, tokens, share), "tp", split_axis=0, concat_axis=0, tiled=True
    )
    return placed.transpose(2, 1, 0, 3).reshape(tokens, width)


def per_device(features, conv_weight, decay_rates, residues, skip_gain, out_weight):
    tokens, width = features.shape[1:]
    modes, owned = decay_rates.shape
    ctx, tp = lax.axis_size("ctx"), lax.axis_size("tp")
    depth, columns = out_weight.shape
    share = columns // tp
    if owned * SLAB != GROUP or tp != SIDE or share % LANES or ctx // SLAB < 4 or ctx // SLAB % 2:
        return any_size(features, conv_weight, decay_rates, residues, skip_gain, out_weight)
    slabs = ctx // SLAB
    groups = width // GROUP
    me, tp_me = lax.axis_index("ctx"), lax.axis_index("tp")
    z_me, rank = me // SLAB, me % SLAB
    order = ring_order(slabs)
    place = [order.index(z) for z in range(slabs)]
    here = jnp.stack([z_me, rank, tp_me]).astype(jnp.int32)

    def within_slab(array, mask):
        return lax.ppermute(array, "ctx", [(i, i ^ mask) for i in range(ctx)])

    def from_slab(array, by):
        return lax.ppermute(array, "ctx", [(i, (i - by * SLAB) % ctx) for i in range(ctx)])

    def ring(array):
        pairs = []
        for i in range(ctx):
            z, rest = divmod(i, SLAB)
            pairs.append((i, order[(place[z] + 1) % slabs] * SLAB + rest))
        return lax.ppermute(array, "ctx", pairs)

    halo = lax.ppermute(
        features[:, tokens - HALO :, :], "ctx", [(i, i + 1) for i in range(ctx - 1)]
    )
    rows = jnp.concatenate([decay_rates, residues, skip_gain[None]], axis=0)
    rows = jnp.stack([rows] + [from_slab(rows, by) for by in range(1, slabs)])
    rows, halo = lax.optimization_barrier((rows, halo))
    rates = [rows, within_slab(rows, 1), within_slab(rows, 2)]

    beside = within_slab(out_weight, 1)
    slab_weights = lax.all_gather(
        out_weight,
        "ctx",
        axis_index_groups=[list(range(z * SLAB, (z + 1) * SLAB)) for z in range(slabs)],
    )

    limit = pltpu.CompilerParams(vmem_limit_bytes=16 * 1024 * 1024)
    large = pltpu.CompilerParams(vmem_limit_bytes=48 * 1024 * 1024)
    light = pl.CostEstimate(flops=1, bytes_accessed=1, transcendentals=0)
    series_shape = jax.ShapeDtypeStruct((groups, tokens, SUBLANES, LANES), F32)
    state_shape = jax.ShapeDtypeStruct((groups, modes, owned), BF16)
    scratch_rows = pltpu.VMEM((SUBLANES * (tokens + SUBLANES), LANES), F32)
    wide = pltpu.VMEM((SUBLANES * (modes + SUBLANES), LANES), F32)
    series = pl.BlockSpec((1, tokens, SUBLANES, LANES), lambda g, here: (g, 0, 0, 0))
    state_spec = pl.BlockSpec((1, modes, owned), lambda g, here: (g, 0, 0))
    rate_spec = pl.BlockSpec(
        (1, 2 * modes + 1, owned), lambda g, here: (lax.rem(g - here[0] + slabs, slabs), 0, 0)
    )

    def grouped(kernel, name, in_specs, out_specs, out_shape, scratch, groups=groups):
        return pl.pallas_call(
            kernel,
            grid_spec=pltpu.PrefetchScalarGridSpec(
                num_scalar_prefetch=1,
                grid=(groups,),
                in_specs=in_specs,
                out_specs=out_specs,
                scratch_shapes=scratch,
            ),
            out_shape=out_shape,
            compiler_params=limit,
            cost_estimate=light,
            name=name,
        )

    u, query = grouped(
        filter_kernel,
        "short_filters",
        [
            pl.BlockSpec((3, tokens, GROUP), lambda g, here: (0, 0, g)),
            pl.BlockSpec((3, HALO, GROUP), lambda g, here: (0, 0, g)),
            pl.BlockSpec((3, TAPS, GROUP), lambda g, here: (0, 0, here[2] * groups + g)),
        ],
        [series, series],
        [series_shape, series_shape],
        [pltpu.VMEM((3 * TAPS, SUBLANES, LANES), F32), scratch_rows, scratch_rows, scratch_rows],
    )(here, features, halo, conv_weight)

    passed, u = lax.optimization_barrier((rates[2], u))
    rates.append(within_slab(passed, 1))

    left = grouped(
        functools.partial(state_kernel, modes),
        "block_states",
        [series] + [rate_spec] * SLAB,
        [state_spec] * SLAB,
        [state_shape] * SLAB,
        [wide],
    )(here, u, *rates)
    left = [left[0]] + [within_slab(left[d], d) for d in range(1, SLAB)]

    local = grouped(
        functools.partial(local_kernel, modes),
        "local_convolution",
        [series] + [rate_spec] * SLAB,
        series,
        series_shape,
        [wide],
    )(here, u, *rates)
    left, local = lax.optimization_barrier((left, local))

    smem = pl.BlockSpec(memory_space=pltpu.SMEM)
    vmem = pl.BlockSpec(memory_space=pltpu.VMEM)
    slab_left = pl.pallas_call(
        functools.partial(slab_kernel, tokens),
        in_specs=[smem] + [vmem] * (1 + SLAB),
        out_specs=vmem,
        out_shape=state_shape,
        compiler_params=limit,
        cost_estimate=light,
        name="slab_states",
    )(here, rates[0], *left)
    earlier = [from_slab(slab_left, -by) for by in range(1, slabs)]

    incoming = pl.pallas_call(
        functools.partial(incoming_kernel, tokens),
        in_specs=[smem] + [vmem] * (SLAB + slabs),
        out_specs=[vmem] * SLAB,
        out_shape=[state_shape] * SLAB,
        compiler_params=limit,
        cost_estimate=light,
        name="incoming_states",
    )(here, rates[0], *left, *earlier)
    incoming = [incoming[0]] + [within_slab(incoming[d], d) for d in range(1, SLAB)]

    def gated_half(half):
        count = groups // SIDE
        first = half * count

        def shifted(spec):
            return pl.BlockSpec(spec.block_shape, lambda g, here: spec.index_map(g + first, here))

        return grouped(
            functools.partial(gated_kernel, modes),
            "gated_block",
            [shifted(s) for s in [series] * 2 + [rate_spec] * SLAB + [state_spec] * SLAB],
            pl.BlockSpec((tokens, GROUP), lambda g, here: (0, g)),
            jax.ShapeDtypeStruct((tokens, width // SIDE), BF16),
            [wide, scratch_rows],
            count,
        )(here, query, local, *rates, *incoming)

    def project(blocks, sources, picks, share_index, partial=None, halves=(0, 1)):
        scalars = jnp.stack([share_index if share_index is not None else 0, rank ^ 2, rank ^ 3])
        run = depth // SIDE
        wide_share = columns if share_index is None else share
        shape = (len(blocks), len(picks), tokens, share)
        if share_index is None:
            out = jax.ShapeDtypeStruct((tp, *shape), F32)
        else:
            out = jax.ShapeDtypeStruct(shape, BF16)
        return pl.pallas_call(
            functools.partial(
                project_kernel, len(blocks), picks, halves[0] * run, partial is not None
            ),
            in_specs=[smem]
            + [pl.BlockSpec(memory_space=pl.ANY)] * (len(halves) * len(blocks))
            + [pl.BlockSpec(memory_space=pltpu.HBM)] * len(sources)
            + ([vmem] if partial is not None else []),
            out_specs=vmem,
            out_shape=out,
            scratch_shapes=[
                pltpu.VMEM((len(picks), len(halves) * run, wide_share), BF16),
                pltpu.VMEM((len(halves) * len(blocks), tokens, run), BF16),
                pltpu.SemaphoreType.DMA((len(picks) + len(halves) * len(blocks),)),
            ],
            compiler_params=large,
            cost_estimate=light,
            name="project_block",
        )(
            scalars.astype(jnp.int32),
            *[b[h] for b in blocks for h in halves],
            *sources,
            *([partial] if partial is not None else []),
        )

    def project_away(blocks, sources, picks):
        away = project(blocks, sources, picks, 1 - tp_me)
        return away, lax.ppermute(away, "tp", [(0, 1), (1, 0)])

    def project_mine(blocks, sources, picks, after):
        blocks, _ = lax.optimization_barrier((blocks, after))
        return project(blocks, sources, picks, tp_me)

    def total(mine, got):
        return (mine.astype(F32) + got.astype(F32)).astype(BF16)

    half_of = [z * tp // slabs for z in range(slabs)]

    def deliver(classes, by):
        pairs = []
        for i in range(ctx):
            z, rest = divmod(i, SLAB)
            for t in range(tp):
                target = order[(place[z] - by - t * slabs // tp) % slabs] * SLAB + rest
                pairs.append((i * tp + t, target * tp + half_of[z]))
        moved = jnp.where(tp_me == 0, classes[by], classes[(by + slabs // tp) % slabs])
        return lax.ppermute(moved, ("ctx", "tp"), pairs)

    near, far, both = (
        ((0, None), (1, None)),
        ((0, 1), (0, 2)),
        ((0, None), (1, None), (2, 1), (2, 2)),
    )
    blocks = [[gated_half(h) for h in range(SIDE)]]
    kept_parts, got_parts = [], []
    mine, got = None, None
    for step in range(slabs - 1):
        first, second = block = blocks[step]
        if step:
            second, mine = lax.optimization_barrier((second, mine))
            block, _ = lax.optimization_barrier((block, mine))
        blocks.append([ring(first), ring(second)])
        away, coming = project_away([block], [out_weight, beside], near)
        mine = project_mine([block], [out_weight, beside], near, (away, got))
        got = coming
        kept_parts.append(mine)
        got_parts.append(got)
    slab_weights, _ = lax.optimization_barrier((slab_weights, mine))
    away, batch_got = project_away(blocks[: slabs - 1], [slab_weights], far)
    batch_mine = project_mine(blocks[: slabs - 1], [slab_weights], far, away)
    sources = [out_weight, beside, slab_weights]
    head, _ = lax.optimization_barrier((blocks[-1][0], batch_mine))
    partial = project([[head]], sources, both, None, None, (0,))
    tail = blocks[-1][1]
    last_away = project([[None, tail]], sources, both, 1 - tp_me, partial, (1,))
    last_got = lax.ppermute(last_away, "tp", [(0, 1), (1, 0)])
    batch_got, got_parts, _ = lax.optimization_barrier((batch_got, got_parts, last_away))
    near_sums = [total(m, g)[0] for m, g in zip(kept_parts, got_parts)]
    sums = [jnp.concatenate(parts) for parts in zip(near_sums, total(batch_mine, batch_got))]
    late = ((slabs - 1) % (slabs // tp), slabs - 1)
    arrived = {by: [deliver(sums, by)] for by in range(slabs) if by not in late}
    tail, _ = lax.optimization_barrier((tail, (last_away, arrived[0])))
    last_mine = project([[None, tail]], sources, both, tp_me, partial, (1,))
    sums.append(total(last_mine, last_got)[0])
    for by in late:
        arrived[by] = [deliver(sums, by)]
    arrived = [arrived[by] for by in range(slabs)]

    def place_of(z):
        return sum(jnp.where(z == k, place[k], 0) for k in range(slabs))

    kept = slabs // tp
    which = [
        lax.rem(place_of(tp_me * kept + j) - place_of(z_me) + slabs + t * slabs // tp, slabs)
        for j in range(kept)
        for t in range(tp)
    ]
    counts = [len(parts) for parts in arrived]
    return pl.pallas_call(
        functools.partial(place_kernel, kept, counts),
        in_specs=[smem] + [vmem] * sum(counts),
        out_specs=vmem,
        out_shape=jax.ShapeDtypeStruct((tokens, width), BF16),
        compiler_params=limit,
        cost_estimate=light,
        name="place_columns",
    )(jnp.stack([rank, *which]).astype(jnp.int32), *[a for parts in arrived for a in parts])


def solution(mesh):
    in_specs = (
        P(None, "ctx", "tp"),
        P(),
        P(None, ("tp", "ctx")),
        P(None, ("tp", "ctx")),
        P(("tp", "ctx")),
        P("tp", "ctx"),
    )
    out_specs = P("ctx", "tp")
    return jax.shard_map(
        per_device, mesh=mesh, in_specs=in_specs, out_specs=out_specs, check_vma=False
    )
```

```python
import functools

import jax
import jax.numpy as jnp
from jax import lax
from jax.experimental import pallas as pl
from jax.experimental.pallas import tpu as pltpu
from jax.sharding import PartitionSpec as P

LANES = 128
SUBLANES = 8
GROUP = LANES * SUBLANES
HALO = 2
TAPS = 3
SIDE = 2
SLAB = SIDE * SIDE
F32 = jnp.float32
BF16 = jnp.bfloat16


def spread(scratch, halo, block, pitch):
    tokens = block.shape[0]
    for tile in range(SUBLANES):
        lanes = pl.ds(tile * LANES, LANES)
        scratch[pl.ds(tile * pitch + SUBLANES - HALO, HALO), :] = halo[:, lanes].astype(F32)
        scratch[pl.ds(tile * pitch + SUBLANES, tokens), :] = block[:, lanes].astype(F32)


def token(scratch, index, pitch):
    return scratch[pl.ds(index, SUBLANES, stride=pitch), :]


def tree_sum(terms):
    while len(terms) > 1:
        terms = [a + b for a, b in zip(terms[::2], terms[1::2])] + terms[len(terms) & ~1 :]
    return terms[0]


def filter_kernel(here, features, halo, taps, u_ref, query_ref, tap_rows, *rows):
    tokens = features.shape[1]
    pitch = tokens + SUBLANES
    for tile in range(SUBLANES):
        for which in range(3):
            for j in range(TAPS):
                row = which * TAPS + j
                tap_rows[row, tile : tile + 1] = taps[which, j : j + 1, tile * LANES : (tile + 1) * LANES]
    for which in range(3):
        spread(rows[which], halo.at[which], features.at[which], pitch)
    weights = [[tap_rows[which * TAPS + j] for j in range(TAPS)] for which in range(3)]

    def step(index, carry):
        carry = list(carry)
        for inner in range(SUBLANES):
            now = index * SUBLANES + inner
            filtered = []
            for which in range(3):
                last, before = carry[which]
                fresh = token(rows[which], now + SUBLANES, pitch)
                filtered.append(
                    weights[which][0] * fresh + weights[which][1] * last + weights[which][2] * before
                )
                carry[which] = (fresh, last)
            query_ref[0, now] = filtered[0]
            u_ref[0, now] = (filtered[1] * filtered[2]).astype(BF16).astype(F32)
        return tuple(carry)

    start = tuple(
        (token(rows[which], SUBLANES - 1, pitch), token(rows[which], SUBLANES - 2, pitch))
        for which in range(3)
    )
    lax.fori_loop(0, tokens // SUBLANES, step, start)


def registers(refs, rank, wide, first, count):
    pitch = wide.shape[0] // SUBLANES
    each = SUBLANES // SLAB
    for d in range(SLAB):
        for j in range(each):
            start = pl.multiple_of(((d ^ rank) * each + j) * pitch, SUBLANES)
            rows = refs[d][0, first : first + count, j * LANES : (j + 1) * LANES]
            wide[pl.ds(start, count), :] = rows.astype(F32)
    return [wide[pl.ds(m, SUBLANES, stride=pitch), :] for m in range(count)]


def state_kernel(modes, here, u_ref, *refs):
    rates, outs, wide = refs[:SLAB], refs[SLAB : 2 * SLAB], refs[-1]
    rank = here[1]
    tokens = u_ref.shape[1]
    decay = [jnp.exp(-rate) for rate in registers(rates, rank, wide, 0, modes)]

    def step(index, states):
        for inner in range(SUBLANES):
            u = u_ref[0, index * SUBLANES + inner]
            states = tuple(states[m] * decay[m] + u for m in range(modes))
        return states

    zero = tuple(jnp.zeros((SUBLANES, LANES), F32) for _ in range(modes))
    states = lax.fori_loop(0, tokens // SUBLANES, step, zero)
    each = SUBLANES // SLAB
    pitch = wide.shape[0] // SUBLANES
    for m in range(modes):
        wide[pl.ds(m, SUBLANES, stride=pitch), :] = states[m]
    for d in range(SLAB):
        for j in range(each):
            start = pl.multiple_of(((d ^ rank) * each + j) * pitch, SUBLANES)
            outs[d][0, :, j * LANES : (j + 1) * LANES] = wide[pl.ds(start, modes), :].astype(BF16)


def slab_kernel(tokens, here, rates, *refs):
    states, out = refs[:SLAB], refs[SLAB]
    slabs = rates.shape[0]
    for g in range(slabs):
        rate = rates[lax.rem(g - here[0] + slabs, slabs), : states[0].shape[1]]
        total = None
        for d in range(SLAB):
            later = (SLAB - 1 - (here[1] ^ d)).astype(F32) * float(tokens)
            term = jnp.exp(-later * rate) * states[d][g].astype(F32)
            total = term if total is None else total + term
        out[g] = total.astype(BF16)


def incoming_kernel(tokens, here, rates, *refs):
    slabs = rates.shape[0]
    states, earlier, outs = refs[:SLAB], refs[SLAB : SLAB + slabs - 1], refs[SLAB + slabs - 1 :]
    for g in range(slabs):
        rate = rates[lax.rem(g - here[0] + slabs, slabs), : states[0].shape[1]]
        entering = jnp.zeros(rate.shape, F32)
        for k in range(slabs - 1):
            term = jnp.exp(-float(k * SLAB * tokens) * rate) * earlier[k][g].astype(F32)
            entering += jnp.where(here[0] > k, term, jnp.zeros_like(term))
        for d in range(SLAB):
            block = here[1] ^ d
            total = jnp.exp(-(block.astype(F32) * float(tokens)) * rate) * entering
            for e in range(SLAB):
                if e != d:
                    between = block - 1 - (here[1] ^ e)
                    factor = jnp.exp(-(jnp.maximum(between, 0).astype(F32) * float(tokens)) * rate)
                    factor = jnp.where(between >= 0, factor, jnp.zeros_like(factor))
                    total += factor * states[e][g].astype(F32)
            outs[d][g] = total.astype(BF16)


def local_kernel(modes, here, u_ref, *refs):
    rates, y_ref, wide = refs[:SLAB], refs[-2], refs[-1]
    tokens = u_ref.shape[1]
    rate = registers(rates, here[1], wide, 0, modes)
    rest = registers(rates, here[1], wide, modes, modes + 1)
    decay = [jnp.exp(-r) for r in rate]
    weight = [rest[m] * jnp.sqrt(2.0 * rate[m]) for m in range(modes)]
    skip = rest[modes]

    def step(index, states):
        for inner in range(SUBLANES):
            now = index * SUBLANES + inner
            u = u_ref[0, now]
            states = tuple(states[m] * decay[m] + u for m in range(modes))
            y_ref[0, now] = tree_sum([weight[m] * states[m] for m in range(modes)] + [skip * u])
        return states

    zero = tuple(jnp.zeros((SUBLANES, LANES), F32) for _ in range(modes))
    lax.fori_loop(0, tokens // SUBLANES, step, zero)


def gated_kernel(modes, here, query_ref, y_ref, *refs):
    rates, incoming = refs[:SLAB], refs[SLAB : 2 * SLAB]
    out_ref, wide, out_rows = refs[2 * SLAB :]
    tokens = query_ref.shape[1]
    pitch = tokens + SUBLANES
    rate = registers(rates, here[1], wide, 0, modes)
    rest = registers(rates, here[1], wide, modes, modes)
    state = registers(incoming, here[1], wide, 0, modes)
    decay = [jnp.exp(-r) for r in rate]
    weighted = tuple(rest[m] * jnp.sqrt(2.0 * rate[m]) * state[m] for m in range(modes))

    def step(index, weighted):
        for inner in range(SUBLANES):
            now = index * SUBLANES + inner
            weighted = tuple(weighted[m] * decay[m] for m in range(modes))
            long_out = tree_sum([y_ref[0, now], *weighted])
            long_out = long_out.astype(BF16).astype(F32)
            out_rows[pl.ds(now, SUBLANES, stride=pitch), :] = query_ref[0, now] * long_out
        return weighted

    lax.fori_loop(0, tokens // SUBLANES, step, weighted)
    for tile in range(SUBLANES):
        out_ref[:, pl.ds(tile * LANES, LANES)] = out_rows[pl.ds(tile * pitch, tokens), :].astype(BF16)


def project_kernel(count, picks, first, added, here, *refs):
    out_ref, slots, held, sems = refs[-4:]
    depth, share = slots.shape[1:]
    runs = held.shape[0] // count
    blocks, sources = refs[: runs * count], refs[runs * count : -4]
    rows = pl.ds(first, depth)
    columns = pl.ds(pl.multiple_of(here[0] * share, share), share)
    copies = []
    for i, (which, rank) in enumerate(picks):
        source = sources[which] if rank is None else sources[which].at[here[rank]]
        copies.append(pltpu.make_async_copy(source.at[rows, columns], slots.at[i], sems.at[i]))
    fetches = [
        pltpu.make_async_copy(block, held.at[k], sems.at[len(picks) + k]) for k, block in enumerate(blocks)
    ]
    copies[0].start()
    for copy in fetches + copies[1:]:
        copy.start()
    for copy in fetches:
        copy.wait()
    for i in range(len(picks)):
        copies[i].wait()
        for j in range(count):
            total = sources[-1][here[0], j, i] if added else None
            for h in range(runs):
                size = depth // runs
                term = jnp.dot(
                    held[runs * j + h],
                    slots[i, h * size : (h + 1) * size],
                    preferred_element_type=F32,
                )
                total = term if total is None else total + term
            if out_ref.ndim == 4:
                out_ref[j, i] = total.astype(out_ref.dtype)
            else:
                part = out_ref.shape[-1]
                for t in range(out_ref.shape[0]):
                    out_ref[t, j, i] = total[:, t * part : (t + 1) * part].astype(out_ref.dtype)


def place_kernel(kept, counts, here, *refs):
    out_ref = refs[-1]
    share = refs[0].shape[2]
    rank = here[0]
    starts = [sum(counts[:k]) for k in range(len(counts))]
    for slot in range(kept):
        for t in range(SIDE):
            for k, count in enumerate(counts):

                @pl.when(here[1 + slot * SIDE + t] == k)
                def _(slot=slot, t=t, k=k, count=count):
                    for piece in range(SLAB):
                        each = SLAB // count
                        source = refs[starts[k] + piece // each]
                        start = ((slot * SLAB + (rank ^ piece)) * SIDE + t) * share
                        out_ref[:, pl.ds(pl.multiple_of(start, share), share)] = source[piece % each]


def ring_order(count):
    return [0] + list(range(1, count, 2)) + [i for i in range(count - 1, 0, -1) if i % 2 == 0]


def any_size(features, conv_weight, decay_rates, residues, skip_gain, out_weight):
    tokens, width = features.shape[1:]
    ctx, tp = lax.axis_size("ctx"), lax.axis_size("tp")
    me, tp_me = lax.axis_index("ctx"), lax.axis_index("tp")
    halo = lax.ppermute(features[:, tokens - HALO :], "ctx", [(i, i + 1) for i in range(ctx - 1)])
    extended = jnp.concatenate([halo, features], axis=1).astype(F32)
    taps = lax.dynamic_slice_in_dim(conv_weight, tp_me * width, width, 2)
    filtered = sum(taps[:, j, None] * extended[:, HALO - j : HALO - j + tokens] for j in range(TAPS))
    u = (filtered[1] * filtered[2]).astype(BF16).astype(F32)
    rates, weights, skip = (
        lax.all_gather(a, "ctx", axis=a.ndim - 1, tiled=True) for a in (decay_rates, residues, skip_gain)
    )
    weights = weights * jnp.sqrt(2.0 * rates)
    decay = jnp.exp(-rates)
    zero = jnp.zeros(rates.shape, F32)
    left = lax.fori_loop(0, tokens, lambda t, s: s * decay + u[t], zero)
    lefts = lax.all_gather(left, "ctx")
    block_decay = jnp.exp(-float(tokens) * rates)
    entering = lax.fori_loop(0, me, lambda b, s: s * block_decay + lefts[b], zero)

    def advance(states, now):
        states = states * decay + now
        return states, jnp.sum(weights * states, axis=0) + skip * now

    long_out = lax.scan(advance, entering, u)[1].astype(BF16).astype(F32)
    gated = (filtered[0] * long_out).astype(BF16)
    whole = lax.all_gather(gated, "ctx", axis=0, tiled=True)
    partial = jnp.dot(whole, out_weight, preferred_element_type=F32).astype(BF16)
    share = partial.shape[1] // tp
    partial = partial.reshape(ctx * tokens, tp, share).transpose(1, 0, 2)
    partial = lax.all_to_all(partial, "tp", split_axis=0, concat_axis=0, tiled=True)
    summed = jnp.sum(partial.astype(F32), axis=0).astype(BF16).reshape(ctx, tokens, share)
    summed = lax.all_to_all(summed, "ctx", split_axis=0, concat_axis=0, tiled=True)
    placed = lax.all_to_all(
        summed.reshape(tp, ctx // tp, tokens, share), "tp", split_axis=0, concat_axis=0, tiled=True
    )
    return placed.transpose(2, 1, 0, 3).reshape(tokens, width)


def per_device(features, conv_weight, decay_rates, residues, skip_gain, out_weight):
    tokens, width = features.shape[1:]
    modes, owned = decay_rates.shape
    ctx, tp = lax.axis_size("ctx"), lax.axis_size("tp")
    depth, columns = out_weight.shape
    share = columns // tp
    if owned * SLAB != GROUP or tp != SIDE or share % LANES or ctx // SLAB < 4 or ctx // SLAB % 2:
        return any_size(features, conv_weight, decay_rates, residues, skip_gain, out_weight)
    slabs = ctx // SLAB
    groups = width // GROUP
    me, tp_me = lax.axis_index("ctx"), lax.axis_index("tp")
    z_me, rank = me // SLAB, me % SLAB
    order = ring_order(slabs)
    place = [order.index(z) for z in range(slabs)]
    here = jnp.stack([z_me, rank, tp_me]).astype(jnp.int32)

    def within_slab(array, mask):
        return lax.ppermute(array, "ctx", [(i, i ^ mask) for i in range(ctx)])

    def from_slab(array, by):
        return lax.ppermute(array, "ctx", [(i, (i - by * SLAB) % ctx) for i in range(ctx)])

    def ring(array):
        pairs = []
        for i in range(ctx):
            z, rest = divmod(i, SLAB)
            pairs.append((i, order[(place[z] + 1) % slabs] * SLAB + rest))
        return lax.ppermute(array, "ctx", pairs)

    halo = lax.ppermute(
        features[:, tokens - HALO :, :], "ctx", [(i, i + 1) for i in range(ctx - 1)]
    )
    rows = jnp.concatenate([decay_rates, residues, skip_gain[None]], axis=0)
    rows = jnp.stack([rows] + [from_slab(rows, by) for by in range(1, slabs)])
    rows, halo = lax.optimization_barrier((rows, halo))
    rates = [rows, within_slab(rows, 1), within_slab(rows, 2)]

    beside = within_slab(out_weight, 1)
    slab_weights = lax.all_gather(
        out_weight,
        "ctx",
        axis_index_groups=[list(range(z * SLAB, (z + 1) * SLAB)) for z in range(slabs)],
    )

    limit = pltpu.CompilerParams(vmem_limit_bytes=16 * 1024 * 1024)
    large = pltpu.CompilerParams(vmem_limit_bytes=48 * 1024 * 1024)
    light = pl.CostEstimate(flops=1, bytes_accessed=1, transcendentals=0)
    series_shape = jax.ShapeDtypeStruct((groups, tokens, SUBLANES, LANES), F32)
    state_shape = jax.ShapeDtypeStruct((groups, modes, owned), BF16)
    scratch_rows = pltpu.VMEM((SUBLANES * (tokens + SUBLANES), LANES), F32)
    wide = pltpu.VMEM((SUBLANES * (modes + SUBLANES), LANES), F32)
    series = pl.BlockSpec((1, tokens, SUBLANES, LANES), lambda g, here: (g, 0, 0, 0))
    state_spec = pl.BlockSpec((1, modes, owned), lambda g, here: (g, 0, 0))
    rate_spec = pl.BlockSpec(
        (1, 2 * modes + 1, owned), lambda g, here: (lax.rem(g - here[0] + slabs, slabs), 0, 0)
    )

    def grouped(kernel, name, in_specs, out_specs, out_shape, scratch, groups=groups):
        return pl.pallas_call(
            kernel,
            grid_spec=pltpu.PrefetchScalarGridSpec(
                num_scalar_prefetch=1,
                grid=(groups,),
                in_specs=in_specs,
                out_specs=out_specs,
                scratch_shapes=scratch,
            ),
            out_shape=out_shape,
            compiler_params=limit,
            cost_estimate=light,
            name=name,
        )

    u, query = grouped(
        filter_kernel,
        "short_filters",
        [
            pl.BlockSpec((3, tokens, GROUP), lambda g, here: (0, 0, g)),
            pl.BlockSpec((3, HALO, GROUP), lambda g, here: (0, 0, g)),
            pl.BlockSpec((3, TAPS, GROUP), lambda g, here: (0, 0, here[2] * groups + g)),
        ],
        [series, series],
        [series_shape, series_shape],
        [pltpu.VMEM((3 * TAPS, SUBLANES, LANES), F32), scratch_rows, scratch_rows, scratch_rows],
    )(here, features, halo, conv_weight)

    passed, u = lax.optimization_barrier((rates[2], u))
    rates.append(within_slab(passed, 1))

    left = grouped(
        functools.partial(state_kernel, modes),
        "block_states",
        [series] + [rate_spec] * SLAB,
        [state_spec] * SLAB,
        [state_shape] * SLAB,
        [wide],
    )(here, u, *rates)
    left = [left[0]] + [within_slab(left[d], d) for d in range(1, SLAB)]

    local = grouped(
        functools.partial(local_kernel, modes),
        "local_convolution",
        [series] + [rate_spec] * SLAB,
        series,
        series_shape,
        [wide],
    )(here, u, *rates)
    left, local = lax.optimization_barrier((left, local))

    smem = pl.BlockSpec(memory_space=pltpu.SMEM)
    vmem = pl.BlockSpec(memory_space=pltpu.VMEM)
    slab_left = pl.pallas_call(
        functools.partial(slab_kernel, tokens),
        in_specs=[smem] + [vmem] * (1 + SLAB),
        out_specs=vmem,
        out_shape=state_shape,
        compiler_params=limit,
        cost_estimate=light,
        name="slab_states",
    )(here, rates[0], *left)
    earlier = [from_slab(slab_left, -by) for by in range(1, slabs)]

    incoming = pl.pallas_call(
        functools.partial(incoming_kernel, tokens),
        in_specs=[smem] + [vmem] * (SLAB + slabs),
        out_specs=[vmem] * SLAB,
        out_shape=[state_shape] * SLAB,
        compiler_params=limit,
        cost_estimate=light,
        name="incoming_states",
    )(here, rates[0], *left, *earlier)
    incoming = [incoming[0]] + [within_slab(incoming[d], d) for d in range(1, SLAB)]

    def gated_half(half):
        count = groups // SIDE
        first = half * count

        def shifted(spec):
            return pl.BlockSpec(spec.block_shape, lambda g, here: spec.index_map(g + first, here))

        return grouped(
            functools.partial(gated_kernel, modes),
            "gated_block",
            [shifted(s) for s in [series] * 2 + [rate_spec] * SLAB + [state_spec] * SLAB],
            pl.BlockSpec((tokens, GROUP), lambda g, here: (0, g)),
            jax.ShapeDtypeStruct((tokens, width // SIDE), BF16),
            [wide, scratch_rows],
            count,
        )(here, query, local, *rates, *incoming)

    def project(blocks, sources, picks, share_index, partial=None, halves=(0, 1)):
        scalars = jnp.stack([share_index if share_index is not None else 0, rank ^ 2, rank ^ 3])
        run = depth // SIDE
        wide_share = columns if share_index is None else share
        shape = (len(blocks), len(picks), tokens, share)
        if share_index is None:
            out = jax.ShapeDtypeStruct((tp, *shape), F32)
        else:
            out = jax.ShapeDtypeStruct(shape, BF16)
        return pl.pallas_call(
            functools.partial(
                project_kernel, len(blocks), picks, halves[0] * run, partial is not None
            ),
            in_specs=[smem]
            + [pl.BlockSpec(memory_space=pl.ANY)] * (len(halves) * len(blocks))
            + [pl.BlockSpec(memory_space=pltpu.HBM)] * len(sources)
            + ([vmem] if partial is not None else []),
            out_specs=vmem,
            out_shape=out,
            scratch_shapes=[
                pltpu.VMEM((len(picks), len(halves) * run, wide_share), BF16),
                pltpu.VMEM((len(halves) * len(blocks), tokens, run), BF16),
                pltpu.SemaphoreType.DMA((len(picks) + len(halves) * len(blocks),)),
            ],
            compiler_params=large,
            cost_estimate=light,
            name="project_block",
        )(
            scalars.astype(jnp.int32),
            *[b[h] for b in blocks for h in halves],
            *sources,
            *([partial] if partial is not None else []),
        )

    def project_away(blocks, sources, picks):
        away = project(blocks, sources, picks, 1 - tp_me)
        return away, lax.ppermute(away, "tp", [(0, 1), (1, 0)])

    def project_mine(blocks, sources, picks, after):
        blocks, _ = lax.optimization_barrier((blocks, after))
        return project(blocks, sources, picks, tp_me)

    def total(mine, got):
        return (mine.astype(F32) + got.astype(F32)).astype(BF16)

    half_of = [z * tp // slabs for z in range(slabs)]

    def deliver(classes, by):
        pairs = []
        for i in range(ctx):
            z, rest = divmod(i, SLAB)
            for t in range(tp):
                target = order[(place[z] - by - t * slabs // tp) % slabs] * SLAB + rest
                pairs.append((i * tp + t, target * tp + half_of[z]))
        moved = jnp.where(tp_me == 0, classes[by], classes[(by + slabs // tp) % slabs])
        return lax.ppermute(moved, ("ctx", "tp"), pairs)

    near, far, both = (
        ((0, None), (1, None)),
        ((0, 1), (0, 2)),
        ((0, None), (1, None), (2, 1), (2, 2)),
    )
    blocks = [[gated_half(h) for h in range(SIDE)]]
    kept_parts, got_parts = [], []
    mine, got = None, None
    for step in range(slabs - 1):
        first, second = block = blocks[step]
        if step:
            second, mine = lax.optimization_barrier((second, mine))
            block, _ = lax.optimization_barrier((block, mine))
        blocks.append([ring(first), ring(second)])
        away, coming = project_away([block], [out_weight, beside], near)
        mine = project_mine([block], [out_weight, beside], near, (away, got))
        got = coming
        kept_parts.append(mine)
        got_parts.append(got)
    slab_weights, _ = lax.optimization_barrier((slab_weights, mine))
    away, batch_got = project_away(blocks[: slabs - 1], [slab_weights], far)
    sources = [out_weight, beside, slab_weights]
    head, _ = lax.optimization_barrier((blocks[-1][0], away))
    partial = project([[head]], sources, both, None, None, (0,))
    tail = blocks[-1][1]
    last_away = project([[None, tail]], sources, both, 1 - tp_me, partial, (1,))
    last_got = lax.ppermute(last_away, "tp", [(0, 1), (1, 0)])
    batch_mine = project_mine(blocks[: slabs - 1], [slab_weights], far, last_away)
    batch_got, got_parts, _ = lax.optimization_barrier((batch_got, got_parts, last_away))
    near_sums = [total(m, g)[0] for m, g in zip(kept_parts, got_parts)]
    sums = [jnp.concatenate(parts) for parts in zip(near_sums, total(batch_mine, batch_got))]
    late = ((slabs - 1) % (slabs // tp), slabs - 1)
    arrived = {by: [deliver(sums, by)] for by in range(slabs) if by not in late}
    tail, _ = lax.optimization_barrier((tail, batch_mine))
    last_mine = project([[None, tail]], sources, both, tp_me, partial, (1,))
    sums.append(total(last_mine, last_got)[0])
    for by in late:
        arrived[by] = [deliver(sums, by)]
    arrived = [arrived[by] for by in range(slabs)]

    def place_of(z):
        return sum(jnp.where(z == k, place[k], 0) for k in range(slabs))

    kept = slabs // tp
    which = [
        lax.rem(place_of(tp_me * kept + j) - place_of(z_me) + slabs + t * slabs // tp, slabs)
        for j in range(kept)
        for t in range(tp)
    ]
    counts = [len(parts) for parts in arrived]
    return pl.pallas_call(
        functools.partial(place_kernel, kept, counts),
        in_specs=[smem] + [vmem] * sum(counts),
        out_specs=vmem,
        out_shape=jax.ShapeDtypeStruct((tokens, width), BF16),
        compiler_params=limit,
        cost_estimate=light,
        name="place_columns",
    )(jnp.stack([rank, *which]).astype(jnp.int32), *[a for parts in arrived for a in parts])


def solution(mesh):
    in_specs = (
        P(None, "ctx", "tp"),
        P(),
        P(None, ("tp", "ctx")),
        P(None, ("tp", "ctx")),
        P(("tp", "ctx")),
        P("tp", "ctx"),
    )
    out_specs = P("ctx", "tp")
    return jax.shard_map(
        per_device, mesh=mesh, in_specs=in_specs, out_specs=out_specs, check_vma=False
    )
```

```python
import functools

import jax
import jax.numpy as jnp
from jax import lax
from jax.experimental import pallas as pl
from jax.experimental.pallas import tpu as pltpu
from jax.sharding import PartitionSpec as P

LANES = 128
SUBLANES = 8
GROUP = LANES * SUBLANES
HALO = 2
TAPS = 3
SIDE = 2
SLAB = SIDE * SIDE
WIDE = 512
F32 = jnp.float32
BF16 = jnp.bfloat16


def spread(scratch, halo, block, pitch):
    tokens = block.shape[0]
    for tile in range(SUBLANES):
        lanes = pl.ds(tile * LANES, LANES)
        scratch[pl.ds(tile * pitch + SUBLANES - HALO, HALO), :] = halo[:, lanes].astype(F32)
        scratch[pl.ds(tile * pitch + SUBLANES, tokens), :] = block[:, lanes].astype(F32)


def token(scratch, index, pitch):
    return scratch[pl.ds(index, SUBLANES, stride=pitch), :]


def tree_sum(terms):
    while len(terms) > 1:
        terms = [a + b for a, b in zip(terms[::2], terms[1::2])] + terms[len(terms) & ~1 :]
    return terms[0]


def filter_kernel(here, features, halo, taps, u_ref, query_ref, tap_rows, *rows):
    tokens = features.shape[1]
    pitch = tokens + SUBLANES
    for tile in range(SUBLANES):
        for which in range(3):
            for j in range(TAPS):
                row = which * TAPS + j
                tap_rows[row, tile : tile + 1] = taps[which, j : j + 1, tile * LANES : (tile + 1) * LANES]
    for which in range(3):
        spread(rows[which], halo.at[which], features.at[which], pitch)
    weights = [[tap_rows[which * TAPS + j] for j in range(TAPS)] for which in range(3)]

    def step(index, carry):
        carry = list(carry)
        for inner in range(SUBLANES):
            now = index * SUBLANES + inner
            filtered = []
            for which in range(3):
                last, before = carry[which]
                fresh = token(rows[which], now + SUBLANES, pitch)
                filtered.append(
                    weights[which][0] * fresh + weights[which][1] * last + weights[which][2] * before
                )
                carry[which] = (fresh, last)
            query_ref[0, now] = filtered[0]
            u_ref[0, now] = (filtered[1] * filtered[2]).astype(BF16).astype(F32)
        return tuple(carry)

    start = tuple(
        (token(rows[which], SUBLANES - 1, pitch), token(rows[which], SUBLANES - 2, pitch))
        for which in range(3)
    )
    lax.fori_loop(0, tokens // SUBLANES, step, start)


def registers(refs, rank, wide, first, count):
    pitch = wide.shape[0] // SUBLANES
    each = SUBLANES // SLAB
    for d in range(SLAB):
        for j in range(each):
            start = pl.multiple_of(((d ^ rank) * each + j) * pitch, SUBLANES)
            rows = refs[d][0, first : first + count, j * LANES : (j + 1) * LANES]
            wide[pl.ds(start, count), :] = rows.astype(F32)
    return [wide[pl.ds(m, SUBLANES, stride=pitch), :] for m in range(count)]


def state_kernel(modes, here, u_ref, *refs):
    rates, outs, wide = refs[:SLAB], refs[SLAB : 2 * SLAB], refs[-1]
    rank = here[1]
    tokens = u_ref.shape[1]
    decay = [jnp.exp(-rate) for rate in registers(rates, rank, wide, 0, modes)]

    def step(index, states):
        for inner in range(SUBLANES):
            u = u_ref[0, index * SUBLANES + inner]
            states = tuple(states[m] * decay[m] + u for m in range(modes))
        return states

    zero = tuple(jnp.zeros((SUBLANES, LANES), F32) for _ in range(modes))
    states = lax.fori_loop(0, tokens // SUBLANES, step, zero)
    each = SUBLANES // SLAB
    pitch = wide.shape[0] // SUBLANES
    for m in range(modes):
        wide[pl.ds(m, SUBLANES, stride=pitch), :] = states[m]
    for d in range(SLAB):
        for j in range(each):
            start = pl.multiple_of(((d ^ rank) * each + j) * pitch, SUBLANES)
            outs[d][0, :, j * LANES : (j + 1) * LANES] = wide[pl.ds(start, modes), :].astype(BF16)


def slab_kernel(tokens, here, rates, *refs):
    states, out = refs[:SLAB], refs[SLAB]
    slabs = rates.shape[0]
    for g in range(slabs):
        rate = rates[lax.rem(g - here[0] + slabs, slabs), : states[0].shape[1]]
        total = None
        for d in range(SLAB):
            later = (SLAB - 1 - (here[1] ^ d)).astype(F32) * float(tokens)
            term = jnp.exp(-later * rate) * states[d][g].astype(F32)
            total = term if total is None else total + term
        out[g] = total.astype(BF16)


def incoming_kernel(tokens, here, rates, *refs):
    slabs = rates.shape[0]
    states, earlier, outs = refs[:SLAB], refs[SLAB : SLAB + slabs - 1], refs[SLAB + slabs - 1 :]
    for g in range(slabs):
        rate = rates[lax.rem(g - here[0] + slabs, slabs), : states[0].shape[1]]
        entering = jnp.zeros(rate.shape, F32)
        for k in range(slabs - 1):
            term = jnp.exp(-float(k * SLAB * tokens) * rate) * earlier[k][g].astype(F32)
            entering += jnp.where(here[0] > k, term, jnp.zeros_like(term))
        for d in range(SLAB):
            block = here[1] ^ d
            total = jnp.exp(-(block.astype(F32) * float(tokens)) * rate) * entering
            for e in range(SLAB):
                if e != d:
                    between = block - 1 - (here[1] ^ e)
                    factor = jnp.exp(-(jnp.maximum(between, 0).astype(F32) * float(tokens)) * rate)
                    factor = jnp.where(between >= 0, factor, jnp.zeros_like(factor))
                    total += factor * states[e][g].astype(F32)
            outs[d][g] = total.astype(BF16)


def local_kernel(modes, here, u_ref, *refs):
    rates, y_ref, wide = refs[:SLAB], refs[-2], refs[-1]
    tokens = u_ref.shape[1]
    rate = registers(rates, here[1], wide, 0, modes)
    rest = registers(rates, here[1], wide, modes, modes + 1)
    decay = [jnp.exp(-r) for r in rate]
    weight = [rest[m] * jnp.sqrt(2.0 * rate[m]) for m in range(modes)]
    skip = rest[modes]

    def step(index, states):
        for inner in range(SUBLANES):
            now = index * SUBLANES + inner
            u = u_ref[0, now]
            states = tuple(states[m] * decay[m] + u for m in range(modes))
            y_ref[0, now] = tree_sum([weight[m] * states[m] for m in range(modes)] + [skip * u])
        return states

    zero = tuple(jnp.zeros((SUBLANES, LANES), F32) for _ in range(modes))
    lax.fori_loop(0, tokens // SUBLANES, step, zero)


def gated_kernel(modes, here, query_ref, y_ref, *refs):
    rates, incoming = refs[:SLAB], refs[SLAB : 2 * SLAB]
    out_ref, wide, out_rows = refs[2 * SLAB :]
    tokens = query_ref.shape[1]
    pitch = tokens + SUBLANES
    rate = registers(rates, here[1], wide, 0, modes)
    rest = registers(rates, here[1], wide, modes, modes)
    state = registers(incoming, here[1], wide, 0, modes)
    decay = [jnp.exp(-r) for r in rate]
    weighted = tuple(rest[m] * jnp.sqrt(2.0 * rate[m]) * state[m] for m in range(modes))

    def step(index, weighted):
        for inner in range(SUBLANES):
            now = index * SUBLANES + inner
            weighted = tuple(weighted[m] * decay[m] for m in range(modes))
            long_out = tree_sum([y_ref[0, now], *weighted])
            long_out = long_out.astype(BF16).astype(F32)
            out_rows[pl.ds(now, SUBLANES, stride=pitch), :] = query_ref[0, now] * long_out
        return weighted

    lax.fori_loop(0, tokens // SUBLANES, step, weighted)
    for tile in range(SUBLANES):
        out_ref[:, pl.ds(tile * LANES, LANES)] = out_rows[pl.ds(tile * pitch, tokens), :].astype(BF16)


def project_kernel(count, picks, first, added, here, *refs):
    out_ref, slots, held, sems = refs[-4:]
    pieces = len(picks)
    depth, share = slots.shape[0], slots.shape[1] // pieces
    runs, size = held.shape[0] // count, held.shape[2]
    blocks, sources = refs[: runs * count], refs[runs * count : -4]
    columns = pl.ds(pl.multiple_of(here[0] * share, share), share)
    copies = []
    for h in range(runs):
        for i, (which, rank) in enumerate(picks):
            source = sources[which] if rank is None else sources[which].at[here[rank]]
            source = source.at[pl.ds(first + h * size, size), columns]
            target = slots.at[pl.ds(h * size, size), pl.ds(i * share, share)]
            copies.append(pltpu.make_async_copy(source, target, sems.at[h * pieces + i]))
    fetches = [
        pltpu.make_async_copy(block, held.at[k], sems.at[runs * pieces + k])
        for k, block in enumerate(blocks)
    ]
    for copy in copies[:pieces] + fetches + copies[pieces:]:
        copy.start()
    for copy in fetches:
        copy.wait()
    together = max(WIDE // share, 1)
    for start in range(0, pieces, together):
        totals = [None] * count
        for h in range(runs):
            for i in range(start, start + together):
                copies[h * pieces + i].wait()
            for j in range(count):
                term = jnp.dot(
                    held[runs * j + h],
                    slots[h * size : (h + 1) * size, start * share : (start + together) * share],
                    preferred_element_type=F32,
                )
                totals[j] = term if totals[j] is None else totals[j] + term
        for j in range(count):
            for i in range(start, start + together):
                total = totals[j][:, (i - start) * share : (i - start + 1) * share]
                if added:
                    total = sources[-1][here[0], j, i] + total
                if out_ref.ndim == 4:
                    out_ref[j, i] = total.astype(out_ref.dtype)
                else:
                    part = out_ref.shape[-1]
                    for t in range(out_ref.shape[0]):
                        out_ref[t, j, i] = total[:, t * part : (t + 1) * part].astype(out_ref.dtype)


def place_kernel(kept, counts, here, *refs):
    out_ref = refs[-1]
    share = refs[0].shape[2]
    rank = here[0]
    starts = [sum(counts[:k]) for k in range(len(counts))]
    for slot in range(kept):
        for t in range(SIDE):
            for k, count in enumerate(counts):

                @pl.when(here[1 + slot * SIDE + t] == k)
                def _(slot=slot, t=t, k=k, count=count):
                    for piece in range(SLAB):
                        each = SLAB // count
                        source = refs[starts[k] + piece // each]
                        start = ((slot * SLAB + (rank ^ piece)) * SIDE + t) * share
                        out_ref[:, pl.ds(pl.multiple_of(start, share), share)] = source[piece % each]


def ring_order(count):
    return [0] + list(range(1, count, 2)) + [i for i in range(count - 1, 0, -1) if i % 2 == 0]


def any_size(features, conv_weight, decay_rates, residues, skip_gain, out_weight):
    tokens, width = features.shape[1:]
    ctx, tp = lax.axis_size("ctx"), lax.axis_size("tp")
    me, tp_me = lax.axis_index("ctx"), lax.axis_index("tp")
    halo = lax.ppermute(features[:, tokens - HALO :], "ctx", [(i, i + 1) for i in range(ctx - 1)])
    extended = jnp.concatenate([halo, features], axis=1).astype(F32)
    taps = lax.dynamic_slice_in_dim(conv_weight, tp_me * width, width, 2)
    filtered = sum(taps[:, j, None] * extended[:, HALO - j : HALO - j + tokens] for j in range(TAPS))
    u = (filtered[1] * filtered[2]).astype(BF16).astype(F32)
    rates, weights, skip = (
        lax.all_gather(a, "ctx", axis=a.ndim - 1, tiled=True) for a in (decay_rates, residues, skip_gain)
    )
    weights = weights * jnp.sqrt(2.0 * rates)
    decay = jnp.exp(-rates)
    zero = jnp.zeros(rates.shape, F32)
    left = lax.fori_loop(0, tokens, lambda t, s: s * decay + u[t], zero)
    lefts = lax.all_gather(left, "ctx")
    block_decay = jnp.exp(-float(tokens) * rates)
    entering = lax.fori_loop(0, me, lambda b, s: s * block_decay + lefts[b], zero)

    def advance(states, now):
        states = states * decay + now
        return states, jnp.sum(weights * states, axis=0) + skip * now

    long_out = lax.scan(advance, entering, u)[1].astype(BF16).astype(F32)
    gated = (filtered[0] * long_out).astype(BF16)
    whole = lax.all_gather(gated, "ctx", axis=0, tiled=True)
    partial = jnp.dot(whole, out_weight, preferred_element_type=F32).astype(BF16)
    share = partial.shape[1] // tp
    partial = partial.reshape(ctx * tokens, tp, share).transpose(1, 0, 2)
    partial = lax.all_to_all(partial, "tp", split_axis=0, concat_axis=0, tiled=True)
    summed = jnp.sum(partial.astype(F32), axis=0).astype(BF16).reshape(ctx, tokens, share)
    summed = lax.all_to_all(summed, "ctx", split_axis=0, concat_axis=0, tiled=True)
    placed = lax.all_to_all(
        summed.reshape(tp, ctx // tp, tokens, share), "tp", split_axis=0, concat_axis=0, tiled=True
    )
    return placed.transpose(2, 1, 0, 3).reshape(tokens, width)


def per_device(features, conv_weight, decay_rates, residues, skip_gain, out_weight):
    tokens, width = features.shape[1:]
    modes, owned = decay_rates.shape
    ctx, tp = lax.axis_size("ctx"), lax.axis_size("tp")
    depth, columns = out_weight.shape
    share = columns // tp
    if owned * SLAB != GROUP or tp != SIDE or share % LANES or ctx // SLAB < 4 or ctx // SLAB % 2:
        return any_size(features, conv_weight, decay_rates, residues, skip_gain, out_weight)
    slabs = ctx // SLAB
    groups = width // GROUP
    me, tp_me = lax.axis_index("ctx"), lax.axis_index("tp")
    z_me, rank = me // SLAB, me % SLAB
    order = ring_order(slabs)
    place = [order.index(z) for z in range(slabs)]
    here = jnp.stack([z_me, rank, tp_me]).astype(jnp.int32)

    def within_slab(array, mask):
        return lax.ppermute(array, "ctx", [(i, i ^ mask) for i in range(ctx)])

    def from_slab(array, by):
        return lax.ppermute(array, "ctx", [(i, (i - by * SLAB) % ctx) for i in range(ctx)])

    def ring(array):
        pairs = []
        for i in range(ctx):
            z, rest = divmod(i, SLAB)
            pairs.append((i, order[(place[z] + 1) % slabs] * SLAB + rest))
        return lax.ppermute(array, "ctx", pairs)

    halo = lax.ppermute(
        features[:, tokens - HALO :, :], "ctx", [(i, i + 1) for i in range(ctx - 1)]
    )
    rows = jnp.concatenate([decay_rates, residues, skip_gain[None]], axis=0)
    rows = jnp.stack([rows] + [from_slab(rows, by) for by in range(1, slabs)])
    rows, halo = lax.optimization_barrier((rows, halo))
    rates = [rows, within_slab(rows, 1), within_slab(rows, 2)]

    beside = within_slab(out_weight, 1)
    slab_weights = lax.all_gather(
        out_weight,
        "ctx",
        axis_index_groups=[list(range(z * SLAB, (z + 1) * SLAB)) for z in range(slabs)],
    )

    limit = pltpu.CompilerParams(vmem_limit_bytes=16 * 1024 * 1024)
    large = pltpu.CompilerParams(vmem_limit_bytes=48 * 1024 * 1024)
    light = pl.CostEstimate(flops=1, bytes_accessed=1, transcendentals=0)
    series_shape = jax.ShapeDtypeStruct((groups, tokens, SUBLANES, LANES), F32)
    state_shape = jax.ShapeDtypeStruct((groups, modes, owned), BF16)
    scratch_rows = pltpu.VMEM((SUBLANES * (tokens + SUBLANES), LANES), F32)
    wide = pltpu.VMEM((SUBLANES * (modes + SUBLANES), LANES), F32)
    series = pl.BlockSpec((1, tokens, SUBLANES, LANES), lambda g, here: (g, 0, 0, 0))
    state_spec = pl.BlockSpec((1, modes, owned), lambda g, here: (g, 0, 0))
    rate_spec = pl.BlockSpec(
        (1, 2 * modes + 1, owned), lambda g, here: (lax.rem(g - here[0] + slabs, slabs), 0, 0)
    )

    def grouped(kernel, name, in_specs, out_specs, out_shape, scratch, groups=groups):
        return pl.pallas_call(
            kernel,
            grid_spec=pltpu.PrefetchScalarGridSpec(
                num_scalar_prefetch=1,
                grid=(groups,),
                in_specs=in_specs,
                out_specs=out_specs,
                scratch_shapes=scratch,
            ),
            out_shape=out_shape,
            compiler_params=limit,
            cost_estimate=light,
            name=name,
        )

    u, query = grouped(
        filter_kernel,
        "short_filters",
        [
            pl.BlockSpec((3, tokens, GROUP), lambda g, here: (0, 0, g)),
            pl.BlockSpec((3, HALO, GROUP), lambda g, here: (0, 0, g)),
            pl.BlockSpec((3, TAPS, GROUP), lambda g, here: (0, 0, here[2] * groups + g)),
        ],
        [series, series],
        [series_shape, series_shape],
        [pltpu.VMEM((3 * TAPS, SUBLANES, LANES), F32), scratch_rows, scratch_rows, scratch_rows],
    )(here, features, halo, conv_weight)

    passed, u = lax.optimization_barrier((rates[2], u))
    rates.append(within_slab(passed, 1))

    left = grouped(
        functools.partial(state_kernel, modes),
        "block_states",
        [series] + [rate_spec] * SLAB,
        [state_spec] * SLAB,
        [state_shape] * SLAB,
        [wide],
    )(here, u, *rates)
    left = [left[0]] + [within_slab(left[d], d) for d in range(1, SLAB)]

    local = grouped(
        functools.partial(local_kernel, modes),
        "local_convolution",
        [series] + [rate_spec] * SLAB,
        series,
        series_shape,
        [wide],
    )(here, u, *rates)
    left, local = lax.optimization_barrier((left, local))

    smem = pl.BlockSpec(memory_space=pltpu.SMEM)
    vmem = pl.BlockSpec(memory_space=pltpu.VMEM)
    slab_left = pl.pallas_call(
        functools.partial(slab_kernel, tokens),
        in_specs=[smem] + [vmem] * (1 + SLAB),
        out_specs=vmem,
        out_shape=state_shape,
        compiler_params=limit,
        cost_estimate=light,
        name="slab_states",
    )(here, rates[0], *left)
    earlier = [from_slab(slab_left, -by) for by in range(1, slabs)]

    incoming = pl.pallas_call(
        functools.partial(incoming_kernel, tokens),
        in_specs=[smem] + [vmem] * (SLAB + slabs),
        out_specs=[vmem] * SLAB,
        out_shape=[state_shape] * SLAB,
        compiler_params=limit,
        cost_estimate=light,
        name="incoming_states",
    )(here, rates[0], *left, *earlier)
    incoming = [incoming[0]] + [within_slab(incoming[d], d) for d in range(1, SLAB)]

    def gated_half(half):
        count = groups // SIDE
        first = half * count

        def shifted(spec):
            return pl.BlockSpec(spec.block_shape, lambda g, here: spec.index_map(g + first, here))

        return grouped(
            functools.partial(gated_kernel, modes),
            "gated_block",
            [shifted(s) for s in [series] * 2 + [rate_spec] * SLAB + [state_spec] * SLAB],
            pl.BlockSpec((tokens, GROUP), lambda g, here: (0, g)),
            jax.ShapeDtypeStruct((tokens, width // SIDE), BF16),
            [wide, scratch_rows],
            count,
        )(here, query, local, *rates, *incoming)

    def project(blocks, sources, picks, share_index, partial=None, halves=(0, 1)):
        scalars = jnp.stack([share_index if share_index is not None else 0, rank ^ 2, rank ^ 3])
        run = depth // SIDE
        wide_share = columns if share_index is None else share
        shape = (len(blocks), len(picks), tokens, share)
        if share_index is None:
            out = jax.ShapeDtypeStruct((tp, *shape), F32)
        else:
            out = jax.ShapeDtypeStruct(shape, BF16)
        return pl.pallas_call(
            functools.partial(
                project_kernel, len(blocks), picks, halves[0] * run, partial is not None
            ),
            in_specs=[smem]
            + [pl.BlockSpec(memory_space=pl.ANY)] * (len(halves) * len(blocks))
            + [pl.BlockSpec(memory_space=pltpu.HBM)] * len(sources)
            + ([vmem] if partial is not None else []),
            out_specs=vmem,
            out_shape=out,
            scratch_shapes=[
                pltpu.VMEM((len(halves) * run, len(picks) * wide_share), BF16),
                pltpu.VMEM((len(halves) * len(blocks), tokens, run), BF16),
                pltpu.SemaphoreType.DMA((len(halves) * (len(picks) + len(blocks)),)),
            ],
            compiler_params=large,
            cost_estimate=light,
            name="project_block",
        )(
            scalars.astype(jnp.int32),
            *[b[h] for b in blocks for h in halves],
            *sources,
            *([partial] if partial is not None else []),
        )

    def project_away(blocks, sources, picks):
        away = project(blocks, sources, picks, 1 - tp_me)
        return away, lax.ppermute(away, "tp", [(0, 1), (1, 0)])

    def project_mine(blocks, sources, picks, after):
        blocks, _ = lax.optimization_barrier((blocks, after))
        return project(blocks, sources, picks, tp_me)

    def total(mine, got):
        return (mine.astype(F32) + got.astype(F32)).astype(BF16)

    half_of = [z * tp // slabs for z in range(slabs)]

    def deliver(classes, by):
        pairs = []
        for i in range(ctx):
            z, rest = divmod(i, SLAB)
            for t in range(tp):
                target = order[(place[z] - by - t * slabs // tp) % slabs] * SLAB + rest
                pairs.append((i * tp + t, target * tp + half_of[z]))
        moved = jnp.where(tp_me == 0, classes[by], classes[(by + slabs // tp) % slabs])
        return lax.ppermute(moved, ("ctx", "tp"), pairs)

    near, far, both = (
        ((0, None), (1, None)),
        ((0, 1), (0, 2)),
        ((0, None), (1, None), (2, 1), (2, 2)),
    )
    blocks = [[gated_half(h) for h in range(SIDE)]]
    kept_parts, got_parts = [], []
    mine, got = None, None
    for step in range(slabs - 1):
        first, second = block = blocks[step]
        if step:
            second, mine = lax.optimization_barrier((second, mine))
            block, _ = lax.optimization_barrier((block, mine))
        blocks.append([ring(first), ring(second)])
        away, coming = project_away([block], [out_weight, beside], near)
        mine = project_mine([block], [out_weight, beside], near, (away, got))
        got = coming
        kept_parts.append(mine)
        got_parts.append(got)
    slab_weights, _ = lax.optimization_barrier((slab_weights, mine))
    away, batch_got = project_away(blocks[: slabs - 1], [slab_weights], far)
    batch_mine = project_mine(blocks[: slabs - 1], [slab_weights], far, away)
    sources = [out_weight, beside, slab_weights]
    head, _ = lax.optimization_barrier((blocks[-1][0], batch_mine))
    partial = project([[head]], sources, both, None, None, (0,))
    tail = blocks[-1][1]
    last_away = project([[None, tail]], sources, both, 1 - tp_me, partial, (1,))
    last_got = lax.ppermute(last_away, "tp", [(0, 1), (1, 0)])
    batch_got, got_parts, _ = lax.optimization_barrier((batch_got, got_parts, last_away))
    near_sums = [total(m, g)[0] for m, g in zip(kept_parts, got_parts)]
    sums = [jnp.concatenate(parts) for parts in zip(near_sums, total(batch_mine, batch_got))]
    late = ((slabs - 1) % (slabs // tp), slabs - 1)
    arrived = {by: [deliver(sums, by)] for by in range(slabs) if by not in late}
    tail, _ = lax.optimization_barrier((tail, (last_away, arrived[0])))
    last_mine = project([[None, tail]], sources, both, tp_me, partial, (1,))
    sums.append(total(last_mine, last_got)[0])
    for by in late:
        arrived[by] = [deliver(sums, by)]
    arrived = [arrived[by] for by in range(slabs)]

    def place_of(z):
        return sum(jnp.where(z == k, place[k], 0) for k in range(slabs))

    kept = slabs // tp
    which = [
        lax.rem(place_of(tp_me * kept + j) - place_of(z_me) + slabs + t * slabs // tp, slabs)
        for j in range(kept)
        for t in range(tp)
    ]
    counts = [len(parts) for parts in arrived]
    return pl.pallas_call(
        functools.partial(place_kernel, kept, counts),
        in_specs=[smem] + [vmem] * sum(counts),
        out_specs=vmem,
        out_shape=jax.ShapeDtypeStruct((tokens, width), BF16),
        compiler_params=limit,
        cost_estimate=light,
        name="place_columns",
    )(jnp.stack([rank, *which]).astype(jnp.int32), *[a for parts in arrived for a in parts])


def solution(mesh):
    in_specs = (
        P(None, "ctx", "tp"),
        P(),
        P(None, ("tp", "ctx")),
        P(None, ("tp", "ctx")),
        P(("tp", "ctx")),
        P("tp", "ctx"),
    )
    out_specs = P("ctx", "tp")
    return jax.shard_map(
        per_device, mesh=mesh, in_specs=in_specs, out_specs=out_specs, check_vma=False
    )
```

```python
import functools

import jax
import jax.numpy as jnp
from jax import lax
from jax.experimental import pallas as pl
from jax.experimental.pallas import tpu as pltpu
from jax.sharding import PartitionSpec as P

LANES = 128
SUBLANES = 8
GROUP = LANES * SUBLANES
HALO = 2
TAPS = 3
SIDE = 2
SLAB = SIDE * SIDE
F32 = jnp.float32
BF16 = jnp.bfloat16


def spread(scratch, halo, block, pitch):
    tokens = block.shape[0]
    for tile in range(SUBLANES):
        lanes = pl.ds(tile * LANES, LANES)
        scratch[pl.ds(tile * pitch + SUBLANES - HALO, HALO), :] = halo[:, lanes].astype(F32)
        scratch[pl.ds(tile * pitch + SUBLANES, tokens), :] = block[:, lanes].astype(F32)


def token(scratch, index, pitch):
    return scratch[pl.ds(index, SUBLANES, stride=pitch), :]


def tree_sum(terms):
    while len(terms) > 1:
        terms = [a + b for a, b in zip(terms[::2], terms[1::2])] + terms[len(terms) & ~1 :]
    return terms[0]


def filter_kernel(here, features, halo, taps, u_ref, query_ref, tap_rows, *rows):
    tokens = features.shape[1]
    pitch = tokens + SUBLANES
    for tile in range(SUBLANES):
        for which in range(3):
            for j in range(TAPS):
                row = which * TAPS + j
                tap_rows[row, tile : tile + 1] = taps[which, j : j + 1, tile * LANES : (tile + 1) * LANES]
    for which in range(3):
        spread(rows[which], halo.at[which], features.at[which], pitch)
    weights = [[tap_rows[which * TAPS + j] for j in range(TAPS)] for which in range(3)]

    def step(index, carry):
        carry = list(carry)
        for inner in range(SUBLANES):
            now = index * SUBLANES + inner
            filtered = []
            for which in range(3):
                last, before = carry[which]
                fresh = token(rows[which], now + SUBLANES, pitch)
                filtered.append(
                    weights[which][0] * fresh + weights[which][1] * last + weights[which][2] * before
                )
                carry[which] = (fresh, last)
            query_ref[0, now] = filtered[0]
            u_ref[0, now] = (filtered[1] * filtered[2]).astype(BF16).astype(F32)
        return tuple(carry)

    start = tuple(
        (token(rows[which], SUBLANES - 1, pitch), token(rows[which], SUBLANES - 2, pitch))
        for which in range(3)
    )
    lax.fori_loop(0, tokens // SUBLANES, step, start)


def registers(refs, rank, wide, first, count):
    pitch = wide.shape[0] // SUBLANES
    each = SUBLANES // SLAB
    for d in range(SLAB):
        for j in range(each):
            start = pl.multiple_of(((d ^ rank) * each + j) * pitch, SUBLANES)
            rows = refs[d][0, first : first + count, j * LANES : (j + 1) * LANES]
            wide[pl.ds(start, count), :] = rows.astype(F32)
    return [wide[pl.ds(m, SUBLANES, stride=pitch), :] for m in range(count)]


def state_kernel(modes, here, u_ref, *refs):
    rates, outs, wide = refs[:SLAB], refs[SLAB : 2 * SLAB], refs[-1]
    rank = here[1]
    tokens = u_ref.shape[1]
    decay = [jnp.exp(-rate) for rate in registers(rates, rank, wide, 0, modes)]

    def step(index, states):
        for inner in range(SUBLANES):
            u = u_ref[0, index * SUBLANES + inner]
            states = tuple(states[m] * decay[m] + u for m in range(modes))
        return states

    zero = tuple(jnp.zeros((SUBLANES, LANES), F32) for _ in range(modes))
    states = lax.fori_loop(0, tokens // SUBLANES, step, zero)
    each = SUBLANES // SLAB
    pitch = wide.shape[0] // SUBLANES
    for m in range(modes):
        wide[pl.ds(m, SUBLANES, stride=pitch), :] = states[m]
    for d in range(SLAB):
        for j in range(each):
            start = pl.multiple_of(((d ^ rank) * each + j) * pitch, SUBLANES)
            outs[d][0, :, j * LANES : (j + 1) * LANES] = wide[pl.ds(start, modes), :].astype(BF16)


def slab_kernel(tokens, here, rates, *refs):
    states, out = refs[:SLAB], refs[SLAB]
    slabs = rates.shape[0]
    for g in range(slabs):
        rate = rates[lax.rem(g - here[0] + slabs, slabs), : states[0].shape[1]]
        total = None
        for d in range(SLAB):
            later = (SLAB - 1 - (here[1] ^ d)).astype(F32) * float(tokens)
            term = jnp.exp(-later * rate) * states[d][g].astype(F32)
            total = term if total is None else total + term
        out[g] = total.astype(BF16)


def incoming_kernel(tokens, here, rates, *refs):
    slabs = rates.shape[0]
    states, earlier, outs = refs[:SLAB], refs[SLAB : SLAB + slabs - 1], refs[SLAB + slabs - 1 :]
    for g in range(slabs):
        rate = rates[lax.rem(g - here[0] + slabs, slabs), : states[0].shape[1]]
        entering = jnp.zeros(rate.shape, F32)
        for k in range(slabs - 1):
            term = jnp.exp(-float(k * SLAB * tokens) * rate) * earlier[k][g].astype(F32)
            entering += jnp.where(here[0] > k, term, jnp.zeros_like(term))
        for d in range(SLAB):
            block = here[1] ^ d
            total = jnp.exp(-(block.astype(F32) * float(tokens)) * rate) * entering
            for e in range(SLAB):
                if e != d:
                    between = block - 1 - (here[1] ^ e)
                    factor = jnp.exp(-(jnp.maximum(between, 0).astype(F32) * float(tokens)) * rate)
                    factor = jnp.where(between >= 0, factor, jnp.zeros_like(factor))
                    total += factor * states[e][g].astype(F32)
            outs[d][g] = total.astype(BF16)


def local_kernel(modes, here, u_ref, *refs):
    rates, y_ref, wide = refs[:SLAB], refs[-2], refs[-1]
    tokens = u_ref.shape[1]
    rate = registers(rates, here[1], wide, 0, modes)
    rest = registers(rates, here[1], wide, modes, modes + 1)
    decay = [jnp.exp(-r) for r in rate]
    weight = [rest[m] * jnp.sqrt(2.0 * rate[m]) for m in range(modes)]
    skip = rest[modes]

    def step(index, states):
        for inner in range(SUBLANES):
            now = index * SUBLANES + inner
            u = u_ref[0, now]
            states = tuple(states[m] * decay[m] + u for m in range(modes))
            y_ref[0, now] = tree_sum([weight[m] * states[m] for m in range(modes)] + [skip * u])
        return states

    zero = tuple(jnp.zeros((SUBLANES, LANES), F32) for _ in range(modes))
    lax.fori_loop(0, tokens // SUBLANES, step, zero)


def gated_kernel(modes, here, query_ref, y_ref, *refs):
    rates, incoming = refs[:SLAB], refs[SLAB : 2 * SLAB]
    out_ref, wide, out_rows = refs[2 * SLAB :]
    tokens = query_ref.shape[1]
    pitch = tokens + SUBLANES
    rate = registers(rates, here[1], wide, 0, modes)
    rest = registers(rates, here[1], wide, modes, modes)
    state = registers(incoming, here[1], wide, 0, modes)
    decay = [jnp.exp(-r) for r in rate]
    weighted = tuple(rest[m] * jnp.sqrt(2.0 * rate[m]) * state[m] for m in range(modes))

    def step(index, weighted):
        for inner in range(SUBLANES):
            now = index * SUBLANES + inner
            weighted = tuple(weighted[m] * decay[m] for m in range(modes))
            long_out = tree_sum([y_ref[0, now], *weighted])
            long_out = long_out.astype(BF16).astype(F32)
            out_rows[pl.ds(now, SUBLANES, stride=pitch), :] = query_ref[0, now] * long_out
        return weighted

    lax.fori_loop(0, tokens // SUBLANES, step, weighted)
    for tile in range(SUBLANES):
        out_ref[:, pl.ds(tile * LANES, LANES)] = out_rows[pl.ds(tile * pitch, tokens), :].astype(BF16)


def project_kernel(count, picks, first, added, here, *refs):
    out_ref, slots, held, sems = refs[-4:]
    depth, share = slots.shape[1:]
    runs = held.shape[0] // count
    blocks, sources = refs[: runs * count], refs[runs * count : -4]
    rows = pl.ds(first, depth)
    columns = pl.ds(pl.multiple_of(here[0] * share, share), share)
    copies = []
    for i, (which, rank) in enumerate(picks):
        source = sources[which] if rank is None else sources[which].at[here[rank]]
        copies.append(pltpu.make_async_copy(source.at[rows, columns], slots.at[i], sems.at[i]))
    fetches = [
        pltpu.make_async_copy(block, held.at[k], sems.at[len(picks) + k]) for k, block in enumerate(blocks)
    ]
    copies[0].start()
    for copy in fetches + copies[1:]:
        copy.start()
    for copy in fetches:
        copy.wait()
    for i in range(len(picks)):
        copies[i].wait()
        for j in range(count):
            total = sources[-1][here[0], j, i] if added else None
            for h in range(runs):
                size = depth // runs
                term = jnp.dot(
                    held[runs * j + h],
                    slots[i, h * size : (h + 1) * size],
                    preferred_element_type=F32,
                )
                total = term if total is None else total + term
            if out_ref.ndim == 4:
                out_ref[j, i] = total.astype(out_ref.dtype)
            else:
                part = out_ref.shape[-1]
                for t in range(out_ref.shape[0]):
                    out_ref[t, j, i] = total[:, t * part : (t + 1) * part].astype(out_ref.dtype)


def place_kernel(kept, counts, here, *refs):
    out_ref = refs[-1]
    share = refs[0].shape[2]
    rank = here[0]
    starts = [sum(counts[:k]) for k in range(len(counts))]
    for slot in range(kept):
        for t in range(SIDE):
            for k, count in enumerate(counts):

                @pl.when(here[1 + slot * SIDE + t] == k)
                def _(slot=slot, t=t, k=k, count=count):
                    for piece in range(SLAB):
                        each = SLAB // count
                        source = refs[starts[k] + piece // each]
                        start = ((slot * SLAB + (rank ^ piece)) * SIDE + t) * share
                        out_ref[:, pl.ds(pl.multiple_of(start, share), share)] = source[piece % each]


def ring_order(count):
    return [0] + list(range(1, count, 2)) + [i for i in range(count - 1, 0, -1) if i % 2 == 0]


def any_size(features, conv_weight, decay_rates, residues, skip_gain, out_weight):
    tokens, width = features.shape[1:]
    ctx, tp = lax.axis_size("ctx"), lax.axis_size("tp")
    me, tp_me = lax.axis_index("ctx"), lax.axis_index("tp")
    halo = lax.ppermute(features[:, tokens - HALO :], "ctx", [(i, i + 1) for i in range(ctx - 1)])
    extended = jnp.concatenate([halo, features], axis=1).astype(F32)
    taps = lax.dynamic_slice_in_dim(conv_weight, tp_me * width, width, 2)
    filtered = sum(taps[:, j, None] * extended[:, HALO - j : HALO - j + tokens] for j in range(TAPS))
    u = (filtered[1] * filtered[2]).astype(BF16).astype(F32)
    rates, weights, skip = (
        lax.all_gather(a, "ctx", axis=a.ndim - 1, tiled=True) for a in (decay_rates, residues, skip_gain)
    )
    weights = weights * jnp.sqrt(2.0 * rates)
    decay = jnp.exp(-rates)
    zero = jnp.zeros(rates.shape, F32)
    left = lax.fori_loop(0, tokens, lambda t, s: s * decay + u[t], zero)
    lefts = lax.all_gather(left, "ctx")
    block_decay = jnp.exp(-float(tokens) * rates)
    entering = lax.fori_loop(0, me, lambda b, s: s * block_decay + lefts[b], zero)

    def advance(states, now):
        states = states * decay + now
        return states, jnp.sum(weights * states, axis=0) + skip * now

    long_out = lax.scan(advance, entering, u)[1].astype(BF16).astype(F32)
    gated = (filtered[0] * long_out).astype(BF16)
    whole = lax.all_gather(gated, "ctx", axis=0, tiled=True)
    partial = jnp.dot(whole, out_weight, preferred_element_type=F32).astype(BF16)
    share = partial.shape[1] // tp
    partial = partial.reshape(ctx * tokens, tp, share).transpose(1, 0, 2)
    partial = lax.all_to_all(partial, "tp", split_axis=0, concat_axis=0, tiled=True)
    summed = jnp.sum(partial.astype(F32), axis=0).astype(BF16).reshape(ctx, tokens, share)
    summed = lax.all_to_all(summed, "ctx", split_axis=0, concat_axis=0, tiled=True)
    placed = lax.all_to_all(
        summed.reshape(tp, ctx // tp, tokens, share), "tp", split_axis=0, concat_axis=0, tiled=True
    )
    return placed.transpose(2, 1, 0, 3).reshape(tokens, width)


def per_device(features, conv_weight, decay_rates, residues, skip_gain, out_weight):
    tokens, width = features.shape[1:]
    modes, owned = decay_rates.shape
    ctx, tp = lax.axis_size("ctx"), lax.axis_size("tp")
    depth, columns = out_weight.shape
    share = columns // tp
    if owned * SLAB != GROUP or tp != SIDE or share % LANES or ctx // SLAB < 4 or ctx // SLAB % 2:
        return any_size(features, conv_weight, decay_rates, residues, skip_gain, out_weight)
    slabs = ctx // SLAB
    groups = width // GROUP
    me, tp_me = lax.axis_index("ctx"), lax.axis_index("tp")
    z_me, rank = me // SLAB, me % SLAB
    order = ring_order(slabs)
    place = [order.index(z) for z in range(slabs)]
    here = jnp.stack([z_me, rank, tp_me]).astype(jnp.int32)

    def within_slab(array, mask):
        return lax.ppermute(array, "ctx", [(i, i ^ mask) for i in range(ctx)])

    def from_slab(array, by):
        return lax.ppermute(array, "ctx", [(i, (i - by * SLAB) % ctx) for i in range(ctx)])

    def ring(array):
        pairs = []
        for i in range(ctx):
            z, rest = divmod(i, SLAB)
            pairs.append((i, order[(place[z] + 1) % slabs] * SLAB + rest))
        return lax.ppermute(array, "ctx", pairs)

    halo = lax.ppermute(
        features[:, tokens - HALO :, :], "ctx", [(i, i + 1) for i in range(ctx - 1)]
    )
    rows = jnp.concatenate([decay_rates, residues, skip_gain[None]], axis=0)
    rows = jnp.stack([rows] + [from_slab(rows, by) for by in range(1, slabs)])
    rows, halo = lax.optimization_barrier((rows, halo))
    rates = [rows, within_slab(rows, 1), within_slab(rows, 2)]

    beside = within_slab(out_weight, 1)
    slab_weights = lax.all_gather(
        out_weight,
        "ctx",
        axis_index_groups=[list(range(z * SLAB, (z + 1) * SLAB)) for z in range(slabs)],
    )

    limit = pltpu.CompilerParams(vmem_limit_bytes=16 * 1024 * 1024)
    large = pltpu.CompilerParams(vmem_limit_bytes=48 * 1024 * 1024)
    light = pl.CostEstimate(flops=1, bytes_accessed=1, transcendentals=0)
    series_shape = jax.ShapeDtypeStruct((groups, tokens, SUBLANES, LANES), F32)
    state_shape = jax.ShapeDtypeStruct((groups, modes, owned), BF16)
    scratch_rows = pltpu.VMEM((SUBLANES * (tokens + SUBLANES), LANES), F32)
    wide = pltpu.VMEM((SUBLANES * (modes + SUBLANES), LANES), F32)
    series = pl.BlockSpec((1, tokens, SUBLANES, LANES), lambda g, here: (g, 0, 0, 0))
    state_spec = pl.BlockSpec((1, modes, owned), lambda g, here: (g, 0, 0))
    rate_spec = pl.BlockSpec(
        (1, 2 * modes + 1, owned), lambda g, here: (lax.rem(g - here[0] + slabs, slabs), 0, 0)
    )

    def grouped(kernel, name, in_specs, out_specs, out_shape, scratch, groups=groups):
        return pl.pallas_call(
            kernel,
            grid_spec=pltpu.PrefetchScalarGridSpec(
                num_scalar_prefetch=1,
                grid=(groups,),
                in_specs=in_specs,
                out_specs=out_specs,
                scratch_shapes=scratch,
            ),
            out_shape=out_shape,
            compiler_params=limit,
            cost_estimate=light,
            name=name,
        )

    u, query = grouped(
        filter_kernel,
        "short_filters",
        [
            pl.BlockSpec((3, tokens, GROUP), lambda g, here: (0, 0, g)),
            pl.BlockSpec((3, HALO, GROUP), lambda g, here: (0, 0, g)),
            pl.BlockSpec((3, TAPS, GROUP), lambda g, here: (0, 0, here[2] * groups + g)),
        ],
        [series, series],
        [series_shape, series_shape],
        [pltpu.VMEM((3 * TAPS, SUBLANES, LANES), F32), scratch_rows, scratch_rows, scratch_rows],
    )(here, features, halo, conv_weight)

    passed, u = lax.optimization_barrier((rates[2], u))
    rates.append(within_slab(passed, 1))

    left = grouped(
        functools.partial(state_kernel, modes),
        "block_states",
        [series] + [rate_spec] * SLAB,
        [state_spec] * SLAB,
        [state_shape] * SLAB,
        [wide],
    )(here, u, *rates)
    left = [left[0]] + [within_slab(left[d], d) for d in range(1, SLAB)]

    local = grouped(
        functools.partial(local_kernel, modes),
        "local_convolution",
        [series] + [rate_spec] * SLAB,
        series,
        series_shape,
        [wide],
    )(here, u, *rates)
    left, local = lax.optimization_barrier((left, local))

    smem = pl.BlockSpec(memory_space=pltpu.SMEM)
    vmem = pl.BlockSpec(memory_space=pltpu.VMEM)
    slab_left = pl.pallas_call(
        functools.partial(slab_kernel, tokens),
        in_specs=[smem] + [vmem] * (1 + SLAB),
        out_specs=vmem,
        out_shape=state_shape,
        compiler_params=limit,
        cost_estimate=light,
        name="slab_states",
    )(here, rates[0], *left)
    earlier = [from_slab(slab_left, -by) for by in range(1, slabs)]

    incoming = pl.pallas_call(
        functools.partial(incoming_kernel, tokens),
        in_specs=[smem] + [vmem] * (SLAB + slabs),
        out_specs=[vmem] * SLAB,
        out_shape=[state_shape] * SLAB,
        compiler_params=limit,
        cost_estimate=light,
        name="incoming_states",
    )(here, rates[0], *left, *earlier)
    incoming = [incoming[0]] + [within_slab(incoming[d], d) for d in range(1, SLAB)]

    def gated_half(half):
        count = groups // SIDE
        first = half * count

        def shifted(spec):
            return pl.BlockSpec(spec.block_shape, lambda g, here: spec.index_map(g + first, here))

        return grouped(
            functools.partial(gated_kernel, modes),
            "gated_block",
            [shifted(s) for s in [series] * 2 + [rate_spec] * SLAB + [state_spec] * SLAB],
            pl.BlockSpec((tokens, GROUP), lambda g, here: (0, g)),
            jax.ShapeDtypeStruct((tokens, width // SIDE), BF16),
            [wide, scratch_rows],
            count,
        )(here, query, local, *rates, *incoming)

    def project(blocks, sources, picks, share_index, partial=None, halves=(0, 1)):
        scalars = jnp.stack([share_index if share_index is not None else 0, rank ^ 2, rank ^ 3])
        run = depth // SIDE
        wide_share = columns if share_index is None else share
        shape = (len(blocks), len(picks), tokens, share)
        if share_index is None:
            out = jax.ShapeDtypeStruct((tp, *shape), F32)
        else:
            out = jax.ShapeDtypeStruct(shape, BF16)
        return pl.pallas_call(
            functools.partial(
                project_kernel, len(blocks), picks, halves[0] * run, partial is not None
            ),
            in_specs=[smem]
            + [pl.BlockSpec(memory_space=pl.ANY)] * (len(halves) * len(blocks))
            + [pl.BlockSpec(memory_space=pltpu.HBM)] * len(sources)
            + ([vmem] if partial is not None else []),
            out_specs=vmem,
            out_shape=out,
            scratch_shapes=[
                pltpu.VMEM((len(picks), len(halves) * run, wide_share), BF16),
                pltpu.VMEM((len(halves) * len(blocks), tokens, run), BF16),
                pltpu.SemaphoreType.DMA((len(picks) + len(halves) * len(blocks),)),
            ],
            compiler_params=large,
            cost_estimate=light,
            name="project_block",
        )(
            scalars.astype(jnp.int32),
            *[b[h] for b in blocks for h in halves],
            *sources,
            *([partial] if partial is not None else []),
        )

    def project_away(blocks, sources, picks):
        away = project(blocks, sources, picks, 1 - tp_me)
        return away, lax.ppermute(away, "tp", [(0, 1), (1, 0)])

    def project_mine(blocks, sources, picks, after):
        blocks, _ = lax.optimization_barrier((blocks, after))
        return project(blocks, sources, picks, tp_me)

    def total(mine, got):
        return (mine.astype(F32) + got.astype(F32)).astype(BF16)

    half_of = [z * tp // slabs for z in range(slabs)]

    def deliver(classes, by):
        pairs = []
        for i in range(ctx):
            z, rest = divmod(i, SLAB)
            for t in range(tp):
                target = order[(place[z] - by - t * slabs // tp) % slabs] * SLAB + rest
                pairs.append((i * tp + t, target * tp + half_of[z]))
        moved = jnp.where(tp_me == 0, classes[by], classes[(by + slabs // tp) % slabs])
        return lax.ppermute(moved, ("ctx", "tp"), pairs)

    near, far, both = (
        ((0, None), (1, None)),
        ((0, 1), (0, 2)),
        ((0, None), (1, None), (2, 1), (2, 2)),
    )
    blocks = [[gated_half(h) for h in range(SIDE)]]
    kept_parts, got_parts = [], []
    mine, got = None, None
    for step in range(slabs - 1):
        first, second = block = blocks[step]
        if step:
            second, mine = lax.optimization_barrier((second, mine))
            block, _ = lax.optimization_barrier((block, mine))
        blocks.append([ring(first), ring(second)])
        away, coming = project_away([block], [out_weight, beside], near)
        mine = project_mine([block], [out_weight, beside], near, (away, got))
        got = coming
        kept_parts.append(mine)
        got_parts.append(got)
    slab_weights, _ = lax.optimization_barrier((slab_weights, mine))
    away, batch_got = project_away(blocks[: slabs - 1], [slab_weights], far)
    batch_mine = project_mine(blocks[: slabs - 1], [slab_weights], far, away)
    sources = [out_weight, beside, slab_weights]
    head, _ = lax.optimization_barrier((blocks[-1][0], batch_mine))
    partial = project([[head]], sources, both, None, None, (0,))
    tail = blocks[-1][1]
    last_away = project([[None, tail]], sources, both, 1 - tp_me, partial, (1,))
    last_got = lax.ppermute(last_away, "tp", [(0, 1), (1, 0)])
    tail, _ = lax.optimization_barrier((tail, last_away))
    last_mine = project([[None, tail]], sources, both, tp_me, partial, (1,))
    batch_got, got_parts, _ = lax.optimization_barrier((batch_got, got_parts, last_mine))
    near_sums = [total(m, g)[0] for m, g in zip(kept_parts, got_parts)]
    sums = [jnp.concatenate(parts) for parts in zip(near_sums, total(batch_mine, batch_got))]
    late = ((slabs - 1) % (slabs // tp), slabs - 1)
    arrived = {by: [deliver(sums, by)] for by in range(slabs) if by not in late}
    last_got, _ = lax.optimization_barrier((last_got, arrived[0]))
    sums.append(total(last_mine, last_got)[0])
    for by in late:
        arrived[by] = [deliver(sums, by)]
    arrived = [arrived[by] for by in range(slabs)]

    def place_of(z):
        return sum(jnp.where(z == k, place[k], 0) for k in range(slabs))

    kept = slabs // tp
    which = [
        lax.rem(place_of(tp_me * kept + j) - place_of(z_me) + slabs + t * slabs // tp, slabs)
        for j in range(kept)
        for t in range(tp)
    ]
    counts = [len(parts) for parts in arrived]
    return pl.pallas_call(
        functools.partial(place_kernel, kept, counts),
        in_specs=[smem] + [vmem] * sum(counts),
        out_specs=vmem,
        out_shape=jax.ShapeDtypeStruct((tokens, width), BF16),
        compiler_params=limit,
        cost_estimate=light,
        name="place_columns",
    )(jnp.stack([rank, *which]).astype(jnp.int32), *[a for parts in arrived for a in parts])


def solution(mesh):
    in_specs = (
        P(None, "ctx", "tp"),
        P(),
        P(None, ("tp", "ctx")),
        P(None, ("tp", "ctx")),
        P(("tp", "ctx")),
        P("tp", "ctx"),
    )
    out_specs = P("ctx", "tp")
    return jax.shard_map(
        per_device, mesh=mesh, in_specs=in_specs, out_specs=out_specs, check_vma=False
    )
```

```python
import functools

import jax
import jax.numpy as jnp
from jax import lax
from jax.experimental import pallas as pl
from jax.experimental.pallas import tpu as pltpu
from jax.sharding import PartitionSpec as P

LANES = 128
SUBLANES = 8
GROUP = LANES * SUBLANES
HALO = 2
TAPS = 3
SIDE = 2
SLAB = SIDE * SIDE
F32 = jnp.float32
BF16 = jnp.bfloat16


def spread(scratch, halo, block, pitch):
    tokens = block.shape[0]
    for tile in range(SUBLANES):
        lanes = pl.ds(tile * LANES, LANES)
        scratch[pl.ds(tile * pitch + SUBLANES - HALO, HALO), :] = halo[:, lanes].astype(F32)
        scratch[pl.ds(tile * pitch + SUBLANES, tokens), :] = block[:, lanes].astype(F32)


def token(scratch, index, pitch):
    return scratch[pl.ds(index, SUBLANES, stride=pitch), :]


def tree_sum(terms):
    while len(terms) > 1:
        terms = [a + b for a, b in zip(terms[::2], terms[1::2])] + terms[len(terms) & ~1 :]
    return terms[0]


def filter_kernel(here, features, halo, taps, u_ref, query_ref, tap_rows, *rows):
    tokens = features.shape[1]
    pitch = tokens + SUBLANES
    for tile in range(SUBLANES):
        for which in range(3):
            for j in range(TAPS):
                row = which * TAPS + j
                tap_rows[row, tile : tile + 1] = taps[which, j : j + 1, tile * LANES : (tile + 1) * LANES]
    for which in range(3):
        spread(rows[which], halo.at[which], features.at[which], pitch)
    weights = [[tap_rows[which * TAPS + j] for j in range(TAPS)] for which in range(3)]

    def step(index, carry):
        carry = list(carry)
        for inner in range(SUBLANES):
            now = index * SUBLANES + inner
            filtered = []
            for which in range(3):
                last, before = carry[which]
                fresh = token(rows[which], now + SUBLANES, pitch)
                filtered.append(
                    weights[which][0] * fresh + weights[which][1] * last + weights[which][2] * before
                )
                carry[which] = (fresh, last)
            query_ref[0, now] = filtered[0]
            u_ref[0, now] = (filtered[1] * filtered[2]).astype(BF16).astype(F32)
        return tuple(carry)

    start = tuple(
        (token(rows[which], SUBLANES - 1, pitch), token(rows[which], SUBLANES - 2, pitch))
        for which in range(3)
    )
    lax.fori_loop(0, tokens // SUBLANES, step, start)


def registers(refs, rank, wide, first, count):
    pitch = wide.shape[0] // SUBLANES
    each = SUBLANES // SLAB
    for d in range(SLAB):
        for j in range(each):
            start = pl.multiple_of(((d ^ rank) * each + j) * pitch, SUBLANES)
            rows = refs[d][0, first : first + count, j * LANES : (j + 1) * LANES]
            wide[pl.ds(start, count), :] = rows.astype(F32)
    return [wide[pl.ds(m, SUBLANES, stride=pitch), :] for m in range(count)]


def state_kernel(modes, here, u_ref, *refs):
    rates, outs, wide = refs[:SLAB], refs[SLAB : 2 * SLAB], refs[-1]
    rank = here[1]
    tokens = u_ref.shape[1]
    decay = [jnp.exp(-rate) for rate in registers(rates, rank, wide, 0, modes)]

    def step(index, states):
        for inner in range(SUBLANES):
            u = u_ref[0, index * SUBLANES + inner]
            states = tuple(states[m] * decay[m] + u for m in range(modes))
        return states

    zero = tuple(jnp.zeros((SUBLANES, LANES), F32) for _ in range(modes))
    states = lax.fori_loop(0, tokens // SUBLANES, step, zero)
    each = SUBLANES // SLAB
    pitch = wide.shape[0] // SUBLANES
    for m in range(modes):
        wide[pl.ds(m, SUBLANES, stride=pitch), :] = states[m]
    for d in range(SLAB):
        for j in range(each):
            start = pl.multiple_of(((d ^ rank) * each + j) * pitch, SUBLANES)
            outs[d][0, :, j * LANES : (j + 1) * LANES] = wide[pl.ds(start, modes), :].astype(BF16)


def slab_kernel(tokens, here, rates, *refs):
    states, out = refs[:SLAB], refs[SLAB]
    slabs = rates.shape[0]
    for g in range(slabs):
        rate = rates[lax.rem(g - here[0] + slabs, slabs), : states[0].shape[1]]
        total = None
        for d in range(SLAB):
            later = (SLAB - 1 - (here[1] ^ d)).astype(F32) * float(tokens)
            term = jnp.exp(-later * rate) * states[d][g].astype(F32)
            total = term if total is None else total + term
        out[g] = total.astype(BF16)


def incoming_kernel(tokens, here, rates, *refs):
    slabs = rates.shape[0]
    states, earlier, outs = refs[:SLAB], refs[SLAB : SLAB + slabs - 1], refs[SLAB + slabs - 1 :]
    for g in range(slabs):
        rate = rates[lax.rem(g - here[0] + slabs, slabs), : states[0].shape[1]]
        entering = jnp.zeros(rate.shape, F32)
        for k in range(slabs - 1):
            term = jnp.exp(-float(k * SLAB * tokens) * rate) * earlier[k][g].astype(F32)
            entering += jnp.where(here[0] > k, term, jnp.zeros_like(term))
        for d in range(SLAB):
            block = here[1] ^ d
            total = jnp.exp(-(block.astype(F32) * float(tokens)) * rate) * entering
            for e in range(SLAB):
                if e != d:
                    between = block - 1 - (here[1] ^ e)
                    factor = jnp.exp(-(jnp.maximum(between, 0).astype(F32) * float(tokens)) * rate)
                    factor = jnp.where(between >= 0, factor, jnp.zeros_like(factor))
                    total += factor * states[e][g].astype(F32)
            outs[d][g] = total.astype(BF16)


def local_kernel(modes, here, u_ref, *refs):
    rates, y_ref, wide = refs[:SLAB], refs[-2], refs[-1]
    tokens = u_ref.shape[1]
    rate = registers(rates, here[1], wide, 0, modes)
    rest = registers(rates, here[1], wide, modes, modes + 1)
    decay = [jnp.exp(-r) for r in rate]
    weight = [rest[m] * jnp.sqrt(2.0 * rate[m]) for m in range(modes)]
    skip = rest[modes]

    def step(index, states):
        for inner in range(SUBLANES):
            now = index * SUBLANES + inner
            u = u_ref[0, now]
            states = tuple(states[m] * decay[m] + u for m in range(modes))
            y_ref[0, now] = tree_sum([weight[m] * states[m] for m in range(modes)] + [skip * u])
        return states

    zero = tuple(jnp.zeros((SUBLANES, LANES), F32) for _ in range(modes))
    lax.fori_loop(0, tokens // SUBLANES, step, zero)


def gated_kernel(modes, here, query_ref, y_ref, *refs):
    rates, incoming = refs[:SLAB], refs[SLAB : 2 * SLAB]
    out_ref, wide, out_rows = refs[2 * SLAB :]
    tokens = query_ref.shape[1]
    pitch = tokens + SUBLANES
    rate = registers(rates, here[1], wide, 0, modes)
    rest = registers(rates, here[1], wide, modes, modes)
    state = registers(incoming, here[1], wide, 0, modes)
    decay = [jnp.exp(-r) for r in rate]
    weighted = tuple(rest[m] * jnp.sqrt(2.0 * rate[m]) * state[m] for m in range(modes))

    def step(index, weighted):
        for inner in range(SUBLANES):
            now = index * SUBLANES + inner
            weighted = tuple(weighted[m] * decay[m] for m in range(modes))
            long_out = tree_sum([y_ref[0, now], *weighted])
            long_out = long_out.astype(BF16).astype(F32)
            out_rows[pl.ds(now, SUBLANES, stride=pitch), :] = query_ref[0, now] * long_out
        return weighted

    lax.fori_loop(0, tokens // SUBLANES, step, weighted)
    for tile in range(SUBLANES):
        out_ref[:, pl.ds(tile * LANES, LANES)] = out_rows[pl.ds(tile * pitch, tokens), :].astype(BF16)


def project_kernel(count, picks, first, added, here, *refs):
    out_ref, slots, held, sems = refs[-4:]
    depth, share = slots.shape[1:]
    runs = held.shape[0] // count
    blocks, sources = refs[: runs * count], refs[runs * count : -4]
    rows = pl.ds(first, depth)
    columns = pl.ds(pl.multiple_of(here[0] * share, share), share)
    copies = []
    for i, (which, rank) in enumerate(picks):
        source = sources[which] if rank is None else sources[which].at[here[rank]]
        copies.append(pltpu.make_async_copy(source.at[rows, columns], slots.at[i], sems.at[i]))
    fetches = [
        pltpu.make_async_copy(block, held.at[k], sems.at[len(picks) + k]) for k, block in enumerate(blocks)
    ]
    copies[0].start()
    for copy in fetches + copies[1:]:
        copy.start()
    for copy in fetches:
        copy.wait()
    for i in range(len(picks)):
        copies[i].wait()
        for j in range(count):
            total = sources[-1][here[0], j, i] if added else None
            for h in range(runs):
                size = depth // runs
                term = jnp.dot(
                    held[runs * j + h],
                    slots[i, h * size : (h + 1) * size],
                    preferred_element_type=F32,
                )
                total = term if total is None else total + term
            if out_ref.ndim == 4:
                out_ref[j, i] = total.astype(out_ref.dtype)
            else:
                part = out_ref.shape[-1]
                for t in range(out_ref.shape[0]):
                    out_ref[t, j, i] = total[:, t * part : (t + 1) * part].astype(out_ref.dtype)


def place_kernel(kept, counts, here, *refs):
    out_ref = refs[-1]
    share = refs[0].shape[2]
    rank = here[0]
    starts = [sum(counts[:k]) for k in range(len(counts))]
    for slot in range(kept):
        for t in range(SIDE):
            for k, count in enumerate(counts):

                @pl.when(here[1 + slot * SIDE + t] == k)
                def _(slot=slot, t=t, k=k, count=count):
                    for piece in range(SLAB):
                        each = SLAB // count
                        source = refs[starts[k] + piece // each]
                        start = ((slot * SLAB + (rank ^ piece)) * SIDE + t) * share
                        out_ref[:, pl.ds(pl.multiple_of(start, share), share)] = source[piece % each]


def ring_order(count):
    return [0] + list(range(1, count, 2)) + [i for i in range(count - 1, 0, -1) if i % 2 == 0]


def any_size(features, conv_weight, decay_rates, residues, skip_gain, out_weight):
    tokens, width = features.shape[1:]
    ctx, tp = lax.axis_size("ctx"), lax.axis_size("tp")
    me, tp_me = lax.axis_index("ctx"), lax.axis_index("tp")
    halo = lax.ppermute(features[:, tokens - HALO :], "ctx", [(i, i + 1) for i in range(ctx - 1)])
    extended = jnp.concatenate([halo, features], axis=1).astype(F32)
    taps = lax.dynamic_slice_in_dim(conv_weight, tp_me * width, width, 2)
    filtered = sum(taps[:, j, None] * extended[:, HALO - j : HALO - j + tokens] for j in range(TAPS))
    u = (filtered[1] * filtered[2]).astype(BF16).astype(F32)
    rates, weights, skip = (
        lax.all_gather(a, "ctx", axis=a.ndim - 1, tiled=True) for a in (decay_rates, residues, skip_gain)
    )
    weights = weights * jnp.sqrt(2.0 * rates)
    decay = jnp.exp(-rates)
    zero = jnp.zeros(rates.shape, F32)
    left = lax.fori_loop(0, tokens, lambda t, s: s * decay + u[t], zero)
    lefts = lax.all_gather(left, "ctx")
    block_decay = jnp.exp(-float(tokens) * rates)
    entering = lax.fori_loop(0, me, lambda b, s: s * block_decay + lefts[b], zero)

    def advance(states, now):
        states = states * decay + now
        return states, jnp.sum(weights * states, axis=0) + skip * now

    long_out = lax.scan(advance, entering, u)[1].astype(BF16).astype(F32)
    gated = (filtered[0] * long_out).astype(BF16)
    whole = lax.all_gather(gated, "ctx", axis=0, tiled=True)
    partial = jnp.dot(whole, out_weight, preferred_element_type=F32).astype(BF16)
    share = partial.shape[1] // tp
    partial = partial.reshape(ctx * tokens, tp, share).transpose(1, 0, 2)
    partial = lax.all_to_all(partial, "tp", split_axis=0, concat_axis=0, tiled=True)
    summed = jnp.sum(partial.astype(F32), axis=0).astype(BF16).reshape(ctx, tokens, share)
    summed = lax.all_to_all(summed, "ctx", split_axis=0, concat_axis=0, tiled=True)
    placed = lax.all_to_all(
        summed.reshape(tp, ctx // tp, tokens, share), "tp", split_axis=0, concat_axis=0, tiled=True
    )
    return placed.transpose(2, 1, 0, 3).reshape(tokens, width)


def per_device(features, conv_weight, decay_rates, residues, skip_gain, out_weight):
    tokens, width = features.shape[1:]
    modes, owned = decay_rates.shape
    ctx, tp = lax.axis_size("ctx"), lax.axis_size("tp")
    depth, columns = out_weight.shape
    share = columns // tp
    if owned * SLAB != GROUP or tp != SIDE or share % LANES or ctx // SLAB < 4 or ctx // SLAB % 2:
        return any_size(features, conv_weight, decay_rates, residues, skip_gain, out_weight)
    slabs = ctx // SLAB
    groups = width // GROUP
    me, tp_me = lax.axis_index("ctx"), lax.axis_index("tp")
    z_me, rank = me // SLAB, me % SLAB
    order = ring_order(slabs)
    place = [order.index(z) for z in range(slabs)]
    here = jnp.stack([z_me, rank, tp_me]).astype(jnp.int32)

    def within_slab(array, mask):
        return lax.ppermute(array, "ctx", [(i, i ^ mask) for i in range(ctx)])

    def from_slab(array, by):
        return lax.ppermute(array, "ctx", [(i, (i - by * SLAB) % ctx) for i in range(ctx)])

    def ring(array):
        pairs = []
        for i in range(ctx):
            z, rest = divmod(i, SLAB)
            pairs.append((i, order[(place[z] + 1) % slabs] * SLAB + rest))
        return lax.ppermute(array, "ctx", pairs)

    halo = lax.ppermute(
        features[:, tokens - HALO :, :], "ctx", [(i, i + 1) for i in range(ctx - 1)]
    )
    rows = jnp.concatenate([decay_rates, residues, skip_gain[None]], axis=0)
    rows = jnp.stack([rows] + [from_slab(rows, by) for by in range(1, slabs)])
    rows, halo = lax.optimization_barrier((rows, halo))
    rates = [rows, within_slab(rows, 1), within_slab(rows, 2)]

    beside = within_slab(out_weight, 1)
    slab_weights = lax.all_gather(
        out_weight,
        "ctx",
        axis_index_groups=[list(range(z * SLAB, (z + 1) * SLAB)) for z in range(slabs)],
    )

    limit = pltpu.CompilerParams(vmem_limit_bytes=16 * 1024 * 1024)
    large = pltpu.CompilerParams(vmem_limit_bytes=48 * 1024 * 1024)
    light = pl.CostEstimate(flops=1, bytes_accessed=1, transcendentals=0)
    series_shape = jax.ShapeDtypeStruct((groups, tokens, SUBLANES, LANES), F32)
    state_shape = jax.ShapeDtypeStruct((groups, modes, owned), BF16)
    scratch_rows = pltpu.VMEM((SUBLANES * (tokens + SUBLANES), LANES), F32)
    wide = pltpu.VMEM((SUBLANES * (modes + SUBLANES), LANES), F32)
    series = pl.BlockSpec((1, tokens, SUBLANES, LANES), lambda g, here: (g, 0, 0, 0))
    state_spec = pl.BlockSpec((1, modes, owned), lambda g, here: (g, 0, 0))
    rate_spec = pl.BlockSpec(
        (1, 2 * modes + 1, owned), lambda g, here: (lax.rem(g - here[0] + slabs, slabs), 0, 0)
    )

    def grouped(kernel, name, in_specs, out_specs, out_shape, scratch, groups=groups):
        return pl.pallas_call(
            kernel,
            grid_spec=pltpu.PrefetchScalarGridSpec(
                num_scalar_prefetch=1,
                grid=(groups,),
                in_specs=in_specs,
                out_specs=out_specs,
                scratch_shapes=scratch,
            ),
            out_shape=out_shape,
            compiler_params=limit,
            cost_estimate=light,
            name=name,
        )

    u, query = grouped(
        filter_kernel,
        "short_filters",
        [
            pl.BlockSpec((3, tokens, GROUP), lambda g, here: (0, 0, g)),
            pl.BlockSpec((3, HALO, GROUP), lambda g, here: (0, 0, g)),
            pl.BlockSpec((3, TAPS, GROUP), lambda g, here: (0, 0, here[2] * groups + g)),
        ],
        [series, series],
        [series_shape, series_shape],
        [pltpu.VMEM((3 * TAPS, SUBLANES, LANES), F32), scratch_rows, scratch_rows, scratch_rows],
    )(here, features, halo, conv_weight)

    passed, u = lax.optimization_barrier((rates[2], u))
    rates.append(within_slab(passed, 1))

    left = grouped(
        functools.partial(state_kernel, modes),
        "block_states",
        [series] + [rate_spec] * SLAB,
        [state_spec] * SLAB,
        [state_shape] * SLAB,
        [wide],
    )(here, u, *rates)
    left = [left[0]] + [within_slab(left[d], d) for d in range(1, SLAB)]

    local = grouped(
        functools.partial(local_kernel, modes),
        "local_convolution",
        [series] + [rate_spec] * SLAB,
        series,
        series_shape,
        [wide],
    )(here, u, *rates)
    left, local = lax.optimization_barrier((left, local))

    smem = pl.BlockSpec(memory_space=pltpu.SMEM)
    vmem = pl.BlockSpec(memory_space=pltpu.VMEM)
    slab_left = pl.pallas_call(
        functools.partial(slab_kernel, tokens),
        in_specs=[smem] + [vmem] * (1 + SLAB),
        out_specs=vmem,
        out_shape=state_shape,
        compiler_params=limit,
        cost_estimate=light,
        name="slab_states",
    )(here, rates[0], *left)
    earlier = [from_slab(slab_left, -by) for by in range(1, slabs)]

    incoming = pl.pallas_call(
        functools.partial(incoming_kernel, tokens),
        in_specs=[smem] + [vmem] * (SLAB + slabs),
        out_specs=[vmem] * SLAB,
        out_shape=[state_shape] * SLAB,
        compiler_params=limit,
        cost_estimate=light,
        name="incoming_states",
    )(here, rates[0], *left, *earlier)
    incoming = [incoming[0]] + [within_slab(incoming[d], d) for d in range(1, SLAB)]

    def gated_half(half):
        count = groups // SIDE
        first = half * count

        def shifted(spec):
            return pl.BlockSpec(spec.block_shape, lambda g, here: spec.index_map(g + first, here))

        return grouped(
            functools.partial(gated_kernel, modes),
            "gated_block",
            [shifted(s) for s in [series] * 2 + [rate_spec] * SLAB + [state_spec] * SLAB],
            pl.BlockSpec((tokens, GROUP), lambda g, here: (0, g)),
            jax.ShapeDtypeStruct((tokens, width // SIDE), BF16),
            [wide, scratch_rows],
            count,
        )(here, query, local, *rates, *incoming)

    def project(blocks, sources, picks, share_index, partial=None, halves=(0, 1)):
        scalars = jnp.stack([share_index if share_index is not None else 0, rank ^ 2, rank ^ 3])
        run = depth // SIDE
        wide_share = columns if share_index is None else share
        shape = (len(blocks), len(picks), tokens, share)
        if share_index is None:
            out = jax.ShapeDtypeStruct((tp, *shape), F32)
        else:
            out = jax.ShapeDtypeStruct(shape, BF16)
        return pl.pallas_call(
            functools.partial(
                project_kernel, len(blocks), picks, halves[0] * run, partial is not None
            ),
            in_specs=[smem]
            + [pl.BlockSpec(memory_space=pl.ANY)] * (len(halves) * len(blocks))
            + [pl.BlockSpec(memory_space=pltpu.HBM)] * len(sources)
            + ([vmem] if partial is not None else []),
            out_specs=vmem,
            out_shape=out,
            scratch_shapes=[
                pltpu.VMEM((len(picks), len(halves) * run, wide_share), BF16),
                pltpu.VMEM((len(halves) * len(blocks), tokens, run), BF16),
                pltpu.SemaphoreType.DMA((len(picks) + len(halves) * len(blocks),)),
            ],
            compiler_params=large,
            cost_estimate=light,
            name="project_block",
        )(
            scalars.astype(jnp.int32),
            *[b[h] for b in blocks for h in halves],
            *sources,
            *([partial] if partial is not None else []),
        )

    def project_away(blocks, sources, picks):
        away = project(blocks, sources, picks, 1 - tp_me)
        return away, lax.ppermute(away, "tp", [(0, 1), (1, 0)])

    def project_mine(blocks, sources, picks, after):
        blocks, _ = lax.optimization_barrier((blocks, after))
        return project(blocks, sources, picks, tp_me)

    def total(mine, got):
        return (mine.astype(F32) + got.astype(F32)).astype(BF16)

    half_of = [z * tp // slabs for z in range(slabs)]

    def deliver(classes, by):
        pairs = []
        for i in range(ctx):
            z, rest = divmod(i, SLAB)
            for t in range(tp):
                target = order[(place[z] - by - t * slabs // tp) % slabs] * SLAB + rest
                pairs.append((i * tp + t, target * tp + half_of[z]))
        moved = jnp.where(tp_me == 0, classes[by], classes[(by + slabs // tp) % slabs])
        return lax.ppermute(moved, ("ctx", "tp"), pairs)

    near, far, both = (
        ((0, None), (1, None)),
        ((0, 1), (0, 2)),
        ((0, None), (1, None), (2, 1), (2, 2)),
    )
    blocks = [[gated_half(h) for h in range(SIDE)]]
    kept_parts, got_parts = [], []
    mine, got = None, None
    for step in range(slabs - 1):
        first, second = block = blocks[step]
        if step:
            second, mine = lax.optimization_barrier((second, mine))
            block, _ = lax.optimization_barrier((block, mine))
        blocks.append([ring(first), ring(second)])
        away, coming = project_away([block], [out_weight, beside], near)
        mine = project_mine([block], [out_weight, beside], near, (away, got))
        got = coming
        kept_parts.append(mine)
        got_parts.append(got)
    slab_weights, _ = lax.optimization_barrier((slab_weights, mine))
    away, batch_got = project_away(blocks[: slabs - 1], [slab_weights], far)
    batch_mine = project_mine(blocks[: slabs - 1], [slab_weights], far, away)
    sources = [out_weight, beside, slab_weights]
    head, _ = lax.optimization_barrier((blocks[-1][0], batch_mine))
    partial = project([[head]], sources, both, None, None, (0,))
    tail = blocks[-1][1]
    last_away = project([[None, tail]], sources, both, 1 - tp_me, partial, (1,))
    last_got = lax.ppermute(last_away, "tp", [(0, 1), (1, 0)])
    batch_got, got_parts, _ = lax.optimization_barrier((batch_got, got_parts, last_away))
    near_sums = [total(m, g)[0] for m, g in zip(kept_parts, got_parts)]
    sums = [jnp.concatenate(parts) for parts in zip(near_sums, total(batch_mine, batch_got))]
    late = ((slabs - 1) % (slabs // tp), slabs - 1)
    arrived = {by: [deliver(sums, by)] for by in range(slabs) if by not in late}
    tail, _ = lax.optimization_barrier((tail, last_away))
    last_mine = project([[None, tail]], sources, both, tp_me, partial, (1,))
    sums.append(total(last_mine, last_got)[0])
    for by in late:
        arrived[by] = [deliver(sums, by)]
    arrived = [arrived[by] for by in range(slabs)]

    def place_of(z):
        return sum(jnp.where(z == k, place[k], 0) for k in range(slabs))

    kept = slabs // tp
    which = [
        lax.rem(place_of(tp_me * kept + j) - place_of(z_me) + slabs + t * slabs // tp, slabs)
        for j in range(kept)
        for t in range(tp)
    ]
    counts = [len(parts) for parts in arrived]
    return pl.pallas_call(
        functools.partial(place_kernel, kept, counts),
        in_specs=[smem] + [vmem] * sum(counts),
        out_specs=vmem,
        out_shape=jax.ShapeDtypeStruct((tokens, width), BF16),
        compiler_params=limit,
        cost_estimate=light,
        name="place_columns",
    )(jnp.stack([rank, *which]).astype(jnp.int32), *[a for parts in arrived for a in parts])


def solution(mesh):
    in_specs = (
        P(None, "ctx", "tp"),
        P(),
        P(None, ("tp", "ctx")),
        P(None, ("tp", "ctx")),
        P(("tp", "ctx")),
        P("tp", "ctx"),
    )
    out_specs = P("ctx", "tp")
    return jax.shard_map(
        per_device, mesh=mesh, in_specs=in_specs, out_specs=out_specs, check_vma=False
    )
```
